128 devices in a mesh: east: 4 (over y), north: 16 (over x, z), layer: 2 (over core).
Axes of the slice: x: 4, y: 4, z: 4, core: 2. Of those that a mesh axis runs over, the one named last changes fastest.
Arguments:
- head_old: float32 [8, 2048, 1024], P('layer', 'north', 'east'), may hold values from -6 to 6
- head_target: float32 [8, 2048, 1024], P('layer', 'north', 'east'), may hold values from -12 to 12
- conductivity_east: bfloat16 [8, 2048, 1024], P('layer', 'north', 'east'), may hold values from 0.05 to 6, as said below
- conductivity_north: bfloat16 [8, 2048, 1024], P('layer', 'north', 'east'), may hold values from 0.099609375 to 2
- conductivity_vertical: bfloat16 [8, 2048, 1024], P('layer', 'north', 'east'), may hold values from 0.019897461 to 0.5
- storage: bfloat16 [8, 2048, 1024], P('layer', 'north', 'east'), may hold values from 0.19921875 to 2
- well_east: int32 [3000], replicated, may hold values from 0 to 1023
- well_north: int32 [3000], replicated, may hold values from 0 to 2047
- screen_top: int32 [3000], replicated, may hold values from 0 to 3
- screen_bottom: int32 [3000], replicated, may hold values from 3 to 7
- tariff_band: int32 [3000], replicated, may hold values from 0 to 3
- pump_rates: float32 [3000], replicated, may hold values from 0.2 to 2
- ground_level: float32 [3000], replicated, may hold values from 2 to 6
- band_prices: float32 [4], replicated, may hold values from 0.5 to 4
Outputs:
- head_new: float32 [8, 2048, 1024], P('layer', 'north', 'east')
- adjoint_head: float32 [8, 2048, 1024], P('layer', 'north', 'east')
- rate_gradient: float32 [3000], replicated
- pumping_cost: float32 [], replicated
- misfit: float32 [], replicated
The draws below stay inside these ranges and needn't reach their ends.
Inputs may be any that keep to these rules, and one draw needn't show every extreme that they name: Every screen spans at least one layer: screen_top <= screen_bottom for each well. `conductivity_east`: conductivity along x, positive.
All inputs are finite; a program needn't handle non-finite values.
Results may differ from the reference program's by a relative error of at most 0.0003.
Values may be sent and summed in bfloat16 or wider, within the bound.
A program may use at most 128 MiB of HBM per device.

```python
import math
import jax
import jax.numpy as jnp

WELLS = 3000
BANDS = 4
SWEEPS = 3
NZ = 8
NY = 2048
NX = 1024


def draw_conductivity_east(key, part):
    key = jax.random.fold_in(key, 11)
    depth = jnp.arange(NZ, dtype=jnp.float32)[:, None, None] / (NZ - 1)
    base = jnp.exp(jax.random.uniform(key, (NZ, NY, NX), jnp.float32, math.log(0.1), 0.0))
    return (base * jnp.power(3.0, depth)).astype(jnp.bfloat16)


def draw_head_target(key, part):
    key = jax.random.fold_in(key, 23)
    north_pos = jnp.arange(NY, dtype=jnp.float32)[None, :, None] / (NY - 1)
    base = jax.random.truncated_normal(key, -4.0, 4.0, (NZ, NY, NX), jnp.float32)
    return base * jnp.power(3.0, north_pos)


def plant(result, rng, low, top_value):
    longest = result.shape.index(max(result.shape))
    spots = []
    for shift in (0, 1):
        where = [jax.random.randint(jax.random.fold_in(rng, axis), (), 0, length) for axis, length in enumerate(result.shape)]
        where[longest] = (where[longest] + shift) % result.shape[longest]
        spots.append(tuple(where))
    return result.at[spots[0]].set(low).at[spots[1]].set(top_value)


def levels(stream_key, extent, cuts, low, largest):
    level = 1.0
    for dim, blocks in cuts:
        steps = jax.random.uniform(jax.random.fold_in(jax.random.fold_in(stream_key, 6), dim), (blocks,), jnp.float32, low / len(cuts), largest / len(cuts))
        level = level * jnp.repeat(jnp.exp(steps), extent[dim] // blocks).reshape((-1,) + (1,) * (len(extent) - 1 - dim))
    return level


def noise(key, extent, scale, bound, shards=(), held_as=jnp.bfloat16):
    drawn = scale * jax.random.normal(key, extent, jnp.float32)
    if shards:
        drawn = drawn * levels(key, extent, shards, -0.22, 0.18)
    return jnp.clip(drawn, -bound, bound).astype(held_as)


def setup_inputs(seed: int = 0) -> dict:
    key_list = jax.random.split(jax.random.key(seed), 15)
    head_old = noise(key_list[0], (NZ, NY, NX), 1.0, 6.0, ((0, 2), (1, 16), (2, 4)), jnp.float32)
    head_target = draw_head_target(jax.random.fold_in(key_list[14], 71), 0)
    conductivity_east = draw_conductivity_east(jax.random.fold_in(key_list[14], 71), 0)
    conductivity_north = jnp.clip(jnp.exp(math.log(2.0) - 2.9996462 * jax.random.uniform(key_list[3], (NZ, NY, NX), jnp.float32) ** levels(key_list[3], (NZ, NY, NX), ((0, 2), (1, 16), (2, 4)), -0.2, 0.2)), 0.099609375, 2.0).astype(jnp.bfloat16)
    conductivity_vertical = jnp.clip(jnp.exp(math.log(0.5) - 3.224016 * jax.random.uniform(key_list[4], (NZ, NY, NX), jnp.float32) ** levels(key_list[4], (NZ, NY, NX), ((0, 2), (1, 16), (2, 4)), -0.2, 0.2)), 0.019897461, 0.5).astype(jnp.bfloat16)
    storage = jnp.clip(jnp.exp(math.log(2.0) - 2.306499 * jax.random.uniform(key_list[5], (NZ, NY, NX), jnp.float32) ** levels(key_list[5], (NZ, NY, NX), ((0, 2), (1, 16), (2, 4)), -0.2, 0.2)), 0.19921875, 2.0).astype(jnp.bfloat16)
    well_east = plant(jax.random.randint(key_list[6], (WELLS,), 0, NX), jax.random.fold_in(key_list[6], 1), 0, NX - 1).astype(jnp.int32)
    well_north = plant(jax.random.randint(key_list[7], (WELLS,), 0, NY), jax.random.fold_in(key_list[7], 1), 0, NY - 1).astype(jnp.int32)
    screen_top = plant(jax.random.randint(key_list[8], (WELLS,), 0, NZ // 2), jax.random.fold_in(key_list[8], 1), 0, (NZ // 2) - 1).astype(jnp.int32)
    screen_bottom = plant(jax.random.randint(key_list[9], (WELLS,), NZ // 2 - 1, NZ), jax.random.fold_in(key_list[9], 1), NZ // 2 - 1, NZ - 1).astype(jnp.int32)
    tariff_band = plant(jax.random.randint(key_list[10], (WELLS,), 0, BANDS), jax.random.fold_in(key_list[10], 1), 0, BANDS - 1).astype(jnp.int32)
    pump_rates = jnp.clip(jnp.exp(jax.random.uniform(key_list[11], (WELLS,), jnp.float32, math.log(0.2), math.log(2.0))), 0.2, 2.0)
    ground_level = jnp.clip(jax.random.uniform(key_list[12], (WELLS,), jnp.float32, 2.0, 6.0), 2.0, 6.0)
    band_prices = jnp.clip(jnp.exp(jax.random.uniform(key_list[13], (BANDS,), jnp.float32, math.log(0.5), math.log(4.0))), 0.5, 4.0)
    return dict(head_old=head_old, head_target=head_target, conductivity_east=conductivity_east, conductivity_north=conductivity_north, conductivity_vertical=conductivity_vertical, storage=storage, well_east=well_east, well_north=well_north, screen_top=screen_top, screen_bottom=screen_bottom, tariff_band=tariff_band, pump_rates=pump_rates, ground_level=ground_level, band_prices=band_prices)


CENTRE = 1.0
HALF_WIDTH = 0.95


def harmonic(first, second):
    return 2.0 * first * second / (first + second)


def apply_operator(padded, storage_part, face_east, face_north, face_up):
    center = padded[1:-1, 1:-1, 1:-1]
    step_east = padded[1:-1, 1:-1, 1:] - padded[1:-1, 1:-1, :-1]
    step_north = padded[1:-1, 1:, 1:-1] - padded[1:-1, :-1, 1:-1]
    step_up = padded[1:, 1:-1, 1:-1] - padded[:-1, 1:-1, 1:-1]
    flux_east = face_east * step_east
    flux_north = face_north * step_north
    flux_up = face_up * step_up
    total = storage_part * center + (flux_east[:, :, :-1] - flux_east[:, :, 1:])
    total = total + (flux_north[:, :-1] - flux_north[:, 1:])
    return total + (flux_up[:-1] - flux_up[1:])


def diagonal_of(storage_part, face_east, face_north, face_up):
    total = storage_part + face_east[:, :, :-1] + face_east[:, :, 1:]
    total = total + face_north[:, :-1] + face_north[:, 1:]
    return total + face_up[:-1] + face_up[1:]


def chebyshev(start, rhs, operate, trim, precondition):
    if start is None:
        residual = rhs
    else:
        residual = trim(rhs) - operate(start)
    direction = precondition(residual) / CENTRE
    if start is None:
        iterate = direction
    else:
        iterate = trim(start) + direction
    sigma = CENTRE / HALF_WIDTH
    factor = 1.0 / sigma
    for sweep_index in range(SWEEPS - 1):
        residual = trim(residual) - operate(direction)
        factor_next = 1.0 / (2.0 * sigma - factor)
        direction = (factor_next * factor) * trim(direction) + (2.0 * factor_next / HALF_WIDTH) * precondition(residual)
        iterate = trim(iterate) + direction
        factor = factor_next
    return iterate


def reference(head_old, head_target, conductivity_east, conductivity_north, conductivity_vertical, storage, well_east, well_north, screen_top, screen_bottom, tariff_band, pump_rates, ground_level, band_prices):
    k_east = conductivity_east.astype(jnp.float32)
    k_north = conductivity_north.astype(jnp.float32)
    k_up = conductivity_vertical.astype(jnp.float32)
    stored = storage.astype(jnp.float32)
    face_east = jnp.pad(harmonic(k_east[:, :, :-1], k_east[:, :, 1:]), ((0, 0), (0, 0), (1, 1)))
    face_north = jnp.pad(harmonic(k_north[:, :-1], k_north[:, 1:]), ((0, 0), (1, 1), (0, 0)))
    face_up = jnp.pad(harmonic(k_up[:-1], k_up[1:]), ((1, 1), (0, 0), (0, 0)))
    inverse = 1.0 / diagonal_of(stored, face_east, face_north, face_up)

    def operate(field):
        return apply_operator(jnp.pad(field, 1), stored, face_east, face_north, face_up)

    def keep_whole(field):
        return field

    def precondition(residual):
        return inverse * residual

    cells = (well_north * NX + well_east).astype(jnp.int32)
    depth = jnp.arange(NZ, dtype=jnp.int32)[:, None]
    screened = ((depth >= screen_top[None, :]) & (depth <= screen_bottom[None, :])).astype(jnp.float32)
    weights = k_east.reshape(NZ, NY * NX)[:, cells] * screened
    totals = jnp.sum(weights, axis=0)
    shares = weights / totals[None, :]
    source = jnp.zeros((NZ, NY * NX), jnp.float32).at[:, cells].add(pump_rates[None, :] * shares).reshape(NZ, NY, NX)
    head_new = chebyshev(head_old, stored * head_old - source, operate, keep_whole, precondition)
    departure = head_new - head_target
    misfit = jnp.sum(departure * departure) / float(NZ * NY * NX)
    head_screen = jnp.sum(shares * head_new.reshape(NZ, NY * NX)[:, cells], axis=0)
    lift = ground_level - head_screen
    prices = band_prices[tariff_band]
    load = departure.reshape(NZ, NY * NX).at[:, cells].add(-(prices * pump_rates)[None, :] * shares).reshape(NZ, NY, NX)
    adjoint_head = chebyshev(None, load, operate, keep_whole, precondition)
    adjoint_screen = jnp.sum(shares * adjoint_head.reshape(NZ, NY * NX)[:, cells], axis=0)
    rate_gradient = prices * lift - adjoint_screen
    pumping_cost = jnp.sum(prices * pump_rates * lift)
    return head_new, adjoint_head, rate_gradient, pumping_cost, misfit
```

```python
import functools

import jax
import jax.numpy as jnp
from jax import lax
from jax.experimental import pallas as pl
from jax.experimental.pallas import tpu as pltpu
from jax.sharding import PartitionSpec as P

MESH = pl.DeviceIdType.MESH
F32 = jnp.float32
BF16 = jnp.bfloat16

SWEEPS = 3
CENTRE = 1.0
HALF_WIDTH = 0.95

HALO = 8
REACH = 5
LANES = 128
SLOTS = 128


def steps_of():
    sigma = CENTRE / HALF_WIDTH
    factor = 1.0 / sigma
    found = []
    for _ in range(SWEEPS - 1):
        after = 1.0 / (2.0 * sigma - factor)
        found.append((after * factor, 2.0 * after / HALF_WIDTH))
        factor = after
    return found


def iota(shape, dim):
    return lax.broadcasted_iota(jnp.int32, shape, dim)


def roll(value, shift, dim):
    shift = shift % value.shape[dim]
    return pltpu.roll(value, shift, dim) if shift else value


def exchange(
    sizes,
    head, target, k_east, k_north, k_up, stored,
    p_head, p_target, p_east, p_north, p_up, p_stored,
    nf, nb, ef, eb, cf, cb,
    p_nf, p_nb, p_ef, p_eb, p_cf, p_cb,
    s_nf, s_nb, s_ef, s_eb, s_cf, s_cb,
    send_sem, recv_sem,
):
    n_east, n_north = sizes
    depth, rows, cols = head.shape
    me_e, me_n, me_l = lax.axis_index("east"), lax.axis_index("north"), lax.axis_index("layer")

    def east_of(side):
        return lax.rem(me_e + (n_east - 1 if side == 0 else 1), n_east)

    def north_of(side):
        return lax.rem(me_n + (n_north - 1 if side == 0 else 1), n_north)

    partner = (me_e, me_n, 1 - me_l)
    to_north = [(me_e, north_of(s), me_l) for s in (0, 1)]
    to_east = [(east_of(s), me_n, me_l) for s in (0, 1)]
    to_corner = [(east_of(c), north_of(r), me_l) for r in (0, 1) for c in (0, 1)]

    barrier = pltpu.get_barrier_semaphore()
    for device in [partner] + to_north + to_east + to_corner:
        pl.semaphore_signal(barrier, inc=1, device_id=device, device_id_type=MESH)

    lane = iota((8, LANES), 1)
    sub = iota((8, LANES), 0)
    group = lane // HALO
    wide_sub = iota((8, cols), 0)
    coefs = (k_east, k_north, k_up, stored)
    last = cols - LANES

    def pack(z, carry):
        for side in (0, 1):
            c0 = last * side
            kept = jnp.zeros((8, LANES), F32)
            fields = [jnp.zeros((8, LANES), F32) for _ in coefs]
            for pair in range(rows // 16):
                tiles = [
                    ref[z, pl.ds(16 * pair, 16), pl.ds(c0, LANES)].astype(F32) for ref in coefs
                ]
                for half in (0, 1):
                    j = 2 * pair + half
                    shift = HALO * j - (LANES - HALO) * side
                    h = head[z, pl.ds(8 * j, 8), pl.ds(c0, LANES)]
                    t = target[z, pl.ds(8 * j, 8), pl.ds(c0, LANES)]
                    if side == 0:
                        both = jnp.where(lane >= HALO - 2, roll(t, HALO - 2, 1), h)
                    else:
                        both = jnp.where(lane < LANES - HALO + 2, roll(t, 2 - HALO, 1), h)
                    here = group == j
                    kept = jnp.where(here, roll(both, shift, 1), kept)
                    for a in range(4):
                        piece = tiles[a][8 * half:8 * half + 8]
                        fields[a] = jnp.where(here, roll(piece, shift, 1), fields[a])
            s_ef[side, z] = kept
            s_eb[side, z, pl.ds(0, 16)] = jnp.concatenate(fields[:2], axis=0).astype(BF16)
            s_eb[side, z, pl.ds(16, 16)] = jnp.concatenate(fields[2:], axis=0).astype(BF16)
            r0 = (rows - 8) * side
            h = head[z, pl.ds(r0, 8), :]
            t = target[z, pl.ds(r0, 8), :]
            if side == 0:
                both = jnp.where(wide_sub >= HALO - 2, roll(t, HALO - 2, 0), h)
            else:
                both = jnp.where(wide_sub < 2, roll(t, 2, 0), h)
            s_nf[side, z] = both
            edge = [
                ref[z, pl.ds((rows - 16) * side, 16), :].astype(F32)[8 * side:8 * side + 8]
                for ref in coefs
            ]
            s_nb[side, z, pl.ds(0, 16)] = jnp.concatenate(edge[:2], axis=0).astype(BF16)
            s_nb[side, z, pl.ds(16, 16)] = jnp.concatenate(edge[2:], axis=0).astype(BF16)
        return carry

    lax.fori_loop(0, depth, pack, 0)

    for r in (0, 1):
        for c in (0, 1):
            c0 = last * c
            kept = jnp.zeros((8, LANES), F32)
            mixed = jnp.zeros((8, LANES), F32)
            for z in range(depth):
                both = s_nf[r, z, :, pl.ds(c0, LANES)]
                kept = jnp.where(group == z, roll(both, HALO * z - (LANES - HALO) * c, 1), kept)
                for half in (0, 1):
                    two = s_nb[r, z, pl.ds(16 * half, 16), pl.ds(c0, LANES)].astype(F32)
                    for k in (0, 1):
                        slot = (2 * half + k) * depth + z
                        moved = roll(two[8 * k:8 * k + 8], HALO * slot - (LANES - HALO) * c, 1)
                        mixed = jnp.where(group == slot, moved, mixed)
            s_cf[2 * r + c] = kept
            s_cb[2 * r + c] = jnp.concatenate([mixed, mixed], axis=0).astype(BF16)

    pl.semaphore_wait(barrier, 9)

    count = [0]

    def send(src, dst, device):
        copy = pltpu.make_async_remote_copy(
            src_ref=src,
            dst_ref=dst,
            send_sem=send_sem.at[count[0]],
            recv_sem=recv_sem.at[count[0]],
            device_id=device,
            device_id_type=MESH,
        )
        count[0] += 1
        copy.start()
        return copy

    halos = []
    for side in (0, 1):
        halos.append(send(s_nb.at[side], nb.at[side], to_north[side]))
        halos.append(send(s_nf.at[side], nf.at[side], to_north[side]))
    for side in (0, 1):
        halos.append(send(s_eb.at[side], eb.at[side], to_east[side]))
        halos.append(send(s_ef.at[side], ef.at[side], to_east[side]))
    for d in range(4):
        halos.append(send(s_cb.at[d], cb.at[d], to_corner[d]))
        halos.append(send(s_cf.at[d], cf.at[d], to_corner[d]))
    blocks = [
        send(src, dst, partner)
        for src, dst in (
            (head, p_head), (target, p_target), (k_east, p_east),
            (k_north, p_north), (k_up, p_up), (stored, p_stored),
        )
    ]
    for copy in halos:
        copy.wait_recv()
    forwards = [
        send(src, dst, partner)
        for src, dst in (
            (nf, p_nf), (nb, p_nb), (ef, p_ef), (eb, p_eb), (cf, p_cf), (cb, p_cb),
        )
    ]
    for copy in halos:
        copy.wait_send()
    for copy in blocks + forwards:
        copy.wait()


def run_exchange(sizes, head, target, k_east, k_north, k_up, stored):
    depth, rows, cols = head.shape
    fields = [head, target, k_east, k_north, k_up, stored]
    blocks = [jax.ShapeDtypeStruct(x.shape, x.dtype) for x in fields]
    halos = [
        ((2, depth, 8, cols), F32),
        ((2, depth, 32, cols), BF16),
        ((2, depth, 8, LANES), F32),
        ((2, depth, 32, LANES), BF16),
        ((4, 8, LANES), F32),
        ((4, 16, LANES), BF16),
    ]
    shaped = [jax.ShapeDtypeStruct(s, d) for s, d in halos]
    outs = blocks + shaped + shaped
    copies = 16 + 6 + 6
    return pl.pallas_call(
        functools.partial(exchange, sizes),
        out_shape=outs,
        in_specs=[pl.BlockSpec(memory_space=pltpu.VMEM)] * 6,
        out_specs=[pl.BlockSpec(memory_space=pl.ANY)] * len(outs),
        scratch_shapes=[pltpu.VMEM(s, d) for s, d in halos]
        + [pltpu.SemaphoreType.DMA((copies,)), pltpu.SemaphoreType.DMA((copies,))],
        compiler_params=pltpu.CompilerParams(
            collective_id=0, has_side_effects=True, vmem_limit_bytes=32 * 1024 * 1024
        ),
        name="exchange",
    )(*fields)


def split(value, parts):
    found = []
    for _ in range(parts):
        top = value.astype(BF16)
        found.append(top)
        value = value - top.astype(F32)
    return found


def dot(a, b, dims):
    return lax.dot_general(a, b, (dims, ((), ())), preferred_element_type=F32)


NN = ((1,), (0,))
NT = ((1,), (1,))


def reciprocal(x):
    first = pl.reciprocal(x, approx=True)
    second = first * (2.0 - x * first)
    return second * (2.0 - x * second)


def solve(
    sizes,
    head, target, k_east, k_north, k_up, stored,
    p_head, p_target, p_east, p_north, p_up, p_stored,
    nf, nb, ef, eb, cf, cb,
    p_nf, p_nb, p_ef, p_eb, p_cf, p_cb,
    wells,
    head_new, adjoint, parts,
    hx, tx, ke, kn, kv, st, fe, fn, fu, inv, src, lw, d0, d1, s1, pt, comps, shares,
):
    n_east, n_north = sizes
    depth, rows, cols = head.shape
    layers, ext_rows, ext_cols = hx.shape
    chunks_of_rows = ext_rows // 8
    n_wells = wells.shape[1]
    groups = n_wells // LANES
    me_e, me_n, me_l = lax.axis_index("east"), lax.axis_index("north"), lax.axis_index("layer")

    lane = iota((8, LANES), 1)
    low_half = lane < LANES // 2
    extra = pl.ds(cols, LANES)
    inside_cols = pl.ds(0, cols)

    for own, src_refs in (
        (True, (head, target, k_east, k_north, k_up, stored, nf, nb, ef, eb, cf, cb)),
        (False, (p_head, p_target, p_east, p_north, p_up, p_stored, p_nf, p_nb, p_ef, p_eb, p_cf, p_cb)),
    ):
        b_head, b_target, b_e, b_n, b_u, b_s, bnf, bnb, bef, beb, bcf, bcb = src_refs
        base = depth * (me_l if own else 1 - me_l)

        def fill(z, carry):
            zz = base + z
            inner = pl.ds(8, rows)
            hx[zz, inner, inside_cols] = b_head[z]
            tx[zz, inner, inside_cols] = b_target[z]
            for a, (dst, ref) in enumerate(((ke, b_e), (kn, b_n), (kv, b_u), (st, b_s))):
                dst[zz, inner, inside_cols] = ref[z].astype(F32)
            for side, r0 in ((0, rows + 8), (1, 0)):
                both = bnf[side, z]
                hx[zz, pl.ds(r0, 8), inside_cols] = both
                tx[zz, pl.ds(r0, 8), inside_cols] = roll(both, 2 if side == 0 else 6, 0)
                for half, pair in ((0, (ke, kn)), (1, (kv, st))):
                    two = bnb[side, z, pl.ds(16 * half, 16)].astype(F32)
                    pair[0][zz, pl.ds(r0, 8), inside_cols] = two[:8]
                    pair[1][zz, pl.ds(r0, 8), inside_cols] = two[8:]
            right, left = bef[0, z], bef[1, z]
            for j in range(rows // 8):
                both = jnp.where(
                    low_half, roll(right, -HALO * j, 1), roll(left, LANES - HALO - HALO * j, 1)
                )
                hx[zz, pl.ds(8 + 8 * j, 8), extra] = both
                tx[zz, pl.ds(8 + 8 * j, 8), extra] = jnp.where(
                    low_half, roll(both, 2 - HALO, 1), roll(both, HALO - 2, 1)
                )
            for half, pair in ((0, (ke, kn)), (1, (kv, st))):
                rights = beb[0, z, pl.ds(16 * half, 16)].astype(F32)
                lefts = beb[1, z, pl.ds(16 * half, 16)].astype(F32)
                for k in (0, 1):
                    right, left = rights[8 * k:8 * k + 8], lefts[8 * k:8 * k + 8]
                    for j in range(rows // 8):
                        pair[k][zz, pl.ds(8 + 8 * j, 8), extra] = jnp.where(
                            low_half,
                            roll(right, -HALO * j, 1),
                            roll(left, LANES - HALO - HALO * j, 1),
                        )
            return carry

        lax.fori_loop(0, depth, fill, 0)
        for r, r0 in ((0, rows + 8), (1, 0)):
            at = pl.ds(r0, 8)
            right, left = bcf[2 * r], bcf[2 * r + 1]
            rights, lefts = bcb[2 * r].astype(F32)[:8], bcb[2 * r + 1].astype(F32)[:8]
            for z in range(depth):
                both = jnp.where(
                    low_half, roll(right, -HALO * z, 1), roll(left, LANES - HALO - HALO * z, 1)
                )
                hx[base + z, at, extra] = both
                tx[base + z, at, extra] = roll(both, 2 if r == 0 else 6, 0)
                for a, dst in enumerate((ke, kn, kv, st)):
                    slot = a * depth + z
                    dst[base + z, at, extra] = jnp.where(
                        low_half,
                        roll(rights, -HALO * slot, 1),
                        roll(lefts, LANES - HALO - HALO * slot, 1),
                    )

    at_east = wells[0:1, :] - (me_e * cols).astype(F32)
    at_north = wells[1:2, :] - (me_n * rows).astype(F32)
    near = (
        (at_east >= -REACH) & (at_east < cols + REACH)
        & (at_north >= -REACH) & (at_north < rows + REACH)
    )
    mine = (at_east >= 0) & (at_east < cols) & (at_north >= 0) & (at_north < rows)
    near_row = jnp.where(near, 1.0, 0.0)
    near_tile = jnp.concatenate(
        [near_row[:, LANES * k:LANES * (k + 1)] for k in range(groups)], axis=0
    )
    before = (iota((LANES, LANES), 0) < iota((LANES, LANES), 1)).astype(F32).astype(BF16)
    in_row = dot(near_tile.astype(BF16), before, NN)
    above = (iota((groups, groups), 1) < iota((groups, groups), 0)).astype(F32).astype(BF16)
    rows_above = jnp.sum(dot(above, near_tile.astype(BF16), NN), axis=1, keepdims=True)
    rank = jnp.where(near_tile > 0, in_row + rows_above, -1.0)
    total_near = jnp.sum(near_tile).astype(jnp.int32)
    chunks = (total_near + (SLOTS - 1)) // SLOTS

    place = jnp.concatenate(
        [
            jnp.where(at_east < 0, at_east + ext_cols, at_east),
            at_north + 8.0,
            wells[2:7, :],
            jnp.where(mine, 1.0, 0.0),
        ],
        axis=0,
    )
    place_parts = jnp.concatenate([p.astype(F32) for p in split(place, 3)], axis=0).astype(BF16)
    slot_of = iota((SLOTS, LANES), 0).astype(F32)

    def build_places(chunk):
        first = (chunk * SLOTS).astype(F32) if not isinstance(chunk, int) else float(chunk * SLOTS)
        for k in range(groups):
            row = rank[k:k + 1, :] - first
            pt[:, pl.ds(LANES * k, LANES)] = jnp.where(slot_of == row, 1.0, 0.0).astype(BF16)

    def one_hots(comp):
        col = jnp.where(iota((ext_cols, SLOTS), 0).astype(F32) == comp[0:1], 1.0, 0.0)
        row = jnp.where(iota((ext_rows, SLOTS), 0).astype(F32) == comp[1:2], 1.0, 0.0)
        return col.astype(BF16), row

    def add_wells(chunk, first):
        build_places(chunk)
        three = dot(place_parts, pt[...], NT)
        comp = three[0:8] + three[8:16] + three[16:24]
        comps[chunk] = comp
        col_hot, row_hot = one_hots(comp)
        weights = []
        for z in range(layers):
            found = dot(ke[z].astype(BF16), col_hot, NN)
            k_at = jnp.sum(found * row_hot, axis=0, keepdims=True)
            screened = (comp[2:3] <= z) & (comp[3:4] >= z)
            weights.append(jnp.where(screened, k_at, 0.0))
        weight = jnp.concatenate(weights, axis=0)
        total = jnp.sum(weight, axis=0, keepdims=True)
        share = weight / jnp.where(total > 0, total, 1.0)
        shares[chunk] = share
        pumped = share * comp[4:5]
        priced = pumped * comp[5:6]
        col_two = jnp.concatenate([col_hot, col_hot], axis=1)
        for z in range(layers):
            left = []
            for value in (pumped, priced):
                top, rest = split(value[z:z + 1], 2)
                left.append(
                    jnp.concatenate([row_hot * top.astype(F32), row_hot * rest.astype(F32)], axis=1)
                )
            left = jnp.concatenate(left, axis=0).astype(BF16)
            field = dot(left, col_two, NT)
            if first:
                src[z] = field[:ext_rows]
                lw[z] = field[ext_rows:]
            else:
                src[z] = src[z] + field[:ext_rows]
                lw[z] = lw[z] + field[ext_rows:]

    add_wells(0, True)

    def more_wells(chunk, carry):
        add_wells(chunk, False)
        return carry

    lax.fori_loop(1, chunks, more_wells, 0)

    wide = (8, ext_cols)
    sub = iota(wide, 0)
    col = iota(wide, 1)
    closed_col = ((col == cols - 1) & (me_e == n_east - 1)) | ((col == ext_cols - 1) & (me_e == 0))
    open_east = jnp.where(closed_col, 0.0, 2.0)
    open_low = jnp.where((sub == 7) & (me_n == 0), 0.0, 2.0)
    open_high = jnp.where((sub == 7) & (me_n == n_north - 1), 0.0, 2.0)

    def east(v):
        return roll(v, ext_cols - 1, 1)

    def west(v):
        return roll(v, 1, 1)

    def north(now, after):
        return jnp.where(sub < 7, roll(now, 7, 0), roll(after, 7, 0))

    def south(now, prior):
        return jnp.where(sub > 0, roll(now, 1, 0), roll(prior, 1, 0))

    def at(j):
        return pl.ds(8 * j, 8)

    fu[0] = jnp.zeros((ext_rows, ext_cols), F32)

    def start(z, carry):
        up = jnp.minimum(z + 1, layers - 1)
        down = jnp.maximum(z - 1, 0)
        open_up = jnp.where(z < layers - 1, 2.0, 0.0)
        fn_prior = jnp.zeros(wide, F32)
        gn_prior = jnp.zeros(wide, F32)
        k_n, h = kn[z, at(0)], hx[z, at(0)]
        for j in range(chunks_of_rows):
            j_after = min(j + 1, chunks_of_rows - 1)
            k_e, k_u, k_u2 = ke[z, at(j)], kv[z, at(j)], kv[up, at(j)]
            k_e2 = east(k_e)
            k_after, h_after = kn[z, at(j_after)], hx[z, at(j_after)]
            k_n2 = north(k_n, k_after)
            f_e = open_east * k_e * k_e2 * reciprocal(k_e + k_e2)
            opened = open_low if j == 0 else open_high if j == chunks_of_rows - 2 else 2.0
            f_n = opened * k_n * k_n2 * reciprocal(k_n + k_n2)
            f_u = open_up * k_u * k_u2 * reciprocal(k_u + k_u2)
            f_d = fu[z, at(j)]
            fe[z, at(j)] = f_e
            fn[z, at(j)] = f_n
            fu[z + 1, at(j)] = f_u
            diagonal = st[z, at(j)] + f_e + west(f_e) + f_n + south(f_n, fn_prior) + f_u + f_d
            inverse = reciprocal(diagonal)
            inv[z, at(j)] = inverse
            g_e = f_e * (east(h) - h)
            g_n = f_n * (north(h, h_after) - h)
            g_u = f_u * (hx[up, at(j)] - h)
            g_d = f_d * (h - hx[down, at(j)])
            residual = (g_e - west(g_e)) + (g_n - south(g_n, gn_prior)) + (g_u - g_d)
            d0[z, at(j)] = inverse * (residual - src[z, at(j)])
            fn_prior, gn_prior, k_n, h = f_n, g_n, k_after, h_after
        return carry

    lax.fori_loop(0, layers, start, 0)

    def sweep(field, margin, finish, chunk_from, chunk_to):
        def layer(i, carry):
            z = (depth - margin) * me_l + i
            up = jnp.minimum(z + 1, layers - 1)
            down = jnp.maximum(z - 1, 0)
            if chunk_from == 0:
                b_prior = jnp.zeros(wide, F32)
            else:
                b_prior = fn[z, at(chunk_from - 1)] * field[z, at(chunk_from - 1)]
            d = field[z, at(chunk_from)]
            for j in range(chunk_from, chunk_to):
                d_after = field[z, at(min(j + 1, chunks_of_rows - 1))]
                f_e, f_n = fe[z, at(j)], fn[z, at(j)]
                b = f_n * d
                moved = f_e * east(d) + west(f_e * d)
                moved = moved + f_n * north(d, d_after) + south(b, b_prior)
                moved = moved + fu[z + 1, at(j)] * field[up, at(j)] + fu[z, at(j)] * field[down, at(j)]
                finish(i, z, j, d, inv[z, at(j)] * moved)
                b_prior, d = b, d_after
            return carry

        lax.fori_loop(0, depth + margin, layer, 0)

    (a1, b1), (a2, b2) = steps_of()

    def first_sweep(i, z, j, d, pulled):
        s1[z, at(j)] = pulled
        d1[z, at(j)] = a1 * d + b1 * pulled

    def end_forward(i, z, j, d, pulled):
        s2 = s1[z, at(j)] - d + pulled
        d2 = a2 * d + b2 * s2
        new = hx[z, at(j)] + d0[z, at(j)] + d + d2
        hx[z, at(j)] = new
        load = new - tx[z, at(j)] - lw[z, at(j)]
        src[z, at(j)] = inv[z, at(j)] * load

    sweep(d0, 3, first_sweep, 0, chunks_of_rows)
    sweep(d1, 2, end_forward, 0, chunks_of_rows)
    sweep(src, 1, first_sweep, 0, chunks_of_rows)

    parts[...] = jnp.zeros(parts.shape, F32)
    st[0, at(0)] = jnp.zeros(wide, F32)

    def end_adjoint(i, z, j, d, pulled):
        s2 = s1[z, at(j)] - d + pulled
        d2 = a2 * d + b2 * s2
        adj = src[z, at(j)] + d + d2
        adjoint[i, at(j - 1)] = adj[:, :cols]
        new = hx[z, at(j), inside_cols]
        head_new[i, at(j - 1)] = new
        departure = new - tx[z, at(j), inside_cols]
        st[0, at(0), inside_cols] = st[0, at(0), inside_cols] + departure * departure

    sweep(d1, 0, end_adjoint, 1, chunks_of_rows - 1)

    squared = st[0, at(0), inside_cols]
    squared = jnp.sum(squared, axis=0, keepdims=True)
    squared = sum(squared[:, LANES * k:LANES * (k + 1)] for k in range(cols // LANES))
    squared = squared * (1.0 / (float(layers * rows * cols) * n_east * n_north))
    base_layer = jnp.where(me_l == 0, 1.0, 0.0)

    def collect(chunk, first):
        comp = comps[chunk]
        share = shares[chunk]
        col_hot, row_hot = one_hots(comp)
        col_hot, row_hot = col_hot[:cols], row_hot[8:8 + rows]
        head_at = jnp.zeros((1, SLOTS), F32)
        adj_at = jnp.zeros((1, SLOTS), F32)
        for i in range(depth):
            z_share = jnp.where(me_l == 0, share[i:i + 1], share[depth + i:depth + i + 1])
            stack = split(head_new[i], 2) + split(adjoint[i], 2)
            found = [dot(piece, col_hot, NN) for piece in stack]
            head_at += z_share * jnp.sum((found[0] + found[1]) * row_hot, axis=0, keepdims=True)
            adj_at += z_share * jnp.sum((found[2] + found[3]) * row_hot, axis=0, keepdims=True)
        lift = (comp[6:7] * base_layer - head_at) * comp[7:8]
        priced = comp[5:6] * lift
        slope = priced - adj_at * comp[7:8]
        three = jnp.concatenate(
            [p.astype(F32) for p in split(slope, 3)] + [jnp.zeros((5, SLOTS), F32)], axis=0
        ).astype(BF16)
        if not first:
            build_places(chunk)
        spread = dot(three, pt[...], NN)
        spread = spread[0:1] + spread[1:2] + spread[2:3]
        tile = jnp.concatenate(
            [spread[:, LANES * k:LANES * (k + 1)] for k in range(groups)], axis=0
        )
        parts[pl.ds(0, groups)] += tile
        parts[pl.ds(groups, 1)] += priced * comp[4:5]

    @pl.when(chunks > 1)
    def _():
        build_places(0)

    collect(0, True)

    def collect_more(chunk, carry):
        collect(chunk, False)
        return carry

    lax.fori_loop(1, chunks, collect_more, 0)
    parts[pl.ds(groups + 1, 1)] = squared


def run_solve(sizes, fields, moved, wells):
    depth, rows, cols = fields[0].shape
    layers, ext_rows, ext_cols = 2 * depth, rows + 16, cols + LANES
    groups = wells.shape[1] // LANES
    out = jax.ShapeDtypeStruct((depth, rows, cols), F32)
    ext = pltpu.VMEM((layers, ext_rows, ext_cols), F32)
    return pl.pallas_call(
        functools.partial(solve, sizes),
        out_shape=[out, out, jax.ShapeDtypeStruct((groups + 8, LANES), F32)],
        in_specs=[pl.BlockSpec(memory_space=pltpu.VMEM)] * (len(fields) + len(moved) + 1),
        out_specs=[pl.BlockSpec(memory_space=pltpu.VMEM)] * 3,
        scratch_shapes=[ext] * 8
        + [pltpu.VMEM((layers + 1, ext_rows, ext_cols), F32)]
        + [ext] * 6
        + [
            pltpu.VMEM((SLOTS, wells.shape[1]), BF16),
            pltpu.VMEM((groups, 8, SLOTS), F32),
            pltpu.VMEM((groups, 8, SLOTS), F32),
        ],
        compiler_params=pltpu.CompilerParams(vmem_limit_bytes=56 * 1024 * 1024),
        name="solve",
    )(*fields, *moved, wells)


def add_up(sizes, part, out, box0, box1, box2, box3, send_sem, recv_sem):
    n_east, n_x, n_z = sizes
    me_e, me_n, me_l = lax.axis_index("east"), lax.axis_index("north"), lax.axis_index("layer")
    me_x, me_z = me_n // n_z, lax.rem(me_n, n_z)
    phases = (
        (box0, 2, me_l, lambda i: (me_e, me_n, i)),
        (box1, n_z, me_z, lambda i: (me_e, me_x * n_z + i, me_l)),
        (box2, n_east, me_e, lambda i: (i, me_n, me_l)),
        (box3, n_x, me_x, lambda i: (me_e, i * n_z + me_z, me_l)),
    )
    barrier = pltpu.get_barrier_semaphore()
    peers = 0
    for _, size, mine, device in phases:
        for k in range(1, size):
            pl.semaphore_signal(
                barrier, inc=1, device_id=device(lax.rem(mine + k, size)), device_id_type=MESH
            )
            peers += 1
    pl.semaphore_wait(barrier, peers)
    total = part[...]
    used = 0
    for box, size, mine, device in phases:
        box[mine] = total
        copies = []
        for k in range(1, size):
            copy = pltpu.make_async_remote_copy(
                src_ref=box.at[mine],
                dst_ref=box.at[mine],
                send_sem=send_sem.at[used],
                recv_sem=recv_sem.at[used],
                device_id=device(lax.rem(mine + k, size)),
                device_id_type=MESH,
            )
            copy.start()
            copies.append(copy)
            used += 1
        for copy in copies:
            copy.wait()
        total = box[0]
        for k in range(1, size):
            total = total + box[k]
    tail = part.shape[0] - 8
    out[pl.ds(0, tail)] = total[:tail]
    out[pl.ds(tail, 8)] = jnp.broadcast_to(
        jnp.sum(total[tail:], axis=1, keepdims=True), (8, LANES)
    )


def run_add_up(sizes, part):
    peers = 1 + sum(n - 1 for n in sizes)
    return pl.pallas_call(
        functools.partial(add_up, sizes),
        out_shape=jax.ShapeDtypeStruct(part.shape, F32),
        in_specs=[pl.BlockSpec(memory_space=pltpu.VMEM)],
        out_specs=pl.BlockSpec(memory_space=pltpu.VMEM),
        scratch_shapes=[
            pltpu.VMEM((n,) + part.shape, F32) for n in (2, sizes[2], sizes[0], sizes[1])
        ]
        + [pltpu.SemaphoreType.DMA((peers,)), pltpu.SemaphoreType.DMA((peers,))],
        compiler_params=pltpu.CompilerParams(collective_id=1, has_side_effects=True),
        name="add_up",
    )(part)


def per_device(
    sizes,
    head_old, head_target, conductivity_east, conductivity_north, conductivity_vertical, storage,
    well_east, well_north, screen_top, screen_bottom, tariff_band, pump_rates, ground_level,
    band_prices,
):
    n_east, n_x, n_z = sizes
    n_wells = well_east.shape[0]
    band_ids = jnp.arange(band_prices.shape[0], dtype=jnp.int32)
    prices = jnp.sum(
        jnp.where(tariff_band[None, :] == band_ids[:, None], band_prices[:, None], 0.0), axis=0
    )
    padded = -(-n_wells // LANES) * LANES
    rows = [well_east, well_north, screen_top, screen_bottom, pump_rates, prices, ground_level]
    rows = jnp.stack([r.astype(F32) for r in rows] + [jnp.zeros((n_wells,), F32)])
    wells = jnp.pad(rows, ((0, 0), (0, padded - n_wells)), constant_values=-1e6)
    fields = (
        head_old, head_target, conductivity_east, conductivity_north, conductivity_vertical, storage
    )
    moved = run_exchange((n_east, n_x * n_z), *fields)
    head_new, adjoint, part = run_solve((n_east, n_x * n_z), fields, moved, wells)
    total = run_add_up(sizes, part)
    tail = part.shape[0] - 8
    rate_gradient = total[:tail].reshape(padded)[:n_wells]
    return head_new, adjoint, rate_gradient, total[tail, 0], total[tail + 1, 0]


def solution(mesh):
    field = P("layer", "north", "east")
    n_north = mesh.shape["north"]
    n_x = 4 if n_north % 4 == 0 else 1
    sizes = (mesh.shape["east"], n_x, n_north // n_x)
    return jax.shard_map(
        functools.partial(per_device, sizes),
        mesh=mesh,
        in_specs=(field,) * 6 + (P(),) * 8,
        out_specs=(field, field, P(), P(), P()),
        check_vma=False,
    )
```

```python
import functools

import jax
import jax.numpy as jnp
from jax import lax
from jax.experimental import pallas as pl
from jax.experimental.pallas import tpu as pltpu
from jax.sharding import PartitionSpec as P

MESH = pl.DeviceIdType.MESH
F32 = jnp.float32
BF16 = jnp.bfloat16

SWEEPS = 3
CENTRE = 1.0
HALF_WIDTH = 0.95

HALO = 8
REACH = 5
LANES = 128
SLOTS = 128


def steps_of():
    sigma = CENTRE / HALF_WIDTH
    factor = 1.0 / sigma
    found = []
    for _ in range(SWEEPS - 1):
        after = 1.0 / (2.0 * sigma - factor)
        found.append((after * factor, 2.0 * after / HALF_WIDTH))
        factor = after
    return found


def iota(shape, dim):
    return lax.broadcasted_iota(jnp.int32, shape, dim)


def roll(value, shift, dim):
    shift = shift % value.shape[dim]
    return pltpu.roll(value, shift, dim) if shift else value


def exchange(
    sizes,
    h_head, h_target, h_east, h_north, h_up, h_stored,
    p_head, p_target, p_east, p_north, p_up, p_stored,
    nf, nb, ef, eb, cf, cb,
    p_nf, p_nb, p_ef, p_eb, p_cf, p_cb,
    head, target, k_east, k_north, k_up, stored,
    s_nf, s_nb, s_ef, s_eb, s_cf, s_cb,
    load_sem, send_sem, recv_sem,
):
    n_east, n_north = sizes
    depth, rows, cols = head.shape
    me_e, me_n, me_l = lax.axis_index("east"), lax.axis_index("north"), lax.axis_index("layer")

    def east_of(side):
        return lax.rem(me_e + (n_east - 1 if side == 0 else 1), n_east)

    def north_of(side):
        return lax.rem(me_n + (n_north - 1 if side == 0 else 1), n_north)

    partner = (me_e, me_n, 1 - me_l)
    to_north = [(me_e, north_of(s), me_l) for s in (0, 1)]
    to_east = [(east_of(s), me_n, me_l) for s in (0, 1)]
    to_corner = [(east_of(c), north_of(r), me_l) for r in (0, 1) for c in (0, 1)]

    barrier = pltpu.get_barrier_semaphore()
    for device in [partner] + to_north + to_east + to_corner:
        pl.semaphore_signal(barrier, inc=1, device_id=device, device_id_type=MESH)

    loads = [
        pltpu.make_async_copy(src, dst, load_sem.at[k])
        for k, (src, dst) in enumerate((
            (h_head, head), (h_target, target), (h_east, k_east),
            (h_north, k_north), (h_up, k_up), (h_stored, stored),
        ))
    ]
    for load in loads:
        load.start()

    lane = iota((8, LANES), 1)
    sub = iota((8, LANES), 0)
    group = lane // HALO
    wide_sub = iota((8, cols), 0)
    coefs = (k_east, k_north, k_up, stored)
    last = cols - LANES

    def pack(z, carry):
        for side in (0, 1):
            c0 = last * side
            kept = jnp.zeros((8, LANES), F32)
            fields = [jnp.zeros((8, LANES), F32) for _ in coefs]
            for pair in range(rows // 16):
                tiles = [
                    ref[z, pl.ds(16 * pair, 16), pl.ds(c0, LANES)].astype(F32) for ref in coefs
                ]
                for half in (0, 1):
                    j = 2 * pair + half
                    shift = HALO * j - (LANES - HALO) * side
                    h = head[z, pl.ds(8 * j, 8), pl.ds(c0, LANES)]
                    t = target[z, pl.ds(8 * j, 8), pl.ds(c0, LANES)]
                    if side == 0:
                        both = jnp.where(lane >= HALO - 2, roll(t, HALO - 2, 1), h)
                    else:
                        both = jnp.where(lane < LANES - HALO + 2, roll(t, 2 - HALO, 1), h)
                    here = group == j
                    kept = jnp.where(here, roll(both, shift, 1), kept)
                    for a in range(4):
                        piece = tiles[a][8 * half:8 * half + 8]
                        fields[a] = jnp.where(here, roll(piece, shift, 1), fields[a])
            s_ef[side, z] = kept
            s_eb[side, z, pl.ds(0, 16)] = jnp.concatenate(fields[:2], axis=0).astype(BF16)
            s_eb[side, z, pl.ds(16, 16)] = jnp.concatenate(fields[2:], axis=0).astype(BF16)
            r0 = (rows - 8) * side
            h = head[z, pl.ds(r0, 8), :]
            t = target[z, pl.ds(r0, 8), :]
            if side == 0:
                both = jnp.where(wide_sub >= HALO - 2, roll(t, HALO - 2, 0), h)
            else:
                both = jnp.where(wide_sub < 2, roll(t, 2, 0), h)
            s_nf[side, z] = both
            edge = [
                ref[z, pl.ds((rows - 16) * side, 16), :].astype(F32)[8 * side:8 * side + 8]
                for ref in coefs
            ]
            s_nb[side, z, pl.ds(0, 16)] = jnp.concatenate(edge[:2], axis=0).astype(BF16)
            s_nb[side, z, pl.ds(16, 16)] = jnp.concatenate(edge[2:], axis=0).astype(BF16)
        return carry

    for load in loads:
        load.wait()
    lax.fori_loop(0, depth, pack, 0)

    for r in (0, 1):
        for c in (0, 1):
            c0 = last * c
            kept = jnp.zeros((8, LANES), F32)
            mixed = jnp.zeros((8, LANES), F32)
            for z in range(depth):
                both = s_nf[r, z, :, pl.ds(c0, LANES)]
                kept = jnp.where(group == z, roll(both, HALO * z - (LANES - HALO) * c, 1), kept)
                for half in (0, 1):
                    two = s_nb[r, z, pl.ds(16 * half, 16), pl.ds(c0, LANES)].astype(F32)
                    for k in (0, 1):
                        slot = (2 * half + k) * depth + z
                        moved = roll(two[8 * k:8 * k + 8], HALO * slot - (LANES - HALO) * c, 1)
                        mixed = jnp.where(group == slot, moved, mixed)
            s_cf[2 * r + c] = kept
            s_cb[2 * r + c] = jnp.concatenate([mixed, mixed], axis=0).astype(BF16)

    pl.semaphore_wait(barrier, 9)

    count = [0]

    def send(src, dst, device):
        copy = pltpu.make_async_remote_copy(
            src_ref=src,
            dst_ref=dst,
            send_sem=send_sem.at[count[0]],
            recv_sem=recv_sem.at[count[0]],
            device_id=device,
            device_id_type=MESH,
        )
        count[0] += 1
        copy.start()
        return copy

    halos = []
    for side in (0, 1):
        halos.append(send(s_nb.at[side], nb.at[side], to_north[side]))
        halos.append(send(s_nf.at[side], nf.at[side], to_north[side]))
    for side in (0, 1):
        halos.append(send(s_eb.at[side], eb.at[side], to_east[side]))
        halos.append(send(s_ef.at[side], ef.at[side], to_east[side]))
    for d in range(4):
        halos.append(send(s_cb.at[d], cb.at[d], to_corner[d]))
        halos.append(send(s_cf.at[d], cf.at[d], to_corner[d]))
    blocks = [
        send(src, dst, partner)
        for src, dst in (
            (h_head, p_head), (h_target.at[pl.ds((depth - 2) * (1 - me_l), 2)], p_target),
            (h_east, p_east), (h_north, p_north), (h_up, p_up), (h_stored, p_stored),
        )
    ]
    for copy in halos:
        copy.wait_recv()
    forwards = [
        send(src, dst, partner)
        for src, dst in (
            (nf, p_nf), (nb, p_nb), (ef, p_ef), (eb, p_eb), (cf, p_cf), (cb, p_cb),
        )
    ]
    for copy in halos:
        copy.wait_send()
    for copy in blocks + forwards:
        copy.wait()


def run_exchange(sizes, head, target, k_east, k_north, k_up, stored):
    depth, rows, cols = head.shape
    fields = [head, target, k_east, k_north, k_up, stored]
    blocks = [jax.ShapeDtypeStruct(x.shape, x.dtype) for x in fields]
    blocks[1] = jax.ShapeDtypeStruct((2, rows, cols), F32)
    halos = [
        ((2, depth, 8, cols), F32),
        ((2, depth, 32, cols), BF16),
        ((2, depth, 8, LANES), F32),
        ((2, depth, 32, LANES), BF16),
        ((4, 8, LANES), F32),
        ((4, 16, LANES), BF16),
    ]
    shaped = [jax.ShapeDtypeStruct(s, d) for s, d in halos]
    outs = blocks + shaped + shaped
    copies = 16 + 6 + 6
    return pl.pallas_call(
        functools.partial(exchange, sizes),
        out_shape=outs,
        in_specs=[pl.BlockSpec(memory_space=pltpu.HBM)] * 6,
        out_specs=[pl.BlockSpec(memory_space=pltpu.HBM)] * len(outs),
        scratch_shapes=[pltpu.VMEM(x.shape, x.dtype) for x in fields]
        + [pltpu.VMEM(s, d) for s, d in halos]
        + [pltpu.SemaphoreType.DMA((6,))]
        + [pltpu.SemaphoreType.DMA((copies,)), pltpu.SemaphoreType.DMA((copies,))],
        compiler_params=pltpu.CompilerParams(
            collective_id=0, has_side_effects=True, vmem_limit_bytes=60 * 1024 * 1024
        ),
        name="exchange",
    )(*fields)


def split(value, parts):
    found = []
    for _ in range(parts):
        top = value.astype(BF16)
        found.append(top)
        value = value - top.astype(F32)
    return found


def dot(a, b, dims):
    return lax.dot_general(a, b, (dims, ((), ())), preferred_element_type=F32)


NN = ((1,), (0,))
NT = ((1,), (1,))


def reciprocal(x):
    first = pl.reciprocal(x, approx=True)
    second = first * (2.0 - x * first)
    return second * (2.0 - x * second)


def solve(
    sizes,
    *refs,
):
    n_east, n_north = sizes
    fields, refs = (refs[:6], refs[6:12]), refs[12:]
    halos, refs = (refs[:6], refs[6:12]), refs[12:]
    well_refs, refs = refs[:8], refs[8:]
    head_new, adjoint, parts = refs[:3]
    hx, tx, ke, kn, kv, st, fe, fn, fu, inv, src, lw, d0, d1, s1, pt, comps, shares = refs[3:21]
    staged, refs = refs[21:25], refs[25:]
    nbs, efs, ebs, cfs, cbs = refs[:5]
    well_rows, wells, sems = refs[5:13], refs[13], refs[14]
    depth, rows, cols = head_new.shape
    layers, ext_rows, ext_cols = hx.shape
    chunks_of_rows = ext_rows // 8
    n_wells = wells.shape[1]
    groups = n_wells // LANES
    me_e, me_n, me_l = lax.axis_index("east"), lax.axis_index("north"), lax.axis_index("layer")

    lane = iota((8, LANES), 1)
    low_half = lane < LANES // 2
    extra = pl.ds(cols, LANES)
    inside_cols = pl.ds(0, cols)
    inner = pl.ds(8, rows)
    starts = (depth * me_l, depth * (1 - me_l))
    high, low = pl.ds(rows + 8, 8), pl.ds(0, 8)

    small, large = [], []

    def load(found, src_ref, dst_ref):
        copy = pltpu.make_async_copy(src_ref, dst_ref, sems.at[len(small) + len(large)])
        copy.start()
        found.append(copy)

    for src_ref, dst_ref in zip(well_refs, well_rows):
        load(small, src_ref, dst_ref)
    for who in (0, 1):
        here = pl.ds(starts[who], depth)
        for a in range(4):
            load(large, fields[who][2 + a], staged[a].at[here])
        b_nf, b_nb, b_ef, b_eb, b_cf, b_cb = halos[who]
        load(large, b_nb, nbs.at[who])
        load(large, b_eb, ebs.at[who])
        load(large, b_cb, cbs.at[who])
        load(large, fields[who][0], hx.at[here, inner, inside_cols])
        load(large, b_nf.at[0], hx.at[here, high, inside_cols])
        load(large, b_nf.at[1], hx.at[here, low, inside_cols])
        load(large, b_ef, efs.at[who])
        load(large, b_cf, cfs.at[who])
        there = here if who == 0 else pl.ds(depth - 2 * me_l, 2)
        load(large, fields[who][1], tx.at[there, inner, inside_cols])

    def fill_fields():
        for who in (0, 1):
            base = starts[who]

            def fill(z, carry):
                zz = base + z
                for dst, ref in zip((ke, kn, kv, st), staged):
                    dst[zz, inner, inside_cols] = ref[zz].astype(F32)
                for side, at_rows in ((0, high), (1, low)):
                    tx[zz, at_rows, inside_cols] = roll(
                        hx[zz, at_rows, inside_cols], 2 if side == 0 else 6, 0
                    )
                    for half, pair in ((0, (ke, kn)), (1, (kv, st))):
                        two = nbs[who, side, z, pl.ds(16 * half, 16)].astype(F32)
                        pair[0][zz, at_rows, inside_cols] = two[:8]
                        pair[1][zz, at_rows, inside_cols] = two[8:]
                right, left = efs[who, 0, z], efs[who, 1, z]
                for j in range(rows // 8):
                    both = jnp.where(
                        low_half, roll(right, -HALO * j, 1), roll(left, LANES - HALO - HALO * j, 1)
                    )
                    hx[zz, pl.ds(8 + 8 * j, 8), extra] = both
                    tx[zz, pl.ds(8 + 8 * j, 8), extra] = jnp.where(
                        low_half, roll(both, 2 - HALO, 1), roll(both, HALO - 2, 1)
                    )
                for half, pair in ((0, (ke, kn)), (1, (kv, st))):
                    rights = ebs[who, 0, z, pl.ds(16 * half, 16)].astype(F32)
                    lefts = ebs[who, 1, z, pl.ds(16 * half, 16)].astype(F32)
                    for k in (0, 1):
                        right, left = rights[8 * k:8 * k + 8], lefts[8 * k:8 * k + 8]
                        for j in range(rows // 8):
                            pair[k][zz, pl.ds(8 + 8 * j, 8), extra] = jnp.where(
                                low_half,
                                roll(right, -HALO * j, 1),
                                roll(left, LANES - HALO - HALO * j, 1),
                            )
                return carry

            lax.fori_loop(0, depth, fill, 0)
            for r, at_rows in ((0, high), (1, low)):
                right, left = cfs[who, 2 * r], cfs[who, 2 * r + 1]
                rights = cbs[who, 2 * r].astype(F32)[:8]
                lefts = cbs[who, 2 * r + 1].astype(F32)[:8]
                for z in range(depth):
                    both = jnp.where(
                        low_half, roll(right, -HALO * z, 1), roll(left, LANES - HALO - HALO * z, 1)
                    )
                    hx[base + z, at_rows, extra] = both
                    tx[base + z, at_rows, extra] = roll(both, 2 if r == 0 else 6, 0)
                    for a, dst in enumerate((ke, kn, kv, st)):
                        slot = a * depth + z
                        dst[base + z, at_rows, extra] = jnp.where(
                            low_half,
                            roll(rights, -HALO * slot, 1),
                            roll(lefts, LANES - HALO - HALO * slot, 1),
                        )

    for copy in small:
        copy.wait()
    wells[...] = jnp.full(wells.shape, -1e6, F32)
    width = pl.ds(0, well_rows[0].shape[1])
    for row, ref in enumerate(well_rows[:5]):
        wells[pl.ds(row, 1), width] = ref[...].astype(F32)
    band = well_rows[5][...]
    bands = well_rows[7][...]
    price = jnp.zeros(band.shape, F32)
    for b in range(bands.shape[1]):
        price = jnp.where(band == b, bands[0:1, b:b + 1], price)
    wells[pl.ds(5, 1), width] = price
    wells[pl.ds(6, 1), width] = well_rows[6][...]

    at_east = wells[0:1, :] - (me_e * cols).astype(F32)
    at_north = wells[1:2, :] - (me_n * rows).astype(F32)
    near = (
        (at_east >= -REACH) & (at_east < cols + REACH)
        & (at_north >= -REACH) & (at_north < rows + REACH)
    )
    mine = (at_east >= 0) & (at_east < cols) & (at_north >= 0) & (at_north < rows)
    near_row = jnp.where(near, 1.0, 0.0)
    near_tile = jnp.concatenate(
        [near_row[:, LANES * k:LANES * (k + 1)] for k in range(groups)], axis=0
    )
    before = (iota((LANES, LANES), 0) < iota((LANES, LANES), 1)).astype(F32).astype(BF16)
    in_row = dot(near_tile.astype(BF16), before, NN)
    above = (iota((groups, groups), 1) < iota((groups, groups), 0)).astype(F32).astype(BF16)
    rows_above = jnp.sum(dot(above, near_tile.astype(BF16), NN), axis=1, keepdims=True)
    rank = jnp.where(near_tile > 0, in_row + rows_above, -1.0)
    total_near = jnp.sum(near_tile).astype(jnp.int32)
    chunks = (total_near + (SLOTS - 1)) // SLOTS

    place = jnp.concatenate(
        [
            jnp.where(at_east < 0, at_east + ext_cols, at_east),
            at_north + 8.0,
            wells[2:7, :],
            jnp.where(mine, 1.0, 0.0),
        ],
        axis=0,
    )
    place_parts = jnp.concatenate([p.astype(F32) for p in split(place, 3)], axis=0).astype(BF16)
    slot_of = iota((SLOTS, LANES), 0).astype(F32)

    def build_places(chunk):
        first = (chunk * SLOTS).astype(F32) if not isinstance(chunk, int) else float(chunk * SLOTS)
        for k in range(groups):
            row = rank[k:k + 1, :] - first
            pt[:, pl.ds(LANES * k, LANES)] = jnp.where(slot_of == row, 1.0, 0.0).astype(BF16)

    def one_hots(comp):
        col = jnp.where(iota((ext_cols, SLOTS), 0).astype(F32) == comp[0:1], 1.0, 0.0)
        row = jnp.where(iota((ext_rows, SLOTS), 0).astype(F32) == comp[1:2], 1.0, 0.0)
        return col.astype(BF16), row

    def add_wells(chunk, first):
        build_places(chunk)
        three = dot(place_parts, pt[...], NT)
        comp = three[0:8] + three[8:16] + three[16:24]
        comps[chunk] = comp
        col_hot, row_hot = one_hots(comp)
        weights = []
        for z in range(layers):
            found = dot(ke[z].astype(BF16), col_hot, NN)
            k_at = jnp.sum(found * row_hot, axis=0, keepdims=True)
            screened = (comp[2:3] <= z) & (comp[3:4] >= z)
            weights.append(jnp.where(screened, k_at, 0.0))
        weight = jnp.concatenate(weights, axis=0)
        total = jnp.sum(weight, axis=0, keepdims=True)
        share = weight / jnp.where(total > 0, total, 1.0)
        shares[chunk] = share
        pumped = share * comp[4:5]
        priced = pumped * comp[5:6]
        col_two = jnp.concatenate([col_hot, col_hot], axis=1)
        for z in range(layers):
            left = []
            for value in (pumped, priced):
                top, rest = split(value[z:z + 1], 2)
                left.append(
                    jnp.concatenate([row_hot * top.astype(F32), row_hot * rest.astype(F32)], axis=1)
                )
            left = jnp.concatenate(left, axis=0).astype(BF16)
            field = dot(left, col_two, NT)
            if first:
                src[z] = field[:ext_rows]
                lw[z] = field[ext_rows:]
            else:
                src[z] = src[z] + field[:ext_rows]
                lw[z] = lw[z] + field[ext_rows:]

    for copy in large:
        copy.wait()
    fill_fields()
    add_wells(0, True)

    def more_wells(chunk, carry):
        add_wells(chunk, False)
        return carry

    lax.fori_loop(1, chunks, more_wells, 0)

    wide = (8, ext_cols)
    sub = iota(wide, 0)
    col = iota(wide, 1)
    closed_col = ((col == cols - 1) & (me_e == n_east - 1)) | ((col == ext_cols - 1) & (me_e == 0))
    open_east = jnp.where(closed_col, 0.0, 2.0)
    open_low = jnp.where((sub == 7) & (me_n == 0), 0.0, 2.0)
    open_high = jnp.where((sub == 7) & (me_n == n_north - 1), 0.0, 2.0)

    def east(v):
        return roll(v, ext_cols - 1, 1)

    def west(v):
        return roll(v, 1, 1)

    def north(now, after):
        return jnp.where(sub < 7, roll(now, 7, 0), roll(after, 7, 0))

    def south(now, prior):
        return jnp.where(sub > 0, roll(now, 1, 0), roll(prior, 1, 0))

    def at(j):
        return pl.ds(8 * j, 8)

    fu[0] = jnp.zeros((ext_rows, ext_cols), F32)

    def start(z, carry):
        up = jnp.minimum(z + 1, layers - 1)
        down = jnp.maximum(z - 1, 0)
        open_up = jnp.where(z < layers - 1, 2.0, 0.0)
        fn_prior = jnp.zeros(wide, F32)
        gn_prior = jnp.zeros(wide, F32)
        k_n, h = kn[z, at(0)], hx[z, at(0)]
        for j in range(chunks_of_rows):
            j_after = min(j + 1, chunks_of_rows - 1)
            k_e, k_u, k_u2 = ke[z, at(j)], kv[z, at(j)], kv[up, at(j)]
            k_e2 = east(k_e)
            k_after, h_after = kn[z, at(j_after)], hx[z, at(j_after)]
            k_n2 = north(k_n, k_after)
            f_e = open_east * k_e * k_e2 * reciprocal(k_e + k_e2)
            opened = open_low if j == 0 else open_high if j == chunks_of_rows - 2 else 2.0
            f_n = opened * k_n * k_n2 * reciprocal(k_n + k_n2)
            f_u = open_up * k_u * k_u2 * reciprocal(k_u + k_u2)
            f_d = fu[z, at(j)]
            fe[z, at(j)] = f_e
            fn[z, at(j)] = f_n
            fu[z + 1, at(j)] = f_u
            diagonal = st[z, at(j)] + f_e + west(f_e) + f_n + south(f_n, fn_prior) + f_u + f_d
            inverse = reciprocal(diagonal)
            inv[z, at(j)] = inverse
            g_e = f_e * (east(h) - h)
            g_n = f_n * (north(h, h_after) - h)
            g_u = f_u * (hx[up, at(j)] - h)
            g_d = f_d * (h - hx[down, at(j)])
            residual = (g_e - west(g_e)) + (g_n - south(g_n, gn_prior)) + (g_u - g_d)
            d0[z, at(j)] = inverse * (residual - src[z, at(j)])
            fn_prior, gn_prior, k_n, h = f_n, g_n, k_after, h_after
        return carry

    lax.fori_loop(0, layers, start, 0)

    def sweep(field, margin, finish, chunk_from, chunk_to):
        def layer(i, carry):
            z = (depth - margin) * me_l + i
            up = jnp.minimum(z + 1, layers - 1)
            down = jnp.maximum(z - 1, 0)
            if chunk_from == 0:
                b_prior = jnp.zeros(wide, F32)
            else:
                b_prior = fn[z, at(chunk_from - 1)] * field[z, at(chunk_from - 1)]
            d = field[z, at(chunk_from)]
            for j in range(chunk_from, chunk_to):
                d_after = field[z, at(min(j + 1, chunks_of_rows - 1))]
                f_e, f_n = fe[z, at(j)], fn[z, at(j)]
                b = f_n * d
                moved = f_e * east(d) + west(f_e * d)
                moved = moved + f_n * north(d, d_after) + south(b, b_prior)
                moved = moved + fu[z + 1, at(j)] * field[up, at(j)] + fu[z, at(j)] * field[down, at(j)]
                finish(i, z, j, d, inv[z, at(j)] * moved)
                b_prior, d = b, d_after
            return carry

        lax.fori_loop(0, depth + margin, layer, 0)

    (a1, b1), (a2, b2) = steps_of()

    def first_sweep(i, z, j, d, pulled):
        s1[z, at(j)] = pulled
        d1[z, at(j)] = a1 * d + b1 * pulled

    def end_forward(i, z, j, d, pulled):
        s2 = s1[z, at(j)] - d + pulled
        d2 = a2 * d + b2 * s2
        new = hx[z, at(j)] + d0[z, at(j)] + d + d2
        hx[z, at(j)] = new
        load = new - tx[z, at(j)] - lw[z, at(j)]
        src[z, at(j)] = inv[z, at(j)] * load

    sweep(d0, 3, first_sweep, 0, chunks_of_rows)
    sweep(d1, 2, end_forward, 0, chunks_of_rows)
    sweep(src, 1, first_sweep, 0, chunks_of_rows)

    parts[...] = jnp.zeros(parts.shape, F32)
    st[0, at(0)] = jnp.zeros(wide, F32)

    def end_adjoint(i, z, j, d, pulled):
        s2 = s1[z, at(j)] - d + pulled
        d2 = a2 * d + b2 * s2
        adj = src[z, at(j)] + d + d2
        adjoint[i, at(j - 1)] = adj[:, :cols]
        new = hx[z, at(j), inside_cols]
        head_new[i, at(j - 1)] = new
        departure = new - tx[z, at(j), inside_cols]
        st[0, at(0), inside_cols] = st[0, at(0), inside_cols] + departure * departure

    sweep(d1, 0, end_adjoint, 1, chunks_of_rows - 1)

    squared = st[0, at(0), inside_cols]
    squared = jnp.sum(squared, axis=0, keepdims=True)
    squared = sum(squared[:, LANES * k:LANES * (k + 1)] for k in range(cols // LANES))
    squared = squared * (1.0 / (float(layers * rows * cols) * n_east * n_north))
    base_layer = jnp.where(me_l == 0, 1.0, 0.0)

    def collect(chunk, first):
        comp = comps[chunk]
        share = shares[chunk]
        col_hot, row_hot = one_hots(comp)
        col_hot, row_hot = col_hot[:cols], row_hot[8:8 + rows]
        head_at = jnp.zeros((1, SLOTS), F32)
        adj_at = jnp.zeros((1, SLOTS), F32)
        for i in range(depth):
            z_share = jnp.where(me_l == 0, share[i:i + 1], share[depth + i:depth + i + 1])
            stack = split(head_new[i], 2) + split(adjoint[i], 2)
            found = [dot(piece, col_hot, NN) for piece in stack]
            head_at += z_share * jnp.sum((found[0] + found[1]) * row_hot, axis=0, keepdims=True)
            adj_at += z_share * jnp.sum((found[2] + found[3]) * row_hot, axis=0, keepdims=True)
        lift = (comp[6:7] * base_layer - head_at) * comp[7:8]
        priced = comp[5:6] * lift
        slope = priced - adj_at * comp[7:8]
        three = jnp.concatenate(
            [p.astype(F32) for p in split(slope, 3)] + [jnp.zeros((5, SLOTS), F32)], axis=0
        ).astype(BF16)
        if not first:
            build_places(chunk)
        spread = dot(three, pt[...], NN)
        spread = spread[0:1] + spread[1:2] + spread[2:3]
        tile = jnp.concatenate(
            [spread[:, LANES * k:LANES * (k + 1)] for k in range(groups)], axis=0
        )
        parts[pl.ds(0, groups)] += tile
        parts[pl.ds(groups, 1)] += priced * comp[4:5]

    @pl.when(chunks > 1)
    def _():
        build_places(0)

    collect(0, True)

    def collect_more(chunk, carry):
        collect(chunk, False)
        return carry

    lax.fori_loop(1, chunks, collect_more, 0)
    parts[pl.ds(groups + 1, 1)] = squared


def run_solve(sizes, fields, moved, wells):
    depth, rows, cols = fields[0].shape
    layers, ext_rows, ext_cols = 2 * depth, rows + 16, cols + LANES
    n_wells = wells[0].shape[1]
    groups = -(-n_wells // LANES)
    out = jax.ShapeDtypeStruct((depth, rows, cols), F32)
    ext = pltpu.VMEM((layers, ext_rows, ext_cols), F32)
    operands = (*fields, *moved, *wells)
    return pl.pallas_call(
        functools.partial(solve, sizes),
        out_shape=[out, out, jax.ShapeDtypeStruct((groups + 8, LANES), F32)],
        in_specs=[pl.BlockSpec(memory_space=pltpu.HBM)] * len(operands),
        out_specs=[pl.BlockSpec(memory_space=pltpu.VMEM)] * 3,
        scratch_shapes=[ext] * 8
        + [pltpu.VMEM((layers + 1, ext_rows, ext_cols), F32)]
        + [ext] * 6
        + [
            pltpu.VMEM((SLOTS, groups * LANES), BF16),
            pltpu.VMEM((groups, 8, SLOTS), F32),
            pltpu.VMEM((groups, 8, SLOTS), F32),
        ]
        + [pltpu.VMEM((layers, rows, cols), BF16)] * 4
        + [
            pltpu.VMEM((2, 2, depth, 32, cols), BF16),
            pltpu.VMEM((2, 2, depth, 8, LANES), F32),
            pltpu.VMEM((2, 2, depth, 32, LANES), BF16),
            pltpu.VMEM((2, 4, 8, LANES), F32),
            pltpu.VMEM((2, 4, 16, LANES), BF16),
        ]
        + [pltpu.VMEM(w.shape, w.dtype) for w in wells]
        + [pltpu.VMEM((8, groups * LANES), F32), pltpu.SemaphoreType.DMA((8 + 26,))],
        compiler_params=pltpu.CompilerParams(vmem_limit_bytes=60 * 1024 * 1024),
        name="solve",
    )(*operands)


def add_up(sizes, part, out, box0, box1, box2, box3, send_sem, recv_sem):
    n_east, n_x, n_z = sizes
    me_e, me_n, me_l = lax.axis_index("east"), lax.axis_index("north"), lax.axis_index("layer")
    me_x, me_z = me_n // n_z, lax.rem(me_n, n_z)
    phases = (
        (box0, 2, me_l, lambda i: (me_e, me_n, i)),
        (box1, n_z, me_z, lambda i: (me_e, me_x * n_z + i, me_l)),
        (box2, n_east, me_e, lambda i: (i, me_n, me_l)),
        (box3, n_x, me_x, lambda i: (me_e, i * n_z + me_z, me_l)),
    )
    barrier = pltpu.get_barrier_semaphore()
    peers = 0
    for _, size, mine, device in phases:
        for k in range(1, size):
            pl.semaphore_signal(
                barrier, inc=1, device_id=device(lax.rem(mine + k, size)), device_id_type=MESH
            )
            peers += 1
    pl.semaphore_wait(barrier, peers)
    total = part[...]
    used = 0
    for box, size, mine, device in phases:
        box[mine] = total
        copies = []
        for k in range(1, size):
            copy = pltpu.make_async_remote_copy(
                src_ref=box.at[mine],
                dst_ref=box.at[mine],
                send_sem=send_sem.at[used],
                recv_sem=recv_sem.at[used],
                device_id=device(lax.rem(mine + k, size)),
                device_id_type=MESH,
            )
            copy.start()
            copies.append(copy)
            used += 1
        for copy in copies:
            copy.wait()
        total = box[0]
        for k in range(1, size):
            total = total + box[k]
    tail = part.shape[0] - 8
    out[pl.ds(0, tail)] = total[:tail]
    out[pl.ds(tail, 8)] = jnp.broadcast_to(
        jnp.sum(total[tail:], axis=1, keepdims=True), (8, LANES)
    )


def run_add_up(sizes, part):
    peers = 1 + sum(n - 1 for n in sizes)
    return pl.pallas_call(
        functools.partial(add_up, sizes),
        out_shape=jax.ShapeDtypeStruct(part.shape, F32),
        in_specs=[pl.BlockSpec(memory_space=pltpu.VMEM)],
        out_specs=pl.BlockSpec(memory_space=pltpu.VMEM),
        scratch_shapes=[
            pltpu.VMEM((n,) + part.shape, F32) for n in (2, sizes[2], sizes[0], sizes[1])
        ]
        + [pltpu.SemaphoreType.DMA((peers,)), pltpu.SemaphoreType.DMA((peers,))],
        compiler_params=pltpu.CompilerParams(collective_id=1, has_side_effects=True),
        name="add_up",
    )(part)


def per_device(
    sizes,
    head_old, head_target, conductivity_east, conductivity_north, conductivity_vertical, storage,
    well_east, well_north, screen_top, screen_bottom, tariff_band, pump_rates, ground_level,
    band_prices,
):
    n_east, n_x, n_z = sizes
    n_wells = well_east.shape[0]
    wells = [
        w.reshape(1, -1)
        for w in (
            well_east, well_north, screen_top, screen_bottom, pump_rates, tariff_band,
            ground_level, band_prices,
        )
    ]
    fields = (
        head_old, head_target, conductivity_east, conductivity_north, conductivity_vertical, storage
    )
    moved = run_exchange((n_east, n_x * n_z), *fields)
    head_new, adjoint, part = run_solve((n_east, n_x * n_z), fields, moved, wells)
    total = run_add_up(sizes, part)
    tail = part.shape[0] - 8
    rate_gradient = total[:tail].reshape(-1)[:n_wells]
    return head_new, adjoint, rate_gradient, total[tail, 0], total[tail + 1, 0]


def solution(mesh):
    field = P("layer", "north", "east")
    n_north = mesh.shape["north"]
    n_x = 4 if n_north % 4 == 0 else 1
    sizes = (mesh.shape["east"], n_x, n_north // n_x)
    return jax.shard_map(
        functools.partial(per_device, sizes),
        mesh=mesh,
        in_specs=(field,) * 6 + (P(),) * 8,
        out_specs=(field, field, P(), P(), P()),
        check_vma=False,
    )
```

```python
import functools

import jax
import jax.numpy as jnp
from jax import lax
from jax.experimental import pallas as pl
from jax.experimental.pallas import tpu as pltpu
from jax.sharding import PartitionSpec as P

MESH = pl.DeviceIdType.MESH
F32 = jnp.float32
BF16 = jnp.bfloat16

SWEEPS = 3
CENTRE = 1.0
HALF_WIDTH = 0.95

HALO = 8
REACH = 5
LANES = 128
SLOTS = 128
START_UNIT, SWEEP_UNIT, LAST_UNIT = 9, 18, 16


def steps_of():
    sigma = CENTRE / HALF_WIDTH
    factor = 1.0 / sigma
    found = []
    for _ in range(SWEEPS - 1):
        after = 1.0 / (2.0 * sigma - factor)
        found.append((after * factor, 2.0 * after / HALF_WIDTH))
        factor = after
    return found


def iota(shape, dim):
    return lax.broadcasted_iota(jnp.int32, shape, dim)


def roll(value, shift, dim):
    shift = shift % value.shape[dim]
    return pltpu.roll(value, shift, dim) if shift else value


def exchange(
    sizes,
    h_head, h_target, h_east, h_north, h_up, h_stored,
    p_head, p_target, p_east, p_north, p_up, p_stored,
    nf, nb, ef, eb, cf, cb,
    p_nf, p_nb, p_ef, p_eb, p_cf, p_cb,
    head, target, k_east, k_north, k_up, stored,
    s_nf, s_nb, s_ef, s_eb, s_cf, s_cb,
    load_sem, send_sem, recv_sem,
):
    n_east, n_north = sizes
    depth, rows, cols = head.shape
    me_e, me_n, me_l = lax.axis_index("east"), lax.axis_index("north"), lax.axis_index("layer")

    def east_of(side):
        return lax.rem(me_e + (n_east - 1 if side == 0 else 1), n_east)

    def north_of(side):
        return lax.rem(me_n + (n_north - 1 if side == 0 else 1), n_north)

    partner = (me_e, me_n, 1 - me_l)
    to_north = [(me_e, north_of(s), me_l) for s in (0, 1)]
    to_east = [(east_of(s), me_n, me_l) for s in (0, 1)]
    to_corner = [(east_of(c), north_of(r), me_l) for r in (0, 1) for c in (0, 1)]

    barrier = pltpu.get_barrier_semaphore()
    for device in [partner] + to_north + to_east + to_corner:
        pl.semaphore_signal(barrier, inc=1, device_id=device, device_id_type=MESH)

    loads = [
        pltpu.make_async_copy(src, dst, load_sem.at[k])
        for k, (src, dst) in enumerate((
            (h_head, head), (h_target, target), (h_east, k_east),
            (h_north, k_north), (h_up, k_up), (h_stored, stored),
        ))
    ]
    for load in loads:
        load.start()

    lane = iota((8, LANES), 1)
    sub = iota((8, LANES), 0)
    group = lane // HALO
    wide_sub = iota((8, cols), 0)
    coefs = (k_east, k_north, k_up, stored)
    last = cols - LANES

    def pack(z, carry):
        for side in (0, 1):
            c0 = last * side
            kept = jnp.zeros((8, LANES), F32)
            fields = [jnp.zeros((8, LANES), F32) for _ in coefs]
            for pair in range(rows // 16):
                tiles = [
                    ref[z, pl.ds(16 * pair, 16), pl.ds(c0, LANES)].astype(F32) for ref in coefs
                ]
                for half in (0, 1):
                    j = 2 * pair + half
                    shift = HALO * j - (LANES - HALO) * side
                    h = head[z, pl.ds(8 * j, 8), pl.ds(c0, LANES)]
                    t = target[z, pl.ds(8 * j, 8), pl.ds(c0, LANES)]
                    if side == 0:
                        both = jnp.where(lane >= HALO - 2, roll(t, HALO - 2, 1), h)
                    else:
                        both = jnp.where(lane < LANES - HALO + 2, roll(t, 2 - HALO, 1), h)
                    here = group == j
                    kept = jnp.where(here, roll(both, shift, 1), kept)
                    for a in range(4):
                        piece = tiles[a][8 * half:8 * half + 8]
                        fields[a] = jnp.where(here, roll(piece, shift, 1), fields[a])
            s_ef[side, z] = kept
            s_eb[side, z, pl.ds(0, 16)] = jnp.concatenate(fields[:2], axis=0).astype(BF16)
            s_eb[side, z, pl.ds(16, 16)] = jnp.concatenate(fields[2:], axis=0).astype(BF16)
            r0 = (rows - 8) * side
            h = head[z, pl.ds(r0, 8), :]
            t = target[z, pl.ds(r0, 8), :]
            if side == 0:
                both = jnp.where(wide_sub >= HALO - 2, roll(t, HALO - 2, 0), h)
            else:
                both = jnp.where(wide_sub < 2, roll(t, 2, 0), h)
            s_nf[side, z] = both
            edge = [
                ref[z, pl.ds((rows - 16) * side, 16), :].astype(F32)[8 * side:8 * side + 8]
                for ref in coefs
            ]
            s_nb[side, z, pl.ds(0, 16)] = jnp.concatenate(edge[:2], axis=0).astype(BF16)
            s_nb[side, z, pl.ds(16, 16)] = jnp.concatenate(edge[2:], axis=0).astype(BF16)
        return carry

    for load in loads:
        load.wait()
    lax.fori_loop(0, depth, pack, 0)

    for r in (0, 1):
        for c in (0, 1):
            c0 = last * c
            kept = jnp.zeros((8, LANES), F32)
            mixed = jnp.zeros((8, LANES), F32)
            for z in range(depth):
                both = s_nf[r, z, :, pl.ds(c0, LANES)]
                kept = jnp.where(group == z, roll(both, HALO * z - (LANES - HALO) * c, 1), kept)
                for half in (0, 1):
                    two = s_nb[r, z, pl.ds(16 * half, 16), pl.ds(c0, LANES)].astype(F32)
                    for k in (0, 1):
                        slot = (2 * half + k) * depth + z
                        moved = roll(two[8 * k:8 * k + 8], HALO * slot - (LANES - HALO) * c, 1)
                        mixed = jnp.where(group == slot, moved, mixed)
            s_cf[2 * r + c] = kept
            s_cb[2 * r + c] = jnp.concatenate([mixed, mixed], axis=0).astype(BF16)

    pl.semaphore_wait(barrier, 9)

    count = [0]

    def send(src, dst, device):
        copy = pltpu.make_async_remote_copy(
            src_ref=src,
            dst_ref=dst,
            send_sem=send_sem.at[count[0]],
            recv_sem=recv_sem.at[count[0]],
            device_id=device,
            device_id_type=MESH,
        )
        count[0] += 1
        copy.start()
        return copy

    halos = []
    for side in (0, 1):
        halos.append(send(s_nb.at[side], nb.at[side], to_north[side]))
        halos.append(send(s_nf.at[side], nf.at[side], to_north[side]))
    for side in (0, 1):
        halos.append(send(s_eb.at[side], eb.at[side], to_east[side]))
        halos.append(send(s_ef.at[side], ef.at[side], to_east[side]))
    for d in range(4):
        halos.append(send(s_cb.at[d], cb.at[d], to_corner[d]))
        halos.append(send(s_cf.at[d], cf.at[d], to_corner[d]))
    blocks = [
        send(src, dst, partner)
        for src, dst in (
            (h_head, p_head), (h_target.at[pl.ds((depth - 2) * (1 - me_l), 2)], p_target),
            (h_east, p_east), (h_north, p_north), (h_up, p_up), (h_stored, p_stored),
        )
    ]
    for copy in halos:
        copy.wait_recv()
    forwards = [
        send(src, dst, partner)
        for src, dst in (
            (nf, p_nf), (nb, p_nb), (ef, p_ef), (eb, p_eb), (cf, p_cf), (cb, p_cb),
        )
    ]
    for copy in halos:
        copy.wait_send()
    for copy in blocks + forwards:
        copy.wait()


def run_exchange(sizes, head, target, k_east, k_north, k_up, stored):
    depth, rows, cols = head.shape
    fields = [head, target, k_east, k_north, k_up, stored]
    blocks = [jax.ShapeDtypeStruct(x.shape, x.dtype) for x in fields]
    blocks[1] = jax.ShapeDtypeStruct((2, rows, cols), F32)
    halos = [
        ((2, depth, 8, cols), F32),
        ((2, depth, 32, cols), BF16),
        ((2, depth, 8, LANES), F32),
        ((2, depth, 32, LANES), BF16),
        ((4, 8, LANES), F32),
        ((4, 16, LANES), BF16),
    ]
    shaped = [jax.ShapeDtypeStruct(s, d) for s, d in halos]
    outs = blocks + shaped + shaped
    copies = 16 + 6 + 6
    return pl.pallas_call(
        functools.partial(exchange, sizes),
        out_shape=outs,
        in_specs=[pl.BlockSpec(memory_space=pltpu.HBM)] * 6,
        out_specs=[pl.BlockSpec(memory_space=pltpu.HBM)] * len(outs),
        scratch_shapes=[pltpu.VMEM(x.shape, x.dtype) for x in fields]
        + [pltpu.VMEM(s, d) for s, d in halos]
        + [pltpu.SemaphoreType.DMA((6,))]
        + [pltpu.SemaphoreType.DMA((copies,)), pltpu.SemaphoreType.DMA((copies,))],
        compiler_params=pltpu.CompilerParams(
            collective_id=0, has_side_effects=True, vmem_limit_bytes=60 * 1024 * 1024
        ),
        name="exchange",
    )(*fields)


def split(value, parts):
    found = []
    for _ in range(parts):
        top = value.astype(BF16)
        found.append(top)
        value = value - top.astype(F32)
    return found


def dot(a, b, dims):
    return lax.dot_general(a, b, (dims, ((), ())), preferred_element_type=F32)


NN = ((1,), (0,))
NT = ((1,), (1,))


def reciprocal(x):
    first = pl.reciprocal(x, approx=True)
    return first * (2.0 - x * first)


def solve(
    sizes,
    *refs,
):
    n_east, n_north = sizes
    fields, refs = (refs[:6], refs[6:12]), refs[12:]
    halos, refs = (refs[:6], refs[6:12]), refs[12:]
    well_refs, refs = refs[:8], refs[8:]
    head_new, adjoint, parts = refs[:3]
    hx, tx, ke, kn, kv, st, fe, fn, fu, inv, src, lw, d0, d1, s1, pt, comps, shares = refs[3:21]
    staged, refs = refs[21:25], refs[25:]
    nbs, efs, ebs, cfs, cbs = refs[:5]
    well_rows, wells, sems = refs[5:13], refs[13], refs[14]
    depth, rows, cols = head_new.shape
    layers, ext_rows, ext_cols = hx.shape
    chunks_of_rows = ext_rows // 8
    n_wells = wells.shape[1]
    groups = n_wells // LANES
    me_e, me_n, me_l = lax.axis_index("east"), lax.axis_index("north"), lax.axis_index("layer")

    lane = iota((8, LANES), 1)
    low_half = lane < LANES // 2
    extra = pl.ds(cols, LANES)
    inside_cols = pl.ds(0, cols)
    inner = pl.ds(8, rows)
    starts = (depth * me_l, depth * (1 - me_l))
    high, low = pl.ds(rows + 8, 8), pl.ds(0, 8)

    small, large = [], []

    def load(found, src_ref, dst_ref):
        copy = pltpu.make_async_copy(src_ref, dst_ref, sems.at[len(small) + len(large)])
        copy.start()
        found.append(copy)

    for src_ref, dst_ref in zip(well_refs, well_rows):
        load(small, src_ref, dst_ref)
    for who in (0, 1):
        here = pl.ds(starts[who], depth)
        for a in range(4):
            load(large, fields[who][2 + a], staged[a].at[here])
        b_nf, b_nb, b_ef, b_eb, b_cf, b_cb = halos[who]
        load(large, b_nb, nbs.at[who])
        load(large, b_eb, ebs.at[who])
        load(large, b_cb, cbs.at[who])
        load(large, fields[who][0], hx.at[here, inner, inside_cols])
        load(large, b_nf.at[0], hx.at[here, high, inside_cols])
        load(large, b_nf.at[1], hx.at[here, low, inside_cols])
        load(large, b_ef, efs.at[who])
        load(large, b_cf, cfs.at[who])
        there = here if who == 0 else pl.ds(depth - 2 * me_l, 2)
        load(large, fields[who][1], tx.at[there, inner, inside_cols])

    def fill_fields():
        for who in (0, 1):
            base = starts[who]

            def fill(z, carry):
                zz = base + z
                for dst, ref in zip((ke, kn, kv, st), staged):
                    dst[zz, inner, inside_cols] = ref[zz].astype(F32)
                for side, at_rows in ((0, high), (1, low)):
                    tx[zz, at_rows, inside_cols] = roll(
                        hx[zz, at_rows, inside_cols], 2 if side == 0 else 6, 0
                    )
                    for half, pair in ((0, (ke, kn)), (1, (kv, st))):
                        two = nbs[who, side, z, pl.ds(16 * half, 16)].astype(F32)
                        pair[0][zz, at_rows, inside_cols] = two[:8]
                        pair[1][zz, at_rows, inside_cols] = two[8:]
                right, left = efs[who, 0, z], efs[who, 1, z]
                for j in range(rows // 8):
                    both = jnp.where(
                        low_half, roll(right, -HALO * j, 1), roll(left, LANES - HALO - HALO * j, 1)
                    )
                    hx[zz, pl.ds(8 + 8 * j, 8), extra] = both
                    tx[zz, pl.ds(8 + 8 * j, 8), extra] = jnp.where(
                        low_half, roll(both, 2 - HALO, 1), roll(both, HALO - 2, 1)
                    )
                for half, pair in ((0, (ke, kn)), (1, (kv, st))):
                    rights = ebs[who, 0, z, pl.ds(16 * half, 16)].astype(F32)
                    lefts = ebs[who, 1, z, pl.ds(16 * half, 16)].astype(F32)
                    for k in (0, 1):
                        right, left = rights[8 * k:8 * k + 8], lefts[8 * k:8 * k + 8]
                        for j in range(rows // 8):
                            pair[k][zz, pl.ds(8 + 8 * j, 8), extra] = jnp.where(
                                low_half,
                                roll(right, -HALO * j, 1),
                                roll(left, LANES - HALO - HALO * j, 1),
                            )
                return carry

            lax.fori_loop(0, depth, fill, 0)
            for r, at_rows in ((0, high), (1, low)):
                right, left = cfs[who, 2 * r], cfs[who, 2 * r + 1]
                rights = cbs[who, 2 * r].astype(F32)[:8]
                lefts = cbs[who, 2 * r + 1].astype(F32)[:8]
                for z in range(depth):
                    both = jnp.where(
                        low_half, roll(right, -HALO * z, 1), roll(left, LANES - HALO - HALO * z, 1)
                    )
                    hx[base + z, at_rows, extra] = both
                    tx[base + z, at_rows, extra] = roll(both, 2 if r == 0 else 6, 0)
                    for a, dst in enumerate((ke, kn, kv, st)):
                        slot = a * depth + z
                        dst[base + z, at_rows, extra] = jnp.where(
                            low_half,
                            roll(rights, -HALO * slot, 1),
                            roll(lefts, LANES - HALO - HALO * slot, 1),
                        )

    for copy in small:
        copy.wait()
    wells[...] = jnp.full(wells.shape, -1e6, F32)
    width = pl.ds(0, well_rows[0].shape[1])
    for row, ref in enumerate(well_rows[:5]):
        wells[pl.ds(row, 1), width] = ref[...].astype(F32)
    band = well_rows[5][...]
    bands = well_rows[7][...]
    price = jnp.zeros(band.shape, F32)
    for b in range(bands.shape[1]):
        price = jnp.where(band == b, bands[0:1, b:b + 1], price)
    wells[pl.ds(5, 1), width] = price
    wells[pl.ds(6, 1), width] = well_rows[6][...]

    at_east = wells[0:1, :] - (me_e * cols).astype(F32)
    at_north = wells[1:2, :] - (me_n * rows).astype(F32)
    near = (
        (at_east >= -REACH) & (at_east < cols + REACH)
        & (at_north >= -REACH) & (at_north < rows + REACH)
    )
    mine = (at_east >= 0) & (at_east < cols) & (at_north >= 0) & (at_north < rows)
    near_row = jnp.where(near, 1.0, 0.0)
    near_tile = jnp.concatenate(
        [near_row[:, LANES * k:LANES * (k + 1)] for k in range(groups)], axis=0
    )
    before = (iota((LANES, LANES), 0) < iota((LANES, LANES), 1)).astype(F32).astype(BF16)
    in_row = dot(near_tile.astype(BF16), before, NN)
    above = (iota((groups, groups), 1) < iota((groups, groups), 0)).astype(F32).astype(BF16)
    rows_above = jnp.sum(dot(above, near_tile.astype(BF16), NN), axis=1, keepdims=True)
    rank = jnp.where(near_tile > 0, in_row + rows_above, -1.0)
    total_near = jnp.sum(near_tile).astype(jnp.int32)
    chunks = (total_near + (SLOTS - 1)) // SLOTS

    place = jnp.concatenate(
        [
            jnp.where(at_east < 0, at_east + ext_cols, at_east),
            at_north + 8.0,
            wells[2:7, :],
            jnp.where(mine, 1.0, 0.0),
        ],
        axis=0,
    )
    place_parts = jnp.concatenate([p.astype(F32) for p in split(place, 3)], axis=0).astype(BF16)
    slot_of = iota((SLOTS, LANES), 0).astype(F32)

    def build_places(chunk):
        first = (chunk * SLOTS).astype(F32) if not isinstance(chunk, int) else float(chunk * SLOTS)
        for k in range(groups):
            row = rank[k:k + 1, :] - first
            pt[:, pl.ds(LANES * k, LANES)] = jnp.where(slot_of == row, 1.0, 0.0).astype(BF16)

    def one_hots(comp):
        col = jnp.where(iota((ext_cols, SLOTS), 0).astype(F32) == comp[0:1], 1.0, 0.0)
        row = jnp.where(iota((ext_rows, SLOTS), 0).astype(F32) == comp[1:2], 1.0, 0.0)
        return col.astype(BF16), row

    def add_wells(chunk, first):
        build_places(chunk)
        three = dot(place_parts, pt[...], NT)
        comp = three[0:8] + three[8:16] + three[16:24]
        comps[chunk] = comp
        col_hot, row_hot = one_hots(comp)
        weights = []
        for z in range(layers):
            found = dot(ke[z].astype(BF16), col_hot, NN)
            k_at = jnp.sum(found * row_hot, axis=0, keepdims=True)
            screened = (comp[2:3] <= z) & (comp[3:4] >= z)
            weights.append(jnp.where(screened, k_at, 0.0))
        weight = jnp.concatenate(weights, axis=0)
        total = jnp.sum(weight, axis=0, keepdims=True)
        share = weight / jnp.where(total > 0, total, 1.0)
        shares[chunk] = share
        pumped = share * comp[4:5]
        priced = pumped * comp[5:6]
        col_two = jnp.concatenate([col_hot, col_hot], axis=1)
        for z in range(layers):
            left = []
            for value in (pumped, priced):
                top, rest = split(value[z:z + 1], 2)
                left.append(
                    jnp.concatenate([row_hot * top.astype(F32), row_hot * rest.astype(F32)], axis=1)
                )
            left = jnp.concatenate(left, axis=0).astype(BF16)
            field = dot(left, col_two, NT)
            if first:
                src[z] = field[:ext_rows]
                lw[z] = field[ext_rows:]
            else:
                src[z] = src[z] + field[:ext_rows]
                lw[z] = lw[z] + field[ext_rows:]

    for copy in large:
        copy.wait()
    fill_fields()
    add_wells(0, True)

    def more_wells(chunk, carry):
        add_wells(chunk, False)
        return carry

    lax.fori_loop(1, chunks, more_wells, 0)

    wide = (8, ext_cols)
    sub = iota(wide, 0)
    col = iota(wide, 1)
    closed_col = ((col == cols - 1) & (me_e == n_east - 1)) | ((col == ext_cols - 1) & (me_e == 0))
    open_east = jnp.where(closed_col, 0.0, 2.0)
    open_low = jnp.where((sub == 7) & (me_n == 0), 0.0, 2.0)
    open_high = jnp.where((sub == 7) & (me_n == n_north - 1), 0.0, 2.0)

    def east(v):
        return roll(v, ext_cols - 1, 1)

    def west(v):
        return roll(v, 1, 1)

    def north(now, after):
        return jnp.where(sub < 7, roll(now, 7, 0), roll(after, 7, 0))

    def south(now, prior):
        return jnp.where(sub > 0, roll(now, 1, 0), roll(prior, 1, 0))

    fu[0] = jnp.zeros((ext_rows, ext_cols), F32)

    def row_chunks(begin, end, unit, body, carry):
        if end - begin == unit:
            for j in range(begin, end):
                carry = body(j, carry)
            return carry

        def several(k, carry):
            for i in range(unit):
                carry = body(begin + k * unit + i, carry)
            return carry

        return lax.fori_loop(0, (end - begin) // unit, several, carry)

    def at(j):
        return pl.ds(8 * j if isinstance(j, int) else pl.multiple_of(8 * j, 8), 8)

    def next_of(j):
        return min(j + 1, chunks_of_rows - 1) if isinstance(j, int) else jnp.minimum(j + 1, chunks_of_rows - 1)

    def start(z, carry):
        up = jnp.minimum(z + 1, layers - 1)
        down = jnp.maximum(z - 1, 0)
        open_up = jnp.where(z < layers - 1, 2.0, 0.0)

        def chunk(j, carry):
            fn_prior, gn_prior, k_n, h = carry
            k_e, k_u, k_u2 = ke[z, at(j)], kv[z, at(j)], kv[up, at(j)]
            k_e2 = east(k_e)
            k_after, h_after = kn[z, at(next_of(j))], hx[z, at(next_of(j))]
            k_n2 = north(k_n, k_after)
            f_e = open_east * k_e * k_e2 * reciprocal(k_e + k_e2)
            if isinstance(j, int):
                opened = open_low if j == 0 else open_high if j == chunks_of_rows - 2 else 2.0
            else:
                edge = ((j == 0) & (me_n == 0)) | ((j == chunks_of_rows - 2) & (me_n == n_north - 1))
                opened = jnp.where((sub == 7) & edge, 0.0, 2.0)
            f_n = opened * k_n * k_n2 * reciprocal(k_n + k_n2)
            f_u = open_up * k_u * k_u2 * reciprocal(k_u + k_u2)
            f_d = fu[z, at(j)]
            fe[z, at(j)] = f_e
            fn[z, at(j)] = f_n
            fu[z + 1, at(j)] = f_u
            diagonal = st[z, at(j)] + f_e + west(f_e) + f_n + south(f_n, fn_prior) + f_u + f_d
            inverse = reciprocal(diagonal)
            inv[z, at(j)] = inverse
            g_e = f_e * (east(h) - h)
            g_n = f_n * (north(h, h_after) - h)
            g_u = f_u * (hx[up, at(j)] - h)
            g_d = f_d * (h - hx[down, at(j)])
            residual = (g_e - west(g_e)) + (g_n - south(g_n, gn_prior)) + (g_u - g_d)
            d0[z, at(j)] = inverse * (residual - src[z, at(j)])
            return f_n, g_n, k_after, h_after

        none = jnp.zeros(wide, F32)
        row_chunks(0, chunks_of_rows, START_UNIT, chunk, (none, none, kn[z, at(0)], hx[z, at(0)]))
        return carry

    lax.fori_loop(0, layers, start, 0)

    def sweep(field, margin, finish, chunk_from, chunk_to):
        def layer(i, carry):
            z = (depth - margin) * me_l + i
            up = jnp.minimum(z + 1, layers - 1)
            down = jnp.maximum(z - 1, 0)

            def chunk(j, carry):
                b_prior, d = carry
                d_after = field[z, at(next_of(j))]
                f_e, f_n = fe[z, at(j)], fn[z, at(j)]
                b = f_n * d
                moved = f_e * east(d) + west(f_e * d)
                moved = moved + f_n * north(d, d_after) + south(b, b_prior)
                moved = moved + fu[z + 1, at(j)] * field[up, at(j)] + fu[z, at(j)] * field[down, at(j)]
                finish(i, z, j, d, inv[z, at(j)] * moved)
                return b, d_after

            if chunk_from == 0:
                b_prior = jnp.zeros(wide, F32)
            else:
                b_prior = fn[z, at(chunk_from - 1)] * field[z, at(chunk_from - 1)]
            unit = SWEEP_UNIT if chunk_from == 0 else LAST_UNIT
            row_chunks(chunk_from, chunk_to, unit, chunk, (b_prior, field[z, at(chunk_from)]))
            return carry

        lax.fori_loop(0, depth + margin, layer, 0)

    (a1, b1), (a2, b2) = steps_of()

    def first_sweep(i, z, j, d, pulled):
        s1[z, at(j)] = pulled
        d1[z, at(j)] = a1 * d + b1 * pulled

    def end_forward(i, z, j, d, pulled):
        s2 = s1[z, at(j)] - d + pulled
        d2 = a2 * d + b2 * s2
        new = hx[z, at(j)] + d0[z, at(j)] + d + d2
        hx[z, at(j)] = new
        load = new - tx[z, at(j)] - lw[z, at(j)]
        src[z, at(j)] = inv[z, at(j)] * load

    sweep(d0, 3, first_sweep, 0, chunks_of_rows)
    sweep(d1, 2, end_forward, 0, chunks_of_rows)
    sweep(src, 1, first_sweep, 0, chunks_of_rows)

    parts[...] = jnp.zeros(parts.shape, F32)
    st[0, at(0)] = jnp.zeros(wide, F32)

    def end_adjoint(i, z, j, d, pulled):
        s2 = s1[z, at(j)] - d + pulled
        d2 = a2 * d + b2 * s2
        adj = src[z, at(j)] + d + d2
        adjoint[i, at(j - 1)] = adj[:, :cols]
        new = hx[z, at(j), inside_cols]
        head_new[i, at(j - 1)] = new
        departure = new - tx[z, at(j), inside_cols]
        st[0, at(0), inside_cols] = st[0, at(0), inside_cols] + departure * departure

    sweep(d1, 0, end_adjoint, 1, chunks_of_rows - 1)

    squared = st[0, at(0), inside_cols]
    squared = jnp.sum(squared, axis=0, keepdims=True)
    squared = sum(squared[:, LANES * k:LANES * (k + 1)] for k in range(cols // LANES))
    squared = squared * (1.0 / (float(layers * rows * cols) * n_east * n_north))
    base_layer = jnp.where(me_l == 0, 1.0, 0.0)

    def collect(chunk, first):
        comp = comps[chunk]
        share = shares[chunk]
        col_hot, row_hot = one_hots(comp)
        col_hot, row_hot = col_hot[:cols], row_hot[8:8 + rows]
        head_at = jnp.zeros((1, SLOTS), F32)
        adj_at = jnp.zeros((1, SLOTS), F32)
        for i in range(depth):
            z_share = jnp.where(me_l == 0, share[i:i + 1], share[depth + i:depth + i + 1])
            stack = split(head_new[i], 2) + split(adjoint[i], 2)
            found = [dot(piece, col_hot, NN) for piece in stack]
            head_at += z_share * jnp.sum((found[0] + found[1]) * row_hot, axis=0, keepdims=True)
            adj_at += z_share * jnp.sum((found[2] + found[3]) * row_hot, axis=0, keepdims=True)
        lift = (comp[6:7] * base_layer - head_at) * comp[7:8]
        priced = comp[5:6] * lift
        slope = priced - adj_at * comp[7:8]
        three = jnp.concatenate(
            [p.astype(F32) for p in split(slope, 3)] + [jnp.zeros((5, SLOTS), F32)], axis=0
        ).astype(BF16)
        if not first:
            build_places(chunk)
        spread = dot(three, pt[...], NN)
        spread = spread[0:1] + spread[1:2] + spread[2:3]
        tile = jnp.concatenate(
            [spread[:, LANES * k:LANES * (k + 1)] for k in range(groups)], axis=0
        )
        parts[pl.ds(0, groups)] += tile
        parts[pl.ds(groups, 1)] += priced * comp[4:5]

    @pl.when(chunks > 1)
    def _():
        build_places(0)

    collect(0, True)

    def collect_more(chunk, carry):
        collect(chunk, False)
        return carry

    lax.fori_loop(1, chunks, collect_more, 0)
    parts[pl.ds(groups + 1, 1)] = squared


def run_solve(sizes, fields, moved, wells):
    depth, rows, cols = fields[0].shape
    layers, ext_rows, ext_cols = 2 * depth, rows + 16, cols + LANES
    n_wells = wells[0].shape[1]
    groups = -(-n_wells // LANES)
    out = jax.ShapeDtypeStruct((depth, rows, cols), F32)
    ext = pltpu.VMEM((layers, ext_rows, ext_cols), F32)
    operands = (*fields, *moved, *wells)
    return pl.pallas_call(
        functools.partial(solve, sizes),
        out_shape=[out, out, jax.ShapeDtypeStruct((groups + 8, LANES), F32)],
        in_specs=[pl.BlockSpec(memory_space=pltpu.HBM)] * len(operands),
        out_specs=[pl.BlockSpec(memory_space=pltpu.VMEM)] * 3,
        scratch_shapes=[ext] * 8
        + [pltpu.VMEM((layers + 1, ext_rows, ext_cols), F32)]
        + [ext] * 6
        + [
            pltpu.VMEM((SLOTS, groups * LANES), BF16),
            pltpu.VMEM((groups, 8, SLOTS), F32),
            pltpu.VMEM((groups, 8, SLOTS), F32),
        ]
        + [pltpu.VMEM((layers, rows, cols), BF16)] * 4
        + [
            pltpu.VMEM((2, 2, depth, 32, cols), BF16),
            pltpu.VMEM((2, 2, depth, 8, LANES), F32),
            pltpu.VMEM((2, 2, depth, 32, LANES), BF16),
            pltpu.VMEM((2, 4, 8, LANES), F32),
            pltpu.VMEM((2, 4, 16, LANES), BF16),
        ]
        + [pltpu.VMEM(w.shape, w.dtype) for w in wells]
        + [pltpu.VMEM((8, groups * LANES), F32), pltpu.SemaphoreType.DMA((8 + 26,))],
        compiler_params=pltpu.CompilerParams(vmem_limit_bytes=60 * 1024 * 1024),
        name="solve",
    )(*operands)


def add_up(sizes, part, out, box0, box1, box2, box3, send_sem, recv_sem):
    n_east, n_x, n_z = sizes
    me_e, me_n, me_l = lax.axis_index("east"), lax.axis_index("north"), lax.axis_index("layer")
    me_x, me_z = me_n // n_z, lax.rem(me_n, n_z)
    phases = (
        (box0, 2, me_l, lambda i: (me_e, me_n, i)),
        (box1, n_z, me_z, lambda i: (me_e, me_x * n_z + i, me_l)),
        (box2, n_east, me_e, lambda i: (i, me_n, me_l)),
        (box3, n_x, me_x, lambda i: (me_e, i * n_z + me_z, me_l)),
    )
    barrier = pltpu.get_barrier_semaphore()
    peers = 0
    for _, size, mine, device in phases:
        for k in range(1, size):
            pl.semaphore_signal(
                barrier, inc=1, device_id=device(lax.rem(mine + k, size)), device_id_type=MESH
            )
            peers += 1
    pl.semaphore_wait(barrier, peers)
    total = part[...]
    used = 0
    for box, size, mine, device in phases:
        box[mine] = total
        copies = []
        for k in range(1, size):
            copy = pltpu.make_async_remote_copy(
                src_ref=box.at[mine],
                dst_ref=box.at[mine],
                send_sem=send_sem.at[used],
                recv_sem=recv_sem.at[used],
                device_id=device(lax.rem(mine + k, size)),
                device_id_type=MESH,
            )
            copy.start()
            copies.append(copy)
            used += 1
        for copy in copies:
            copy.wait()
        total = box[0]
        for k in range(1, size):
            total = total + box[k]
    tail = part.shape[0] - 8
    out[pl.ds(0, tail)] = total[:tail]
    out[pl.ds(tail, 8)] = jnp.broadcast_to(
        jnp.sum(total[tail:], axis=1, keepdims=True), (8, LANES)
    )


def run_add_up(sizes, part):
    peers = 1 + sum(n - 1 for n in sizes)
    return pl.pallas_call(
        functools.partial(add_up, sizes),
        out_shape=jax.ShapeDtypeStruct(part.shape, F32),
        in_specs=[pl.BlockSpec(memory_space=pltpu.VMEM)],
        out_specs=pl.BlockSpec(memory_space=pltpu.VMEM),
        scratch_shapes=[
            pltpu.VMEM((n,) + part.shape, F32) for n in (2, sizes[2], sizes[0], sizes[1])
        ]
        + [pltpu.SemaphoreType.DMA((peers,)), pltpu.SemaphoreType.DMA((peers,))],
        compiler_params=pltpu.CompilerParams(collective_id=1, has_side_effects=True),
        name="add_up",
    )(part)


def per_device(
    sizes,
    head_old, head_target, conductivity_east, conductivity_north, conductivity_vertical, storage,
    well_east, well_north, screen_top, screen_bottom, tariff_band, pump_rates, ground_level,
    band_prices,
):
    n_east, n_x, n_z = sizes
    n_wells = well_east.shape[0]
    wells = [
        w.reshape(1, -1)
        for w in (
            well_east, well_north, screen_top, screen_bottom, pump_rates, tariff_band,
            ground_level, band_prices,
        )
    ]
    fields = (
        head_old, head_target, conductivity_east, conductivity_north, conductivity_vertical, storage
    )
    moved = run_exchange((n_east, n_x * n_z), *fields)
    head_new, adjoint, part = run_solve((n_east, n_x * n_z), fields, moved, wells)
    total = run_add_up(sizes, part)
    tail = part.shape[0] - 8
    rate_gradient = total[:tail].reshape(-1)[:n_wells]
    return head_new, adjoint, rate_gradient, total[tail, 0], total[tail + 1, 0]


def solution(mesh):
    field = P("layer", "north", "east")
    n_north = mesh.shape["north"]
    n_x = 4 if n_north % 4 == 0 else 1
    sizes = (mesh.shape["east"], n_x, n_north // n_x)
    return jax.shard_map(
        functools.partial(per_device, sizes),
        mesh=mesh,
        in_specs=(field,) * 6 + (P(),) * 8,
        out_specs=(field, field, P(), P(), P()),
        check_vma=False,
    )
```

```python
import functools

import jax
import jax.numpy as jnp
from jax import lax
from jax.experimental import pallas as pl
from jax.experimental.layout import Layout, with_layout_constraint
from jax.experimental.pallas import tpu as pltpu
from jax.sharding import PartitionSpec as P

MESH = pl.DeviceIdType.MESH
F32 = jnp.float32
BF16 = jnp.bfloat16

SWEEPS = 3
CENTRE = 1.0
HALF_WIDTH = 0.95

HALO = 8
REACH = 5
LANES = 128
SLOTS = 128
START_UNIT, SWEEP_UNIT, LAST_UNIT = 9, 18, 16


def steps_of():
    sigma = CENTRE / HALF_WIDTH
    factor = 1.0 / sigma
    found = []
    for _ in range(SWEEPS - 1):
        after = 1.0 / (2.0 * sigma - factor)
        found.append((after * factor, 2.0 * after / HALF_WIDTH))
        factor = after
    return found


def iota(shape, dim):
    return lax.broadcasted_iota(jnp.int32, shape, dim)


def roll(value, shift, dim):
    shift = shift % value.shape[dim]
    return pltpu.roll(value, shift, dim) if shift else value


def extended(value, sides, width):
    for axis, dim in sides:
        size, length = (lax.axis_size(axis), value.shape[dim])
        up = [(i, (i + 1) % size) for i in range(size - 1)]
        down = [(j, i) for i, j in up]
        last = lax.slice_in_dim(value, length - width, length, axis=dim)
        initial = lax.slice_in_dim(value, 0, width, axis=dim)
        before = lax.ppermute(last, axis, up)
        after = lax.ppermute(initial, axis, down)
        value = jnp.concatenate([before, value, after], axis=dim)
    return value


def harmonic(first, second):
    total = first + second
    return 2.0 * first * second / jnp.where(total > 0, total, 1.0)


def face_terms(east_pad, north_pad, up_pad, stored):
    face_east = harmonic(east_pad[:, :, :-1], east_pad[:, :, 1:])
    face_north = harmonic(north_pad[:, :-1], north_pad[:, 1:])
    face_up = harmonic(up_pad[:-1], up_pad[1:])
    diagonal = stored + face_east[:, :, :-1] + face_east[:, :, 1:]
    diagonal = diagonal + face_north[:, :-1] + face_north[:, 1:]
    diagonal = diagonal + face_up[:-1] + face_up[1:]
    positive = diagonal > 0
    inverse = jnp.where(positive, 1.0 / jnp.where(positive, diagonal, 1.0), 0.0)
    return (stored, face_east, face_north, face_up, inverse)


def coefficients(padded_coefs):
    stacked = padded_coefs.astype(jnp.float32)
    east_pad = stacked[0][1:-1, 1:-1, :]
    north_pad = stacked[1][1:-1, :, 1:-1]
    up_pad = stacked[2][:, 1:-1, 1:-1]
    stored = stacked[3][1:-1, 1:-1, 1:-1]
    return face_terms(east_pad, north_pad, up_pad, stored)


def apply_operator(padded, storage_part, face_east, face_north, face_up):
    center = padded[1:-1, 1:-1, 1:-1]
    step_east = padded[1:-1, 1:-1, 1:] - padded[1:-1, 1:-1, :-1]
    step_north = padded[1:-1, 1:, 1:-1] - padded[1:-1, :-1, 1:-1]
    step_up = padded[1:, 1:-1, 1:-1] - padded[:-1, 1:-1, 1:-1]
    flux_east = face_east * step_east
    flux_north = face_north * step_north
    flux_up = face_up * step_up
    total = storage_part * center + (flux_east[:, :, :-1] - flux_east[:, :, 1:])
    total = total + (flux_north[:, :-1] - flux_north[:, 1:])
    return total + (flux_up[:-1] - flux_up[1:])


def keep_whole(field):
    return field


def chebyshev(start, rhs, operate, trim, precondition):
    if start is None:
        residual = rhs
    else:
        residual = trim(rhs) - operate(start)
    direction = precondition(residual) / CENTRE
    if start is None:
        iterate = direction
    else:
        iterate = trim(start) + direction
    sigma = CENTRE / HALF_WIDTH
    factor = 1.0 / sigma
    for sweep_index in range(SWEEPS - 1):
        residual = trim(residual) - operate(direction)
        factor_next = 1.0 / (2.0 * sigma - factor)
        direction = factor_next * factor * trim(
            direction
        ) + 2.0 * factor_next / HALF_WIDTH * precondition(residual)
        iterate = trim(iterate) + direction
        factor = factor_next
    return iterate


def plain(
    head_old,
    head_target,
    conductivity_east,
    conductivity_north,
    conductivity_vertical,
    storage,
    well_east,
    well_north,
    screen_top,
    screen_bottom,
    tariff_band,
    pump_rates,
    ground_level,
    band_prices,
):
    depth_cells, north_cells, east_cells = head_old.shape
    stacked_coefs = jnp.stack(
        (conductivity_east, conductivity_north, conductivity_vertical, storage)
    )
    padded_coefs = extended(stacked_coefs, (("east", 3), ("north", 2), ("layer", 1)), 1)
    margin = 0
    top_level = coefficients(padded_coefs)
    levels = [None] * (margin + 1)
    levels[margin] = top_level

    def margin_of(field):
        return (field.shape[0] - depth_cells) // 2

    def precondition(residual):
        return levels[margin_of(residual)][4] * residual

    def operate(field):
        padded = extended(field, (("east", 2), ("north", 1), ("layer", 0)), 1)
        level = levels[0]
        return apply_operator(padded, level[0], level[1], level[2], level[3])

    east_start = lax.axis_index("east") * east_cells
    north_start = lax.axis_index("north") * north_cells
    layer_start = lax.axis_index("layer") * depth_cells
    local_east = well_east - east_start
    local_north = well_north - north_start
    owning = (
        (local_east >= 0)
        & (local_east < east_cells)
        & (local_north >= 0)
        & (local_north < north_cells)
    ).astype(jnp.float32)
    cells = jnp.clip(local_north, 0, north_cells - 1) * east_cells + jnp.clip(
        local_east, 0, east_cells - 1
    )
    depth = layer_start + jnp.arange(depth_cells, dtype=jnp.int32)[:, None]
    screened = ((depth >= screen_top[None, :]) & (depth <= screen_bottom[None, :])).astype(
        jnp.float32
    ) * owning[None, :]
    weights = (
        conductivity_east.reshape(depth_cells, north_cells * east_cells)[:, cells].astype(
            jnp.float32
        )
        * screened
    )
    totals = lax.psum(jnp.sum(weights, axis=0), "layer")
    shares = weights / (totals + (1.0 - owning))[None, :]
    flat_shape = (depth_cells, north_cells * east_cells)
    source = (
        jnp.zeros(flat_shape, jnp.float32)
        .at[:, cells]
        .add(pump_rates[None, :] * shares)
        .reshape(head_old.shape)
    )
    stored = storage.astype(jnp.float32)
    rhs = stored * head_old - source
    head_new = chebyshev(head_old, rhs, operate, keep_whole, precondition)
    departure = head_new - head_target
    misfit_part = jnp.sum(departure * departure)
    all_cells = float(
        depth_cells
        * north_cells
        * east_cells
        * lax.axis_size("east")
        * lax.axis_size("north")
        * lax.axis_size("layer")
    )
    head_part = jnp.sum(shares * head_new.reshape(flat_shape)[:, cells], axis=0)
    head_screen, misfit_total = lax.psum((head_part, misfit_part), ("east", "north", "layer"))
    band_ids = jnp.arange(band_prices.shape[0], dtype=jnp.int32)
    prices = jnp.sum(
        jnp.where(tariff_band[:, None] == band_ids[None, :], band_prices[None, :], 0.0), axis=1
    )
    load = (
        departure.reshape(flat_shape)
        .at[:, cells]
        .add(-(prices * pump_rates)[None, :] * shares)
        .reshape(head_old.shape)
    )
    adjoint_head = chebyshev(None, load, operate, keep_whole, precondition)
    adjoint_part = jnp.sum(shares * adjoint_head.reshape(flat_shape)[:, cells], axis=0)
    adjoint_screen = lax.psum(adjoint_part, ("east", "north", "layer"))
    misfit = misfit_total / all_cells
    lift = ground_level - head_screen
    rate_gradient = prices * lift - adjoint_screen
    pumping_cost = jnp.sum(prices * pump_rates * lift)
    return (head_new, adjoint_head, rate_gradient, pumping_cost, misfit)


def split(value, parts):
    found = []
    for _ in range(parts):
        top = value.astype(BF16)
        found.append(top)
        value = value - top.astype(F32)
    return found


def dot(a, b, dims):
    return lax.dot_general(a, b, (dims, ((), ())), preferred_element_type=F32)


NN = ((1,), (0,))
NT = ((1,), (1,))


def reciprocal(x):
    first = pl.reciprocal(x, approx=True)
    return first * (2.0 - x * first)


def kernel(sizes, *refs):
    n_east, n_x, n_z = sizes
    n_north = n_x * n_z
    fields, well_refs, refs = refs[:6], refs[6:14], refs[14:]
    out_new, out_adjoint, out_slope, out_cost, out_misfit, out_crowded = refs[:6]
    hx, tx, ke, kn, kv, st, fe, fn, fu, inv, src, lw, d0, d1, s1, pt = refs[6:22]
    head_new, adjoint, parts = refs[22:25]
    staged, (nbs, efs, ebs, cfs, cbs), refs = refs[25:29], refs[29:34], refs[34:]
    (s_nf, s_nb, s_ef, s_eb, s_cf, s_cb), refs = refs[:6], refs[6:]
    well_rows, wells, boxes, refs = refs[:8], refs[8], refs[9:13], refs[13:]
    load_sem, send_sem, recv_sem, sum_send, sum_recv = refs
    depth, rows, cols = head_new.shape
    layers, ext_rows, ext_cols = hx.shape
    chunks_of_rows = ext_rows // 8
    groups = wells.shape[1] // LANES
    me_e, me_n, me_l = lax.axis_index("east"), lax.axis_index("north"), lax.axis_index("layer")
    me_x, me_z = me_n // n_z, lax.rem(me_n, n_z)
    own, other = depth * me_l, depth * (1 - me_l)
    own_layers = pl.ds(own, depth)

    def east_of(side):
        return lax.rem(me_e + (n_east - 1 if side == 0 else 1), n_east)

    def north_of(side):
        return lax.rem(me_n + (n_north - 1 if side == 0 else 1), n_north)

    partner = (me_e, me_n, 1 - me_l)
    to_north = [(me_e, north_of(s), me_l) for s in (0, 1)]
    to_east = [(east_of(s), me_n, me_l) for s in (0, 1)]
    to_corner = [(east_of(c), north_of(r), me_l) for r in (0, 1) for c in (0, 1)]
    phases = []
    for box, size, mine, device in (
        (boxes[0], 2, me_l, lambda i: (me_e, me_n, i)),
        (boxes[1], n_z, me_z, lambda i: (me_e, me_x * n_z + i, me_l)),
        (boxes[2], n_east, me_e, lambda i: (i, me_n, me_l)),
        (boxes[3], n_x, me_x, lambda i: (me_e, i * n_z + me_z, me_l)),
    ):
        phases.append((box, mine, [device(lax.rem(mine + k, size)) for k in range(1, size)]))

    greeted = [partner] + to_north + to_east + to_corner
    for _, _, peers in phases:
        greeted = greeted + peers
    barrier = pltpu.get_barrier_semaphore()
    for device in greeted:
        pl.semaphore_signal(barrier, inc=1, device_id=device, device_id_type=MESH)

    loaded = [0]

    def load(src_ref, dst_ref):
        copy = pltpu.make_async_copy(src_ref, dst_ref, load_sem.at[loaded[0]])
        loaded[0] += 1
        copy.start()
        return copy

    lane = iota((8, LANES), 1)
    group = lane // HALO
    wide_sub = iota((8, cols), 0)
    last = cols - LANES
    low_half = lane < LANES // 2
    extra = pl.ds(cols, LANES)
    inside_cols = pl.ds(0, cols)
    inner = pl.ds(8, rows)
    edge_rows = (pl.ds(rows + 8, 8), pl.ds(0, 8))

    block_loads = [
        load(fields[0], hx.at[own_layers, inner, inside_cols]),
        load(fields[1], tx.at[own_layers, inner, inside_cols]),
    ] + [load(fields[2 + a], staged[a].at[own_layers]) for a in range(4)]
    well_loads = [load(a, b) for a, b in zip(well_refs, well_rows)]
    for copy in block_loads:
        copy.wait()

    def pack(z, carry):
        for side in (0, 1):
            c0 = last * side
            kept = jnp.zeros((8, LANES), F32)
            fields = [jnp.zeros((8, LANES), F32) for _ in staged]
            for pair in range(rows // 16):
                tiles = [
                    ref[own + z, pl.ds(16 * pair, 16), pl.ds(c0, LANES)].astype(F32) for ref in staged
                ]
                for half in (0, 1):
                    j = 2 * pair + half
                    shift = HALO * j - (LANES - HALO) * side
                    h = hx[own + z, pl.ds(8 + 8 * j, 8), pl.ds(c0, LANES)]
                    t = tx[own + z, pl.ds(8 + 8 * j, 8), pl.ds(c0, LANES)]
                    if side == 0:
                        both = jnp.where(lane >= HALO - 2, roll(t, HALO - 2, 1), h)
                    else:
                        both = jnp.where(lane < LANES - HALO + 2, roll(t, 2 - HALO, 1), h)
                    here = group == j
                    kept = jnp.where(here, roll(both, shift, 1), kept)
                    for a in range(4):
                        piece = tiles[a][8 * half:8 * half + 8]
                        fields[a] = jnp.where(here, roll(piece, shift, 1), fields[a])
            s_ef[side, z] = kept
            s_eb[side, z, pl.ds(0, 16)] = jnp.concatenate(fields[:2], axis=0).astype(BF16)
            s_eb[side, z, pl.ds(16, 16)] = jnp.concatenate(fields[2:], axis=0).astype(BF16)
            r0 = (rows - 8) * side
            h = hx[own + z, pl.ds(8 + r0, 8), inside_cols]
            t = tx[own + z, pl.ds(8 + r0, 8), inside_cols]
            if side == 0:
                both = jnp.where(wide_sub >= HALO - 2, roll(t, HALO - 2, 0), h)
            else:
                both = jnp.where(wide_sub < 2, roll(t, 2, 0), h)
            s_nf[side, z] = both
            edge = [
                ref[own + z, pl.ds((rows - 16) * side, 16), :].astype(F32)[8 * side:8 * side + 8]
                for ref in staged
            ]
            s_nb[side, z, pl.ds(0, 16)] = jnp.concatenate(edge[:2], axis=0).astype(BF16)
            s_nb[side, z, pl.ds(16, 16)] = jnp.concatenate(edge[2:], axis=0).astype(BF16)
        return carry

    lax.fori_loop(0, depth, pack, 0)

    for r in (0, 1):
        for c in (0, 1):
            c0 = last * c
            kept = jnp.zeros((8, LANES), F32)
            mixed = jnp.zeros((8, LANES), F32)
            for z in range(depth):
                both = s_nf[r, z, :, pl.ds(c0, LANES)]
                kept = jnp.where(group == z, roll(both, HALO * z - (LANES - HALO) * c, 1), kept)
                for half in (0, 1):
                    two = s_nb[r, z, pl.ds(16 * half, 16), pl.ds(c0, LANES)].astype(F32)
                    for k in (0, 1):
                        slot = (2 * half + k) * depth + z
                        moved = roll(two[8 * k:8 * k + 8], HALO * slot - (LANES - HALO) * c, 1)
                        mixed = jnp.where(group == slot, moved, mixed)
            s_cf[2 * r + c] = kept
            s_cb[2 * r + c] = jnp.concatenate([mixed, mixed], axis=0).astype(BF16)

    pl.semaphore_wait(barrier, len(greeted))

    sent = [0]

    def send(src_ref, dst_ref, device):
        copy = pltpu.make_async_remote_copy(
            src_ref=src_ref,
            dst_ref=dst_ref,
            send_sem=send_sem.at[sent[0]],
            recv_sem=recv_sem.at[sent[0]],
            device_id=device,
            device_id_type=MESH,
        )
        sent[0] += 1
        copy.start()
        return copy

    norths, easts, corners = [], [], []
    for side in (0, 1):
        norths.append(send(s_nb.at[side], nbs.at[0, side], to_north[side]))
        norths.append(
            send(s_nf.at[side], hx.at[own_layers, edge_rows[side], inside_cols], to_north[side])
        )
    for side in (0, 1):
        easts.append(send(s_eb.at[side], ebs.at[0, side], to_east[side]))
        easts.append(send(s_ef.at[side], efs.at[0, side], to_east[side]))
    for d in range(4):
        corners.append(send(s_cb.at[d], cbs.at[0, d], to_corner[d]))
        corners.append(send(s_cf.at[d], cfs.at[0, d], to_corner[d]))
    two = (depth - 2) * (1 - me_l)
    blocks = [send(fields[2 + a], staged[a].at[own_layers], partner) for a in range(4)]
    blocks.append(send(fields[0], hx.at[own_layers, inner, inside_cols], partner))
    blocks.append(
        send(
            fields[1].at[pl.ds(two, 2)], tx.at[pl.ds(own + two, 2), inner, inside_cols], partner
        )
    )

    for copy in well_loads:
        copy.wait()
    wells[...] = jnp.full(wells.shape, -1e6, F32)
    width = pl.ds(0, well_rows[0].shape[1])
    for row, ref in enumerate(well_rows[:5]):
        wells[pl.ds(row, 1), width] = ref[...].astype(F32)
    band = well_rows[5][...]
    bands = well_rows[7][...]
    price = jnp.zeros(band.shape, F32)
    for b in range(bands.shape[1]):
        price = jnp.where(band == b, bands[0:1, b:b + 1], price)
    wells[pl.ds(5, 1), width] = price
    wells[pl.ds(6, 1), width] = well_rows[6][...]

    at_east = wells[0:1, :] - (me_e * cols).astype(F32)
    at_north = wells[1:2, :] - (me_n * rows).astype(F32)
    near = (
        (at_east >= -REACH) & (at_east < cols + REACH)
        & (at_north >= -REACH) & (at_north < rows + REACH)
    )
    mine = (at_east >= 0) & (at_east < cols) & (at_north >= 0) & (at_north < rows)
    near_row = jnp.where(near, 1.0, 0.0)
    near_tile = jnp.concatenate(
        [near_row[:, LANES * k:LANES * (k + 1)] for k in range(groups)], axis=0
    )
    before = (iota((LANES, LANES), 0) < iota((LANES, LANES), 1)).astype(F32).astype(BF16)
    in_row = dot(near_tile.astype(BF16), before, NN)
    above = (iota((groups, groups), 1) < iota((groups, groups), 0)).astype(F32).astype(BF16)
    rows_above = jnp.sum(dot(above, near_tile.astype(BF16), NN), axis=1, keepdims=True)
    rank = jnp.where(near_tile > 0, in_row + rows_above, -1.0)
    found = jnp.sum(jnp.sum(near_tile, axis=1, keepdims=True), axis=0, keepdims=True)
    crowded = jnp.where(found > SLOTS, 1.0, 0.0)

    place = jnp.concatenate(
        [
            jnp.where(at_east < 0, at_east + ext_cols, at_east),
            at_north + 8.0,
            wells[2:7, :],
            jnp.where(mine, 1.0, 0.0),
        ],
        axis=0,
    )
    place_parts = jnp.concatenate([p.astype(F32) for p in split(place, 3)], axis=0).astype(BF16)
    slot_of = iota((SLOTS, LANES), 0).astype(F32)

    for k in range(groups):
        pt[:, pl.ds(LANES * k, LANES)] = jnp.where(slot_of == rank[k:k + 1, :], 1.0, 0.0).astype(BF16)
    three = dot(place_parts, pt[...], NT)
    comp = three[0:8] + three[8:16] + three[16:24]
    col_hot = jnp.where(iota((ext_cols, SLOTS), 0).astype(F32) == comp[0:1], 1.0, 0.0)
    row_hot = jnp.where(iota((ext_rows, SLOTS), 0).astype(F32) == comp[1:2], 1.0, 0.0)
    col_hot = col_hot.astype(BF16)


    def fill_inner(base):
        def fill(z, carry):
            for dst, ref in zip((ke, kn, kv, st), staged):
                dst[base + z, inner, inside_cols] = ref[base + z].astype(F32)
            return carry

        lax.fori_loop(0, depth, fill, 0)

    def fill_east(who, base):
        def fill(z, carry):
            zz = base + z
            right, left = efs[who, 0, z], efs[who, 1, z]
            for j in range(rows // 8):
                both = jnp.where(
                    low_half, roll(right, -HALO * j, 1), roll(left, LANES - HALO - HALO * j, 1)
                )
                hx[zz, pl.ds(8 + 8 * j, 8), extra] = both
                tx[zz, pl.ds(8 + 8 * j, 8), extra] = jnp.where(
                    low_half, roll(both, 2 - HALO, 1), roll(both, HALO - 2, 1)
                )
            for half, pair in ((0, (ke, kn)), (1, (kv, st))):
                rights = ebs[who, 0, z, pl.ds(16 * half, 16)].astype(F32)
                lefts = ebs[who, 1, z, pl.ds(16 * half, 16)].astype(F32)
                for k in (0, 1):
                    right, left = rights[8 * k:8 * k + 8], lefts[8 * k:8 * k + 8]
                    for j in range(rows // 8):
                        pair[k][zz, pl.ds(8 + 8 * j, 8), extra] = jnp.where(
                            low_half,
                            roll(right, -HALO * j, 1),
                            roll(left, LANES - HALO - HALO * j, 1),
                        )
            return carry

        lax.fori_loop(0, depth, fill, 0)

    def fill_north(who, base):
        def fill(z, carry):
            zz = base + z
            for side, at_rows in enumerate(edge_rows):
                tx[zz, at_rows, inside_cols] = roll(
                    hx[zz, at_rows, inside_cols], 2 if side == 0 else 6, 0
                )
                for half, pair in ((0, (ke, kn)), (1, (kv, st))):
                    both = nbs[who, side, z, pl.ds(16 * half, 16)].astype(F32)
                    pair[0][zz, at_rows, inside_cols] = both[:8]
                    pair[1][zz, at_rows, inside_cols] = both[8:]
            return carry

        lax.fori_loop(0, depth, fill, 0)

    def fill_corners(who, base):
        for r, at_rows in enumerate(edge_rows):
            right, left = cfs[who, 2 * r], cfs[who, 2 * r + 1]
            rights = cbs[who, 2 * r].astype(F32)[:8]
            lefts = cbs[who, 2 * r + 1].astype(F32)[:8]
            for z in range(depth):
                both = jnp.where(
                    low_half, roll(right, -HALO * z, 1), roll(left, LANES - HALO - HALO * z, 1)
                )
                hx[base + z, at_rows, extra] = both
                tx[base + z, at_rows, extra] = roll(both, 2 if r == 0 else 6, 0)
                for a, dst in enumerate((ke, kn, kv, st)):
                    slot = a * depth + z
                    dst[base + z, at_rows, extra] = jnp.where(
                        low_half,
                        roll(rights, -HALO * slot, 1),
                        roll(lefts, LANES - HALO - HALO * slot, 1),
                    )

    fill_inner(own)
    for copy in easts:
        copy.wait_recv()
    forwards = [send(efs.at[0], efs.at[1], partner), send(ebs.at[0], ebs.at[1], partner)]
    fill_east(0, own)
    for copy in norths:
        copy.wait_recv()
    forwards.append(send(nbs.at[0], nbs.at[1], partner))
    for side in (0, 1):
        place_of = hx.at[own_layers, edge_rows[side], inside_cols]
        forwards.append(send(place_of, place_of, partner))
    for copy in corners:
        copy.wait_recv()
    forwards.append(send(cfs.at[0], cfs.at[1], partner))
    forwards.append(send(cbs.at[0], cbs.at[1], partner))
    fill_north(0, own)
    fill_corners(0, own)
    for copy in blocks:
        copy.wait_recv()
    fill_inner(other)
    for copy in forwards:
        copy.wait_recv()
    fill_east(1, other)
    fill_north(1, other)
    fill_corners(1, other)
    for copy in norths + easts + corners + blocks + forwards:
        copy.wait_send()

    weights = []
    for z in range(layers):
        found = dot(ke[z].astype(BF16), col_hot, NN)
        k_at = jnp.sum(found * row_hot, axis=0, keepdims=True)
        screened = (comp[2:3] <= z) & (comp[3:4] >= z)
        weights.append(jnp.where(screened, k_at, 0.0))
    weight = jnp.concatenate(weights, axis=0)
    total = jnp.sum(weight, axis=0, keepdims=True)
    share = weight / jnp.where(total > 0, total, 1.0)
    pumped = share * comp[4:5]
    priced = pumped * comp[5:6]
    col_two = jnp.concatenate([col_hot, col_hot], axis=1)
    for z in range(layers):
        left = []
        for value in (pumped, priced):
            top, rest = split(value[z:z + 1], 2)
            left.append(
                jnp.concatenate([row_hot * top.astype(F32), row_hot * rest.astype(F32)], axis=1)
            )
        left = jnp.concatenate(left, axis=0).astype(BF16)
        field = dot(left, col_two, NT)
        src[z] = field[:ext_rows]
        lw[z] = field[ext_rows:]

    wide = (8, ext_cols)
    sub = iota(wide, 0)
    col = iota(wide, 1)
    closed_col = ((col == cols - 1) & (me_e == n_east - 1)) | ((col == ext_cols - 1) & (me_e == 0))
    open_east = jnp.where(closed_col, 0.0, 2.0)
    open_low = jnp.where((sub == 7) & (me_n == 0), 0.0, 2.0)
    open_high = jnp.where((sub == 7) & (me_n == n_north - 1), 0.0, 2.0)

    def east(v):
        return roll(v, ext_cols - 1, 1)

    def west(v):
        return roll(v, 1, 1)

    def north(now, after):
        return jnp.where(sub < 7, roll(now, 7, 0), roll(after, 7, 0))

    def south(now, prior):
        return jnp.where(sub > 0, roll(now, 1, 0), roll(prior, 1, 0))

    fu[0] = jnp.zeros((ext_rows, ext_cols), F32)

    def row_chunks(begin, end, unit, body, carry):
        if end - begin == unit:
            for j in range(begin, end):
                carry = body(j, carry)
            return carry

        def several(k, carry):
            for i in range(unit):
                carry = body(begin + k * unit + i, carry)
            return carry

        return lax.fori_loop(0, (end - begin) // unit, several, carry)

    def at(j):
        return pl.ds(8 * j if isinstance(j, int) else pl.multiple_of(8 * j, 8), 8)

    def next_of(j):
        return min(j + 1, chunks_of_rows - 1) if isinstance(j, int) else jnp.minimum(j + 1, chunks_of_rows - 1)

    def start(z, carry):
        up = jnp.minimum(z + 1, layers - 1)
        down = jnp.maximum(z - 1, 0)
        open_up = jnp.where(z < layers - 1, 2.0, 0.0)

        def chunk(j, carry):
            fn_prior, gn_prior, k_n, h = carry
            k_e, k_u, k_u2 = ke[z, at(j)], kv[z, at(j)], kv[up, at(j)]
            k_e2 = east(k_e)
            k_after, h_after = kn[z, at(next_of(j))], hx[z, at(next_of(j))]
            k_n2 = north(k_n, k_after)
            f_e = open_east * k_e * k_e2 * reciprocal(k_e + k_e2)
            if isinstance(j, int):
                opened = open_low if j == 0 else open_high if j == chunks_of_rows - 2 else 2.0
            else:
                edge = ((j == 0) & (me_n == 0)) | ((j == chunks_of_rows - 2) & (me_n == n_north - 1))
                opened = jnp.where((sub == 7) & edge, 0.0, 2.0)
            f_n = opened * k_n * k_n2 * reciprocal(k_n + k_n2)
            f_u = open_up * k_u * k_u2 * reciprocal(k_u + k_u2)
            f_d = fu[z, at(j)]
            fe[z, at(j)] = f_e
            fn[z, at(j)] = f_n
            fu[z + 1, at(j)] = f_u
            diagonal = st[z, at(j)] + f_e + west(f_e) + f_n + south(f_n, fn_prior) + f_u + f_d
            inverse = reciprocal(diagonal)
            inv[z, at(j)] = inverse
            g_e = f_e * (east(h) - h)
            g_n = f_n * (north(h, h_after) - h)
            g_u = f_u * (hx[up, at(j)] - h)
            g_d = f_d * (h - hx[down, at(j)])
            residual = (g_e - west(g_e)) + (g_n - south(g_n, gn_prior)) + (g_u - g_d)
            d0[z, at(j)] = inverse * (residual - src[z, at(j)])
            return f_n, g_n, k_after, h_after

        none = jnp.zeros(wide, F32)
        row_chunks(0, chunks_of_rows, START_UNIT, chunk, (none, none, kn[z, at(0)], hx[z, at(0)]))
        return carry

    lax.fori_loop(0, layers, start, 0)

    def sweep(field, margin, finish, chunk_from, chunk_to):
        def layer(i, carry):
            z = (depth - margin) * me_l + i
            up = jnp.minimum(z + 1, layers - 1)
            down = jnp.maximum(z - 1, 0)

            def chunk(j, carry):
                b_prior, d = carry
                d_after = field[z, at(next_of(j))]
                f_e, f_n = fe[z, at(j)], fn[z, at(j)]
                b = f_n * d
                moved = f_e * east(d) + west(f_e * d)
                moved = moved + f_n * north(d, d_after) + south(b, b_prior)
                moved = moved + fu[z + 1, at(j)] * field[up, at(j)] + fu[z, at(j)] * field[down, at(j)]
                finish(i, z, j, d, inv[z, at(j)] * moved)
                return b, d_after

            if chunk_from == 0:
                b_prior = jnp.zeros(wide, F32)
            else:
                b_prior = fn[z, at(chunk_from - 1)] * field[z, at(chunk_from - 1)]
            unit = SWEEP_UNIT if chunk_from == 0 else LAST_UNIT
            row_chunks(chunk_from, chunk_to, unit, chunk, (b_prior, field[z, at(chunk_from)]))
            return carry

        lax.fori_loop(0, depth + margin, layer, 0)

    (a1, b1), (a2, b2) = steps_of()

    def first_sweep(i, z, j, d, pulled):
        s1[z, at(j)] = pulled
        d1[z, at(j)] = a1 * d + b1 * pulled

    def end_forward(i, z, j, d, pulled):
        s2 = s1[z, at(j)] - d + pulled
        d2 = a2 * d + b2 * s2
        new = hx[z, at(j)] + d0[z, at(j)] + d + d2
        hx[z, at(j)] = new
        load = new - tx[z, at(j)] - lw[z, at(j)]
        src[z, at(j)] = inv[z, at(j)] * load

    sweep(d0, 3, first_sweep, 0, chunks_of_rows)
    sweep(d1, 2, end_forward, 0, chunks_of_rows)
    sweep(src, 1, first_sweep, 0, chunks_of_rows)

    st[0, at(0)] = jnp.zeros(wide, F32)

    def end_adjoint(i, z, j, d, pulled):
        s2 = s1[z, at(j)] - d + pulled
        d2 = a2 * d + b2 * s2
        adj = src[z, at(j)] + d + d2
        adjoint[i, at(j - 1)] = adj[:, :cols]
        new = hx[z, at(j), inside_cols]
        head_new[i, at(j - 1)] = new
        departure = new - tx[z, at(j), inside_cols]
        st[0, at(0), inside_cols] = st[0, at(0), inside_cols] + departure * departure

    sweep(d1, 0, end_adjoint, 1, chunks_of_rows - 1)

    writes = [load(head_new, out_new), load(adjoint, out_adjoint)]

    squared = st[0, at(0), inside_cols]
    squared = jnp.sum(squared, axis=0, keepdims=True)
    squared = sum(squared[:, LANES * k:LANES * (k + 1)] for k in range(cols // LANES))
    squared = squared * (1.0 / (float(layers * rows * cols) * n_east * n_north))
    base_layer = jnp.where(me_l == 0, 1.0, 0.0)

    col_hot, row_hot = col_hot[:cols], row_hot[8:8 + rows]
    head_at = jnp.zeros((1, SLOTS), F32)
    adj_at = jnp.zeros((1, SLOTS), F32)
    for i in range(depth):
        z_share = jnp.where(me_l == 0, share[i:i + 1], share[depth + i:depth + i + 1])
        stack = split(head_new[i], 2) + split(adjoint[i], 2)
        found = [dot(piece, col_hot, NN) for piece in stack]
        head_at += z_share * jnp.sum((found[0] + found[1]) * row_hot, axis=0, keepdims=True)
        adj_at += z_share * jnp.sum((found[2] + found[3]) * row_hot, axis=0, keepdims=True)
    lift = (comp[6:7] * base_layer - head_at) * comp[7:8]
    priced = comp[5:6] * lift
    slope = priced - adj_at * comp[7:8]
    three = jnp.concatenate(
        [p.astype(F32) for p in split(slope, 3)] + [jnp.zeros((5, SLOTS), F32)], axis=0
    ).astype(BF16)
    spread = dot(three, pt[...], NN)
    spread = spread[0:1] + spread[1:2] + spread[2:3]
    tile = jnp.concatenate(
        [spread[:, LANES * k:LANES * (k + 1)] for k in range(groups)], axis=0
    )
    parts[pl.ds(0, groups)] = tile
    parts[pl.ds(groups, 8)] = jnp.concatenate(
        [
            priced * comp[4:5],
            squared,
            jnp.broadcast_to(crowded, (1, LANES)),
            jnp.zeros((5, LANES), F32),
        ],
        axis=0,
    )

    total = parts[...]
    used = 0
    for box, mine, peers in phases:
        box[mine] = total
        copies = []
        for device in peers:
            copy = pltpu.make_async_remote_copy(
                src_ref=box.at[mine],
                dst_ref=box.at[mine],
                send_sem=sum_send.at[used],
                recv_sem=sum_recv.at[used],
                device_id=device,
                device_id_type=MESH,
            )
            copy.start()
            copies.append(copy)
            used += 1
        for copy in copies:
            copy.wait()
        total = box[0]
        for k in range(1, len(peers) + 1):
            total = total + box[k]
    n_wells = out_slope.shape[1]
    for k in range(groups):
        width = min(LANES, n_wells - LANES * k)
        out_slope[:, pl.ds(LANES * k, width)] = total[k:k + 1, :width]
    sums = jnp.sum(total[groups:], axis=1, keepdims=True)
    out_cost[...] = sums[0:1]
    out_misfit[...] = sums[1:2]
    out_crowded[...] = sums[2:3]
    for copy in writes:
        copy.wait()


def run_kernel(sizes, fields, wells):
    depth, rows, cols = fields[0].shape
    layers, ext_rows, ext_cols = 2 * depth, rows + 16, cols + LANES
    n_wells = wells[0].shape[1]
    groups = -(-n_wells // LANES)
    n_east, n_x, n_z = sizes
    block = jax.ShapeDtypeStruct((depth, rows, cols), F32)
    one = jax.ShapeDtypeStruct((1, 1), F32)
    ext = pltpu.VMEM((layers, ext_rows, ext_cols), F32)
    operands = (*fields, *wells)
    copies = 4 + 4 + 8 + 6 + 7
    peers = 1 + n_z + n_east + n_x - 3
    return pl.pallas_call(
        functools.partial(kernel, sizes),
        out_shape=[block, block, jax.ShapeDtypeStruct((1, n_wells), F32), one, one, one],
        in_specs=[pl.BlockSpec(memory_space=pltpu.HBM)] * len(operands),
        out_specs=[pl.BlockSpec(memory_space=pltpu.HBM)] * 2
        + [pl.BlockSpec(memory_space=pltpu.VMEM)] * 4,
        scratch_shapes=[ext] * 8
        + [pltpu.VMEM((layers + 1, ext_rows, ext_cols), F32)]
        + [ext] * 6
        + [pltpu.VMEM((SLOTS, groups * LANES), BF16)]
        + [pltpu.VMEM((depth, rows, cols), F32)] * 2
        + [pltpu.VMEM((groups + 8, LANES), F32)]
        + [pltpu.VMEM((layers, rows, cols), BF16)] * 4
        + [
            pltpu.VMEM((2, 2, depth, 32, cols), BF16),
            pltpu.VMEM((2, 2, depth, 8, LANES), F32),
            pltpu.VMEM((2, 2, depth, 32, LANES), BF16),
            pltpu.VMEM((2, 4, 8, LANES), F32),
            pltpu.VMEM((2, 4, 16, LANES), BF16),
            pltpu.VMEM((2, depth, 8, cols), F32),
            pltpu.VMEM((2, depth, 32, cols), BF16),
            pltpu.VMEM((2, depth, 8, LANES), F32),
            pltpu.VMEM((2, depth, 32, LANES), BF16),
            pltpu.VMEM((4, 8, LANES), F32),
            pltpu.VMEM((4, 16, LANES), BF16),
        ]
        + [pltpu.VMEM(w.shape, w.dtype) for w in wells]
        + [pltpu.VMEM((8, groups * LANES), F32)]
        + [pltpu.VMEM((n, groups + 8, LANES), F32) for n in (2, n_z, n_east, n_x)]
        + [pltpu.SemaphoreType.DMA((16,))]
        + [pltpu.SemaphoreType.DMA((copies,))] * 2
        + [pltpu.SemaphoreType.DMA((peers,))] * 2,
        compiler_params=pltpu.CompilerParams(
            collective_id=0, has_side_effects=True, vmem_limit_bytes=60 * 1024 * 1024
        ),
        name="whole_step",
    )(*operands)


def in_order(value):
    return with_layout_constraint(value, Layout(major_to_minor=(0, 1, 2)))


def per_device(sizes, *arguments):
    fields = arguments[:6]
    e, n, top, bottom, tariff, rates, ground, prices = arguments[6:]
    wells = [w.reshape(1, -1) for w in (e, n, top, bottom, rates, tariff, ground, prices)]
    new, adjoint, slope, cost, misfit, crowded = run_kernel(sizes, fields, wells)
    found = (new, adjoint, slope.reshape(-1), cost.reshape(()), misfit.reshape(()))

    def again(state):
        blocks = [in_order(x) for x in fields]
        first, second, *others = plain(*blocks, *arguments[6:])
        return jnp.zeros((), F32), (in_order(first), in_order(second), *others)

    return lax.while_loop(lambda state: state[0] > 0, again, (crowded.reshape(()), found))[1]


def solution(mesh):
    field = P("layer", "north", "east")
    n_north = mesh.shape["north"]
    n_x = 4 if n_north % 4 == 0 else 1
    sizes = (mesh.shape["east"], n_x, n_north // n_x)
    return jax.shard_map(
        functools.partial(per_device, sizes),
        mesh=mesh,
        in_specs=(field,) * 6 + (P(),) * 8,
        out_specs=(field, field, P(), P(), P()),
        check_vma=False,
    )
```

```python
import functools

import jax
import jax.numpy as jnp
from jax import lax
from jax.experimental import pallas as pl
from jax.experimental.layout import Layout, with_layout_constraint
from jax.experimental.pallas import tpu as pltpu
from jax.sharding import PartitionSpec as P

MESH = pl.DeviceIdType.MESH
F32 = jnp.float32
BF16 = jnp.bfloat16

SWEEPS = 3
CENTRE = 1.0
HALF_WIDTH = 0.95

HALO = 8
REACH = 5
LANES = 128
SLOTS = 128
START_UNIT, SWEEP_UNIT, LAST_UNIT = 9, 18, 16


def steps_of():
    sigma = CENTRE / HALF_WIDTH
    factor = 1.0 / sigma
    found = []
    for _ in range(SWEEPS - 1):
        after = 1.0 / (2.0 * sigma - factor)
        found.append((after * factor, 2.0 * after / HALF_WIDTH))
        factor = after
    return found


def iota(shape, dim):
    return lax.broadcasted_iota(jnp.int32, shape, dim)


def roll(value, shift, dim):
    shift = shift % value.shape[dim]
    return pltpu.roll(value, shift, dim) if shift else value


def extended(value, sides, width):
    for axis, dim in sides:
        size, length = (lax.axis_size(axis), value.shape[dim])
        up = [(i, (i + 1) % size) for i in range(size - 1)]
        down = [(j, i) for i, j in up]
        last = lax.slice_in_dim(value, length - width, length, axis=dim)
        initial = lax.slice_in_dim(value, 0, width, axis=dim)
        before = lax.ppermute(last, axis, up)
        after = lax.ppermute(initial, axis, down)
        value = jnp.concatenate([before, value, after], axis=dim)
    return value


def harmonic(first, second):
    total = first + second
    return 2.0 * first * second / jnp.where(total > 0, total, 1.0)


def face_terms(east_pad, north_pad, up_pad, stored):
    face_east = harmonic(east_pad[:, :, :-1], east_pad[:, :, 1:])
    face_north = harmonic(north_pad[:, :-1], north_pad[:, 1:])
    face_up = harmonic(up_pad[:-1], up_pad[1:])
    diagonal = stored + face_east[:, :, :-1] + face_east[:, :, 1:]
    diagonal = diagonal + face_north[:, :-1] + face_north[:, 1:]
    diagonal = diagonal + face_up[:-1] + face_up[1:]
    positive = diagonal > 0
    inverse = jnp.where(positive, 1.0 / jnp.where(positive, diagonal, 1.0), 0.0)
    return (stored, face_east, face_north, face_up, inverse)


def coefficients(padded_coefs):
    stacked = padded_coefs.astype(jnp.float32)
    east_pad = stacked[0][1:-1, 1:-1, :]
    north_pad = stacked[1][1:-1, :, 1:-1]
    up_pad = stacked[2][:, 1:-1, 1:-1]
    stored = stacked[3][1:-1, 1:-1, 1:-1]
    return face_terms(east_pad, north_pad, up_pad, stored)


def apply_operator(padded, storage_part, face_east, face_north, face_up):
    center = padded[1:-1, 1:-1, 1:-1]
    step_east = padded[1:-1, 1:-1, 1:] - padded[1:-1, 1:-1, :-1]
    step_north = padded[1:-1, 1:, 1:-1] - padded[1:-1, :-1, 1:-1]
    step_up = padded[1:, 1:-1, 1:-1] - padded[:-1, 1:-1, 1:-1]
    flux_east = face_east * step_east
    flux_north = face_north * step_north
    flux_up = face_up * step_up
    total = storage_part * center + (flux_east[:, :, :-1] - flux_east[:, :, 1:])
    total = total + (flux_north[:, :-1] - flux_north[:, 1:])
    return total + (flux_up[:-1] - flux_up[1:])


def keep_whole(field):
    return field


def chebyshev(start, rhs, operate, trim, precondition):
    if start is None:
        residual = rhs
    else:
        residual = trim(rhs) - operate(start)
    direction = precondition(residual) / CENTRE
    if start is None:
        iterate = direction
    else:
        iterate = trim(start) + direction
    sigma = CENTRE / HALF_WIDTH
    factor = 1.0 / sigma
    for sweep_index in range(SWEEPS - 1):
        residual = trim(residual) - operate(direction)
        factor_next = 1.0 / (2.0 * sigma - factor)
        direction = factor_next * factor * trim(
            direction
        ) + 2.0 * factor_next / HALF_WIDTH * precondition(residual)
        iterate = trim(iterate) + direction
        factor = factor_next
    return iterate


def plain(
    head_old,
    head_target,
    conductivity_east,
    conductivity_north,
    conductivity_vertical,
    storage,
    well_east,
    well_north,
    screen_top,
    screen_bottom,
    tariff_band,
    pump_rates,
    ground_level,
    band_prices,
):
    depth_cells, north_cells, east_cells = head_old.shape
    stacked_coefs = jnp.stack(
        (conductivity_east, conductivity_north, conductivity_vertical, storage)
    )
    padded_coefs = extended(stacked_coefs, (("east", 3), ("north", 2), ("layer", 1)), 1)
    margin = 0
    top_level = coefficients(padded_coefs)
    levels = [None] * (margin + 1)
    levels[margin] = top_level

    def margin_of(field):
        return (field.shape[0] - depth_cells) // 2

    def precondition(residual):
        return levels[margin_of(residual)][4] * residual

    def operate(field):
        padded = extended(field, (("east", 2), ("north", 1), ("layer", 0)), 1)
        level = levels[0]
        return apply_operator(padded, level[0], level[1], level[2], level[3])

    east_start = lax.axis_index("east") * east_cells
    north_start = lax.axis_index("north") * north_cells
    layer_start = lax.axis_index("layer") * depth_cells
    local_east = well_east - east_start
    local_north = well_north - north_start
    owning = (
        (local_east >= 0)
        & (local_east < east_cells)
        & (local_north >= 0)
        & (local_north < north_cells)
    ).astype(jnp.float32)
    cells = jnp.clip(local_north, 0, north_cells - 1) * east_cells + jnp.clip(
        local_east, 0, east_cells - 1
    )
    depth = layer_start + jnp.arange(depth_cells, dtype=jnp.int32)[:, None]
    screened = ((depth >= screen_top[None, :]) & (depth <= screen_bottom[None, :])).astype(
        jnp.float32
    ) * owning[None, :]
    weights = (
        conductivity_east.reshape(depth_cells, north_cells * east_cells)[:, cells].astype(
            jnp.float32
        )
        * screened
    )
    totals = lax.psum(jnp.sum(weights, axis=0), "layer")
    shares = weights / (totals + (1.0 - owning))[None, :]
    flat_shape = (depth_cells, north_cells * east_cells)
    source = (
        jnp.zeros(flat_shape, jnp.float32)
        .at[:, cells]
        .add(pump_rates[None, :] * shares)
        .reshape(head_old.shape)
    )
    stored = storage.astype(jnp.float32)
    rhs = stored * head_old - source
    head_new = chebyshev(head_old, rhs, operate, keep_whole, precondition)
    departure = head_new - head_target
    misfit_part = jnp.sum(departure * departure)
    all_cells = float(
        depth_cells
        * north_cells
        * east_cells
        * lax.axis_size("east")
        * lax.axis_size("north")
        * lax.axis_size("layer")
    )
    head_part = jnp.sum(shares * head_new.reshape(flat_shape)[:, cells], axis=0)
    head_screen, misfit_total = lax.psum((head_part, misfit_part), ("east", "north", "layer"))
    band_ids = jnp.arange(band_prices.shape[0], dtype=jnp.int32)
    prices = jnp.sum(
        jnp.where(tariff_band[:, None] == band_ids[None, :], band_prices[None, :], 0.0), axis=1
    )
    load = (
        departure.reshape(flat_shape)
        .at[:, cells]
        .add(-(prices * pump_rates)[None, :] * shares)
        .reshape(head_old.shape)
    )
    adjoint_head = chebyshev(None, load, operate, keep_whole, precondition)
    adjoint_part = jnp.sum(shares * adjoint_head.reshape(flat_shape)[:, cells], axis=0)
    adjoint_screen = lax.psum(adjoint_part, ("east", "north", "layer"))
    misfit = misfit_total / all_cells
    lift = ground_level - head_screen
    rate_gradient = prices * lift - adjoint_screen
    pumping_cost = jnp.sum(prices * pump_rates * lift)
    return (head_new, adjoint_head, rate_gradient, pumping_cost, misfit)


def split(value, parts):
    found = []
    for _ in range(parts):
        top = value.astype(BF16)
        found.append(top)
        value = value - top.astype(F32)
    return found


def dot(a, b, dims):
    return lax.dot_general(a, b, (dims, ((), ())), preferred_element_type=F32)


NN = ((1,), (0,))
NT = ((1,), (1,))


def reciprocal(x):
    first = pl.reciprocal(x, approx=True)
    return first * (2.0 - x * first)


def kernel(sizes, *refs):
    n_east, n_x, n_z = sizes
    n_north = n_x * n_z
    fields, well_refs, refs = refs[:6], refs[6:14], refs[14:]
    out_new, out_adjoint, out_slope, out_cost, out_misfit, out_crowded = refs[:6]
    hx, tx, ke, kn, kv, st, fe, fn, fu, inv, src, lw, d0, d1, s1, pt = refs[6:22]
    head_new, adjoint, parts = refs[22:25]
    staged, (nbs, efs, ebs, cfs, cbs), refs = refs[25:29], refs[29:34], refs[34:]
    (s_nf, s_nb, s_ef, s_eb, s_cf, s_cb), refs = refs[:6], refs[6:]
    well_rows, wells, boxes, refs = refs[:8], refs[8], refs[9:13], refs[13:]
    load_sem, send_sem, recv_sem, sum_send, sum_recv = refs
    depth, rows, cols = head_new.shape
    layers, ext_rows, ext_cols = hx.shape
    chunks_of_rows = ext_rows // 8
    groups = wells.shape[1] // LANES
    me_e, me_n, me_l = lax.axis_index("east"), lax.axis_index("north"), lax.axis_index("layer")
    me_x, me_z = me_n // n_z, lax.rem(me_n, n_z)
    own, other = depth * me_l, depth * (1 - me_l)
    own_layers = pl.ds(own, depth)

    def east_of(side):
        return lax.rem(me_e + (n_east - 1 if side == 0 else 1), n_east)

    def north_of(side):
        return lax.rem(me_n + (n_north - 1 if side == 0 else 1), n_north)

    partner = (me_e, me_n, 1 - me_l)
    to_north = [(me_e, north_of(s), me_l) for s in (0, 1)]
    to_east = [(east_of(s), me_n, me_l) for s in (0, 1)]
    to_corner = [(east_of(c), north_of(r), me_l) for r in (0, 1) for c in (0, 1)]
    phases = []
    for box, size, mine, device in (
        (boxes[0], 2, me_l, lambda i: (me_e, me_n, i)),
        (boxes[1], n_z, me_z, lambda i: (me_e, me_x * n_z + i, me_l)),
        (boxes[2], n_east, me_e, lambda i: (i, me_n, me_l)),
        (boxes[3], n_x, me_x, lambda i: (me_e, i * n_z + me_z, me_l)),
    ):
        phases.append((box, mine, [device(lax.rem(mine + k, size)) for k in range(1, size)]))

    greeted = [partner] + to_north + to_east + to_corner
    for _, _, peers in phases:
        greeted = greeted + peers
    barrier = pltpu.get_barrier_semaphore()
    for device in greeted:
        pl.semaphore_signal(barrier, inc=1, device_id=device, device_id_type=MESH)

    loaded = [0]

    def load(src_ref, dst_ref):
        copy = pltpu.make_async_copy(src_ref, dst_ref, load_sem.at[loaded[0]])
        loaded[0] += 1
        copy.start()
        return copy

    lane = iota((8, LANES), 1)
    group = lane // HALO
    wide_sub = iota((8, cols), 0)
    last = cols - LANES
    low_half = lane < LANES // 2
    extra = pl.ds(cols, LANES)
    inside_cols = pl.ds(0, cols)
    inner = pl.ds(8, rows)
    edge_rows = (pl.ds(rows + 8, 8), pl.ds(0, 8))

    block_loads = [
        load(fields[0], hx.at[own_layers, inner, inside_cols]),
        load(fields[1], tx.at[own_layers, inner, inside_cols]),
    ] + [load(fields[2 + a], staged[a].at[own_layers]) for a in range(4)]
    well_loads = [load(a, b) for a, b in zip(well_refs, well_rows)]
    for copy in block_loads:
        copy.wait()

    def pack(z, carry):
        for side in (0, 1):
            c0 = last * side
            kept = jnp.zeros((8, LANES), F32)
            fields = [jnp.zeros((8, LANES), F32) for _ in staged]
            for pair in range(rows // 16):
                tiles = [
                    ref[own + z, pl.ds(16 * pair, 16), pl.ds(c0, LANES)].astype(F32) for ref in staged
                ]
                for half in (0, 1):
                    j = 2 * pair + half
                    shift = HALO * j - (LANES - HALO) * side
                    h = hx[own + z, pl.ds(8 + 8 * j, 8), pl.ds(c0, LANES)]
                    t = tx[own + z, pl.ds(8 + 8 * j, 8), pl.ds(c0, LANES)]
                    if side == 0:
                        both = jnp.where(lane >= HALO - 2, roll(t, HALO - 2, 1), h)
                    else:
                        both = jnp.where(lane < LANES - HALO + 2, roll(t, 2 - HALO, 1), h)
                    here = group == j
                    kept = jnp.where(here, roll(both, shift, 1), kept)
                    for a in range(4):
                        piece = tiles[a][8 * half:8 * half + 8]
                        fields[a] = jnp.where(here, roll(piece, shift, 1), fields[a])
            s_ef[side, z] = kept
            s_eb[side, z, pl.ds(0, 16)] = jnp.concatenate(fields[:2], axis=0).astype(BF16)
            s_eb[side, z, pl.ds(16, 16)] = jnp.concatenate(fields[2:], axis=0).astype(BF16)
            r0 = (rows - 8) * side
            h = hx[own + z, pl.ds(8 + r0, 8), inside_cols]
            t = tx[own + z, pl.ds(8 + r0, 8), inside_cols]
            if side == 0:
                both = jnp.where(wide_sub >= HALO - 2, roll(t, HALO - 2, 0), h)
            else:
                both = jnp.where(wide_sub < 2, roll(t, 2, 0), h)
            s_nf[side, z] = both
            edge = [
                ref[own + z, pl.ds((rows - 16) * side, 16), :].astype(F32)[8 * side:8 * side + 8]
                for ref in staged
            ]
            s_nb[side, z, pl.ds(0, 16)] = jnp.concatenate(edge[:2], axis=0).astype(BF16)
            s_nb[side, z, pl.ds(16, 16)] = jnp.concatenate(edge[2:], axis=0).astype(BF16)
        return carry

    lax.fori_loop(0, depth, pack, 0)

    for r in (0, 1):
        for c in (0, 1):
            c0 = last * c
            kept = jnp.zeros((8, LANES), F32)
            mixed = jnp.zeros((8, LANES), F32)
            for z in range(depth):
                both = s_nf[r, z, :, pl.ds(c0, LANES)]
                kept = jnp.where(group == z, roll(both, HALO * z - (LANES - HALO) * c, 1), kept)
                for half in (0, 1):
                    two = s_nb[r, z, pl.ds(16 * half, 16), pl.ds(c0, LANES)].astype(F32)
                    for k in (0, 1):
                        slot = (2 * half + k) * depth + z
                        moved = roll(two[8 * k:8 * k + 8], HALO * slot - (LANES - HALO) * c, 1)
                        mixed = jnp.where(group == slot, moved, mixed)
            s_cf[2 * r + c] = kept
            s_cb[2 * r + c] = jnp.concatenate([mixed, mixed], axis=0).astype(BF16)

    pl.semaphore_wait(barrier, len(greeted))

    sent = [0]

    def send(src_ref, dst_ref, device):
        copy = pltpu.make_async_remote_copy(
            src_ref=src_ref,
            dst_ref=dst_ref,
            send_sem=send_sem.at[sent[0]],
            recv_sem=recv_sem.at[sent[0]],
            device_id=device,
            device_id_type=MESH,
        )
        sent[0] += 1
        copy.start()
        return copy

    norths, easts, corners = [], [], []
    for side in (0, 1):
        norths.append(send(s_nb.at[side], nbs.at[0, side], to_north[side]))
        norths.append(
            send(s_nf.at[side], hx.at[own_layers, edge_rows[side], inside_cols], to_north[side])
        )
    for side in (0, 1):
        easts.append(send(s_eb.at[side], ebs.at[0, side], to_east[side]))
        easts.append(send(s_ef.at[side], efs.at[0, side], to_east[side]))
    for d in range(4):
        corners.append(send(s_cb.at[d], cbs.at[0, d], to_corner[d]))
        corners.append(send(s_cf.at[d], cfs.at[0, d], to_corner[d]))
    two = (depth - 2) * (1 - me_l)
    blocks = [send(fields[2 + a], staged[a].at[own_layers], partner) for a in range(4)]
    blocks.append(send(fields[0], hx.at[own_layers, inner, inside_cols], partner))
    blocks.append(
        send(
            fields[1].at[pl.ds(two, 2)], tx.at[pl.ds(own + two, 2), inner, inside_cols], partner
        )
    )

    for copy in well_loads:
        copy.wait()
    wells[...] = jnp.full(wells.shape, -1e6, F32)
    width = pl.ds(0, well_rows[0].shape[1])
    for row, ref in enumerate(well_rows[:5]):
        wells[pl.ds(row, 1), width] = ref[...].astype(F32)
    band = well_rows[5][...]
    bands = well_rows[7][...]
    price = jnp.zeros(band.shape, F32)
    for b in range(bands.shape[1]):
        price = jnp.where(band == b, bands[0:1, b:b + 1], price)
    wells[pl.ds(5, 1), width] = price
    wells[pl.ds(6, 1), width] = well_rows[6][...]

    at_east = wells[0:1, :] - (me_e * cols).astype(F32)
    at_north = wells[1:2, :] - (me_n * rows).astype(F32)
    near = (
        (at_east >= -REACH) & (at_east < cols + REACH)
        & (at_north >= -REACH) & (at_north < rows + REACH)
    )
    mine = (at_east >= 0) & (at_east < cols) & (at_north >= 0) & (at_north < rows)
    near_row = jnp.where(near, 1.0, 0.0)
    near_tile = jnp.concatenate(
        [near_row[:, LANES * k:LANES * (k + 1)] for k in range(groups)], axis=0
    )
    before = (iota((LANES, LANES), 0) < iota((LANES, LANES), 1)).astype(F32).astype(BF16)
    in_row = dot(near_tile.astype(BF16), before, NN)
    above = (iota((groups, groups), 1) < iota((groups, groups), 0)).astype(F32).astype(BF16)
    rows_above = jnp.sum(dot(above, near_tile.astype(BF16), NN), axis=1, keepdims=True)
    rank = jnp.where(near_tile > 0, in_row + rows_above, -1.0)
    found = jnp.sum(jnp.sum(near_tile, axis=1, keepdims=True), axis=0, keepdims=True)
    crowded = jnp.where(found > SLOTS, 1.0, 0.0)

    place = jnp.concatenate(
        [
            jnp.where(at_east < 0, at_east + ext_cols, at_east),
            at_north + 8.0,
            wells[2:7, :],
            jnp.where(mine, 1.0, 0.0),
        ],
        axis=0,
    )
    place_parts = jnp.concatenate([p.astype(F32) for p in split(place, 3)], axis=0).astype(BF16)
    slot_of = iota((SLOTS, LANES), 0).astype(F32)

    for k in range(groups):
        pt[:, pl.ds(LANES * k, LANES)] = jnp.where(slot_of == rank[k:k + 1, :], 1.0, 0.0).astype(BF16)
    three = dot(place_parts, pt[...], NT)
    comp = three[0:8] + three[8:16] + three[16:24]
    col_hot = jnp.where(iota((ext_cols, SLOTS), 0).astype(F32) == comp[0:1], 1.0, 0.0)
    row_hot = jnp.where(iota((ext_rows, SLOTS), 0).astype(F32) == comp[1:2], 1.0, 0.0)
    col_hot = col_hot.astype(BF16)


    def fill_inner(base):
        def fill(z, carry):
            for dst, ref in zip((ke, kn, kv, st), staged):
                dst[base + z, inner, inside_cols] = ref[base + z].astype(F32)
            return carry

        lax.fori_loop(0, depth, fill, 0)

    def fill_east(who, base):
        def fill(z, carry):
            zz = base + z
            right, left = efs[who, 0, z], efs[who, 1, z]
            for j in range(rows // 8):
                both = jnp.where(
                    low_half, roll(right, -HALO * j, 1), roll(left, LANES - HALO - HALO * j, 1)
                )
                hx[zz, pl.ds(8 + 8 * j, 8), extra] = both
                tx[zz, pl.ds(8 + 8 * j, 8), extra] = jnp.where(
                    low_half, roll(both, 2 - HALO, 1), roll(both, HALO - 2, 1)
                )
            for half, pair in ((0, (ke, kn)), (1, (kv, st))):
                rights = ebs[who, 0, z, pl.ds(16 * half, 16)].astype(F32)
                lefts = ebs[who, 1, z, pl.ds(16 * half, 16)].astype(F32)
                for k in (0, 1):
                    right, left = rights[8 * k:8 * k + 8], lefts[8 * k:8 * k + 8]
                    for j in range(rows // 8):
                        pair[k][zz, pl.ds(8 + 8 * j, 8), extra] = jnp.where(
                            low_half,
                            roll(right, -HALO * j, 1),
                            roll(left, LANES - HALO - HALO * j, 1),
                        )
            return carry

        lax.fori_loop(0, depth, fill, 0)

    def fill_north(who, base):
        def fill(z, carry):
            zz = base + z
            for side, at_rows in enumerate(edge_rows):
                tx[zz, at_rows, inside_cols] = roll(
                    hx[zz, at_rows, inside_cols], 2 if side == 0 else 6, 0
                )
                for half, pair in ((0, (ke, kn)), (1, (kv, st))):
                    both = nbs[who, side, z, pl.ds(16 * half, 16)].astype(F32)
                    pair[0][zz, at_rows, inside_cols] = both[:8]
                    pair[1][zz, at_rows, inside_cols] = both[8:]
            return carry

        lax.fori_loop(0, depth, fill, 0)

    def fill_corners(who, base):
        for r, at_rows in enumerate(edge_rows):
            right, left = cfs[who, 2 * r], cfs[who, 2 * r + 1]
            rights = cbs[who, 2 * r].astype(F32)[:8]
            lefts = cbs[who, 2 * r + 1].astype(F32)[:8]
            for z in range(depth):
                both = jnp.where(
                    low_half, roll(right, -HALO * z, 1), roll(left, LANES - HALO - HALO * z, 1)
                )
                hx[base + z, at_rows, extra] = both
                tx[base + z, at_rows, extra] = roll(both, 2 if r == 0 else 6, 0)
                for a, dst in enumerate((ke, kn, kv, st)):
                    slot = a * depth + z
                    dst[base + z, at_rows, extra] = jnp.where(
                        low_half,
                        roll(rights, -HALO * slot, 1),
                        roll(lefts, LANES - HALO - HALO * slot, 1),
                    )

    fill_inner(own)
    for copy in easts:
        copy.wait_recv()
    forwards = [send(efs.at[0], efs.at[1], partner), send(ebs.at[0], ebs.at[1], partner)]
    fill_east(0, own)
    for copy in norths:
        copy.wait_recv()
    forwards.append(send(nbs.at[0], nbs.at[1], partner))
    for side in (0, 1):
        place_of = hx.at[own_layers, edge_rows[side], inside_cols]
        forwards.append(send(place_of, place_of, partner))
    for copy in corners:
        copy.wait_recv()
    forwards.append(send(cfs.at[0], cfs.at[1], partner))
    forwards.append(send(cbs.at[0], cbs.at[1], partner))
    fill_north(0, own)
    fill_corners(0, own)
    for copy in blocks:
        copy.wait_recv()
    fill_inner(other)
    for copy in forwards:
        copy.wait_recv()
    fill_east(1, other)
    fill_north(1, other)
    fill_corners(1, other)
    for copy in norths + easts + corners + blocks + forwards:
        copy.wait_send()

    weights = []
    for z in range(layers):
        found = dot(ke[z].astype(BF16), col_hot, NN)
        k_at = jnp.sum(found * row_hot, axis=0, keepdims=True)
        screened = (comp[2:3] <= z) & (comp[3:4] >= z)
        weights.append(jnp.where(screened, k_at, 0.0))
    weight = jnp.concatenate(weights, axis=0)
    total = jnp.sum(weight, axis=0, keepdims=True)
    share = weight / jnp.where(total > 0, total, 1.0)
    pumped = share * comp[4:5]
    priced = pumped * comp[5:6]
    col_two = jnp.concatenate([col_hot, col_hot], axis=1)
    for z in range(layers):
        left = []
        for value in (pumped, priced):
            top, rest = split(value[z:z + 1], 2)
            left.append(
                jnp.concatenate([row_hot * top.astype(F32), row_hot * rest.astype(F32)], axis=1)
            )
        left = jnp.concatenate(left, axis=0).astype(BF16)
        field = dot(left, col_two, NT)
        src[z] = field[:ext_rows]
        lw[z] = field[ext_rows:]

    wide = (8, ext_cols)
    sub = iota(wide, 0)
    col = iota(wide, 1)
    closed_col = ((col == cols - 1) & (me_e == n_east - 1)) | ((col == ext_cols - 1) & (me_e == 0))
    open_east = jnp.where(closed_col, 0.0, 2.0)
    open_low = jnp.where((sub == 7) & (me_n == 0), 0.0, 2.0)
    open_high = jnp.where((sub == 7) & (me_n == n_north - 1), 0.0, 2.0)

    def east(v):
        return roll(v, ext_cols - 1, 1)

    def west(v):
        return roll(v, 1, 1)

    def north(now, after):
        return jnp.where(sub < 7, roll(now, 7, 0), roll(after, 7, 0))

    def south(now, prior):
        return jnp.where(sub > 0, roll(now, 1, 0), roll(prior, 1, 0))

    fu[0] = jnp.zeros((ext_rows, ext_cols), F32)

    def row_chunks(begin, end, unit, body, carry):
        if end - begin == unit:
            for j in range(begin, end):
                carry = body(j, carry)
            return carry

        def several(k, carry):
            for i in range(unit):
                carry = body(begin + k * unit + i, carry)
            return carry

        return lax.fori_loop(0, (end - begin) // unit, several, carry)

    def at(j):
        return pl.ds(8 * j if isinstance(j, int) else pl.multiple_of(8 * j, 8), 8)

    def next_of(j):
        return min(j + 1, chunks_of_rows - 1) if isinstance(j, int) else jnp.minimum(j + 1, chunks_of_rows - 1)

    def start(z, carry):
        up = jnp.minimum(z + 1, layers - 1)
        down = jnp.maximum(z - 1, 0)
        open_up = jnp.where(z < layers - 1, 2.0, 0.0)

        def chunk(j, carry):
            fn_prior, gn_prior, k_n, h = carry
            k_e, k_u, k_u2 = ke[z, at(j)], kv[z, at(j)], kv[up, at(j)]
            k_e2 = east(k_e)
            k_after, h_after = kn[z, at(next_of(j))], hx[z, at(next_of(j))]
            k_n2 = north(k_n, k_after)
            f_e = open_east * k_e * k_e2 * reciprocal(k_e + k_e2)
            if isinstance(j, int):
                opened = open_low if j == 0 else open_high if j == chunks_of_rows - 2 else 2.0
            else:
                edge = ((j == 0) & (me_n == 0)) | ((j == chunks_of_rows - 2) & (me_n == n_north - 1))
                opened = jnp.where((sub == 7) & edge, 0.0, 2.0)
            f_n = opened * k_n * k_n2 * reciprocal(k_n + k_n2)
            f_u = open_up * k_u * k_u2 * reciprocal(k_u + k_u2)
            f_d = fu[z, at(j)]
            fe[z, at(j)] = f_e
            fn[z, at(j)] = f_n
            fu[z + 1, at(j)] = f_u
            diagonal = st[z, at(j)] + f_e + west(f_e) + f_n + south(f_n, fn_prior) + f_u + f_d
            inverse = reciprocal(diagonal)
            inv[z, at(j)] = inverse
            g_e = f_e * (east(h) - h)
            g_n = f_n * (north(h, h_after) - h)
            g_u = f_u * (hx[up, at(j)] - h)
            g_d = f_d * (h - hx[down, at(j)])
            residual = (g_e - west(g_e)) + (g_n - south(g_n, gn_prior)) + (g_u - g_d)
            d0[z, at(j)] = inverse * (residual - src[z, at(j)])
            return f_n, g_n, k_after, h_after

        none = jnp.zeros(wide, F32)
        row_chunks(0, chunks_of_rows, START_UNIT, chunk, (none, none, kn[z, at(0)], hx[z, at(0)]))
        return carry

    lax.fori_loop(0, layers, start, 0)

    def sweep(field, margin, finish, chunk_from, chunk_to):
        def layer(i, carry):
            z = (depth - margin) * me_l + i
            up = jnp.minimum(z + 1, layers - 1)
            down = jnp.maximum(z - 1, 0)

            def chunk(j, carry):
                b_prior, d = carry
                d_after = field[z, at(next_of(j))]
                f_e, f_n = fe[z, at(j)], fn[z, at(j)]
                b = f_n * d
                moved = f_e * east(d) + west(f_e * d)
                moved = moved + f_n * north(d, d_after) + south(b, b_prior)
                moved = moved + fu[z + 1, at(j)] * field[up, at(j)] + fu[z, at(j)] * field[down, at(j)]
                finish(i, z, j, d, inv[z, at(j)] * moved)
                return b, d_after

            if chunk_from == 0:
                b_prior = jnp.zeros(wide, F32)
            else:
                b_prior = fn[z, at(chunk_from - 1)] * field[z, at(chunk_from - 1)]
            unit = SWEEP_UNIT if chunk_from == 0 else LAST_UNIT
            row_chunks(chunk_from, chunk_to, unit, chunk, (b_prior, field[z, at(chunk_from)]))
            return carry

        lax.fori_loop(0, depth + margin, layer, 0)

    (a1, b1), (a2, b2) = steps_of()

    def first_sweep(i, z, j, d, pulled):
        s1[z, at(j)] = pulled
        d1[z, at(j)] = a1 * d + b1 * pulled

    def end_forward(i, z, j, d, pulled):
        s2 = s1[z, at(j)] - d + pulled
        d2 = a2 * d + b2 * s2
        new = hx[z, at(j)] + d0[z, at(j)] + d + d2
        hx[z, at(j)] = new
        load = new - tx[z, at(j)] - lw[z, at(j)]
        src[z, at(j)] = inv[z, at(j)] * load

    sweep(d0, 3, first_sweep, 0, chunks_of_rows)
    sweep(d1, 2, end_forward, 0, chunks_of_rows)
    sweep(src, 1, first_sweep, 0, chunks_of_rows)

    st[0, at(0)] = jnp.zeros(wide, F32)

    def end_adjoint(i, z, j, d, pulled):
        s2 = s1[z, at(j)] - d + pulled
        d2 = a2 * d + b2 * s2
        adj = src[z, at(j)] + d + d2
        adjoint[i, at(j - 1)] = adj[:, :cols]
        new = hx[z, at(j), inside_cols]
        head_new[i, at(j - 1)] = new
        departure = new - tx[z, at(j), inside_cols]
        st[0, at(0), inside_cols] = st[0, at(0), inside_cols] + departure * departure

    sweep(d1, 0, end_adjoint, 1, chunks_of_rows - 1)

    writes = [load(head_new, out_new), load(adjoint, out_adjoint)]

    squared = st[0, at(0), inside_cols]
    squared = jnp.sum(squared, axis=0, keepdims=True)
    squared = sum(squared[:, LANES * k:LANES * (k + 1)] for k in range(cols // LANES))
    squared = squared * (1.0 / (float(layers * rows * cols) * n_east * n_north))
    base_layer = jnp.where(me_l == 0, 1.0, 0.0)

    col_hot, row_hot = col_hot[:cols], row_hot[8:8 + rows]
    head_at = jnp.zeros((1, SLOTS), F32)
    adj_at = jnp.zeros((1, SLOTS), F32)
    for i in range(depth):
        z_share = jnp.where(me_l == 0, share[i:i + 1], share[depth + i:depth + i + 1])
        stack = split(head_new[i], 2) + split(adjoint[i], 2)
        found = [dot(piece, col_hot, NN) for piece in stack]
        head_at += z_share * jnp.sum((found[0] + found[1]) * row_hot, axis=0, keepdims=True)
        adj_at += z_share * jnp.sum((found[2] + found[3]) * row_hot, axis=0, keepdims=True)
    lift = (comp[6:7] * base_layer - head_at) * comp[7:8]
    priced = comp[5:6] * lift
    slope = priced - adj_at * comp[7:8]
    three = jnp.concatenate(
        [p.astype(F32) for p in split(slope, 3)] + [jnp.zeros((5, SLOTS), F32)], axis=0
    ).astype(BF16)
    spread = dot(three, pt[...], NN)
    spread = spread[0:1] + spread[1:2] + spread[2:3]
    tile = jnp.concatenate(
        [spread[:, LANES * k:LANES * (k + 1)] for k in range(groups)], axis=0
    )
    parts[pl.ds(0, groups)] = tile
    parts[pl.ds(groups, 8)] = jnp.concatenate(
        [
            priced * comp[4:5],
            squared,
            jnp.broadcast_to(crowded, (1, LANES)),
            jnp.zeros((5, LANES), F32),
        ],
        axis=0,
    )

    total = parts[...]
    used = 0
    for box, mine, peers in phases:
        box[mine] = total
        copies = []
        for device in peers:
            copy = pltpu.make_async_remote_copy(
                src_ref=box.at[mine],
                dst_ref=box.at[mine],
                send_sem=sum_send.at[used],
                recv_sem=sum_recv.at[used],
                device_id=device,
                device_id_type=MESH,
            )
            copy.start()
            copies.append(copy)
            used += 1
        for copy in copies:
            copy.wait()
        total = box[0]
        for k in range(1, len(peers) + 1):
            total = total + box[k]
    n_wells = out_slope.shape[1]
    for k in range(groups):
        width = min(LANES, n_wells - LANES * k)
        out_slope[:, pl.ds(LANES * k, width)] = total[k:k + 1, :width]
    sums = jnp.sum(total[groups:], axis=1, keepdims=True)
    out_cost[...] = sums[0:1]
    out_misfit[...] = sums[1:2]
    out_crowded[...] = sums[2:3]
    for copy in writes:
        copy.wait()


def run_kernel(sizes, fields, wells):
    depth, rows, cols = fields[0].shape
    layers, ext_rows, ext_cols = 2 * depth, rows + 16, cols + LANES
    n_wells = wells[0].shape[1]
    groups = -(-n_wells // LANES)
    n_east, n_x, n_z = sizes
    block = jax.ShapeDtypeStruct((depth, rows, cols), F32)
    one = jax.ShapeDtypeStruct((1, 1), F32)
    ext = pltpu.VMEM((layers, ext_rows, ext_cols), F32)
    operands = (*fields, *wells)
    copies = 4 + 4 + 8 + 6 + 7
    peers = 1 + n_z + n_east + n_x - 3
    return pl.pallas_call(
        functools.partial(kernel, sizes),
        out_shape=[block, block, jax.ShapeDtypeStruct((1, n_wells), F32), one, one, one],
        in_specs=[pl.BlockSpec(memory_space=pltpu.HBM)] * len(operands),
        out_specs=[pl.BlockSpec(memory_space=pltpu.HBM)] * 2
        + [pl.BlockSpec(memory_space=pltpu.VMEM)] * 4,
        scratch_shapes=[ext] * 8
        + [pltpu.VMEM((layers + 1, ext_rows, ext_cols), F32)]
        + [ext] * 6
        + [pltpu.VMEM((SLOTS, groups * LANES), BF16)]
        + [pltpu.VMEM((depth, rows, cols), F32)] * 2
        + [pltpu.VMEM((groups + 8, LANES), F32)]
        + [pltpu.VMEM((layers, rows, cols), BF16)] * 4
        + [
            pltpu.VMEM((2, 2, depth, 32, cols), BF16),
            pltpu.VMEM((2, 2, depth, 8, LANES), F32),
            pltpu.VMEM((2, 2, depth, 32, LANES), BF16),
            pltpu.VMEM((2, 4, 8, LANES), F32),
            pltpu.VMEM((2, 4, 16, LANES), BF16),
            pltpu.VMEM((2, depth, 8, cols), F32),
            pltpu.VMEM((2, depth, 32, cols), BF16),
            pltpu.VMEM((2, depth, 8, LANES), F32),
            pltpu.VMEM((2, depth, 32, LANES), BF16),
            pltpu.VMEM((4, 8, LANES), F32),
            pltpu.VMEM((4, 16, LANES), BF16),
        ]
        + [pltpu.VMEM(w.shape, w.dtype) for w in wells]
        + [pltpu.VMEM((8, groups * LANES), F32)]
        + [pltpu.VMEM((n, groups + 8, LANES), F32) for n in (2, n_z, n_east, n_x)]
        + [pltpu.SemaphoreType.DMA((16,))]
        + [pltpu.SemaphoreType.DMA((copies,))] * 2
        + [pltpu.SemaphoreType.DMA((peers,))] * 2,
        compiler_params=pltpu.CompilerParams(
            collective_id=0, has_side_effects=True, vmem_limit_bytes=60 * 1024 * 1024
        ),
        name="whole_step",
    )(*operands)


def hand_over(*refs):
    count = len(refs) // 2
    copies = [
        pltpu.make_async_copy(refs[k], refs[count + k], refs[-1].at[k]) for k in range(count)
    ]
    for copy in copies:
        copy.start()
    for copy in copies:
        copy.wait()


def run_hand_over(values):
    return pl.pallas_call(
        hand_over,
        out_shape=[jax.ShapeDtypeStruct(v.shape, v.dtype) for v in values],
        in_specs=[pl.BlockSpec(memory_space=pltpu.HBM)] * len(values),
        out_specs=[pl.BlockSpec(memory_space=pltpu.HBM)] * len(values),
        scratch_shapes=[pltpu.SemaphoreType.DMA((len(values),))],
        compiler_params=pltpu.CompilerParams(vmem_limit_bytes=60 * 1024 * 1024),
        name="hand_over",
    )(*values)


def in_order(value):
    return with_layout_constraint(value, Layout(major_to_minor=(0, 1, 2)))


def per_device(sizes, *arguments):
    fields = arguments[:6]
    e, n, top, bottom, tariff, rates, ground, prices = arguments[6:]
    wells = [w.reshape(1, -1) for w in (e, n, top, bottom, rates, tariff, ground, prices)]
    new, adjoint, slope, cost, misfit, crowded = run_kernel(sizes, fields, wells)
    found = (new, adjoint, slope, cost, misfit)

    def again(state):
        blocks = [in_order(x) for x in fields]
        first, second, *others = plain(*blocks, *arguments[6:])
        others = [x.reshape(1, -1) for x in others]
        return jnp.zeros((), F32), (in_order(first), in_order(second), *others)

    _, found = lax.while_loop(lambda state: state[0] > 0, again, (crowded.reshape(()), found))
    new, adjoint, slope, cost, misfit = run_hand_over(found)
    return new, adjoint, slope.reshape(-1), cost.reshape(()), misfit.reshape(())


def solution(mesh):
    field = P("layer", "north", "east")
    n_north = mesh.shape["north"]
    n_x = 4 if n_north % 4 == 0 else 1
    sizes = (mesh.shape["east"], n_x, n_north // n_x)
    return jax.shard_map(
        functools.partial(per_device, sizes),
        mesh=mesh,
        in_specs=(field,) * 6 + (P(),) * 8,
        out_specs=(field, field, P(), P(), P()),
        check_vma=False,
    )
```

```python
import functools

import jax
import jax.numpy as jnp
from jax import lax
from jax.experimental import pallas as pl
from jax.experimental.layout import Layout, with_layout_constraint
from jax.experimental.pallas import tpu as pltpu
from jax.sharding import PartitionSpec as P

MESH = pl.DeviceIdType.MESH
F32 = jnp.float32
BF16 = jnp.bfloat16

SWEEPS = 3
CENTRE = 1.0
HALF_WIDTH = 0.95

HALO = 8
REACH = 5
LANES = 128
SLOTS = 128
START_UNIT, SWEEP_UNIT, LAST_UNIT = 9, 18, 16


def steps_of():
    sigma = CENTRE / HALF_WIDTH
    factor = 1.0 / sigma
    found = []
    for _ in range(SWEEPS - 1):
        after = 1.0 / (2.0 * sigma - factor)
        found.append((after * factor, 2.0 * after / HALF_WIDTH))
        factor = after
    return found


def iota(shape, dim):
    return lax.broadcasted_iota(jnp.int32, shape, dim)


def roll(value, shift, dim):
    shift = shift % value.shape[dim]
    return pltpu.roll(value, shift, dim) if shift else value


def extended(value, sides, width):
    for axis, dim in sides:
        size, length = (lax.axis_size(axis), value.shape[dim])
        up = [(i, (i + 1) % size) for i in range(size - 1)]
        down = [(j, i) for i, j in up]
        last = lax.slice_in_dim(value, length - width, length, axis=dim)
        initial = lax.slice_in_dim(value, 0, width, axis=dim)
        before = lax.ppermute(last, axis, up)
        after = lax.ppermute(initial, axis, down)
        value = jnp.concatenate([before, value, after], axis=dim)
    return value


def harmonic(first, second):
    total = first + second
    return 2.0 * first * second / jnp.where(total > 0, total, 1.0)


def face_terms(east_pad, north_pad, up_pad, stored):
    face_east = harmonic(east_pad[:, :, :-1], east_pad[:, :, 1:])
    face_north = harmonic(north_pad[:, :-1], north_pad[:, 1:])
    face_up = harmonic(up_pad[:-1], up_pad[1:])
    diagonal = stored + face_east[:, :, :-1] + face_east[:, :, 1:]
    diagonal = diagonal + face_north[:, :-1] + face_north[:, 1:]
    diagonal = diagonal + face_up[:-1] + face_up[1:]
    positive = diagonal > 0
    inverse = jnp.where(positive, 1.0 / jnp.where(positive, diagonal, 1.0), 0.0)
    return (stored, face_east, face_north, face_up, inverse)


def coefficients(padded_coefs):
    stacked = padded_coefs.astype(jnp.float32)
    east_pad = stacked[0][1:-1, 1:-1, :]
    north_pad = stacked[1][1:-1, :, 1:-1]
    up_pad = stacked[2][:, 1:-1, 1:-1]
    stored = stacked[3][1:-1, 1:-1, 1:-1]
    return face_terms(east_pad, north_pad, up_pad, stored)


def apply_operator(padded, storage_part, face_east, face_north, face_up):
    center = padded[1:-1, 1:-1, 1:-1]
    step_east = padded[1:-1, 1:-1, 1:] - padded[1:-1, 1:-1, :-1]
    step_north = padded[1:-1, 1:, 1:-1] - padded[1:-1, :-1, 1:-1]
    step_up = padded[1:, 1:-1, 1:-1] - padded[:-1, 1:-1, 1:-1]
    flux_east = face_east * step_east
    flux_north = face_north * step_north
    flux_up = face_up * step_up
    total = storage_part * center + (flux_east[:, :, :-1] - flux_east[:, :, 1:])
    total = total + (flux_north[:, :-1] - flux_north[:, 1:])
    return total + (flux_up[:-1] - flux_up[1:])


def keep_whole(field):
    return field


def chebyshev(start, rhs, operate, trim, precondition):
    if start is None:
        residual = rhs
    else:
        residual = trim(rhs) - operate(start)
    direction = precondition(residual) / CENTRE
    if start is None:
        iterate = direction
    else:
        iterate = trim(start) + direction
    sigma = CENTRE / HALF_WIDTH
    factor = 1.0 / sigma
    for sweep_index in range(SWEEPS - 1):
        residual = trim(residual) - operate(direction)
        factor_next = 1.0 / (2.0 * sigma - factor)
        direction = factor_next * factor * trim(
            direction
        ) + 2.0 * factor_next / HALF_WIDTH * precondition(residual)
        iterate = trim(iterate) + direction
        factor = factor_next
    return iterate


def plain(
    head_old,
    head_target,
    conductivity_east,
    conductivity_north,
    conductivity_vertical,
    storage,
    well_east,
    well_north,
    screen_top,
    screen_bottom,
    tariff_band,
    pump_rates,
    ground_level,
    band_prices,
):
    depth_cells, north_cells, east_cells = head_old.shape
    stacked_coefs = jnp.stack(
        (conductivity_east, conductivity_north, conductivity_vertical, storage)
    )
    padded_coefs = extended(stacked_coefs, (("east", 3), ("north", 2), ("layer", 1)), 1)
    margin = 0
    top_level = coefficients(padded_coefs)
    levels = [None] * (margin + 1)
    levels[margin] = top_level

    def margin_of(field):
        return (field.shape[0] - depth_cells) // 2

    def precondition(residual):
        return levels[margin_of(residual)][4] * residual

    def operate(field):
        padded = extended(field, (("east", 2), ("north", 1), ("layer", 0)), 1)
        level = levels[0]
        return apply_operator(padded, level[0], level[1], level[2], level[3])

    east_start = lax.axis_index("east") * east_cells
    north_start = lax.axis_index("north") * north_cells
    layer_start = lax.axis_index("layer") * depth_cells
    local_east = well_east - east_start
    local_north = well_north - north_start
    owning = (
        (local_east >= 0)
        & (local_east < east_cells)
        & (local_north >= 0)
        & (local_north < north_cells)
    ).astype(jnp.float32)
    cells = jnp.clip(local_north, 0, north_cells - 1) * east_cells + jnp.clip(
        local_east, 0, east_cells - 1
    )
    depth = layer_start + jnp.arange(depth_cells, dtype=jnp.int32)[:, None]
    screened = ((depth >= screen_top[None, :]) & (depth <= screen_bottom[None, :])).astype(
        jnp.float32
    ) * owning[None, :]
    weights = (
        conductivity_east.reshape(depth_cells, north_cells * east_cells)[:, cells].astype(
            jnp.float32
        )
        * screened
    )
    totals = lax.psum(jnp.sum(weights, axis=0), "layer")
    shares = weights / (totals + (1.0 - owning))[None, :]
    flat_shape = (depth_cells, north_cells * east_cells)
    source = (
        jnp.zeros(flat_shape, jnp.float32)
        .at[:, cells]
        .add(pump_rates[None, :] * shares)
        .reshape(head_old.shape)
    )
    stored = storage.astype(jnp.float32)
    rhs = stored * head_old - source
    head_new = chebyshev(head_old, rhs, operate, keep_whole, precondition)
    departure = head_new - head_target
    misfit_part = jnp.sum(departure * departure)
    all_cells = float(
        depth_cells
        * north_cells
        * east_cells
        * lax.axis_size("east")
        * lax.axis_size("north")
        * lax.axis_size("layer")
    )
    head_part = jnp.sum(shares * head_new.reshape(flat_shape)[:, cells], axis=0)
    head_screen, misfit_total = lax.psum((head_part, misfit_part), ("east", "north", "layer"))
    band_ids = jnp.arange(band_prices.shape[0], dtype=jnp.int32)
    prices = jnp.sum(
        jnp.where(tariff_band[:, None] == band_ids[None, :], band_prices[None, :], 0.0), axis=1
    )
    load = (
        departure.reshape(flat_shape)
        .at[:, cells]
        .add(-(prices * pump_rates)[None, :] * shares)
        .reshape(head_old.shape)
    )
    adjoint_head = chebyshev(None, load, operate, keep_whole, precondition)
    adjoint_part = jnp.sum(shares * adjoint_head.reshape(flat_shape)[:, cells], axis=0)
    adjoint_screen = lax.psum(adjoint_part, ("east", "north", "layer"))
    misfit = misfit_total / all_cells
    lift = ground_level - head_screen
    rate_gradient = prices * lift - adjoint_screen
    pumping_cost = jnp.sum(prices * pump_rates * lift)
    return (head_new, adjoint_head, rate_gradient, pumping_cost, misfit)


def split(value, parts):
    found = []
    for _ in range(parts):
        top = value.astype(BF16)
        found.append(top)
        value = value - top.astype(F32)
    return found


def dot(a, b, dims):
    return lax.dot_general(a, b, (dims, ((), ())), preferred_element_type=F32)


NN = ((1,), (0,))
NT = ((1,), (1,))


def reciprocal(x):
    first = pl.reciprocal(x, approx=True)
    return first * (2.0 - x * first)


def kernel(sizes, *refs):
    n_east, n_x, n_z = sizes
    n_north = n_x * n_z
    fields, well_refs, refs = refs[:6], refs[6:14], refs[14:]
    out_new, out_adjoint, out_slope, out_cost, out_misfit, out_crowded = refs[:6]
    hx, tx, ke, kn, kv, st, fe, fn, fu, inv, src, lw, d0, d1, s1, pt = refs[6:22]
    head_new, adjoint, parts = refs[22:25]
    staged, (nbs, efs, ebs, cfs, cbs), refs = refs[25:29], refs[29:34], refs[34:]
    (s_nf, s_nb, s_ef, s_eb, s_cf, s_cb), refs = refs[:6], refs[6:]
    well_rows, wells, boxes, refs = refs[:8], refs[8], refs[9:13], refs[13:]
    load_sem, send_sem, recv_sem, sum_send, sum_recv = refs
    depth, rows, cols = head_new.shape
    layers, ext_rows, ext_cols = hx.shape
    chunks_of_rows = ext_rows // 8
    groups = wells.shape[1] // LANES
    me_e, me_n, me_l = lax.axis_index("east"), lax.axis_index("north"), lax.axis_index("layer")
    me_x, me_z = me_n // n_z, lax.rem(me_n, n_z)
    own, other = depth * me_l, depth * (1 - me_l)
    own_layers = pl.ds(own, depth)

    def east_of(side):
        return lax.rem(me_e + (n_east - 1 if side == 0 else 1), n_east)

    def north_of(side):
        return lax.rem(me_n + (n_north - 1 if side == 0 else 1), n_north)

    partner = (me_e, me_n, 1 - me_l)
    to_north = [(me_e, north_of(s), me_l) for s in (0, 1)]
    to_east = [(east_of(s), me_n, me_l) for s in (0, 1)]
    to_corner = [(east_of(c), north_of(r), me_l) for r in (0, 1) for c in (0, 1)]
    phases = []
    for box, size, mine, device in (
        (boxes[0], 2, me_l, lambda i: (me_e, me_n, i)),
        (boxes[1], n_z, me_z, lambda i: (me_e, me_x * n_z + i, me_l)),
        (boxes[2], n_east, me_e, lambda i: (i, me_n, me_l)),
        (boxes[3], n_x, me_x, lambda i: (me_e, i * n_z + me_z, me_l)),
    ):
        phases.append((box, mine, [device(lax.rem(mine + k, size)) for k in range(1, size)]))

    greeted = [partner] + to_north + to_east + to_corner
    for _, _, peers in phases:
        greeted = greeted + peers
    barrier = pltpu.get_barrier_semaphore()
    for device in greeted:
        pl.semaphore_signal(barrier, inc=1, device_id=device, device_id_type=MESH)

    loaded = [0]

    def load(src_ref, dst_ref):
        copy = pltpu.make_async_copy(src_ref, dst_ref, load_sem.at[loaded[0]])
        loaded[0] += 1
        copy.start()
        return copy

    lane = iota((8, LANES), 1)
    group = lane // HALO
    wide_sub = iota((8, cols), 0)
    last = cols - LANES
    low_half = lane < LANES // 2
    extra = pl.ds(cols, LANES)
    inside_cols = pl.ds(0, cols)
    inner = pl.ds(8, rows)
    edge_rows = (pl.ds(rows + 8, 8), pl.ds(0, 8))

    block_loads = [
        load(fields[0], hx.at[own_layers, inner, inside_cols]),
        load(fields[1], tx.at[own_layers, inner, inside_cols]),
    ] + [load(fields[2 + a], staged[a].at[own_layers]) for a in range(4)]
    well_loads = [load(a, b) for a, b in zip(well_refs, well_rows)]
    for copy in block_loads:
        copy.wait()

    def pack(z, carry):
        for side in (0, 1):
            c0 = last * side
            kept = jnp.zeros((8, LANES), F32)
            fields = [jnp.zeros((8, LANES), F32) for _ in staged]
            for pair in range(rows // 16):
                tiles = [
                    ref[own + z, pl.ds(16 * pair, 16), pl.ds(c0, LANES)].astype(F32) for ref in staged
                ]
                for half in (0, 1):
                    j = 2 * pair + half
                    shift = HALO * j - (LANES - HALO) * side
                    h = hx[own + z, pl.ds(8 + 8 * j, 8), pl.ds(c0, LANES)]
                    t = tx[own + z, pl.ds(8 + 8 * j, 8), pl.ds(c0, LANES)]
                    if side == 0:
                        both = jnp.where(lane >= HALO - 2, roll(t, HALO - 2, 1), h)
                    else:
                        both = jnp.where(lane < LANES - HALO + 2, roll(t, 2 - HALO, 1), h)
                    here = group == j
                    kept = jnp.where(here, roll(both, shift, 1), kept)
                    for a in range(4):
                        piece = tiles[a][8 * half:8 * half + 8]
                        fields[a] = jnp.where(here, roll(piece, shift, 1), fields[a])
            s_ef[side, z] = kept
            s_eb[side, z, pl.ds(0, 16)] = jnp.concatenate(fields[:2], axis=0).astype(BF16)
            s_eb[side, z, pl.ds(16, 16)] = jnp.concatenate(fields[2:], axis=0).astype(BF16)
            r0 = (rows - 8) * side
            h = hx[own + z, pl.ds(8 + r0, 8), inside_cols]
            t = tx[own + z, pl.ds(8 + r0, 8), inside_cols]
            if side == 0:
                both = jnp.where(wide_sub >= HALO - 2, roll(t, HALO - 2, 0), h)
            else:
                both = jnp.where(wide_sub < 2, roll(t, 2, 0), h)
            s_nf[side, z] = both
            edge = [
                ref[own + z, pl.ds((rows - 16) * side, 16), :].astype(F32)[8 * side:8 * side + 8]
                for ref in staged
            ]
            s_nb[side, z, pl.ds(0, 16)] = jnp.concatenate(edge[:2], axis=0).astype(BF16)
            s_nb[side, z, pl.ds(16, 16)] = jnp.concatenate(edge[2:], axis=0).astype(BF16)
        return carry

    lax.fori_loop(0, depth, pack, 0)

    for r in (0, 1):
        for c in (0, 1):
            c0 = last * c
            kept = jnp.zeros((8, LANES), F32)
            mixed = jnp.zeros((8, LANES), F32)
            for z in range(depth):
                both = s_nf[r, z, :, pl.ds(c0, LANES)]
                kept = jnp.where(group == z, roll(both, HALO * z - (LANES - HALO) * c, 1), kept)
                for half in (0, 1):
                    two = s_nb[r, z, pl.ds(16 * half, 16), pl.ds(c0, LANES)].astype(F32)
                    for k in (0, 1):
                        slot = (2 * half + k) * depth + z
                        moved = roll(two[8 * k:8 * k + 8], HALO * slot - (LANES - HALO) * c, 1)
                        mixed = jnp.where(group == slot, moved, mixed)
            s_cf[2 * r + c] = kept
            s_cb[2 * r + c] = jnp.concatenate([mixed, mixed], axis=0).astype(BF16)

    pl.semaphore_wait(barrier, len(greeted))

    sent = [0]

    def send(src_ref, dst_ref, device):
        copy = pltpu.make_async_remote_copy(
            src_ref=src_ref,
            dst_ref=dst_ref,
            send_sem=send_sem.at[sent[0]],
            recv_sem=recv_sem.at[sent[0]],
            device_id=device,
            device_id_type=MESH,
        )
        sent[0] += 1
        copy.start()
        return copy

    norths, easts, corners = [], [], []
    for side in (0, 1):
        norths.append(send(s_nb.at[side], nbs.at[0, side], to_north[side]))
        norths.append(
            send(s_nf.at[side], hx.at[own_layers, edge_rows[side], inside_cols], to_north[side])
        )
    for side in (0, 1):
        easts.append(send(s_eb.at[side], ebs.at[0, side], to_east[side]))
        easts.append(send(s_ef.at[side], efs.at[0, side], to_east[side]))
    for d in range(4):
        corners.append(send(s_cb.at[d], cbs.at[0, d], to_corner[d]))
        corners.append(send(s_cf.at[d], cfs.at[0, d], to_corner[d]))
    two = (depth - 2) * (1 - me_l)
    blocks = [send(fields[2 + a], staged[a].at[own_layers], partner) for a in range(4)]
    blocks.append(send(fields[0], hx.at[own_layers, inner, inside_cols], partner))
    blocks.append(
        send(
            fields[1].at[pl.ds(two, 2)], tx.at[pl.ds(own + two, 2), inner, inside_cols], partner
        )
    )

    for copy in well_loads:
        copy.wait()
    wells[...] = jnp.full(wells.shape, -1e6, F32)
    width = pl.ds(0, well_rows[0].shape[1])
    for row, ref in enumerate(well_rows[:5]):
        wells[pl.ds(row, 1), width] = ref[...].astype(F32)
    band = well_rows[5][...]
    bands = well_rows[7][...]
    price = jnp.zeros(band.shape, F32)
    for b in range(bands.shape[1]):
        price = jnp.where(band == b, bands[0:1, b:b + 1], price)
    wells[pl.ds(5, 1), width] = price
    wells[pl.ds(6, 1), width] = well_rows[6][...]

    at_east = wells[0:1, :] - (me_e * cols).astype(F32)
    at_north = wells[1:2, :] - (me_n * rows).astype(F32)
    near = (
        (at_east >= -REACH) & (at_east < cols + REACH)
        & (at_north >= -REACH) & (at_north < rows + REACH)
    )
    mine = (at_east >= 0) & (at_east < cols) & (at_north >= 0) & (at_north < rows)
    near_row = jnp.where(near, 1.0, 0.0)
    near_tile = jnp.concatenate(
        [near_row[:, LANES * k:LANES * (k + 1)] for k in range(groups)], axis=0
    )
    before = (iota((LANES, LANES), 0) < iota((LANES, LANES), 1)).astype(F32).astype(BF16)
    in_row = dot(near_tile.astype(BF16), before, NN)
    above = (iota((groups, groups), 1) < iota((groups, groups), 0)).astype(F32).astype(BF16)
    rows_above = jnp.sum(dot(above, near_tile.astype(BF16), NN), axis=1, keepdims=True)
    rank = jnp.where(near_tile > 0, in_row + rows_above, -1.0)
    found = jnp.sum(jnp.sum(near_tile, axis=1, keepdims=True), axis=0, keepdims=True)
    crowded = jnp.where(found > SLOTS, 1.0, 0.0)

    place = jnp.concatenate(
        [
            jnp.where(at_east < 0, at_east + ext_cols, at_east),
            at_north + 8.0,
            wells[2:7, :],
            jnp.where(mine, 1.0, 0.0),
        ],
        axis=0,
    )
    place_parts = jnp.concatenate([p.astype(F32) for p in split(place, 3)], axis=0).astype(BF16)
    slot_of = iota((SLOTS, LANES), 0).astype(F32)

    for k in range(groups):
        pt[:, pl.ds(LANES * k, LANES)] = jnp.where(slot_of == rank[k:k + 1, :], 1.0, 0.0).astype(BF16)
    three = dot(place_parts, pt[...], NT)
    comp = three[0:8] + three[8:16] + three[16:24]
    col_hot = jnp.where(iota((ext_cols, SLOTS), 0).astype(F32) == comp[0:1], 1.0, 0.0)
    row_hot = jnp.where(iota((ext_rows, SLOTS), 0).astype(F32) == comp[1:2], 1.0, 0.0)
    col_hot = col_hot.astype(BF16)


    def fill_inner(base):
        def fill(z, carry):
            for dst, ref in zip((ke, kn, kv, st), staged):
                dst[base + z, inner, inside_cols] = ref[base + z].astype(F32)
            return carry

        lax.fori_loop(0, depth, fill, 0)

    def fill_east(who, base):
        def fill(z, carry):
            zz = base + z
            right, left = efs[who, 0, z], efs[who, 1, z]
            for j in range(rows // 8):
                both = jnp.where(
                    low_half, roll(right, -HALO * j, 1), roll(left, LANES - HALO - HALO * j, 1)
                )
                hx[zz, pl.ds(8 + 8 * j, 8), extra] = both
                tx[zz, pl.ds(8 + 8 * j, 8), extra] = jnp.where(
                    low_half, roll(both, 2 - HALO, 1), roll(both, HALO - 2, 1)
                )
            for half, pair in ((0, (ke, kn)), (1, (kv, st))):
                rights = ebs[who, 0, z, pl.ds(16 * half, 16)].astype(F32)
                lefts = ebs[who, 1, z, pl.ds(16 * half, 16)].astype(F32)
                for k in (0, 1):
                    right, left = rights[8 * k:8 * k + 8], lefts[8 * k:8 * k + 8]
                    for j in range(rows // 8):
                        pair[k][zz, pl.ds(8 + 8 * j, 8), extra] = jnp.where(
                            low_half,
                            roll(right, -HALO * j, 1),
                            roll(left, LANES - HALO - HALO * j, 1),
                        )
            return carry

        lax.fori_loop(0, depth, fill, 0)

    def fill_north(who, base):
        def fill(z, carry):
            zz = base + z
            for side, at_rows in enumerate(edge_rows):
                tx[zz, at_rows, inside_cols] = roll(
                    hx[zz, at_rows, inside_cols], 2 if side == 0 else 6, 0
                )
                for half, pair in ((0, (ke, kn)), (1, (kv, st))):
                    both = nbs[who, side, z, pl.ds(16 * half, 16)].astype(F32)
                    pair[0][zz, at_rows, inside_cols] = both[:8]
                    pair[1][zz, at_rows, inside_cols] = both[8:]
            return carry

        lax.fori_loop(0, depth, fill, 0)

    def fill_corners(who, base):
        for r, at_rows in enumerate(edge_rows):
            right, left = cfs[who, 2 * r], cfs[who, 2 * r + 1]
            rights = cbs[who, 2 * r].astype(F32)[:8]
            lefts = cbs[who, 2 * r + 1].astype(F32)[:8]
            for z in range(depth):
                both = jnp.where(
                    low_half, roll(right, -HALO * z, 1), roll(left, LANES - HALO - HALO * z, 1)
                )
                hx[base + z, at_rows, extra] = both
                tx[base + z, at_rows, extra] = roll(both, 2 if r == 0 else 6, 0)
                for a, dst in enumerate((ke, kn, kv, st)):
                    slot = a * depth + z
                    dst[base + z, at_rows, extra] = jnp.where(
                        low_half,
                        roll(rights, -HALO * slot, 1),
                        roll(lefts, LANES - HALO - HALO * slot, 1),
                    )

    fill_inner(own)
    for copy in easts:
        copy.wait_recv()
    forwards = [send(efs.at[0], efs.at[1], partner), send(ebs.at[0], ebs.at[1], partner)]
    fill_east(0, own)
    for copy in norths:
        copy.wait_recv()
    forwards.append(send(nbs.at[0], nbs.at[1], partner))
    for side in (0, 1):
        place_of = hx.at[own_layers, edge_rows[side], inside_cols]
        forwards.append(send(place_of, place_of, partner))
    for copy in corners:
        copy.wait_recv()
    forwards.append(send(cfs.at[0], cfs.at[1], partner))
    forwards.append(send(cbs.at[0], cbs.at[1], partner))
    fill_north(0, own)
    fill_corners(0, own)
    for copy in blocks:
        copy.wait_recv()
    fill_inner(other)
    for copy in forwards:
        copy.wait_recv()
    fill_east(1, other)
    fill_north(1, other)
    fill_corners(1, other)
    for copy in norths + easts + corners + blocks + forwards:
        copy.wait_send()

    weights = []
    for z in range(layers):
        found = dot(ke[z].astype(BF16), col_hot, NN)
        k_at = jnp.sum(found * row_hot, axis=0, keepdims=True)
        screened = (comp[2:3] <= z) & (comp[3:4] >= z)
        weights.append(jnp.where(screened, k_at, 0.0))
    weight = jnp.concatenate(weights, axis=0)
    total = jnp.sum(weight, axis=0, keepdims=True)
    share = weight / jnp.where(total > 0, total, 1.0)
    pumped = share * comp[4:5]
    priced = pumped * comp[5:6]
    col_two = jnp.concatenate([col_hot, col_hot], axis=1)
    for z in range(layers):
        left = []
        for value in (pumped, priced):
            top, rest = split(value[z:z + 1], 2)
            left.append(
                jnp.concatenate([row_hot * top.astype(F32), row_hot * rest.astype(F32)], axis=1)
            )
        left = jnp.concatenate(left, axis=0).astype(BF16)
        field = dot(left, col_two, NT)
        src[z] = field[:ext_rows]
        lw[z] = field[ext_rows:]

    wide = (8, ext_cols)
    sub = iota(wide, 0)
    col = iota(wide, 1)
    closed_col = ((col == cols - 1) & (me_e == n_east - 1)) | ((col == ext_cols - 1) & (me_e == 0))
    open_east = jnp.where(closed_col, 0.0, 2.0)
    open_low = jnp.where((sub == 7) & (me_n == 0), 0.0, 2.0)
    open_high = jnp.where((sub == 7) & (me_n == n_north - 1), 0.0, 2.0)

    def east(v):
        return roll(v, ext_cols - 1, 1)

    def west(v):
        return roll(v, 1, 1)

    def north(now, after):
        return jnp.where(sub < 7, roll(now, 7, 0), roll(after, 7, 0))

    def south(now, prior):
        return jnp.where(sub > 0, roll(now, 1, 0), roll(prior, 1, 0))

    fu[0] = jnp.zeros((ext_rows, ext_cols), F32)

    def row_chunks(begin, end, unit, body, carry):
        if end - begin == unit:
            for j in range(begin, end):
                carry = body(j, carry)
            return carry

        def several(k, carry):
            for i in range(unit):
                carry = body(begin + k * unit + i, carry)
            return carry

        return lax.fori_loop(0, (end - begin) // unit, several, carry)

    def at(j):
        return pl.ds(8 * j if isinstance(j, int) else pl.multiple_of(8 * j, 8), 8)

    def next_of(j):
        return min(j + 1, chunks_of_rows - 1) if isinstance(j, int) else jnp.minimum(j + 1, chunks_of_rows - 1)

    def start(z, carry):
        up = jnp.minimum(z + 1, layers - 1)
        down = jnp.maximum(z - 1, 0)
        open_up = jnp.where(z < layers - 1, 2.0, 0.0)

        def chunk(j, carry):
            fn_prior, gn_prior, k_n, h = carry
            k_e, k_u, k_u2 = ke[z, at(j)], kv[z, at(j)], kv[up, at(j)]
            k_e2 = east(k_e)
            k_after, h_after = kn[z, at(next_of(j))], hx[z, at(next_of(j))]
            k_n2 = north(k_n, k_after)
            f_e = open_east * k_e * k_e2 * reciprocal(k_e + k_e2)
            if isinstance(j, int):
                opened = open_low if j == 0 else open_high if j == chunks_of_rows - 2 else 2.0
            else:
                edge = ((j == 0) & (me_n == 0)) | ((j == chunks_of_rows - 2) & (me_n == n_north - 1))
                opened = jnp.where((sub == 7) & edge, 0.0, 2.0)
            f_n = opened * k_n * k_n2 * reciprocal(k_n + k_n2)
            f_u = open_up * k_u * k_u2 * reciprocal(k_u + k_u2)
            f_d = fu[z, at(j)]
            fe[z, at(j)] = f_e
            fn[z, at(j)] = f_n
            fu[z + 1, at(j)] = f_u
            diagonal = st[z, at(j)] + f_e + west(f_e) + f_n + south(f_n, fn_prior) + f_u + f_d
            inverse = reciprocal(diagonal)
            inv[z, at(j)] = inverse
            g_e = f_e * (east(h) - h)
            g_n = f_n * (north(h, h_after) - h)
            g_u = f_u * (hx[up, at(j)] - h)
            g_d = f_d * (h - hx[down, at(j)])
            residual = (g_e - west(g_e)) + (g_n - south(g_n, gn_prior)) + (g_u - g_d)
            d0[z, at(j)] = inverse * (residual - src[z, at(j)])
            return f_n, g_n, k_after, h_after

        none = jnp.zeros(wide, F32)
        row_chunks(0, chunks_of_rows, START_UNIT, chunk, (none, none, kn[z, at(0)], hx[z, at(0)]))
        return carry

    lax.fori_loop(0, layers, start, 0)

    def sweep(field, margin, finish, chunk_from, chunk_to):
        def layer(i, carry):
            z = (depth - margin) * me_l + i
            up = jnp.minimum(z + 1, layers - 1)
            down = jnp.maximum(z - 1, 0)

            def chunk(j, carry):
                b_prior, d = carry
                d_after = field[z, at(next_of(j))]
                f_e, f_n = fe[z, at(j)], fn[z, at(j)]
                b = f_n * d
                moved = f_e * east(d) + west(f_e * d)
                moved = moved + f_n * north(d, d_after) + south(b, b_prior)
                moved = moved + fu[z + 1, at(j)] * field[up, at(j)] + fu[z, at(j)] * field[down, at(j)]
                finish(i, z, j, d, inv[z, at(j)] * moved)
                return b, d_after

            if chunk_from == 0:
                b_prior = jnp.zeros(wide, F32)
            else:
                b_prior = fn[z, at(chunk_from - 1)] * field[z, at(chunk_from - 1)]
            unit = SWEEP_UNIT if chunk_from == 0 else LAST_UNIT
            row_chunks(chunk_from, chunk_to, unit, chunk, (b_prior, field[z, at(chunk_from)]))
            return carry

        lax.fori_loop(0, depth + margin, layer, 0)

    (a1, b1), (a2, b2) = steps_of()

    def first_sweep(i, z, j, d, pulled):
        s1[z, at(j)] = pulled
        d1[z, at(j)] = a1 * d + b1 * pulled

    def end_forward(i, z, j, d, pulled):
        s2 = s1[z, at(j)] - d + pulled
        d2 = a2 * d + b2 * s2
        new = hx[z, at(j)] + d0[z, at(j)] + d + d2
        hx[z, at(j)] = new
        load = new - tx[z, at(j)] - lw[z, at(j)]
        src[z, at(j)] = inv[z, at(j)] * load

    sweep(d0, 3, first_sweep, 0, chunks_of_rows)
    sweep(d1, 2, end_forward, 0, chunks_of_rows)
    sweep(src, 1, first_sweep, 0, chunks_of_rows)

    st[0, at(0)] = jnp.zeros(wide, F32)

    def end_adjoint(i, z, j, d, pulled):
        s2 = s1[z, at(j)] - d + pulled
        d2 = a2 * d + b2 * s2
        adj = src[z, at(j)] + d + d2
        adjoint[i, at(j - 1)] = adj[:, :cols]
        new = hx[z, at(j), inside_cols]
        head_new[i, at(j - 1)] = new
        departure = new - tx[z, at(j), inside_cols]
        st[0, at(0), inside_cols] = st[0, at(0), inside_cols] + departure * departure

    sweep(d1, 0, end_adjoint, 1, chunks_of_rows - 1)

    writes = [load(head_new, out_new), load(adjoint, out_adjoint)]

    squared = st[0, at(0), inside_cols]
    squared = jnp.sum(squared, axis=0, keepdims=True)
    squared = sum(squared[:, LANES * k:LANES * (k + 1)] for k in range(cols // LANES))
    squared = squared * (1.0 / (float(layers * rows * cols) * n_east * n_north))
    base_layer = jnp.where(me_l == 0, 1.0, 0.0)

    col_hot, row_hot = col_hot[:cols], row_hot[8:8 + rows]
    head_at = jnp.zeros((1, SLOTS), F32)
    adj_at = jnp.zeros((1, SLOTS), F32)
    for i in range(depth):
        z_share = jnp.where(me_l == 0, share[i:i + 1], share[depth + i:depth + i + 1])
        stack = split(head_new[i], 2) + split(adjoint[i], 2)
        found = [dot(piece, col_hot, NN) for piece in stack]
        head_at += z_share * jnp.sum((found[0] + found[1]) * row_hot, axis=0, keepdims=True)
        adj_at += z_share * jnp.sum((found[2] + found[3]) * row_hot, axis=0, keepdims=True)
    lift = (comp[6:7] * base_layer - head_at) * comp[7:8]
    priced = comp[5:6] * lift
    slope = priced - adj_at * comp[7:8]
    three = jnp.concatenate(
        [p.astype(F32) for p in split(slope, 3)] + [jnp.zeros((5, SLOTS), F32)], axis=0
    ).astype(BF16)
    spread = dot(three, pt[...], NN)
    spread = spread[0:1] + spread[1:2] + spread[2:3]
    tile = jnp.concatenate(
        [spread[:, LANES * k:LANES * (k + 1)] for k in range(groups)], axis=0
    )
    parts[pl.ds(0, groups)] = tile
    parts[pl.ds(groups, 8)] = jnp.concatenate(
        [
            priced * comp[4:5],
            squared,
            jnp.broadcast_to(crowded, (1, LANES)),
            jnp.zeros((5, LANES), F32),
        ],
        axis=0,
    )

    total = parts[...]
    used = 0
    for box, mine, peers in phases:
        box[mine] = total
        copies = []
        for device in peers:
            copy = pltpu.make_async_remote_copy(
                src_ref=box.at[mine],
                dst_ref=box.at[mine],
                send_sem=sum_send.at[used],
                recv_sem=sum_recv.at[used],
                device_id=device,
                device_id_type=MESH,
            )
            copy.start()
            copies.append(copy)
            used += 1
        for copy in copies:
            copy.wait()
        total = box[0]
        for k in range(1, len(peers) + 1):
            total = total + box[k]
    n_wells = out_slope.shape[1]
    for k in range(groups):
        width = min(LANES, n_wells - LANES * k)
        out_slope[:, pl.ds(LANES * k, width)] = total[k:k + 1, :width]
    sums = jnp.sum(total[groups:], axis=1, keepdims=True)
    out_cost[...] = sums[0:1]
    out_misfit[...] = sums[1:2]
    out_crowded[...] = sums[2:3]
    for copy in writes:
        copy.wait()


def run_kernel(sizes, fields, wells):
    depth, rows, cols = fields[0].shape
    layers, ext_rows, ext_cols = 2 * depth, rows + 16, cols + LANES
    n_wells = wells[0].shape[1]
    groups = -(-n_wells // LANES)
    n_east, n_x, n_z = sizes
    block = jax.ShapeDtypeStruct((depth, rows, cols), F32)
    one = jax.ShapeDtypeStruct((1, 1), F32)
    ext = pltpu.VMEM((layers, ext_rows, ext_cols), F32)
    operands = (*fields, *wells)
    copies = 4 + 4 + 8 + 6 + 7
    peers = 1 + n_z + n_east + n_x - 3
    return pl.pallas_call(
        functools.partial(kernel, sizes),
        out_shape=[block, block, jax.ShapeDtypeStruct((1, n_wells), F32), one, one, one],
        in_specs=[pl.BlockSpec(memory_space=pltpu.HBM)] * len(operands),
        out_specs=[pl.BlockSpec(memory_space=pltpu.HBM)] * 2
        + [pl.BlockSpec(memory_space=pltpu.VMEM)] * 4,
        scratch_shapes=[ext] * 8
        + [pltpu.VMEM((layers + 1, ext_rows, ext_cols), F32)]
        + [ext] * 6
        + [pltpu.VMEM((SLOTS, groups * LANES), BF16)]
        + [pltpu.VMEM((depth, rows, cols), F32)] * 2
        + [pltpu.VMEM((groups + 8, LANES), F32)]
        + [pltpu.VMEM((layers, rows, cols), BF16)] * 4
        + [
            pltpu.VMEM((2, 2, depth, 32, cols), BF16),
            pltpu.VMEM((2, 2, depth, 8, LANES), F32),
            pltpu.VMEM((2, 2, depth, 32, LANES), BF16),
            pltpu.VMEM((2, 4, 8, LANES), F32),
            pltpu.VMEM((2, 4, 16, LANES), BF16),
            pltpu.VMEM((2, depth, 8, cols), F32),
            pltpu.VMEM((2, depth, 32, cols), BF16),
            pltpu.VMEM((2, depth, 8, LANES), F32),
            pltpu.VMEM((2, depth, 32, LANES), BF16),
            pltpu.VMEM((4, 8, LANES), F32),
            pltpu.VMEM((4, 16, LANES), BF16),
        ]
        + [pltpu.VMEM(w.shape, w.dtype) for w in wells]
        + [pltpu.VMEM((8, groups * LANES), F32)]
        + [pltpu.VMEM((n, groups + 8, LANES), F32) for n in (2, n_z, n_east, n_x)]
        + [pltpu.SemaphoreType.DMA((16,))]
        + [pltpu.SemaphoreType.DMA((copies,))] * 2
        + [pltpu.SemaphoreType.DMA((peers,))] * 2,
        compiler_params=pltpu.CompilerParams(
            collective_id=0, has_side_effects=True, vmem_limit_bytes=60 * 1024 * 1024
        ),
        name="whole_step",
    )(*operands)


def hand_over(*refs):
    count = (len(refs) - 2) // 3
    given, out, held = refs[:count], refs[count:2 * count], refs[2 * count:3 * count]
    in_sem, out_sem = refs[3 * count:]
    reads = [pltpu.make_async_copy(given[k], held[k], in_sem.at[k]) for k in range(count)]
    writes = [pltpu.make_async_copy(held[k], out[k], out_sem.at[k]) for k in range(count)]
    for copy in reads:
        copy.start()
    for read, write in zip(reads, writes):
        read.wait()
        write.start()
    for copy in writes:
        copy.wait()


def run_hand_over(values):
    return pl.pallas_call(
        hand_over,
        out_shape=[jax.ShapeDtypeStruct(v.shape, v.dtype) for v in values],
        in_specs=[pl.BlockSpec(memory_space=pltpu.HBM)] * len(values),
        out_specs=[pl.BlockSpec(memory_space=pltpu.HBM)] * len(values),
        scratch_shapes=[pltpu.VMEM(v.shape, v.dtype) for v in values]
        + [pltpu.SemaphoreType.DMA((len(values),))] * 2,
        compiler_params=pltpu.CompilerParams(vmem_limit_bytes=60 * 1024 * 1024),
        name="hand_over",
    )(*values)


def in_order(value):
    return with_layout_constraint(value, Layout(major_to_minor=(0, 1, 2)))


def per_device(sizes, *arguments):
    fields = arguments[:6]
    e, n, top, bottom, tariff, rates, ground, prices = arguments[6:]
    wells = [w.reshape(1, -1) for w in (e, n, top, bottom, rates, tariff, ground, prices)]
    new, adjoint, slope, cost, misfit, crowded = run_kernel(sizes, fields, wells)
    found = (new, adjoint, slope, cost, misfit)

    def again(state):
        blocks = [in_order(x) for x in fields]
        first, second, *others = plain(*blocks, *arguments[6:])
        others = [x.reshape(1, -1) for x in others]
        return jnp.zeros((), F32), (in_order(first), in_order(second), *others)

    _, found = lax.while_loop(lambda state: state[0] > 0, again, (crowded.reshape(()), found))
    new, adjoint, slope, cost, misfit = run_hand_over(found)
    return new, adjoint, slope.reshape(-1), cost.reshape(()), misfit.reshape(())


def solution(mesh):
    field = P("layer", "north", "east")
    n_north = mesh.shape["north"]
    n_x = 4 if n_north % 4 == 0 else 1
    sizes = (mesh.shape["east"], n_x, n_north // n_x)
    return jax.shard_map(
        functools.partial(per_device, sizes),
        mesh=mesh,
        in_specs=(field,) * 6 + (P(),) * 8,
        out_specs=(field, field, P(), P(), P()),
        check_vma=False,
    )
```

```python
import functools

import jax
import jax.numpy as jnp
from jax import lax
from jax.experimental import pallas as pl
from jax.experimental.layout import Layout, with_layout_constraint
from jax.experimental.pallas import tpu as pltpu
from jax.sharding import PartitionSpec as P

MESH = pl.DeviceIdType.MESH
F32 = jnp.float32
BF16 = jnp.bfloat16

SWEEPS = 3
CENTRE = 1.0
HALF_WIDTH = 0.95

HALO = 8
REACH = 5
LANES = 128
SLOTS = 128
START_UNIT, SWEEP_UNIT, LAST_UNIT = 9, 18, 16


def steps_of():
    sigma = CENTRE / HALF_WIDTH
    factor = 1.0 / sigma
    found = []
    for _ in range(SWEEPS - 1):
        after = 1.0 / (2.0 * sigma - factor)
        found.append((after * factor, 2.0 * after / HALF_WIDTH))
        factor = after
    return found


def iota(shape, dim):
    return lax.broadcasted_iota(jnp.int32, shape, dim)


def roll(value, shift, dim):
    shift = shift % value.shape[dim]
    return pltpu.roll(value, shift, dim) if shift else value


def extended(value, sides, width):
    for axis, dim in sides:
        size, length = (lax.axis_size(axis), value.shape[dim])
        up = [(i, (i + 1) % size) for i in range(size - 1)]
        down = [(j, i) for i, j in up]
        last = lax.slice_in_dim(value, length - width, length, axis=dim)
        initial = lax.slice_in_dim(value, 0, width, axis=dim)
        before = lax.ppermute(last, axis, up)
        after = lax.ppermute(initial, axis, down)
        value = jnp.concatenate([before, value, after], axis=dim)
    return value


def harmonic(first, second):
    total = first + second
    return 2.0 * first * second / jnp.where(total > 0, total, 1.0)


def face_terms(east_pad, north_pad, up_pad, stored):
    face_east = harmonic(east_pad[:, :, :-1], east_pad[:, :, 1:])
    face_north = harmonic(north_pad[:, :-1], north_pad[:, 1:])
    face_up = harmonic(up_pad[:-1], up_pad[1:])
    diagonal = stored + face_east[:, :, :-1] + face_east[:, :, 1:]
    diagonal = diagonal + face_north[:, :-1] + face_north[:, 1:]
    diagonal = diagonal + face_up[:-1] + face_up[1:]
    positive = diagonal > 0
    inverse = jnp.where(positive, 1.0 / jnp.where(positive, diagonal, 1.0), 0.0)
    return (stored, face_east, face_north, face_up, inverse)


def coefficients(padded_coefs):
    stacked = padded_coefs.astype(jnp.float32)
    east_pad = stacked[0][1:-1, 1:-1, :]
    north_pad = stacked[1][1:-1, :, 1:-1]
    up_pad = stacked[2][:, 1:-1, 1:-1]
    stored = stacked[3][1:-1, 1:-1, 1:-1]
    return face_terms(east_pad, north_pad, up_pad, stored)


def apply_operator(padded, storage_part, face_east, face_north, face_up):
    center = padded[1:-1, 1:-1, 1:-1]
    step_east = padded[1:-1, 1:-1, 1:] - padded[1:-1, 1:-1, :-1]
    step_north = padded[1:-1, 1:, 1:-1] - padded[1:-1, :-1, 1:-1]
    step_up = padded[1:, 1:-1, 1:-1] - padded[:-1, 1:-1, 1:-1]
    flux_east = face_east * step_east
    flux_north = face_north * step_north
    flux_up = face_up * step_up
    total = storage_part * center + (flux_east[:, :, :-1] - flux_east[:, :, 1:])
    total = total + (flux_north[:, :-1] - flux_north[:, 1:])
    return total + (flux_up[:-1] - flux_up[1:])


def keep_whole(field):
    return field


def chebyshev(start, rhs, operate, trim, precondition):
    if start is None:
        residual = rhs
    else:
        residual = trim(rhs) - operate(start)
    direction = precondition(residual) / CENTRE
    if start is None:
        iterate = direction
    else:
        iterate = trim(start) + direction
    sigma = CENTRE / HALF_WIDTH
    factor = 1.0 / sigma
    for sweep_index in range(SWEEPS - 1):
        residual = trim(residual) - operate(direction)
        factor_next = 1.0 / (2.0 * sigma - factor)
        direction = factor_next * factor * trim(
            direction
        ) + 2.0 * factor_next / HALF_WIDTH * precondition(residual)
        iterate = trim(iterate) + direction
        factor = factor_next
    return iterate


def plain(
    head_old,
    head_target,
    conductivity_east,
    conductivity_north,
    conductivity_vertical,
    storage,
    well_east,
    well_north,
    screen_top,
    screen_bottom,
    tariff_band,
    pump_rates,
    ground_level,
    band_prices,
):
    depth_cells, north_cells, east_cells = head_old.shape
    stacked_coefs = jnp.stack(
        (conductivity_east, conductivity_north, conductivity_vertical, storage)
    )
    padded_coefs = extended(stacked_coefs, (("east", 3), ("north", 2), ("layer", 1)), 1)
    margin = 0
    top_level = coefficients(padded_coefs)
    levels = [None] * (margin + 1)
    levels[margin] = top_level

    def margin_of(field):
        return (field.shape[0] - depth_cells) // 2

    def precondition(residual):
        return levels[margin_of(residual)][4] * residual

    def operate(field):
        padded = extended(field, (("east", 2), ("north", 1), ("layer", 0)), 1)
        level = levels[0]
        return apply_operator(padded, level[0], level[1], level[2], level[3])

    east_start = lax.axis_index("east") * east_cells
    north_start = lax.axis_index("north") * north_cells
    layer_start = lax.axis_index("layer") * depth_cells
    local_east = well_east - east_start
    local_north = well_north - north_start
    owning = (
        (local_east >= 0)
        & (local_east < east_cells)
        & (local_north >= 0)
        & (local_north < north_cells)
    ).astype(jnp.float32)
    cells = jnp.clip(local_north, 0, north_cells - 1) * east_cells + jnp.clip(
        local_east, 0, east_cells - 1
    )
    depth = layer_start + jnp.arange(depth_cells, dtype=jnp.int32)[:, None]
    screened = ((depth >= screen_top[None, :]) & (depth <= screen_bottom[None, :])).astype(
        jnp.float32
    ) * owning[None, :]
    weights = (
        conductivity_east.reshape(depth_cells, north_cells * east_cells)[:, cells].astype(
            jnp.float32
        )
        * screened
    )
    totals = lax.psum(jnp.sum(weights, axis=0), "layer")
    shares = weights / (totals + (1.0 - owning))[None, :]
    flat_shape = (depth_cells, north_cells * east_cells)
    source = (
        jnp.zeros(flat_shape, jnp.float32)
        .at[:, cells]
        .add(pump_rates[None, :] * shares)
        .reshape(head_old.shape)
    )
    stored = storage.astype(jnp.float32)
    rhs = stored * head_old - source
    head_new = chebyshev(head_old, rhs, operate, keep_whole, precondition)
    departure = head_new - head_target
    misfit_part = jnp.sum(departure * departure)
    all_cells = float(
        depth_cells
        * north_cells
        * east_cells
        * lax.axis_size("east")
        * lax.axis_size("north")
        * lax.axis_size("layer")
    )
    head_part = jnp.sum(shares * head_new.reshape(flat_shape)[:, cells], axis=0)
    head_screen, misfit_total = lax.psum((head_part, misfit_part), ("east", "north", "layer"))
    band_ids = jnp.arange(band_prices.shape[0], dtype=jnp.int32)
    prices = jnp.sum(
        jnp.where(tariff_band[:, None] == band_ids[None, :], band_prices[None, :], 0.0), axis=1
    )
    load = (
        departure.reshape(flat_shape)
        .at[:, cells]
        .add(-(prices * pump_rates)[None, :] * shares)
        .reshape(head_old.shape)
    )
    adjoint_head = chebyshev(None, load, operate, keep_whole, precondition)
    adjoint_part = jnp.sum(shares * adjoint_head.reshape(flat_shape)[:, cells], axis=0)
    adjoint_screen = lax.psum(adjoint_part, ("east", "north", "layer"))
    misfit = misfit_total / all_cells
    lift = ground_level - head_screen
    rate_gradient = prices * lift - adjoint_screen
    pumping_cost = jnp.sum(prices * pump_rates * lift)
    return (head_new, adjoint_head, rate_gradient, pumping_cost, misfit)


def split(value, parts):
    found = []
    for _ in range(parts):
        top = value.astype(BF16)
        found.append(top)
        value = value - top.astype(F32)
    return found


def dot(a, b, dims):
    return lax.dot_general(a, b, (dims, ((), ())), preferred_element_type=F32)


NN = ((1,), (0,))
NT = ((1,), (1,))


def reciprocal(x):
    first = pl.reciprocal(x, approx=True)
    return first * (2.0 - x * first)


def kernel(sizes, *refs):
    n_east, n_x, n_z = sizes
    n_north = n_x * n_z
    fields, well_refs, refs = refs[:6], refs[6:14], refs[14:]
    head_new, adjoint, out_slope, out_cost, out_misfit, out_crowded = refs[:6]
    hx, tx, ke, kn, kv, st, fe, fn, fu, inv, src, lw, d0, d1, s1, pt = refs[6:22]
    parts, staged, (nbs, efs, ebs, cfs, cbs), refs = refs[22], refs[23:27], refs[27:32], refs[32:]
    (s_nf, s_nb, s_ef, s_eb, s_cf, s_cb), refs = refs[:6], refs[6:]
    well_rows, wells, boxes, refs = refs[:8], refs[8], refs[9:13], refs[13:]
    load_sem, send_sem, recv_sem, sum_send, sum_recv = refs
    depth, rows, cols = head_new.shape
    layers, ext_rows, ext_cols = hx.shape
    chunks_of_rows = ext_rows // 8
    groups = wells.shape[1] // LANES
    me_e, me_n, me_l = lax.axis_index("east"), lax.axis_index("north"), lax.axis_index("layer")
    me_x, me_z = me_n // n_z, lax.rem(me_n, n_z)
    own, other = depth * me_l, depth * (1 - me_l)
    own_layers = pl.ds(own, depth)

    def east_of(side):
        return lax.rem(me_e + (n_east - 1 if side == 0 else 1), n_east)

    def north_of(side):
        return lax.rem(me_n + (n_north - 1 if side == 0 else 1), n_north)

    partner = (me_e, me_n, 1 - me_l)
    to_north = [(me_e, north_of(s), me_l) for s in (0, 1)]
    to_east = [(east_of(s), me_n, me_l) for s in (0, 1)]
    to_corner = [(east_of(c), north_of(r), me_l) for r in (0, 1) for c in (0, 1)]
    phases = []
    for box, size, mine, device in (
        (boxes[0], 2, me_l, lambda i: (me_e, me_n, i)),
        (boxes[1], n_z, me_z, lambda i: (me_e, me_x * n_z + i, me_l)),
        (boxes[2], n_east, me_e, lambda i: (i, me_n, me_l)),
        (boxes[3], n_x, me_x, lambda i: (me_e, i * n_z + me_z, me_l)),
    ):
        phases.append((box, mine, [device(lax.rem(mine + k, size)) for k in range(1, size)]))

    greeted = [partner] + to_north + to_east + to_corner
    for _, _, peers in phases:
        greeted = greeted + peers
    barrier = pltpu.get_barrier_semaphore()
    for device in greeted:
        pl.semaphore_signal(barrier, inc=1, device_id=device, device_id_type=MESH)

    loaded = [0]

    def load(src_ref, dst_ref):
        copy = pltpu.make_async_copy(src_ref, dst_ref, load_sem.at[loaded[0]])
        loaded[0] += 1
        copy.start()
        return copy

    lane = iota((8, LANES), 1)
    group = lane // HALO
    wide_sub = iota((8, cols), 0)
    last = cols - LANES
    low_half = lane < LANES // 2
    extra = pl.ds(cols, LANES)
    inside_cols = pl.ds(0, cols)
    inner = pl.ds(8, rows)
    edge_rows = (pl.ds(rows + 8, 8), pl.ds(0, 8))

    block_loads = [
        load(fields[0], hx.at[own_layers, inner, inside_cols]),
        load(fields[1], tx.at[own_layers, inner, inside_cols]),
    ] + [load(fields[2 + a], staged[a].at[own_layers]) for a in range(4)]
    well_loads = [load(a, b) for a, b in zip(well_refs, well_rows)]
    for copy in block_loads:
        copy.wait()

    def pack(z, carry):
        for side in (0, 1):
            c0 = last * side
            kept = jnp.zeros((8, LANES), F32)
            fields = [jnp.zeros((8, LANES), F32) for _ in staged]
            for pair in range(rows // 16):
                tiles = [
                    ref[own + z, pl.ds(16 * pair, 16), pl.ds(c0, LANES)].astype(F32) for ref in staged
                ]
                for half in (0, 1):
                    j = 2 * pair + half
                    shift = HALO * j - (LANES - HALO) * side
                    h = hx[own + z, pl.ds(8 + 8 * j, 8), pl.ds(c0, LANES)]
                    t = tx[own + z, pl.ds(8 + 8 * j, 8), pl.ds(c0, LANES)]
                    if side == 0:
                        both = jnp.where(lane >= HALO - 2, roll(t, HALO - 2, 1), h)
                    else:
                        both = jnp.where(lane < LANES - HALO + 2, roll(t, 2 - HALO, 1), h)
                    here = group == j
                    kept = jnp.where(here, roll(both, shift, 1), kept)
                    for a in range(4):
                        piece = tiles[a][8 * half:8 * half + 8]
                        fields[a] = jnp.where(here, roll(piece, shift, 1), fields[a])
            s_ef[side, z] = kept
            s_eb[side, z, pl.ds(0, 16)] = jnp.concatenate(fields[:2], axis=0).astype(BF16)
            s_eb[side, z, pl.ds(16, 16)] = jnp.concatenate(fields[2:], axis=0).astype(BF16)
            r0 = (rows - 8) * side
            h = hx[own + z, pl.ds(8 + r0, 8), inside_cols]
            t = tx[own + z, pl.ds(8 + r0, 8), inside_cols]
            edge = [
                ref[own + z, pl.ds((rows - 16) * side, 16), :].astype(F32)[8 * side:8 * side + 8]
                for ref in staged
            ]
            if side == 0:
                both = jnp.where(wide_sub == 5, roll(edge[1], 1, 0), h)
                both = jnp.where(wide_sub >= 6, roll(t, 6, 0), both)
                first = jnp.where(wide_sub < 4, edge[0], roll(edge[1], 4, 0))
                second = jnp.where(wide_sub < 4, edge[2], roll(edge[3], 4, 0))
            else:
                both = jnp.where(wide_sub == 2, roll(edge[1], 7, 0), h)
                both = jnp.where(wide_sub < 2, roll(t, 2, 0), both)
                first = jnp.where(wide_sub < 4, roll(edge[0], 4, 0), edge[1])
                second = jnp.where(wide_sub < 4, roll(edge[2], 4, 0), edge[3])
            s_nf[side, z] = both
            s_nb[side, z] = jnp.concatenate([first, second], axis=0).astype(BF16)
        return carry

    lax.fori_loop(0, depth, pack, 0)

    for r in (0, 1):
        for c in (0, 1):
            c0 = last * c
            kept = jnp.zeros((8, LANES), F32)
            mixed = jnp.zeros((8, LANES), F32)
            for z in range(depth):
                both = s_nf[r, z, :, pl.ds(c0, LANES)]
                kept = jnp.where(group == z, roll(both, HALO * z - (LANES - HALO) * c, 1), kept)
                pieces = s_nb[r, z, :, pl.ds(c0, LANES)].astype(F32)
                for half in (0, 1):
                    slot = half * depth + z
                    moved = roll(
                        pieces[8 * half:8 * half + 8], HALO * slot - (LANES - HALO) * c, 1
                    )
                    mixed = jnp.where(group == slot, moved, mixed)
            s_cf[2 * r + c] = kept
            s_cb[2 * r + c] = jnp.concatenate([mixed, mixed], axis=0).astype(BF16)

    pl.semaphore_wait(barrier, len(greeted))

    sent = [0]

    def send(src_ref, dst_ref, device):
        copy = pltpu.make_async_remote_copy(
            src_ref=src_ref,
            dst_ref=dst_ref,
            send_sem=send_sem.at[sent[0]],
            recv_sem=recv_sem.at[sent[0]],
            device_id=device,
            device_id_type=MESH,
        )
        sent[0] += 1
        copy.start()
        return copy

    norths, easts, corners = [], [], []
    for side in (0, 1):
        norths.append(send(s_nb.at[side], nbs.at[0, side], to_north[side]))
        norths.append(
            send(s_nf.at[side], hx.at[own_layers, edge_rows[side], inside_cols], to_north[side])
        )
    for side in (0, 1):
        easts.append(send(s_eb.at[side], ebs.at[0, side], to_east[side]))
        easts.append(send(s_ef.at[side], efs.at[0, side], to_east[side]))
    for d in range(4):
        corners.append(send(s_cb.at[d], cbs.at[0, d], to_corner[d]))
        corners.append(send(s_cf.at[d], cfs.at[0, d], to_corner[d]))
    two = (depth - 2) * (1 - me_l)
    blocks = [send(fields[2 + a], staged[a].at[own_layers], partner) for a in range(4)]
    blocks.append(send(fields[0], hx.at[own_layers, inner, inside_cols], partner))
    blocks.append(
        send(
            fields[1].at[pl.ds(two, 2)], tx.at[pl.ds(own + two, 2), inner, inside_cols], partner
        )
    )

    for copy in well_loads:
        copy.wait()
    wells[...] = jnp.full(wells.shape, -1e6, F32)
    width = pl.ds(0, well_rows[0].shape[1])
    for row, ref in enumerate(well_rows[:5]):
        wells[pl.ds(row, 1), width] = ref[...].astype(F32)
    band = well_rows[5][...]
    bands = well_rows[7][...]
    price = jnp.zeros(band.shape, F32)
    for b in range(bands.shape[1]):
        price = jnp.where(band == b, bands[0:1, b:b + 1], price)
    wells[pl.ds(5, 1), width] = price
    wells[pl.ds(6, 1), width] = well_rows[6][...]

    at_east = wells[0:1, :] - (me_e * cols).astype(F32)
    at_north = wells[1:2, :] - (me_n * rows).astype(F32)
    near = (
        (at_east >= -REACH) & (at_east < cols + REACH)
        & (at_north >= -REACH) & (at_north < rows + REACH)
    )
    mine = (at_east >= 0) & (at_east < cols) & (at_north >= 0) & (at_north < rows)
    near_row = jnp.where(near, 1.0, 0.0)
    near_tile = jnp.concatenate(
        [near_row[:, LANES * k:LANES * (k + 1)] for k in range(groups)], axis=0
    )
    before = (iota((LANES, LANES), 0) < iota((LANES, LANES), 1)).astype(F32).astype(BF16)
    in_row = dot(near_tile.astype(BF16), before, NN)
    above = (iota((groups, groups), 1) < iota((groups, groups), 0)).astype(F32).astype(BF16)
    rows_above = jnp.sum(dot(above, near_tile.astype(BF16), NN), axis=1, keepdims=True)
    rank = jnp.where(near_tile > 0, in_row + rows_above, -1.0)
    found = jnp.sum(jnp.sum(near_tile, axis=1, keepdims=True), axis=0, keepdims=True)
    crowded = jnp.where(found > SLOTS, 1.0, 0.0)

    place = jnp.concatenate(
        [
            jnp.where(at_east < 0, at_east + ext_cols, at_east),
            at_north + 8.0,
            wells[2:7, :],
            jnp.where(mine, 1.0, 0.0),
        ],
        axis=0,
    )
    place_parts = jnp.concatenate([p.astype(F32) for p in split(place, 3)], axis=0).astype(BF16)
    slot_of = iota((SLOTS, LANES), 0).astype(F32)

    for k in range(groups):
        pt[:, pl.ds(LANES * k, LANES)] = jnp.where(slot_of == rank[k:k + 1, :], 1.0, 0.0).astype(BF16)
    three = dot(place_parts, pt[...], NT)
    comp = three[0:8] + three[8:16] + three[16:24]
    col_hot = jnp.where(iota((ext_cols, SLOTS), 0).astype(F32) == comp[0:1], 1.0, 0.0)
    row_hot = jnp.where(iota((ext_rows, SLOTS), 0).astype(F32) == comp[1:2], 1.0, 0.0)
    col_hot = col_hot.astype(BF16)


    def fill_inner(base):
        def fill(z, carry):
            for dst, ref in zip((ke, kn, kv, st), staged):
                dst[base + z, inner, inside_cols] = ref[base + z].astype(F32)
            return carry

        lax.fori_loop(0, depth, fill, 0)

    def fill_east(who, base):
        def fill(z, carry):
            zz = base + z
            right, left = efs[who, 0, z], efs[who, 1, z]
            for j in range(rows // 8):
                both = jnp.where(
                    low_half, roll(right, -HALO * j, 1), roll(left, LANES - HALO - HALO * j, 1)
                )
                hx[zz, pl.ds(8 + 8 * j, 8), extra] = both
                tx[zz, pl.ds(8 + 8 * j, 8), extra] = jnp.where(
                    low_half, roll(both, 2 - HALO, 1), roll(both, HALO - 2, 1)
                )
            for half, pair in ((0, (ke, kn)), (1, (kv, st))):
                rights = ebs[who, 0, z, pl.ds(16 * half, 16)].astype(F32)
                lefts = ebs[who, 1, z, pl.ds(16 * half, 16)].astype(F32)
                for k in (0, 1):
                    right, left = rights[8 * k:8 * k + 8], lefts[8 * k:8 * k + 8]
                    for j in range(rows // 8):
                        pair[k][zz, pl.ds(8 + 8 * j, 8), extra] = jnp.where(
                            low_half,
                            roll(right, -HALO * j, 1),
                            roll(left, LANES - HALO - HALO * j, 1),
                        )
            return carry

        lax.fori_loop(0, depth, fill, 0)

    def put_rows(side, zz, at_rows, at_cols, both, first, second):
        row = iota(both.shape, 0)
        if side == 0:
            tx[zz, at_rows, at_cols] = roll(both, 2, 0)
            ke[zz, at_rows, at_cols] = first
            kn[zz, at_rows, at_cols] = jnp.where(row == 4, roll(both, 7, 0), roll(first, 4, 0))
            kv[zz, at_rows, at_cols] = second
            st[zz, at_rows, at_cols] = roll(second, 4, 0)
        else:
            tx[zz, at_rows, at_cols] = roll(both, 6, 0)
            ke[zz, at_rows, at_cols] = roll(first, 4, 0)
            kn[zz, at_rows, at_cols] = jnp.where(row == 3, roll(both, 1, 0), first)
            kv[zz, at_rows, at_cols] = roll(second, 4, 0)
            st[zz, at_rows, at_cols] = second

    def fill_north(who, base):
        def fill(z, carry):
            for side, at_rows in enumerate(edge_rows):
                pieces = nbs[who, side, z].astype(F32)
                both = hx[base + z, at_rows, inside_cols]
                put_rows(side, base + z, at_rows, inside_cols, both, pieces[:8], pieces[8:])
            return carry

        lax.fori_loop(0, depth, fill, 0)

    def fill_corners(who, base):
        for side, at_rows in enumerate(edge_rows):
            right, left = cfs[who, 2 * side], cfs[who, 2 * side + 1]
            rights = cbs[who, 2 * side].astype(F32)[:8]
            lefts = cbs[who, 2 * side + 1].astype(F32)[:8]

            def taken(a, b, slot):
                return jnp.where(
                    low_half, roll(a, -HALO * slot, 1), roll(b, LANES - HALO - HALO * slot, 1)
                )

            for z in range(depth):
                both = taken(right, left, z)
                hx[base + z, at_rows, extra] = both
                put_rows(
                    side, base + z, at_rows, extra, both,
                    taken(rights, lefts, z), taken(rights, lefts, depth + z),
                )

    wide = (8, ext_cols)
    sub = iota(wide, 0)
    col = iota(wide, 1)
    closed_col = ((col == cols - 1) & (me_e == n_east - 1)) | ((col == ext_cols - 1) & (me_e == 0))
    open_east = jnp.where(closed_col, 0.0, 2.0)
    open_low = jnp.where((sub == 7) & (me_n == 0), 0.0, 2.0)
    open_high = jnp.where((sub == 7) & (me_n == n_north - 1), 0.0, 2.0)

    def east(v):
        return roll(v, ext_cols - 1, 1)

    def west(v):
        return roll(v, 1, 1)

    def north(now, after):
        return jnp.where(sub < 7, roll(now, 7, 0), roll(after, 7, 0))

    def south(now, prior):
        return jnp.where(sub > 0, roll(now, 1, 0), roll(prior, 1, 0))

    fu[0] = jnp.zeros((ext_rows, ext_cols), F32)
    fu[layers] = jnp.zeros((ext_rows, ext_cols), F32)

    def row_chunks(begin, end, unit, body, carry):
        if end - begin == unit:
            for j in range(begin, end):
                carry = body(j, carry)
            return carry

        def several(k, carry):
            for i in range(unit):
                carry = body(begin + k * unit + i, carry)
            return carry

        return lax.fori_loop(0, (end - begin) // unit, several, carry)

    def at(j):
        return pl.ds(8 * j if isinstance(j, int) else pl.multiple_of(8 * j, 8), 8)

    def next_of(j):
        return min(j + 1, chunks_of_rows - 1) if isinstance(j, int) else jnp.minimum(j + 1, chunks_of_rows - 1)

    def layer_of(k):
        return jnp.where(me_l == 0, k, layers - 1 - k)

    def start(k, carry, with_wells):
        z = layer_of(k)
        up = layer_of(jnp.minimum(k + 1, layers - 1))
        down = layer_of(jnp.maximum(k - 1, 0))
        open_up = jnp.where(k < layers - 1, 2.0, 0.0)

        def chunk(j, carry):
            fn_prior, gn_prior, k_n, h = carry
            k_e, k_u, k_u2 = ke[z, at(j)], kv[z, at(j)], kv[up, at(j)]
            k_e2 = east(k_e)
            k_after, h_after = kn[z, at(next_of(j))], hx[z, at(next_of(j))]
            k_n2 = north(k_n, k_after)
            f_e = open_east * k_e * k_e2 * reciprocal(k_e + k_e2)
            if isinstance(j, int):
                opened = open_low if j == 0 else open_high if j == chunks_of_rows - 2 else 2.0
            else:
                edge = ((j == 0) & (me_n == 0)) | ((j == chunks_of_rows - 2) & (me_n == n_north - 1))
                opened = jnp.where((sub == 7) & edge, 0.0, 2.0)
            f_n = opened * k_n * k_n2 * reciprocal(k_n + k_n2)
            f_u = open_up * k_u * k_u2 * reciprocal(k_u + k_u2)
            f_d = fu[z + me_l, at(j)]
            fe[z, at(j)] = f_e
            fn[z, at(j)] = f_n
            fu[z + 1 - me_l, at(j)] = f_u
            diagonal = st[z, at(j)] + f_e + west(f_e) + f_n + south(f_n, fn_prior) + f_u + f_d
            inverse = reciprocal(diagonal)
            inv[z, at(j)] = inverse
            g_e = f_e * (east(h) - h)
            g_n = f_n * (north(h, h_after) - h)
            g_u = f_u * (hx[up, at(j)] - h)
            g_d = f_d * (h - hx[down, at(j)])
            residual = (g_e - west(g_e)) + (g_n - south(g_n, gn_prior)) + (g_u - g_d)
            if with_wells:
                residual = residual - src[z, at(j)]
            d0[z, at(j)] = inverse * residual
            return f_n, g_n, k_after, h_after

        none = jnp.zeros(wide, F32)
        row_chunks(0, chunks_of_rows, START_UNIT, chunk, (none, none, kn[z, at(0)], hx[z, at(0)]))
        return carry

    def pump(k, carry):
        z = layer_of(k)
        d0[z] = d0[z] - inv[z] * src[z]
        return carry

    fill_inner(own)
    for copy in easts:
        copy.wait_recv()
    forwards = [send(efs.at[0], efs.at[1], partner), send(ebs.at[0], ebs.at[1], partner)]
    fill_east(0, own)
    for copy in norths:
        copy.wait_recv()
    forwards.append(send(nbs.at[0], nbs.at[1], partner))
    for side in (0, 1):
        place_of = hx.at[own_layers, edge_rows[side], inside_cols]
        forwards.append(send(place_of, place_of, partner))
    for copy in corners:
        copy.wait_recv()
    forwards.append(send(cfs.at[0], cfs.at[1], partner))
    forwards.append(send(cbs.at[0], cbs.at[1], partner))
    fill_north(0, own)
    fill_corners(0, own)
    lax.fori_loop(0, depth - 1, functools.partial(start, with_wells=False), 0)
    for copy in blocks:
        copy.wait_recv()
    fill_inner(other)
    for copy in forwards:
        copy.wait_recv()
    fill_east(1, other)
    fill_north(1, other)
    fill_corners(1, other)
    for copy in norths + easts + corners + blocks + forwards:
        copy.wait_send()

    weights = []
    for z in range(layers):
        found = dot(ke[z].astype(BF16), col_hot, NN)
        k_at = jnp.sum(found * row_hot, axis=0, keepdims=True)
        screened = (comp[2:3] <= z) & (comp[3:4] >= z)
        weights.append(jnp.where(screened, k_at, 0.0))
    weight = jnp.concatenate(weights, axis=0)
    total = jnp.sum(weight, axis=0, keepdims=True)
    share = weight / jnp.where(total > 0, total, 1.0)
    pumped = share * comp[4:5]
    priced = pumped * comp[5:6]
    col_two = jnp.concatenate([col_hot, col_hot], axis=1)
    for z in range(layers):
        left = []
        for value in (pumped, priced):
            top, rest = split(value[z:z + 1], 2)
            left.append(
                jnp.concatenate([row_hot * top.astype(F32), row_hot * rest.astype(F32)], axis=1)
            )
        left = jnp.concatenate(left, axis=0).astype(BF16)
        field = dot(left, col_two, NT)
        src[z] = field[:ext_rows]
        lw[z] = field[ext_rows:]

    lax.fori_loop(0, depth - 1, pump, 0)
    lax.fori_loop(depth - 1, layers, functools.partial(start, with_wells=True), 0)

    def sweep(field, margin, finish, chunk_from, chunk_to):
        def layer(i, carry):
            z = (depth - margin) * me_l + i
            up = jnp.minimum(z + 1, layers - 1)
            down = jnp.maximum(z - 1, 0)

            def chunk(j, carry):
                b_prior, d = carry
                d_after = field[z, at(next_of(j))]
                f_e, f_n = fe[z, at(j)], fn[z, at(j)]
                b = f_n * d
                moved = f_e * east(d) + west(f_e * d)
                moved = moved + f_n * north(d, d_after) + south(b, b_prior)
                moved = moved + fu[z + 1, at(j)] * field[up, at(j)] + fu[z, at(j)] * field[down, at(j)]
                finish(i, z, j, d, inv[z, at(j)] * moved)
                return b, d_after

            if chunk_from == 0:
                b_prior = jnp.zeros(wide, F32)
            else:
                b_prior = fn[z, at(chunk_from - 1)] * field[z, at(chunk_from - 1)]
            unit = SWEEP_UNIT if chunk_from == 0 else LAST_UNIT
            row_chunks(chunk_from, chunk_to, unit, chunk, (b_prior, field[z, at(chunk_from)]))
            return carry

        lax.fori_loop(0, depth + margin, layer, 0)

    (a1, b1), (a2, b2) = steps_of()

    def first_sweep(i, z, j, d, pulled):
        s1[z, at(j)] = pulled
        d1[z, at(j)] = a1 * d + b1 * pulled

    def end_forward(i, z, j, d, pulled):
        s2 = s1[z, at(j)] - d + pulled
        d2 = a2 * d + b2 * s2
        new = hx[z, at(j)] + d0[z, at(j)] + d + d2
        hx[z, at(j)] = new
        load = new - tx[z, at(j)] - lw[z, at(j)]
        src[z, at(j)] = inv[z, at(j)] * load

    sweep(d0, 3, first_sweep, 0, chunks_of_rows)
    sweep(d1, 2, end_forward, 0, chunks_of_rows)
    sweep(src, 1, first_sweep, 0, chunks_of_rows)

    st[0, at(0)] = jnp.zeros(wide, F32)

    def end_adjoint(i, z, j, d, pulled):
        s2 = s1[z, at(j)] - d + pulled
        d2 = a2 * d + b2 * s2
        adj = src[z, at(j)] + d + d2
        adjoint[i, at(j - 1)] = adj[:, :cols]
        new = hx[z, at(j), inside_cols]
        head_new[i, at(j - 1)] = new
        departure = new - tx[z, at(j), inside_cols]
        st[0, at(0), inside_cols] = st[0, at(0), inside_cols] + departure * departure

    sweep(d1, 0, end_adjoint, 1, chunks_of_rows - 1)

    squared = st[0, at(0), inside_cols]
    squared = jnp.sum(squared, axis=0, keepdims=True)
    squared = sum(squared[:, LANES * k:LANES * (k + 1)] for k in range(cols // LANES))
    squared = squared * (1.0 / (float(layers * rows * cols) * n_east * n_north))
    base_layer = jnp.where(me_l == 0, 1.0, 0.0)

    col_hot, row_hot = col_hot[:cols], row_hot[8:8 + rows]
    head_at = jnp.zeros((1, SLOTS), F32)
    adj_at = jnp.zeros((1, SLOTS), F32)
    for i in range(depth):
        z_share = jnp.where(me_l == 0, share[i:i + 1], share[depth + i:depth + i + 1])
        stack = split(head_new[i], 2) + split(adjoint[i], 2)
        found = [dot(piece, col_hot, NN) for piece in stack]
        head_at += z_share * jnp.sum((found[0] + found[1]) * row_hot, axis=0, keepdims=True)
        adj_at += z_share * jnp.sum((found[2] + found[3]) * row_hot, axis=0, keepdims=True)
    lift = (comp[6:7] * base_layer - head_at) * comp[7:8]
    priced = comp[5:6] * lift
    slope = priced - adj_at * comp[7:8]
    three = jnp.concatenate(
        [p.astype(F32) for p in split(slope, 3)] + [jnp.zeros((5, SLOTS), F32)], axis=0
    ).astype(BF16)
    spread = dot(three, pt[...], NN)
    spread = spread[0:1] + spread[1:2] + spread[2:3]
    tile = jnp.concatenate(
        [spread[:, LANES * k:LANES * (k + 1)] for k in range(groups)], axis=0
    )
    parts[pl.ds(0, groups)] = tile
    parts[pl.ds(groups, 8)] = jnp.concatenate(
        [
            priced * comp[4:5],
            squared,
            jnp.broadcast_to(crowded, (1, LANES)),
            jnp.zeros((5, LANES), F32),
        ],
        axis=0,
    )

    total = parts[...]
    used = 0
    for box, mine, peers in phases:
        box[mine] = total
        copies = []
        for device in peers:
            copy = pltpu.make_async_remote_copy(
                src_ref=box.at[mine],
                dst_ref=box.at[mine],
                send_sem=sum_send.at[used],
                recv_sem=sum_recv.at[used],
                device_id=device,
                device_id_type=MESH,
            )
            copy.start()
            copies.append(copy)
            used += 1
        for copy in copies:
            copy.wait()
        total = box[0]
        for k in range(1, len(peers) + 1):
            total = total + box[k]
    n_wells = out_slope.shape[1]
    for k in range(groups):
        width = min(LANES, n_wells - LANES * k)
        out_slope[:, pl.ds(LANES * k, width)] = total[k:k + 1, :width]
    sums = jnp.sum(total[groups:], axis=1, keepdims=True)
    out_cost[...] = sums[0:1]
    out_misfit[...] = sums[1:2]
    out_crowded[...] = sums[2:3]


def run_kernel(sizes, fields, wells):
    depth, rows, cols = fields[0].shape
    layers, ext_rows, ext_cols = 2 * depth, rows + 16, cols + LANES
    n_wells = wells[0].shape[1]
    groups = -(-n_wells // LANES)
    n_east, n_x, n_z = sizes
    block = pltpu.VMEM((depth, rows, cols), F32)
    one = pltpu.VMEM((1, 1), F32)
    ext = pltpu.VMEM((layers, ext_rows, ext_cols), F32)
    operands = (*fields, *wells)
    copies = 4 + 4 + 8 + 6 + 7
    peers = 1 + n_z + n_east + n_x - 3
    return pl.pallas_call(
        functools.partial(kernel, sizes),
        out_shape=[
            block, block, pltpu.VMEM((1, n_wells), F32), one, one,
            jax.ShapeDtypeStruct((1, 1), F32),
        ],
        in_specs=[pl.BlockSpec(memory_space=pltpu.HBM)] * len(operands),
        out_specs=[pl.BlockSpec(memory_space=pltpu.VMEM)] * 6,
        scratch_shapes=[ext] * 8
        + [pltpu.VMEM((layers + 1, ext_rows, ext_cols), F32)]
        + [ext] * 6
        + [pltpu.VMEM((SLOTS, groups * LANES), BF16)]
        + [pltpu.VMEM((groups + 8, LANES), F32)]
        + [pltpu.VMEM((layers, rows, cols), BF16)] * 4
        + [
            pltpu.VMEM((2, 2, depth, 16, cols), BF16),
            pltpu.VMEM((2, 2, depth, 8, LANES), F32),
            pltpu.VMEM((2, 2, depth, 32, LANES), BF16),
            pltpu.VMEM((2, 4, 8, LANES), F32),
            pltpu.VMEM((2, 4, 16, LANES), BF16),
            pltpu.VMEM((2, depth, 8, cols), F32),
            pltpu.VMEM((2, depth, 16, cols), BF16),
            pltpu.VMEM((2, depth, 8, LANES), F32),
            pltpu.VMEM((2, depth, 32, LANES), BF16),
            pltpu.VMEM((4, 8, LANES), F32),
            pltpu.VMEM((4, 16, LANES), BF16),
        ]
        + [pltpu.VMEM(w.shape, w.dtype) for w in wells]
        + [pltpu.VMEM((8, groups * LANES), F32)]
        + [pltpu.VMEM((n, groups + 8, LANES), F32) for n in (2, n_z, n_east, n_x)]
        + [pltpu.SemaphoreType.DMA((14,))]
        + [pltpu.SemaphoreType.DMA((copies,))] * 2
        + [pltpu.SemaphoreType.DMA((peers,))] * 2,
        compiler_params=pltpu.CompilerParams(
            collective_id=0, has_side_effects=True, vmem_limit_bytes=60 * 1024 * 1024
        ),
        name="whole_step",
    )(*operands)


def hand_over(*refs):
    count = len(refs) // 2
    copies = [
        pltpu.make_async_copy(refs[k], refs[count + k], refs[-1].at[k]) for k in range(count)
    ]
    for copy in copies:
        copy.start()
    for copy in copies:
        copy.wait()


def run_hand_over(values):
    return pl.pallas_call(
        hand_over,
        out_shape=[jax.ShapeDtypeStruct(v.shape, v.dtype) for v in values],
        in_specs=[pl.BlockSpec(memory_space=pltpu.VMEM)] * len(values),
        out_specs=[pl.BlockSpec(memory_space=pltpu.HBM)] * len(values),
        scratch_shapes=[pltpu.SemaphoreType.DMA((len(values),))],
        compiler_params=pltpu.CompilerParams(vmem_limit_bytes=60 * 1024 * 1024),
        name="hand_over",
    )(*values)


def in_order(value):
    return with_layout_constraint(value, Layout(major_to_minor=(0, 1, 2)))


def per_device(sizes, *arguments):
    fields = arguments[:6]
    e, n, top, bottom, tariff, rates, ground, prices = arguments[6:]
    wells = [w.reshape(1, -1) for w in (e, n, top, bottom, rates, tariff, ground, prices)]
    new, adjoint, slope, cost, misfit, crowded = run_kernel(sizes, fields, wells)
    found = tuple(run_hand_over((new, adjoint, slope, cost, misfit)))

    def again(state):
        blocks = [in_order(x) for x in fields]
        first, second, *others = plain(*blocks, *arguments[6:])
        others = [x.reshape(1, -1) for x in others]
        return jnp.zeros((), F32), (in_order(first), in_order(second), *others)

    _, found = lax.while_loop(lambda state: state[0] > 0, again, (crowded.reshape(()), found))
    new, adjoint, slope, cost, misfit = found
    return new, adjoint, slope.reshape(-1), cost.reshape(()), misfit.reshape(())


def solution(mesh):
    field = P("layer", "north", "east")
    n_north = mesh.shape["north"]
    n_x = 4 if n_north % 4 == 0 else 1
    sizes = (mesh.shape["east"], n_x, n_north // n_x)
    return jax.shard_map(
        functools.partial(per_device, sizes),
        mesh=mesh,
        in_specs=(field,) * 6 + (P(),) * 8,
        out_specs=(field, field, P(), P(), P()),
        check_vma=False,
    )
```

```python
import functools

import jax
import jax.numpy as jnp
from jax import lax
from jax.experimental import pallas as pl
from jax.experimental.layout import Layout, with_layout_constraint
from jax.experimental.pallas import tpu as pltpu
from jax.sharding import PartitionSpec as P

MESH = pl.DeviceIdType.MESH
F32 = jnp.float32
BF16 = jnp.bfloat16

SWEEPS = 3
CENTRE = 1.0
HALF_WIDTH = 0.95

HALO = 8
REACH = 5
LANES = 128
SLOTS = 128
START_UNIT = 9
SWEEP_LAYERS = 4


def steps_of():
    sigma = CENTRE / HALF_WIDTH
    factor = 1.0 / sigma
    found = []
    for _ in range(SWEEPS - 1):
        after = 1.0 / (2.0 * sigma - factor)
        found.append((after * factor, 2.0 * after / HALF_WIDTH))
        factor = after
    return found


def iota(shape, dim):
    return lax.broadcasted_iota(jnp.int32, shape, dim)


def roll(value, shift, dim):
    shift = shift % value.shape[dim]
    return pltpu.roll(value, shift, dim) if shift else value


def extended(value, sides, width):
    for axis, dim in sides:
        size, length = (lax.axis_size(axis), value.shape[dim])
        up = [(i, (i + 1) % size) for i in range(size - 1)]
        down = [(j, i) for i, j in up]
        last = lax.slice_in_dim(value, length - width, length, axis=dim)
        initial = lax.slice_in_dim(value, 0, width, axis=dim)
        before = lax.ppermute(last, axis, up)
        after = lax.ppermute(initial, axis, down)
        value = jnp.concatenate([before, value, after], axis=dim)
    return value


def harmonic(first, second):
    total = first + second
    return 2.0 * first * second / jnp.where(total > 0, total, 1.0)


def face_terms(east_pad, north_pad, up_pad, stored):
    face_east = harmonic(east_pad[:, :, :-1], east_pad[:, :, 1:])
    face_north = harmonic(north_pad[:, :-1], north_pad[:, 1:])
    face_up = harmonic(up_pad[:-1], up_pad[1:])
    diagonal = stored + face_east[:, :, :-1] + face_east[:, :, 1:]
    diagonal = diagonal + face_north[:, :-1] + face_north[:, 1:]
    diagonal = diagonal + face_up[:-1] + face_up[1:]
    positive = diagonal > 0
    inverse = jnp.where(positive, 1.0 / jnp.where(positive, diagonal, 1.0), 0.0)
    return (stored, face_east, face_north, face_up, inverse)


def coefficients(padded_coefs):
    stacked = padded_coefs.astype(jnp.float32)
    east_pad = stacked[0][1:-1, 1:-1, :]
    north_pad = stacked[1][1:-1, :, 1:-1]
    up_pad = stacked[2][:, 1:-1, 1:-1]
    stored = stacked[3][1:-1, 1:-1, 1:-1]
    return face_terms(east_pad, north_pad, up_pad, stored)


def apply_operator(padded, storage_part, face_east, face_north, face_up):
    center = padded[1:-1, 1:-1, 1:-1]
    step_east = padded[1:-1, 1:-1, 1:] - padded[1:-1, 1:-1, :-1]
    step_north = padded[1:-1, 1:, 1:-1] - padded[1:-1, :-1, 1:-1]
    step_up = padded[1:, 1:-1, 1:-1] - padded[:-1, 1:-1, 1:-1]
    flux_east = face_east * step_east
    flux_north = face_north * step_north
    flux_up = face_up * step_up
    total = storage_part * center + (flux_east[:, :, :-1] - flux_east[:, :, 1:])
    total = total + (flux_north[:, :-1] - flux_north[:, 1:])
    return total + (flux_up[:-1] - flux_up[1:])


def keep_whole(field):
    return field


def chebyshev(start, rhs, operate, trim, precondition):
    if start is None:
        residual = rhs
    else:
        residual = trim(rhs) - operate(start)
    direction = precondition(residual) / CENTRE
    if start is None:
        iterate = direction
    else:
        iterate = trim(start) + direction
    sigma = CENTRE / HALF_WIDTH
    factor = 1.0 / sigma
    for sweep_index in range(SWEEPS - 1):
        residual = trim(residual) - operate(direction)
        factor_next = 1.0 / (2.0 * sigma - factor)
        direction = factor_next * factor * trim(
            direction
        ) + 2.0 * factor_next / HALF_WIDTH * precondition(residual)
        iterate = trim(iterate) + direction
        factor = factor_next
    return iterate


def plain(
    head_old,
    head_target,
    conductivity_east,
    conductivity_north,
    conductivity_vertical,
    storage,
    well_east,
    well_north,
    screen_top,
    screen_bottom,
    tariff_band,
    pump_rates,
    ground_level,
    band_prices,
):
    depth_cells, north_cells, east_cells = head_old.shape
    stacked_coefs = jnp.stack(
        (conductivity_east, conductivity_north, conductivity_vertical, storage)
    )
    padded_coefs = extended(stacked_coefs, (("east", 3), ("north", 2), ("layer", 1)), 1)
    margin = 0
    top_level = coefficients(padded_coefs)
    levels = [None] * (margin + 1)
    levels[margin] = top_level

    def margin_of(field):
        return (field.shape[0] - depth_cells) // 2

    def precondition(residual):
        return levels[margin_of(residual)][4] * residual

    def operate(field):
        padded = extended(field, (("east", 2), ("north", 1), ("layer", 0)), 1)
        level = levels[0]
        return apply_operator(padded, level[0], level[1], level[2], level[3])

    east_start = lax.axis_index("east") * east_cells
    north_start = lax.axis_index("north") * north_cells
    layer_start = lax.axis_index("layer") * depth_cells
    local_east = well_east - east_start
    local_north = well_north - north_start
    owning = (
        (local_east >= 0)
        & (local_east < east_cells)
        & (local_north >= 0)
        & (local_north < north_cells)
    ).astype(jnp.float32)
    cells = jnp.clip(local_north, 0, north_cells - 1) * east_cells + jnp.clip(
        local_east, 0, east_cells - 1
    )
    depth = layer_start + jnp.arange(depth_cells, dtype=jnp.int32)[:, None]
    screened = ((depth >= screen_top[None, :]) & (depth <= screen_bottom[None, :])).astype(
        jnp.float32
    ) * owning[None, :]
    weights = (
        conductivity_east.reshape(depth_cells, north_cells * east_cells)[:, cells].astype(
            jnp.float32
        )
        * screened
    )
    totals = lax.psum(jnp.sum(weights, axis=0), "layer")
    shares = weights / (totals + (1.0 - owning))[None, :]
    flat_shape = (depth_cells, north_cells * east_cells)
    source = (
        jnp.zeros(flat_shape, jnp.float32)
        .at[:, cells]
        .add(pump_rates[None, :] * shares)
        .reshape(head_old.shape)
    )
    stored = storage.astype(jnp.float32)
    rhs = stored * head_old - source
    head_new = chebyshev(head_old, rhs, operate, keep_whole, precondition)
    departure = head_new - head_target
    misfit_part = jnp.sum(departure * departure)
    all_cells = float(
        depth_cells
        * north_cells
        * east_cells
        * lax.axis_size("east")
        * lax.axis_size("north")
        * lax.axis_size("layer")
    )
    head_part = jnp.sum(shares * head_new.reshape(flat_shape)[:, cells], axis=0)
    head_screen, misfit_total = lax.psum((head_part, misfit_part), ("east", "north", "layer"))
    band_ids = jnp.arange(band_prices.shape[0], dtype=jnp.int32)
    prices = jnp.sum(
        jnp.where(tariff_band[:, None] == band_ids[None, :], band_prices[None, :], 0.0), axis=1
    )
    load = (
        departure.reshape(flat_shape)
        .at[:, cells]
        .add(-(prices * pump_rates)[None, :] * shares)
        .reshape(head_old.shape)
    )
    adjoint_head = chebyshev(None, load, operate, keep_whole, precondition)
    adjoint_part = jnp.sum(shares * adjoint_head.reshape(flat_shape)[:, cells], axis=0)
    adjoint_screen = lax.psum(adjoint_part, ("east", "north", "layer"))
    misfit = misfit_total / all_cells
    lift = ground_level - head_screen
    rate_gradient = prices * lift - adjoint_screen
    pumping_cost = jnp.sum(prices * pump_rates * lift)
    return (head_new, adjoint_head, rate_gradient, pumping_cost, misfit)


def split(value, parts):
    found = []
    for _ in range(parts):
        top = value.astype(BF16)
        found.append(top)
        value = value - top.astype(F32)
    return found


def dot(a, b, dims):
    return lax.dot_general(a, b, (dims, ((), ())), preferred_element_type=F32)


NN = ((1,), (0,))
NT = ((1,), (1,))


def reciprocal(x):
    first = pl.reciprocal(x, approx=True)
    return first * (2.0 - x * first)


def kernel(sizes, *refs):
    n_east, n_x, n_z = sizes
    n_north = n_x * n_z
    fields, well_refs, refs = refs[:6], refs[6:14], refs[14:]
    head_new, adjoint, out_slope, out_cost, out_misfit, out_crowded = refs[:6]
    hx, tx, ke, kn, kv, st, fe, fn, fu, inv, src, lw, d0, d1, s1, pt = refs[6:22]
    parts, staged, (nbs, efs, ebs, cfs, cbs), refs = refs[22], refs[23:27], refs[27:32], refs[32:]
    (s_nf, s_nb, s_ef, s_eb, s_cf, s_cb), refs = refs[:6], refs[6:]
    well_rows, wells, boxes, refs = refs[:8], refs[8], refs[9:13], refs[13:]
    load_sem, send_sem, recv_sem, sum_send, sum_recv = refs
    depth, rows, cols = head_new.shape
    layers, ext_rows, ext_cols = hx.shape
    chunks_of_rows = ext_rows // 8
    groups = wells.shape[1] // LANES
    me_e, me_n, me_l = lax.axis_index("east"), lax.axis_index("north"), lax.axis_index("layer")
    me_x, me_z = me_n // n_z, lax.rem(me_n, n_z)
    own, other = depth * me_l, depth * (1 - me_l)
    own_layers = pl.ds(own, depth)

    def east_of(side):
        return lax.rem(me_e + (n_east - 1 if side == 0 else 1), n_east)

    def north_of(side):
        return lax.rem(me_n + (n_north - 1 if side == 0 else 1), n_north)

    partner = (me_e, me_n, 1 - me_l)
    to_north = [(me_e, north_of(s), me_l) for s in (0, 1)]
    to_east = [(east_of(s), me_n, me_l) for s in (0, 1)]
    to_corner = [(east_of(c), north_of(r), me_l) for r in (0, 1) for c in (0, 1)]
    phases = []
    for box, size, mine, device in (
        (boxes[0], 2, me_l, lambda i: (me_e, me_n, i)),
        (boxes[1], n_z, me_z, lambda i: (me_e, me_x * n_z + i, me_l)),
        (boxes[2], n_east, me_e, lambda i: (i, me_n, me_l)),
        (boxes[3], n_x, me_x, lambda i: (me_e, i * n_z + me_z, me_l)),
    ):
        phases.append((box, mine, [device(lax.rem(mine + k, size)) for k in range(1, size)]))

    greeted = [partner] + to_north + to_east + to_corner
    for _, _, peers in phases:
        greeted = greeted + peers
    barrier = pltpu.get_barrier_semaphore()
    for device in greeted:
        pl.semaphore_signal(barrier, inc=1, device_id=device, device_id_type=MESH)

    loaded = [0]

    def load(src_ref, dst_ref):
        copy = pltpu.make_async_copy(src_ref, dst_ref, load_sem.at[loaded[0]])
        loaded[0] += 1
        copy.start()
        return copy

    lane = iota((8, LANES), 1)
    group = lane // HALO
    wide_sub = iota((8, cols), 0)
    last = cols - LANES
    low_half = lane < LANES // 2
    extra = pl.ds(cols, LANES)
    inside_cols = pl.ds(0, cols)
    inner = pl.ds(8, rows)
    edge_rows = (pl.ds(rows + 8, 8), pl.ds(0, 8))

    block_loads = [
        load(fields[0], hx.at[own_layers, inner, inside_cols]),
        load(fields[1], tx.at[own_layers, inner, inside_cols]),
    ] + [load(fields[2 + a], staged[a].at[own_layers]) for a in range(4)]
    well_loads = [load(a, b) for a, b in zip(well_refs, well_rows)]
    for copy in block_loads:
        copy.wait()

    def pack(z, carry):
        for side in (0, 1):
            c0 = last * side
            kept = jnp.zeros((8, LANES), F32)
            fields = [jnp.zeros((8, LANES), F32) for _ in staged]
            for pair in range(rows // 16):
                tiles = [
                    ref[own + z, pl.ds(16 * pair, 16), pl.ds(c0, LANES)].astype(F32) for ref in staged
                ]
                for half in (0, 1):
                    j = 2 * pair + half
                    shift = HALO * j - (LANES - HALO) * side
                    h = hx[own + z, pl.ds(8 + 8 * j, 8), pl.ds(c0, LANES)]
                    t = tx[own + z, pl.ds(8 + 8 * j, 8), pl.ds(c0, LANES)]
                    if side == 0:
                        both = jnp.where(lane >= HALO - 2, roll(t, HALO - 2, 1), h)
                    else:
                        both = jnp.where(lane < LANES - HALO + 2, roll(t, 2 - HALO, 1), h)
                    here = group == j
                    kept = jnp.where(here, roll(both, shift, 1), kept)
                    for a in range(4):
                        piece = tiles[a][8 * half:8 * half + 8]
                        fields[a] = jnp.where(here, roll(piece, shift, 1), fields[a])
            s_ef[side, z] = kept
            s_eb[side, z, pl.ds(0, 16)] = jnp.concatenate(fields[:2], axis=0).astype(BF16)
            s_eb[side, z, pl.ds(16, 16)] = jnp.concatenate(fields[2:], axis=0).astype(BF16)
            r0 = (rows - 8) * side
            h = hx[own + z, pl.ds(8 + r0, 8), inside_cols]
            t = tx[own + z, pl.ds(8 + r0, 8), inside_cols]
            edge = [
                ref[own + z, pl.ds((rows - 16) * side, 16), :].astype(F32)[8 * side:8 * side + 8]
                for ref in staged
            ]
            if side == 0:
                both = jnp.where(wide_sub == 5, roll(edge[1], 1, 0), h)
                both = jnp.where(wide_sub >= 6, roll(t, 6, 0), both)
                first = jnp.where(wide_sub < 4, edge[0], roll(edge[1], 4, 0))
                second = jnp.where(wide_sub < 4, edge[2], roll(edge[3], 4, 0))
            else:
                both = jnp.where(wide_sub == 2, roll(edge[1], 7, 0), h)
                both = jnp.where(wide_sub < 2, roll(t, 2, 0), both)
                first = jnp.where(wide_sub < 4, roll(edge[0], 4, 0), edge[1])
                second = jnp.where(wide_sub < 4, roll(edge[2], 4, 0), edge[3])
            s_nf[side, z] = both
            s_nb[side, z] = jnp.concatenate([first, second], axis=0).astype(BF16)
        return carry

    lax.fori_loop(0, depth, pack, 0)

    for r in (0, 1):
        for c in (0, 1):
            c0 = last * c
            kept = jnp.zeros((8, LANES), F32)
            mixed = jnp.zeros((8, LANES), F32)
            for z in range(depth):
                both = s_nf[r, z, :, pl.ds(c0, LANES)]
                kept = jnp.where(group == z, roll(both, HALO * z - (LANES - HALO) * c, 1), kept)
                pieces = s_nb[r, z, :, pl.ds(c0, LANES)].astype(F32)
                for half in (0, 1):
                    slot = half * depth + z
                    moved = roll(
                        pieces[8 * half:8 * half + 8], HALO * slot - (LANES - HALO) * c, 1
                    )
                    mixed = jnp.where(group == slot, moved, mixed)
            s_cf[2 * r + c] = kept
            s_cb[2 * r + c] = jnp.concatenate([mixed, mixed], axis=0).astype(BF16)

    pl.semaphore_wait(barrier, len(greeted))

    sent = [0]

    def send(src_ref, dst_ref, device):
        copy = pltpu.make_async_remote_copy(
            src_ref=src_ref,
            dst_ref=dst_ref,
            send_sem=send_sem.at[sent[0]],
            recv_sem=recv_sem.at[sent[0]],
            device_id=device,
            device_id_type=MESH,
        )
        sent[0] += 1
        copy.start()
        return copy

    norths, easts, corners = [], [], []
    for side in (0, 1):
        norths.append(send(s_nb.at[side], nbs.at[0, side], to_north[side]))
        norths.append(
            send(s_nf.at[side], hx.at[own_layers, edge_rows[side], inside_cols], to_north[side])
        )
    for side in (0, 1):
        easts.append(send(s_eb.at[side], ebs.at[0, side], to_east[side]))
        easts.append(send(s_ef.at[side], efs.at[0, side], to_east[side]))
    for d in range(4):
        corners.append(send(s_cb.at[d], cbs.at[0, d], to_corner[d]))
        corners.append(send(s_cf.at[d], cfs.at[0, d], to_corner[d]))
    two = (depth - 2) * (1 - me_l)
    blocks = [send(fields[2 + a], staged[a].at[own_layers], partner) for a in range(4)]
    blocks.append(send(fields[0], hx.at[own_layers, inner, inside_cols], partner))
    blocks.append(
        send(
            fields[1].at[pl.ds(two, 2)], tx.at[pl.ds(own + two, 2), inner, inside_cols], partner
        )
    )

    for copy in well_loads:
        copy.wait()
    wells[...] = jnp.full(wells.shape, -1e6, F32)
    width = pl.ds(0, well_rows[0].shape[1])
    for row, ref in enumerate(well_rows[:5]):
        wells[pl.ds(row, 1), width] = ref[...].astype(F32)
    band = well_rows[5][...]
    bands = well_rows[7][...]
    price = jnp.zeros(band.shape, F32)
    for b in range(bands.shape[1]):
        price = jnp.where(band == b, bands[0:1, b:b + 1], price)
    wells[pl.ds(5, 1), width] = price
    wells[pl.ds(6, 1), width] = well_rows[6][...]

    at_east = wells[0:1, :] - (me_e * cols).astype(F32)
    at_north = wells[1:2, :] - (me_n * rows).astype(F32)
    near = (
        (at_east >= -REACH) & (at_east < cols + REACH)
        & (at_north >= -REACH) & (at_north < rows + REACH)
    )
    mine = (at_east >= 0) & (at_east < cols) & (at_north >= 0) & (at_north < rows)
    near_row = jnp.where(near, 1.0, 0.0)
    near_tile = jnp.concatenate(
        [near_row[:, LANES * k:LANES * (k + 1)] for k in range(groups)], axis=0
    )
    before = (iota((LANES, LANES), 0) < iota((LANES, LANES), 1)).astype(F32).astype(BF16)
    in_row = dot(near_tile.astype(BF16), before, NN)
    above = (iota((groups, groups), 1) < iota((groups, groups), 0)).astype(F32).astype(BF16)
    rows_above = jnp.sum(dot(above, near_tile.astype(BF16), NN), axis=1, keepdims=True)
    rank = jnp.where(near_tile > 0, in_row + rows_above, -1.0)
    found = jnp.sum(jnp.sum(near_tile, axis=1, keepdims=True), axis=0, keepdims=True)
    crowded = jnp.where(found > SLOTS, 1.0, 0.0)

    place = jnp.concatenate(
        [
            jnp.where(at_east < 0, at_east + ext_cols, at_east),
            at_north + 8.0,
            wells[2:7, :],
            jnp.where(mine, 1.0, 0.0),
        ],
        axis=0,
    )
    place_parts = jnp.concatenate([p.astype(F32) for p in split(place, 3)], axis=0).astype(BF16)
    slot_of = iota((SLOTS, LANES), 0).astype(F32)

    for k in range(groups):
        pt[:, pl.ds(LANES * k, LANES)] = jnp.where(slot_of == rank[k:k + 1, :], 1.0, 0.0).astype(BF16)
    three = dot(place_parts, pt[...], NT)
    comp = three[0:8] + three[8:16] + three[16:24]
    col_hot = jnp.where(iota((ext_cols, SLOTS), 0).astype(F32) == comp[0:1], 1.0, 0.0)
    row_hot = jnp.where(iota((ext_rows, SLOTS), 0).astype(F32) == comp[1:2], 1.0, 0.0)
    col_hot = col_hot.astype(BF16)


    def fill_inner(base):
        def fill(z, carry):
            for dst, ref in zip((ke, kn, kv, st), staged):
                dst[base + z, inner, inside_cols] = ref[base + z].astype(F32)
            return carry

        lax.fori_loop(0, depth, fill, 0)

    def fill_east(who, base):
        def fill(z, carry):
            zz = base + z
            right, left = efs[who, 0, z], efs[who, 1, z]
            for j in range(rows // 8):
                both = jnp.where(
                    low_half, roll(right, -HALO * j, 1), roll(left, LANES - HALO - HALO * j, 1)
                )
                hx[zz, pl.ds(8 + 8 * j, 8), extra] = both
                tx[zz, pl.ds(8 + 8 * j, 8), extra] = jnp.where(
                    low_half, roll(both, 2 - HALO, 1), roll(both, HALO - 2, 1)
                )
            for half, pair in ((0, (ke, kn)), (1, (kv, st))):
                rights = ebs[who, 0, z, pl.ds(16 * half, 16)].astype(F32)
                lefts = ebs[who, 1, z, pl.ds(16 * half, 16)].astype(F32)
                for k in (0, 1):
                    right, left = rights[8 * k:8 * k + 8], lefts[8 * k:8 * k + 8]
                    for j in range(rows // 8):
                        pair[k][zz, pl.ds(8 + 8 * j, 8), extra] = jnp.where(
                            low_half,
                            roll(right, -HALO * j, 1),
                            roll(left, LANES - HALO - HALO * j, 1),
                        )
            return carry

        lax.fori_loop(0, depth, fill, 0)

    def put_rows(side, zz, at_rows, at_cols, both, first, second):
        row = iota(both.shape, 0)
        if side == 0:
            tx[zz, at_rows, at_cols] = roll(both, 2, 0)
            ke[zz, at_rows, at_cols] = first
            kn[zz, at_rows, at_cols] = jnp.where(row == 4, roll(both, 7, 0), roll(first, 4, 0))
            kv[zz, at_rows, at_cols] = second
            st[zz, at_rows, at_cols] = roll(second, 4, 0)
        else:
            tx[zz, at_rows, at_cols] = roll(both, 6, 0)
            ke[zz, at_rows, at_cols] = roll(first, 4, 0)
            kn[zz, at_rows, at_cols] = jnp.where(row == 3, roll(both, 1, 0), first)
            kv[zz, at_rows, at_cols] = roll(second, 4, 0)
            st[zz, at_rows, at_cols] = second

    def fill_north(who, base):
        def fill(z, carry):
            for side, at_rows in enumerate(edge_rows):
                pieces = nbs[who, side, z].astype(F32)
                both = hx[base + z, at_rows, inside_cols]
                put_rows(side, base + z, at_rows, inside_cols, both, pieces[:8], pieces[8:])
            return carry

        lax.fori_loop(0, depth, fill, 0)

    def fill_corners(who, base):
        for side, at_rows in enumerate(edge_rows):
            right, left = cfs[who, 2 * side], cfs[who, 2 * side + 1]
            rights = cbs[who, 2 * side].astype(F32)[:8]
            lefts = cbs[who, 2 * side + 1].astype(F32)[:8]

            def taken(a, b, slot):
                return jnp.where(
                    low_half, roll(a, -HALO * slot, 1), roll(b, LANES - HALO - HALO * slot, 1)
                )

            for z in range(depth):
                both = taken(right, left, z)
                hx[base + z, at_rows, extra] = both
                put_rows(
                    side, base + z, at_rows, extra, both,
                    taken(rights, lefts, z), taken(rights, lefts, depth + z),
                )

    wide = (8, ext_cols)
    sub = iota(wide, 0)
    col = iota(wide, 1)
    closed_col = ((col == cols - 1) & (me_e == n_east - 1)) | ((col == ext_cols - 1) & (me_e == 0))
    open_east = jnp.where(closed_col, 0.0, 2.0)
    open_low = jnp.where((sub == 7) & (me_n == 0), 0.0, 2.0)
    open_high = jnp.where((sub == 7) & (me_n == n_north - 1), 0.0, 2.0)

    def east(v):
        return roll(v, ext_cols - 1, 1)

    def west(v):
        return roll(v, 1, 1)

    def north(now, after):
        return jnp.where(sub < 7, roll(now, 7, 0), roll(after, 7, 0))

    def south(now, prior):
        return jnp.where(sub > 0, roll(now, 1, 0), roll(prior, 1, 0))

    fu[0] = jnp.zeros((ext_rows, ext_cols), F32)
    fu[layers] = jnp.zeros((ext_rows, ext_cols), F32)

    def row_chunks(begin, end, unit, body, carry):
        if end - begin == unit:
            for j in range(begin, end):
                carry = body(j, carry)
            return carry

        def several(k, carry):
            for i in range(unit):
                carry = body(begin + k * unit + i, carry)
            return carry

        return lax.fori_loop(0, (end - begin) // unit, several, carry)

    def at(j):
        return pl.ds(8 * j if isinstance(j, int) else pl.multiple_of(8 * j, 8), 8)

    def next_of(j):
        return min(j + 1, chunks_of_rows - 1) if isinstance(j, int) else jnp.minimum(j + 1, chunks_of_rows - 1)

    def layer_of(k):
        return jnp.where(me_l == 0, k, layers - 1 - k)

    def start(k, carry, with_wells):
        z = layer_of(k)
        up = layer_of(jnp.minimum(k + 1, layers - 1))
        down = layer_of(jnp.maximum(k - 1, 0))
        open_up = jnp.where(k < layers - 1, 2.0, 0.0)

        def chunk(j, carry):
            fn_prior, gn_prior, k_n, h = carry
            k_e, k_u, k_u2 = ke[z, at(j)], kv[z, at(j)], kv[up, at(j)]
            k_e2 = east(k_e)
            k_after, h_after = kn[z, at(next_of(j))], hx[z, at(next_of(j))]
            k_n2 = north(k_n, k_after)
            f_e = open_east * k_e * k_e2 * reciprocal(k_e + k_e2)
            if isinstance(j, int):
                opened = open_low if j == 0 else open_high if j == chunks_of_rows - 2 else 2.0
            else:
                edge = ((j == 0) & (me_n == 0)) | ((j == chunks_of_rows - 2) & (me_n == n_north - 1))
                opened = jnp.where((sub == 7) & edge, 0.0, 2.0)
            f_n = opened * k_n * k_n2 * reciprocal(k_n + k_n2)
            f_u = open_up * k_u * k_u2 * reciprocal(k_u + k_u2)
            f_d = fu[z + me_l, at(j)]
            fe[z, at(j)] = f_e
            fn[z, at(j)] = f_n
            fu[z + 1 - me_l, at(j)] = f_u
            diagonal = st[z, at(j)] + f_e + west(f_e) + f_n + south(f_n, fn_prior) + f_u + f_d
            inverse = reciprocal(diagonal)
            inv[z, at(j)] = inverse
            g_e = f_e * (east(h) - h)
            g_n = f_n * (north(h, h_after) - h)
            g_u = f_u * (hx[up, at(j)] - h)
            g_d = f_d * (h - hx[down, at(j)])
            residual = (g_e - west(g_e)) + (g_n - south(g_n, gn_prior)) + (g_u - g_d)
            if with_wells:
                residual = residual - src[z, at(j)]
            d0[z, at(j)] = inverse * residual
            return f_n, g_n, k_after, h_after

        none = jnp.zeros(wide, F32)
        row_chunks(0, chunks_of_rows, START_UNIT, chunk, (none, none, kn[z, at(0)], hx[z, at(0)]))
        return carry

    def pump(k, carry):
        z = layer_of(k)
        d0[z] = d0[z] - inv[z] * src[z]
        return carry

    fill_inner(own)
    for copy in easts:
        copy.wait_recv()
    forwards = [send(efs.at[0], efs.at[1], partner), send(ebs.at[0], ebs.at[1], partner)]
    fill_east(0, own)
    for copy in norths:
        copy.wait_recv()
    forwards.append(send(nbs.at[0], nbs.at[1], partner))
    for side in (0, 1):
        place_of = hx.at[own_layers, edge_rows[side], inside_cols]
        forwards.append(send(place_of, place_of, partner))
    for copy in corners:
        copy.wait_recv()
    forwards.append(send(cfs.at[0], cfs.at[1], partner))
    forwards.append(send(cbs.at[0], cbs.at[1], partner))
    fill_north(0, own)
    fill_corners(0, own)
    lax.fori_loop(0, depth - 1, functools.partial(start, with_wells=False), 0)
    for copy in blocks:
        copy.wait_recv()
    fill_inner(other)
    for copy in forwards:
        copy.wait_recv()
    fill_east(1, other)
    fill_north(1, other)
    fill_corners(1, other)
    for copy in norths + easts + corners + blocks + forwards:
        copy.wait_send()

    weights = []
    for z in range(layers):
        found = dot(ke[z].astype(BF16), col_hot, NN)
        k_at = jnp.sum(found * row_hot, axis=0, keepdims=True)
        screened = (comp[2:3] <= z) & (comp[3:4] >= z)
        weights.append(jnp.where(screened, k_at, 0.0))
    weight = jnp.concatenate(weights, axis=0)
    total = jnp.sum(weight, axis=0, keepdims=True)
    share = weight / jnp.where(total > 0, total, 1.0)
    pumped = share * comp[4:5]
    priced = pumped * comp[5:6]
    col_two = jnp.concatenate([col_hot, col_hot], axis=1)
    for z in range(layers):
        left = []
        for value in (pumped, priced):
            top, rest = split(value[z:z + 1], 2)
            left.append(
                jnp.concatenate([row_hot * top.astype(F32), row_hot * rest.astype(F32)], axis=1)
            )
        left = jnp.concatenate(left, axis=0).astype(BF16)
        field = dot(left, col_two, NT)
        src[z] = field[:ext_rows]
        lw[z] = field[ext_rows:]

    lax.fori_loop(0, depth - 1, pump, 0)
    lax.fori_loop(depth - 1, layers, functools.partial(start, with_wells=True), 0)

    def sweep(field, margin, finish, chunk_from, chunk_to):
        first = (depth - margin) * me_l

        def together(i, count):
            zs = [first + i + k for k in range(count)]
            below = jnp.maximum(zs[0] - 1, 0)
            above = jnp.minimum(zs[-1] + 1, layers - 1)
            if chunk_from == 0:
                priors = [jnp.zeros(wide, F32)] * count
            else:
                before = at(chunk_from - 1)
                priors = [fn[z, before] * field[z, before] for z in zs]
            now = [field[z, at(chunk_from)] for z in zs]
            for j in range(chunk_from, chunk_to):
                after = [field[z, at(min(j + 1, chunks_of_rows - 1))] for z in zs]
                stack = [field[below, at(j)]] + now + [field[above, at(j)]]
                for k, z in enumerate(zs):
                    d = now[k]
                    f_e, f_n = fe[z, at(j)], fn[z, at(j)]
                    b = f_n * d
                    moved = f_e * east(d) + west(f_e * d)
                    moved = moved + f_n * north(d, after[k]) + south(b, priors[k])
                    moved = moved + fu[z + 1, at(j)] * stack[k + 2] + fu[z, at(j)] * stack[k]
                    finish(i + k, z, j, d, inv[z, at(j)] * moved)
                    priors[k] = b
                now = after

        def some(i, carry):
            together(SWEEP_LAYERS * i, SWEEP_LAYERS)
            return carry

        total = depth + margin
        lax.fori_loop(0, total // SWEEP_LAYERS, some, 0)
        if total % SWEEP_LAYERS:
            together(total - total % SWEEP_LAYERS, total % SWEEP_LAYERS)

    (a1, b1), (a2, b2) = steps_of()

    def first_sweep(i, z, j, d, pulled):
        s1[z, at(j)] = pulled
        d1[z, at(j)] = a1 * d + b1 * pulled

    def end_forward(i, z, j, d, pulled):
        s2 = s1[z, at(j)] - d + pulled
        d2 = a2 * d + b2 * s2
        new = hx[z, at(j)] + d0[z, at(j)] + d + d2
        hx[z, at(j)] = new
        load = new - tx[z, at(j)] - lw[z, at(j)]
        src[z, at(j)] = inv[z, at(j)] * load

    sweep(d0, 3, first_sweep, 0, chunks_of_rows)
    sweep(d1, 2, end_forward, 0, chunks_of_rows)
    sweep(src, 1, first_sweep, 0, chunks_of_rows)

    st[0, at(0)] = jnp.zeros(wide, F32)

    def end_adjoint(i, z, j, d, pulled):
        s2 = s1[z, at(j)] - d + pulled
        d2 = a2 * d + b2 * s2
        adj = src[z, at(j)] + d + d2
        adjoint[i, at(j - 1)] = adj[:, :cols]
        new = hx[z, at(j), inside_cols]
        head_new[i, at(j - 1)] = new
        departure = new - tx[z, at(j), inside_cols]
        st[0, at(0), inside_cols] = st[0, at(0), inside_cols] + departure * departure

    sweep(d1, 0, end_adjoint, 1, chunks_of_rows - 1)

    squared = st[0, at(0), inside_cols]
    squared = jnp.sum(squared, axis=0, keepdims=True)
    squared = sum(squared[:, LANES * k:LANES * (k + 1)] for k in range(cols // LANES))
    squared = squared * (1.0 / (float(layers * rows * cols) * n_east * n_north))
    base_layer = jnp.where(me_l == 0, 1.0, 0.0)

    col_hot, row_hot = col_hot[:cols], row_hot[8:8 + rows]
    head_at = jnp.zeros((1, SLOTS), F32)
    adj_at = jnp.zeros((1, SLOTS), F32)
    for i in range(depth):
        z_share = jnp.where(me_l == 0, share[i:i + 1], share[depth + i:depth + i + 1])
        stack = split(head_new[i], 2) + split(adjoint[i], 2)
        found = [dot(piece, col_hot, NN) for piece in stack]
        head_at += z_share * jnp.sum((found[0] + found[1]) * row_hot, axis=0, keepdims=True)
        adj_at += z_share * jnp.sum((found[2] + found[3]) * row_hot, axis=0, keepdims=True)
    lift = (comp[6:7] * base_layer - head_at) * comp[7:8]
    priced = comp[5:6] * lift
    slope = priced - adj_at * comp[7:8]
    three = jnp.concatenate(
        [p.astype(F32) for p in split(slope, 3)] + [jnp.zeros((5, SLOTS), F32)], axis=0
    ).astype(BF16)
    spread = dot(three, pt[...], NN)
    spread = spread[0:1] + spread[1:2] + spread[2:3]
    tile = jnp.concatenate(
        [spread[:, LANES * k:LANES * (k + 1)] for k in range(groups)], axis=0
    )
    parts[pl.ds(0, groups)] = tile
    parts[pl.ds(groups, 8)] = jnp.concatenate(
        [
            priced * comp[4:5],
            squared,
            jnp.broadcast_to(crowded, (1, LANES)),
            jnp.zeros((5, LANES), F32),
        ],
        axis=0,
    )

    total = parts[...]
    used = 0
    for box, mine, peers in phases:
        box[mine] = total
        copies = []
        for device in peers:
            copy = pltpu.make_async_remote_copy(
                src_ref=box.at[mine],
                dst_ref=box.at[mine],
                send_sem=sum_send.at[used],
                recv_sem=sum_recv.at[used],
                device_id=device,
                device_id_type=MESH,
            )
            copy.start()
            copies.append(copy)
            used += 1
        for copy in copies:
            copy.wait()
        total = box[0]
        for k in range(1, len(peers) + 1):
            total = total + box[k]
    n_wells = out_slope.shape[1]
    for k in range(groups):
        width = min(LANES, n_wells - LANES * k)
        out_slope[:, pl.ds(LANES * k, width)] = total[k:k + 1, :width]
    sums = jnp.sum(total[groups:], axis=1, keepdims=True)
    out_cost[...] = sums[0:1]
    out_misfit[...] = sums[1:2]
    out_crowded[...] = sums[2:3]


def run_kernel(sizes, fields, wells):
    depth, rows, cols = fields[0].shape
    layers, ext_rows, ext_cols = 2 * depth, rows + 16, cols + LANES
    n_wells = wells[0].shape[1]
    groups = -(-n_wells // LANES)
    n_east, n_x, n_z = sizes
    block = pltpu.VMEM((depth, rows, cols), F32)
    one = pltpu.VMEM((1, 1), F32)
    ext = pltpu.VMEM((layers, ext_rows, ext_cols), F32)
    operands = (*fields, *wells)
    copies = 4 + 4 + 8 + 6 + 7
    peers = 1 + n_z + n_east + n_x - 3
    return pl.pallas_call(
        functools.partial(kernel, sizes),
        out_shape=[
            block, block, pltpu.VMEM((1, n_wells), F32), one, one,
            jax.ShapeDtypeStruct((1, 1), F32),
        ],
        in_specs=[pl.BlockSpec(memory_space=pltpu.HBM)] * len(operands),
        out_specs=[pl.BlockSpec(memory_space=pltpu.VMEM)] * 6,
        scratch_shapes=[ext] * 8
        + [pltpu.VMEM((layers + 1, ext_rows, ext_cols), F32)]
        + [ext] * 6
        + [pltpu.VMEM((SLOTS, groups * LANES), BF16)]
        + [pltpu.VMEM((groups + 8, LANES), F32)]
        + [pltpu.VMEM((layers, rows, cols), BF16)] * 4
        + [
            pltpu.VMEM((2, 2, depth, 16, cols), BF16),
            pltpu.VMEM((2, 2, depth, 8, LANES), F32),
            pltpu.VMEM((2, 2, depth, 32, LANES), BF16),
            pltpu.VMEM((2, 4, 8, LANES), F32),
            pltpu.VMEM((2, 4, 16, LANES), BF16),
            pltpu.VMEM((2, depth, 8, cols), F32),
            pltpu.VMEM((2, depth, 16, cols), BF16),
            pltpu.VMEM((2, depth, 8, LANES), F32),
            pltpu.VMEM((2, depth, 32, LANES), BF16),
            pltpu.VMEM((4, 8, LANES), F32),
            pltpu.VMEM((4, 16, LANES), BF16),
        ]
        + [pltpu.VMEM(w.shape, w.dtype) for w in wells]
        + [pltpu.VMEM((8, groups * LANES), F32)]
        + [pltpu.VMEM((n, groups + 8, LANES), F32) for n in (2, n_z, n_east, n_x)]
        + [pltpu.SemaphoreType.DMA((14,))]
        + [pltpu.SemaphoreType.DMA((copies,))] * 2
        + [pltpu.SemaphoreType.DMA((peers,))] * 2,
        compiler_params=pltpu.CompilerParams(
            collective_id=0, has_side_effects=True, vmem_limit_bytes=60 * 1024 * 1024
        ),
        name="whole_step",
    )(*operands)


def hand_over(*refs):
    count = len(refs) // 2
    copies = [
        pltpu.make_async_copy(refs[k], refs[count + k], refs[-1].at[k]) for k in range(count)
    ]
    for copy in copies:
        copy.start()
    for copy in copies:
        copy.wait()


def run_hand_over(values):
    return pl.pallas_call(
        hand_over,
        out_shape=[jax.ShapeDtypeStruct(v.shape, v.dtype) for v in values],
        in_specs=[pl.BlockSpec(memory_space=pltpu.VMEM)] * len(values),
        out_specs=[pl.BlockSpec(memory_space=pltpu.HBM)] * len(values),
        scratch_shapes=[pltpu.SemaphoreType.DMA((len(values),))],
        compiler_params=pltpu.CompilerParams(vmem_limit_bytes=8 * 1024 * 1024),
        name="hand_over",
    )(*values)


def in_order(value):
    return with_layout_constraint(value, Layout(major_to_minor=(0, 1, 2)))


def per_device(sizes, *arguments):
    fields = arguments[:6]
    e, n, top, bottom, tariff, rates, ground, prices = arguments[6:]
    wells = [w.reshape(1, -1) for w in (e, n, top, bottom, rates, tariff, ground, prices)]
    new, adjoint, slope, cost, misfit, crowded = run_kernel(sizes, fields, wells)
    found = tuple(run_hand_over((new, adjoint, slope, cost, misfit)))

    def again(state):
        blocks = [in_order(x) for x in fields]
        first, second, *others = plain(*blocks, *arguments[6:])
        others = [x.reshape(1, -1) for x in others]
        return jnp.zeros((), F32), (in_order(first), in_order(second), *others)

    _, found = lax.while_loop(lambda state: state[0] > 0, again, (crowded.reshape(()), found))
    new, adjoint, slope, cost, misfit = found
    return new, adjoint, slope.reshape(-1), cost.reshape(()), misfit.reshape(())


def solution(mesh):
    field = P("layer", "north", "east")
    n_north = mesh.shape["north"]
    n_x = 4 if n_north % 4 == 0 else 1
    sizes = (mesh.shape["east"], n_x, n_north // n_x)
    return jax.shard_map(
        functools.partial(per_device, sizes),
        mesh=mesh,
        in_specs=(field,) * 6 + (P(),) * 8,
        out_specs=(field, field, P(), P(), P()),
        check_vma=False,
    )
```

```python
import functools

import jax
import jax.numpy as jnp
from jax import lax
from jax.experimental import pallas as pl
from jax.experimental.layout import Layout, with_layout_constraint
from jax.experimental.pallas import tpu as pltpu
from jax.sharding import PartitionSpec as P

MESH = pl.DeviceIdType.MESH
F32 = jnp.float32
BF16 = jnp.bfloat16

SWEEPS = 3
CENTRE = 1.0
HALF_WIDTH = 0.95

HALO = 8
REACH = 5
LANES = 128
SLOTS = 128
START_UNIT, START_LAYERS = 9, 1
SWEEP_LAYERS = 4


def steps_of():
    sigma = CENTRE / HALF_WIDTH
    factor = 1.0 / sigma
    found = []
    for _ in range(SWEEPS - 1):
        after = 1.0 / (2.0 * sigma - factor)
        found.append((after * factor, 2.0 * after / HALF_WIDTH))
        factor = after
    return found


def iota(shape, dim):
    return lax.broadcasted_iota(jnp.int32, shape, dim)


def roll(value, shift, dim):
    shift = shift % value.shape[dim]
    return pltpu.roll(value, shift, dim) if shift else value


def extended(value, sides, width):
    for axis, dim in sides:
        size, length = (lax.axis_size(axis), value.shape[dim])
        up = [(i, (i + 1) % size) for i in range(size - 1)]
        down = [(j, i) for i, j in up]
        last = lax.slice_in_dim(value, length - width, length, axis=dim)
        initial = lax.slice_in_dim(value, 0, width, axis=dim)
        before = lax.ppermute(last, axis, up)
        after = lax.ppermute(initial, axis, down)
        value = jnp.concatenate([before, value, after], axis=dim)
    return value


def harmonic(first, second):
    total = first + second
    return 2.0 * first * second / jnp.where(total > 0, total, 1.0)


def face_terms(east_pad, north_pad, up_pad, stored):
    face_east = harmonic(east_pad[:, :, :-1], east_pad[:, :, 1:])
    face_north = harmonic(north_pad[:, :-1], north_pad[:, 1:])
    face_up = harmonic(up_pad[:-1], up_pad[1:])
    diagonal = stored + face_east[:, :, :-1] + face_east[:, :, 1:]
    diagonal = diagonal + face_north[:, :-1] + face_north[:, 1:]
    diagonal = diagonal + face_up[:-1] + face_up[1:]
    positive = diagonal > 0
    inverse = jnp.where(positive, 1.0 / jnp.where(positive, diagonal, 1.0), 0.0)
    return (stored, face_east, face_north, face_up, inverse)


def coefficients(padded_coefs):
    stacked = padded_coefs.astype(jnp.float32)
    east_pad = stacked[0][1:-1, 1:-1, :]
    north_pad = stacked[1][1:-1, :, 1:-1]
    up_pad = stacked[2][:, 1:-1, 1:-1]
    stored = stacked[3][1:-1, 1:-1, 1:-1]
    return face_terms(east_pad, north_pad, up_pad, stored)


def apply_operator(padded, storage_part, face_east, face_north, face_up):
    center = padded[1:-1, 1:-1, 1:-1]
    step_east = padded[1:-1, 1:-1, 1:] - padded[1:-1, 1:-1, :-1]
    step_north = padded[1:-1, 1:, 1:-1] - padded[1:-1, :-1, 1:-1]
    step_up = padded[1:, 1:-1, 1:-1] - padded[:-1, 1:-1, 1:-1]
    flux_east = face_east * step_east
    flux_north = face_north * step_north
    flux_up = face_up * step_up
    total = storage_part * center + (flux_east[:, :, :-1] - flux_east[:, :, 1:])
    total = total + (flux_north[:, :-1] - flux_north[:, 1:])
    return total + (flux_up[:-1] - flux_up[1:])


def keep_whole(field):
    return field


def chebyshev(start, rhs, operate, trim, precondition):
    if start is None:
        residual = rhs
    else:
        residual = trim(rhs) - operate(start)
    direction = precondition(residual) / CENTRE
    if start is None:
        iterate = direction
    else:
        iterate = trim(start) + direction
    sigma = CENTRE / HALF_WIDTH
    factor = 1.0 / sigma
    for sweep_index in range(SWEEPS - 1):
        residual = trim(residual) - operate(direction)
        factor_next = 1.0 / (2.0 * sigma - factor)
        direction = factor_next * factor * trim(
            direction
        ) + 2.0 * factor_next / HALF_WIDTH * precondition(residual)
        iterate = trim(iterate) + direction
        factor = factor_next
    return iterate


def plain(
    head_old,
    head_target,
    conductivity_east,
    conductivity_north,
    conductivity_vertical,
    storage,
    well_east,
    well_north,
    screen_top,
    screen_bottom,
    tariff_band,
    pump_rates,
    ground_level,
    band_prices,
):
    depth_cells, north_cells, east_cells = head_old.shape
    stacked_coefs = jnp.stack(
        (conductivity_east, conductivity_north, conductivity_vertical, storage)
    )
    padded_coefs = extended(stacked_coefs, (("east", 3), ("north", 2), ("layer", 1)), 1)
    margin = 0
    top_level = coefficients(padded_coefs)
    levels = [None] * (margin + 1)
    levels[margin] = top_level

    def margin_of(field):
        return (field.shape[0] - depth_cells) // 2

    def precondition(residual):
        return levels[margin_of(residual)][4] * residual

    def operate(field):
        padded = extended(field, (("east", 2), ("north", 1), ("layer", 0)), 1)
        level = levels[0]
        return apply_operator(padded, level[0], level[1], level[2], level[3])

    east_start = lax.axis_index("east") * east_cells
    north_start = lax.axis_index("north") * north_cells
    layer_start = lax.axis_index("layer") * depth_cells
    local_east = well_east - east_start
    local_north = well_north - north_start
    owning = (
        (local_east >= 0)
        & (local_east < east_cells)
        & (local_north >= 0)
        & (local_north < north_cells)
    ).astype(jnp.float32)
    cells = jnp.clip(local_north, 0, north_cells - 1) * east_cells + jnp.clip(
        local_east, 0, east_cells - 1
    )
    depth = layer_start + jnp.arange(depth_cells, dtype=jnp.int32)[:, None]
    screened = ((depth >= screen_top[None, :]) & (depth <= screen_bottom[None, :])).astype(
        jnp.float32
    ) * owning[None, :]
    weights = (
        conductivity_east.reshape(depth_cells, north_cells * east_cells)[:, cells].astype(
            jnp.float32
        )
        * screened
    )
    totals = lax.psum(jnp.sum(weights, axis=0), "layer")
    shares = weights / (totals + (1.0 - owning))[None, :]
    flat_shape = (depth_cells, north_cells * east_cells)
    source = (
        jnp.zeros(flat_shape, jnp.float32)
        .at[:, cells]
        .add(pump_rates[None, :] * shares)
        .reshape(head_old.shape)
    )
    stored = storage.astype(jnp.float32)
    rhs = stored * head_old - source
    head_new = chebyshev(head_old, rhs, operate, keep_whole, precondition)
    departure = head_new - head_target
    misfit_part = jnp.sum(departure * departure)
    all_cells = float(
        depth_cells
        * north_cells
        * east_cells
        * lax.axis_size("east")
        * lax.axis_size("north")
        * lax.axis_size("layer")
    )
    head_part = jnp.sum(shares * head_new.reshape(flat_shape)[:, cells], axis=0)
    head_screen, misfit_total = lax.psum((head_part, misfit_part), ("east", "north", "layer"))
    band_ids = jnp.arange(band_prices.shape[0], dtype=jnp.int32)
    prices = jnp.sum(
        jnp.where(tariff_band[:, None] == band_ids[None, :], band_prices[None, :], 0.0), axis=1
    )
    load = (
        departure.reshape(flat_shape)
        .at[:, cells]
        .add(-(prices * pump_rates)[None, :] * shares)
        .reshape(head_old.shape)
    )
    adjoint_head = chebyshev(None, load, operate, keep_whole, precondition)
    adjoint_part = jnp.sum(shares * adjoint_head.reshape(flat_shape)[:, cells], axis=0)
    adjoint_screen = lax.psum(adjoint_part, ("east", "north", "layer"))
    misfit = misfit_total / all_cells
    lift = ground_level - head_screen
    rate_gradient = prices * lift - adjoint_screen
    pumping_cost = jnp.sum(prices * pump_rates * lift)
    return (head_new, adjoint_head, rate_gradient, pumping_cost, misfit)


def split(value, parts):
    found = []
    for _ in range(parts):
        top = value.astype(BF16)
        found.append(top)
        value = value - top.astype(F32)
    return found


def dot(a, b, dims):
    return lax.dot_general(a, b, (dims, ((), ())), preferred_element_type=F32)


NN = ((1,), (0,))
NT = ((1,), (1,))


def reciprocal(x):
    first = pl.reciprocal(x, approx=True)
    return first * (2.0 - x * first)


def kernel(sizes, *refs):
    n_east, n_x, n_z = sizes
    n_north = n_x * n_z
    fields, well_refs, refs = refs[:6], refs[6:14], refs[14:]
    head_new, adjoint, out_slope, out_sums, out_crowded = refs[:5]
    hx, tx, ke, kn, kv, st, fe, fn, fu, inv, src, lw, d0, d1, s1, pt = refs[5:21]
    parts, staged, (nbs, efs, ebs, cfs, cbs), refs = refs[21], refs[22:26], refs[26:31], refs[31:]
    (s_nf, s_nb, s_ef, s_eb, s_cf, s_cb), refs = refs[:6], refs[6:]
    well_rows, wells, boxes, refs = refs[:8], refs[8], refs[9:13], refs[13:]
    load_sem, send_sem, recv_sem, sum_send, sum_recv = refs
    depth, rows, cols = head_new.shape
    layers, ext_rows, ext_cols = hx.shape
    chunks_of_rows = ext_rows // 8
    groups = wells.shape[1] // LANES
    me_e, me_n, me_l = lax.axis_index("east"), lax.axis_index("north"), lax.axis_index("layer")
    me_x, me_z = me_n // n_z, lax.rem(me_n, n_z)
    own, other = depth * me_l, depth * (1 - me_l)
    own_layers = pl.ds(own, depth)

    def east_of(side):
        return lax.rem(me_e + (n_east - 1 if side == 0 else 1), n_east)

    def north_of(side):
        return lax.rem(me_n + (n_north - 1 if side == 0 else 1), n_north)

    partner = (me_e, me_n, 1 - me_l)
    to_north = [(me_e, north_of(s), me_l) for s in (0, 1)]
    to_east = [(east_of(s), me_n, me_l) for s in (0, 1)]
    to_corner = [(east_of(c), north_of(r), me_l) for r in (0, 1) for c in (0, 1)]
    phases = []
    for box, size, mine, device in (
        (boxes[0], 2, me_l, lambda i: (me_e, me_n, i)),
        (boxes[1], n_z, me_z, lambda i: (me_e, me_x * n_z + i, me_l)),
        (boxes[2], n_east, me_e, lambda i: (i, me_n, me_l)),
        (boxes[3], n_x, me_x, lambda i: (me_e, i * n_z + me_z, me_l)),
    ):
        phases.append((box, mine, [device(lax.rem(mine + k, size)) for k in range(1, size)]))

    greeted = [partner] + to_north + to_east + to_corner
    for _, _, peers in phases:
        greeted = greeted + peers
    barrier = pltpu.get_barrier_semaphore()
    for device in greeted:
        pl.semaphore_signal(barrier, inc=1, device_id=device, device_id_type=MESH)

    loaded = [0]

    def load(src_ref, dst_ref):
        copy = pltpu.make_async_copy(src_ref, dst_ref, load_sem.at[loaded[0]])
        loaded[0] += 1
        copy.start()
        return copy

    lane = iota((8, LANES), 1)
    group = lane // HALO
    wide_sub = iota((8, cols), 0)
    last = cols - LANES
    low_half = lane < LANES // 2
    extra = pl.ds(cols, LANES)
    inside_cols = pl.ds(0, cols)
    inner = pl.ds(8, rows)
    edge_rows = (pl.ds(rows + 8, 8), pl.ds(0, 8))

    block_loads = [
        load(fields[0], hx.at[own_layers, inner, inside_cols]),
        load(fields[1], tx.at[own_layers, inner, inside_cols]),
    ] + [load(fields[2 + a], staged[a].at[own_layers]) for a in range(4)]
    well_loads = [load(a, b) for a, b in zip(well_refs, well_rows)]
    for copy in block_loads:
        copy.wait()

    def pack(z, carry):
        for side in (0, 1):
            c0 = last * side
            kept = jnp.zeros((8, LANES), F32)
            fields = [jnp.zeros((8, LANES), F32) for _ in staged]
            for pair in range(rows // 16):
                tiles = [
                    ref[own + z, pl.ds(16 * pair, 16), pl.ds(c0, LANES)].astype(F32) for ref in staged
                ]
                for half in (0, 1):
                    j = 2 * pair + half
                    shift = HALO * j - (LANES - HALO) * side
                    h = hx[own + z, pl.ds(8 + 8 * j, 8), pl.ds(c0, LANES)]
                    t = tx[own + z, pl.ds(8 + 8 * j, 8), pl.ds(c0, LANES)]
                    if side == 0:
                        both = jnp.where(lane >= HALO - 2, roll(t, HALO - 2, 1), h)
                    else:
                        both = jnp.where(lane < LANES - HALO + 2, roll(t, 2 - HALO, 1), h)
                    here = group == j
                    kept = jnp.where(here, roll(both, shift, 1), kept)
                    for a in range(4):
                        piece = tiles[a][8 * half:8 * half + 8]
                        fields[a] = jnp.where(here, roll(piece, shift, 1), fields[a])
            s_ef[side, z] = kept
            s_eb[side, z, pl.ds(0, 16)] = jnp.concatenate(fields[:2], axis=0).astype(BF16)
            s_eb[side, z, pl.ds(16, 16)] = jnp.concatenate(fields[2:], axis=0).astype(BF16)
            r0 = (rows - 8) * side
            h = hx[own + z, pl.ds(8 + r0, 8), inside_cols]
            t = tx[own + z, pl.ds(8 + r0, 8), inside_cols]
            edge = [
                ref[own + z, pl.ds((rows - 16) * side, 16), :].astype(F32)[8 * side:8 * side + 8]
                for ref in staged
            ]
            if side == 0:
                both = jnp.where(wide_sub == 5, roll(edge[1], 1, 0), h)
                both = jnp.where(wide_sub >= 6, roll(t, 6, 0), both)
                first = jnp.where(wide_sub < 4, edge[0], roll(edge[1], 4, 0))
                second = jnp.where(wide_sub < 4, edge[2], roll(edge[3], 4, 0))
            else:
                both = jnp.where(wide_sub == 2, roll(edge[1], 7, 0), h)
                both = jnp.where(wide_sub < 2, roll(t, 2, 0), both)
                first = jnp.where(wide_sub < 4, roll(edge[0], 4, 0), edge[1])
                second = jnp.where(wide_sub < 4, roll(edge[2], 4, 0), edge[3])
            s_nf[side, z] = both
            s_nb[side, z] = jnp.concatenate([first, second], axis=0).astype(BF16)
        return carry

    lax.fori_loop(0, depth, pack, 0)

    for r in (0, 1):
        for c in (0, 1):
            c0 = last * c
            kept = jnp.zeros((8, LANES), F32)
            mixed = jnp.zeros((8, LANES), F32)
            for z in range(depth):
                both = s_nf[r, z, :, pl.ds(c0, LANES)]
                kept = jnp.where(group == z, roll(both, HALO * z - (LANES - HALO) * c, 1), kept)
                pieces = s_nb[r, z, :, pl.ds(c0, LANES)].astype(F32)
                for half in (0, 1):
                    slot = half * depth + z
                    moved = roll(
                        pieces[8 * half:8 * half + 8], HALO * slot - (LANES - HALO) * c, 1
                    )
                    mixed = jnp.where(group == slot, moved, mixed)
            s_cf[2 * r + c] = kept
            s_cb[2 * r + c] = jnp.concatenate([mixed, mixed], axis=0).astype(BF16)

    pl.semaphore_wait(barrier, len(greeted))

    sent = [0]

    def send(src_ref, dst_ref, device):
        copy = pltpu.make_async_remote_copy(
            src_ref=src_ref,
            dst_ref=dst_ref,
            send_sem=send_sem.at[sent[0]],
            recv_sem=recv_sem.at[sent[0]],
            device_id=device,
            device_id_type=MESH,
        )
        sent[0] += 1
        copy.start()
        return copy

    norths, easts, corners = [], [], []
    for side in (0, 1):
        norths.append(send(s_nb.at[side], nbs.at[0, side], to_north[side]))
        norths.append(
            send(s_nf.at[side], hx.at[own_layers, edge_rows[side], inside_cols], to_north[side])
        )
    for side in (0, 1):
        easts.append(send(s_eb.at[side], ebs.at[0, side], to_east[side]))
        easts.append(send(s_ef.at[side], efs.at[0, side], to_east[side]))
    for d in range(4):
        corners.append(send(s_cb.at[d], cbs.at[0, d], to_corner[d]))
        corners.append(send(s_cf.at[d], cfs.at[0, d], to_corner[d]))
    two = (depth - 2) * (1 - me_l)
    blocks = [send(fields[2 + a], staged[a].at[own_layers], partner) for a in range(4)]
    blocks.append(send(fields[0], hx.at[own_layers, inner, inside_cols], partner))
    blocks.append(
        send(
            fields[1].at[pl.ds(two, 2)], tx.at[pl.ds(own + two, 2), inner, inside_cols], partner
        )
    )

    for copy in well_loads:
        copy.wait()
    wells[...] = jnp.full(wells.shape, -1e6, F32)
    width = pl.ds(0, well_rows[0].shape[1])
    for row, ref in enumerate(well_rows[:5]):
        wells[pl.ds(row, 1), width] = ref[...].astype(F32)
    band = well_rows[5][...]
    bands = well_rows[7][...]
    price = jnp.zeros(band.shape, F32)
    for b in range(bands.shape[1]):
        price = jnp.where(band == b, bands[0:1, b:b + 1], price)
    wells[pl.ds(5, 1), width] = price
    wells[pl.ds(6, 1), width] = well_rows[6][...]

    at_east = wells[0:1, :] - (me_e * cols).astype(F32)
    at_north = wells[1:2, :] - (me_n * rows).astype(F32)
    near = (
        (at_east >= -REACH) & (at_east < cols + REACH)
        & (at_north >= -REACH) & (at_north < rows + REACH)
    )
    mine = (at_east >= 0) & (at_east < cols) & (at_north >= 0) & (at_north < rows)
    near_row = jnp.where(near, 1.0, 0.0)
    near_tile = jnp.concatenate(
        [near_row[:, LANES * k:LANES * (k + 1)] for k in range(groups)], axis=0
    )
    before = (iota((LANES, LANES), 0) < iota((LANES, LANES), 1)).astype(F32).astype(BF16)
    in_row = dot(near_tile.astype(BF16), before, NN)
    above = (iota((groups, groups), 1) < iota((groups, groups), 0)).astype(F32).astype(BF16)
    rows_above = jnp.sum(dot(above, near_tile.astype(BF16), NN), axis=1, keepdims=True)
    rank = jnp.where(near_tile > 0, in_row + rows_above, -1.0)
    found = jnp.sum(jnp.sum(near_tile, axis=1, keepdims=True), axis=0, keepdims=True)
    crowded = jnp.where(found > SLOTS, 1.0, 0.0)

    place = jnp.concatenate(
        [
            jnp.where(at_east < 0, at_east + ext_cols, at_east),
            at_north + 8.0,
            wells[2:7, :],
            jnp.where(mine, 1.0, 0.0),
        ],
        axis=0,
    )
    place_parts = jnp.concatenate([p.astype(F32) for p in split(place, 3)], axis=0).astype(BF16)
    slot_of = iota((SLOTS, LANES), 0).astype(F32)

    for k in range(groups):
        pt[:, pl.ds(LANES * k, LANES)] = jnp.where(slot_of == rank[k:k + 1, :], 1.0, 0.0).astype(BF16)
    three = dot(place_parts, pt[...], NT)
    comp = three[0:8] + three[8:16] + three[16:24]
    col_hot = jnp.where(iota((ext_cols, SLOTS), 0).astype(F32) == comp[0:1], 1.0, 0.0)
    row_hot = jnp.where(iota((ext_rows, SLOTS), 0).astype(F32) == comp[1:2], 1.0, 0.0)
    col_hot = col_hot.astype(BF16)


    def fill_inner(base):
        def fill(z, carry):
            for dst, ref in zip((ke, kn, kv, st), staged):
                dst[base + z, inner, inside_cols] = ref[base + z].astype(F32)
            return carry

        lax.fori_loop(0, depth, fill, 0)

    def fill_east(who, base):
        def fill(z, carry):
            zz = base + z
            right, left = efs[who, 0, z], efs[who, 1, z]
            for j in range(rows // 8):
                both = jnp.where(
                    low_half, roll(right, -HALO * j, 1), roll(left, LANES - HALO - HALO * j, 1)
                )
                hx[zz, pl.ds(8 + 8 * j, 8), extra] = both
                tx[zz, pl.ds(8 + 8 * j, 8), extra] = jnp.where(
                    low_half, roll(both, 2 - HALO, 1), roll(both, HALO - 2, 1)
                )
            for half, pair in ((0, (ke, kn)), (1, (kv, st))):
                rights = ebs[who, 0, z, pl.ds(16 * half, 16)].astype(F32)
                lefts = ebs[who, 1, z, pl.ds(16 * half, 16)].astype(F32)
                for k in (0, 1):
                    right, left = rights[8 * k:8 * k + 8], lefts[8 * k:8 * k + 8]
                    for j in range(rows // 8):
                        pair[k][zz, pl.ds(8 + 8 * j, 8), extra] = jnp.where(
                            low_half,
                            roll(right, -HALO * j, 1),
                            roll(left, LANES - HALO - HALO * j, 1),
                        )
            return carry

        lax.fori_loop(0, depth, fill, 0)

    def put_rows(side, zz, at_rows, at_cols, both, first, second):
        row = iota(both.shape, 0)
        if side == 0:
            tx[zz, at_rows, at_cols] = roll(both, 2, 0)
            ke[zz, at_rows, at_cols] = first
            kn[zz, at_rows, at_cols] = jnp.where(row == 4, roll(both, 7, 0), roll(first, 4, 0))
            kv[zz, at_rows, at_cols] = second
            st[zz, at_rows, at_cols] = roll(second, 4, 0)
        else:
            tx[zz, at_rows, at_cols] = roll(both, 6, 0)
            ke[zz, at_rows, at_cols] = roll(first, 4, 0)
            kn[zz, at_rows, at_cols] = jnp.where(row == 3, roll(both, 1, 0), first)
            kv[zz, at_rows, at_cols] = roll(second, 4, 0)
            st[zz, at_rows, at_cols] = second

    def fill_north(who, base):
        def fill(z, carry):
            for side, at_rows in enumerate(edge_rows):
                pieces = nbs[who, side, z].astype(F32)
                both = hx[base + z, at_rows, inside_cols]
                put_rows(side, base + z, at_rows, inside_cols, both, pieces[:8], pieces[8:])
            return carry

        lax.fori_loop(0, depth, fill, 0)

    def fill_corners(who, base):
        for side, at_rows in enumerate(edge_rows):
            right, left = cfs[who, 2 * side], cfs[who, 2 * side + 1]
            rights = cbs[who, 2 * side].astype(F32)[:8]
            lefts = cbs[who, 2 * side + 1].astype(F32)[:8]

            def taken(a, b, slot):
                return jnp.where(
                    low_half, roll(a, -HALO * slot, 1), roll(b, LANES - HALO - HALO * slot, 1)
                )

            for z in range(depth):
                both = taken(right, left, z)
                hx[base + z, at_rows, extra] = both
                put_rows(
                    side, base + z, at_rows, extra, both,
                    taken(rights, lefts, z), taken(rights, lefts, depth + z),
                )

    wide = (8, ext_cols)
    sub = iota(wide, 0)
    col = iota(wide, 1)
    closed_col = ((col == cols - 1) & (me_e == n_east - 1)) | ((col == ext_cols - 1) & (me_e == 0))
    open_east = jnp.where(closed_col, 0.0, 2.0)

    def east(v):
        return roll(v, ext_cols - 1, 1)

    def west(v):
        return roll(v, 1, 1)

    def north(now, after):
        return jnp.where(sub < 7, roll(now, 7, 0), roll(after, 7, 0))

    def south(now, prior):
        return jnp.where(sub > 0, roll(now, 1, 0), roll(prior, 1, 0))

    fu[0] = jnp.zeros((ext_rows, ext_cols), F32)
    fu[layers] = jnp.zeros((ext_rows, ext_cols), F32)

    def at(j):
        return pl.ds(8 * j if isinstance(j, int) else pl.multiple_of(8 * j, 8), 8)

    def next_of(j):
        return min(j + 1, chunks_of_rows - 1) if isinstance(j, int) else jnp.minimum(j + 1, chunks_of_rows - 1)

    def layer_of(k):
        return jnp.where(me_l == 0, k, layers - 1 - k)

    def start(first, count, with_wells):
        zs = [layer_of(first + i) for i in range(count)]
        above = layer_of(jnp.minimum(first + count, layers - 1))
        below = layer_of(jnp.maximum(first - 1, 0))
        opens = [jnp.where(first + i < layers - 1, 2.0, 0.0) for i in range(count)]

        def chunk(j, carry):
            f_priors, g_priors, k_now, h_now = carry
            k_ups = [kv[z, at(j)] for z in zs] + [kv[above, at(j)]]
            heads = h_now + [hx[above, at(j)]]
            edge = ((j == 0) & (me_n == 0)) | ((j == chunks_of_rows - 2) & (me_n == n_north - 1))
            opened = jnp.where((sub == 7) & edge, 0.0, 2.0)
            f_d = fu[zs[0] + me_l, at(j)]
            g_d = f_d * (h_now[0] - hx[below, at(j)])
            faces, flows, k_after, h_after = [], [], [], []
            for i, z in enumerate(zs):
                k_e, k_n, h = ke[z, at(j)], k_now[i], h_now[i]
                k_after.append(kn[z, at(next_of(j))])
                h_after.append(hx[z, at(next_of(j))])
                k_e2 = east(k_e)
                k_n2 = north(k_n, k_after[i])
                f_e = open_east * k_e * k_e2 * reciprocal(k_e + k_e2)
                f_n = opened * k_n * k_n2 * reciprocal(k_n + k_n2)
                f_u = opens[i] * k_ups[i] * k_ups[i + 1] * reciprocal(k_ups[i] + k_ups[i + 1])
                fe[z, at(j)] = f_e
                fn[z, at(j)] = f_n
                fu[z + 1 - me_l, at(j)] = f_u
                diagonal = st[z, at(j)] + f_e + west(f_e) + f_n + south(f_n, f_priors[i]) + f_u + f_d
                inverse = reciprocal(diagonal)
                inv[z, at(j)] = inverse
                g_e = f_e * (east(h) - h)
                g_n = f_n * (north(h, h_after[i]) - h)
                g_u = f_u * (heads[i + 1] - h)
                residual = (g_e - west(g_e)) + (g_n - south(g_n, g_priors[i])) + (g_u - g_d)
                if with_wells:
                    residual = residual - src[z, at(j)]
                d0[z, at(j)] = inverse * residual
                faces.append(f_n)
                flows.append(g_n)
                f_d, g_d = f_u, g_u
            return faces, flows, k_after, h_after

        def several(i, carry):
            for m in range(START_UNIT):
                carry = chunk(i * START_UNIT + m, carry)
            return carry

        none = [jnp.zeros(wide, F32)] * count
        carry = (none, none, [kn[z, at(0)] for z in zs], [hx[z, at(0)] for z in zs])
        lax.fori_loop(0, chunks_of_rows // START_UNIT, several, carry)

    def start_layers(begin, end, with_wells):
        def some(i, carry):
            start(begin + START_LAYERS * i, START_LAYERS, with_wells)
            return carry

        whole = (end - begin) // START_LAYERS
        lax.fori_loop(0, whole, some, 0)
        if begin + whole * START_LAYERS < end:
            start(begin + whole * START_LAYERS, end - begin - whole * START_LAYERS, with_wells)

    def pump(k, carry):
        z = layer_of(k)
        d0[z] = d0[z] - inv[z] * src[z]
        return carry

    fill_inner(own)
    for copy in easts:
        copy.wait_recv()
    forwards = [send(efs.at[0], efs.at[1], partner), send(ebs.at[0], ebs.at[1], partner)]
    fill_east(0, own)
    for copy in norths:
        copy.wait_recv()
    forwards.append(send(nbs.at[0], nbs.at[1], partner))
    for side in (0, 1):
        place_of = hx.at[own_layers, edge_rows[side], inside_cols]
        forwards.append(send(place_of, place_of, partner))
    for copy in corners:
        copy.wait_recv()
    forwards.append(send(cfs.at[0], cfs.at[1], partner))
    forwards.append(send(cbs.at[0], cbs.at[1], partner))
    fill_north(0, own)
    fill_corners(0, own)
    start_layers(0, depth - 1, False)
    for copy in blocks:
        copy.wait_recv()
    fill_inner(other)
    for copy in forwards:
        copy.wait_recv()
    fill_east(1, other)
    fill_north(1, other)
    fill_corners(1, other)
    for copy in norths + easts + corners + blocks + forwards:
        copy.wait_send()

    weights = []
    for z in range(layers):
        found = dot(ke[z].astype(BF16), col_hot, NN)
        k_at = jnp.sum(found * row_hot, axis=0, keepdims=True)
        screened = (comp[2:3] <= z) & (comp[3:4] >= z)
        weights.append(jnp.where(screened, k_at, 0.0))
    weight = jnp.concatenate(weights, axis=0)
    total = jnp.sum(weight, axis=0, keepdims=True)
    share = weight / jnp.where(total > 0, total, 1.0)
    pumped = share * comp[4:5]
    priced = pumped * comp[5:6]
    col_two = jnp.concatenate([col_hot, col_hot], axis=1)
    for z in range(layers):
        left = []
        for value in (pumped, priced):
            top, rest = split(value[z:z + 1], 2)
            left.append(
                jnp.concatenate([row_hot * top.astype(F32), row_hot * rest.astype(F32)], axis=1)
            )
        left = jnp.concatenate(left, axis=0).astype(BF16)
        field = dot(left, col_two, NT)
        src[z] = field[:ext_rows]
        lw[z] = field[ext_rows:]

    lax.fori_loop(0, depth - 1, pump, 0)
    start_layers(depth - 1, layers, True)

    def sweep(field, margin, finish, chunk_from, chunk_to):
        first = (depth - margin) * me_l

        def together(i, count):
            zs = [first + i + k for k in range(count)]
            below = jnp.maximum(zs[0] - 1, 0)
            above = jnp.minimum(zs[-1] + 1, layers - 1)
            if chunk_from == 0:
                priors = [jnp.zeros(wide, F32)] * count
            else:
                before = at(chunk_from - 1)
                priors = [fn[z, before] * field[z, before] for z in zs]
            now = [field[z, at(chunk_from)] for z in zs]
            for j in range(chunk_from, chunk_to):
                after = [field[z, at(min(j + 1, chunks_of_rows - 1))] for z in zs]
                stack = [field[below, at(j)]] + now + [field[above, at(j)]]
                for k, z in enumerate(zs):
                    d = now[k]
                    f_e, f_n = fe[z, at(j)], fn[z, at(j)]
                    b = f_n * d
                    moved = f_e * east(d) + west(f_e * d)
                    moved = moved + f_n * north(d, after[k]) + south(b, priors[k])
                    moved = moved + fu[z + 1, at(j)] * stack[k + 2] + fu[z, at(j)] * stack[k]
                    finish(i + k, z, j, d, inv[z, at(j)] * moved)
                    priors[k] = b
                now = after

        def some(i, carry):
            together(SWEEP_LAYERS * i, SWEEP_LAYERS)
            return carry

        total = depth + margin
        lax.fori_loop(0, total // SWEEP_LAYERS, some, 0)
        if total % SWEEP_LAYERS:
            together(total - total % SWEEP_LAYERS, total % SWEEP_LAYERS)

    (a1, b1), (a2, b2) = steps_of()

    def first_sweep(i, z, j, d, pulled):
        s1[z, at(j)] = pulled
        d1[z, at(j)] = a1 * d + b1 * pulled

    def end_forward(i, z, j, d, pulled):
        s2 = s1[z, at(j)] - d + pulled
        d2 = a2 * d + b2 * s2
        new = hx[z, at(j)] + d0[z, at(j)] + d + d2
        hx[z, at(j)] = new
        load = new - tx[z, at(j)] - lw[z, at(j)]
        src[z, at(j)] = inv[z, at(j)] * load

    sweep(d0, 3, first_sweep, 0, chunks_of_rows)
    sweep(d1, 2, end_forward, 0, chunks_of_rows)
    sweep(src, 1, first_sweep, 0, chunks_of_rows)

    st[0, at(0)] = jnp.zeros(wide, F32)

    def end_adjoint(i, z, j, d, pulled):
        s2 = s1[z, at(j)] - d + pulled
        d2 = a2 * d + b2 * s2
        adj = src[z, at(j)] + d + d2
        adjoint[i, at(j - 1)] = adj[:, :cols]
        new = hx[z, at(j), inside_cols]
        head_new[i, at(j - 1)] = new
        departure = new - tx[z, at(j), inside_cols]
        st[0, at(0), inside_cols] = st[0, at(0), inside_cols] + departure * departure

    sweep(d1, 0, end_adjoint, 1, chunks_of_rows - 1)

    squared = st[0, at(0), inside_cols]
    squared = jnp.sum(squared, axis=0, keepdims=True)
    squared = sum(squared[:, LANES * k:LANES * (k + 1)] for k in range(cols // LANES))
    squared = squared * (1.0 / (float(layers * rows * cols) * n_east * n_north))
    base_layer = jnp.where(me_l == 0, 1.0, 0.0)

    col_hot, row_hot = col_hot[:cols], row_hot[8:8 + rows]
    head_at = jnp.zeros((1, SLOTS), F32)
    adj_at = jnp.zeros((1, SLOTS), F32)
    for i in range(depth):
        z_share = jnp.where(me_l == 0, share[i:i + 1], share[depth + i:depth + i + 1])
        stack = split(head_new[i], 2) + split(adjoint[i], 2)
        found = [dot(piece, col_hot, NN) for piece in stack]
        head_at += z_share * jnp.sum((found[0] + found[1]) * row_hot, axis=0, keepdims=True)
        adj_at += z_share * jnp.sum((found[2] + found[3]) * row_hot, axis=0, keepdims=True)
    lift = (comp[6:7] * base_layer - head_at) * comp[7:8]
    priced = comp[5:6] * lift
    slope = priced - adj_at * comp[7:8]
    three = jnp.concatenate(
        [p.astype(F32) for p in split(slope, 3)] + [jnp.zeros((5, SLOTS), F32)], axis=0
    ).astype(BF16)
    spread = dot(three, pt[...], NN)
    spread = spread[0:1] + spread[1:2] + spread[2:3]
    tile = jnp.concatenate(
        [spread[:, LANES * k:LANES * (k + 1)] for k in range(groups)], axis=0
    )
    parts[pl.ds(0, groups)] = tile
    parts[pl.ds(groups, 8)] = jnp.concatenate(
        [
            priced * comp[4:5],
            squared,
            jnp.broadcast_to(crowded, (1, LANES)),
            jnp.zeros((5, LANES), F32),
        ],
        axis=0,
    )

    total = parts[...]
    used = 0
    for box, mine, peers in phases:
        box[mine] = total
        copies = []
        for device in peers:
            copy = pltpu.make_async_remote_copy(
                src_ref=box.at[mine],
                dst_ref=box.at[mine],
                send_sem=sum_send.at[used],
                recv_sem=sum_recv.at[used],
                device_id=device,
                device_id_type=MESH,
            )
            copy.start()
            copies.append(copy)
            used += 1
        for copy in copies:
            copy.wait()
        total = box[0]
        for k in range(1, len(peers) + 1):
            total = total + box[k]
    n_wells = out_slope.shape[1]
    for k in range(groups):
        width = min(LANES, n_wells - LANES * k)
        out_slope[:, pl.ds(LANES * k, width)] = total[k:k + 1, :width]
    sums = jnp.sum(total[groups:], axis=1, keepdims=True)
    out_sums[...] = jnp.broadcast_to(sums, out_sums.shape)
    out_crowded[...] = sums[2:3]


def run_kernel(sizes, fields, wells):
    depth, rows, cols = fields[0].shape
    layers, ext_rows, ext_cols = 2 * depth, rows + 16, cols + LANES
    n_wells = wells[0].shape[1]
    groups = -(-n_wells // LANES)
    n_east, n_x, n_z = sizes
    block = pltpu.VMEM((depth, rows, cols), F32)
    ext = pltpu.VMEM((layers, ext_rows, ext_cols), F32)
    operands = (*fields, *wells)
    copies = 4 + 4 + 8 + 6 + 7
    peers = 1 + n_z + n_east + n_x - 3
    return pl.pallas_call(
        functools.partial(kernel, sizes),
        out_shape=[
            block, block, pltpu.VMEM((1, n_wells), F32), pltpu.VMEM((8, LANES), F32),
            jax.ShapeDtypeStruct((1, 1), F32),
        ],
        in_specs=[pl.BlockSpec(memory_space=pltpu.HBM)] * len(operands),
        out_specs=[pl.BlockSpec(memory_space=pltpu.VMEM)] * 5,
        scratch_shapes=[ext] * 8
        + [pltpu.VMEM((layers + 1, ext_rows, ext_cols), F32)]
        + [ext] * 6
        + [pltpu.VMEM((SLOTS, groups * LANES), BF16)]
        + [pltpu.VMEM((groups + 8, LANES), F32)]
        + [pltpu.VMEM((layers, rows, cols), BF16)] * 4
        + [
            pltpu.VMEM((2, 2, depth, 16, cols), BF16),
            pltpu.VMEM((2, 2, depth, 8, LANES), F32),
            pltpu.VMEM((2, 2, depth, 32, LANES), BF16),
            pltpu.VMEM((2, 4, 8, LANES), F32),
            pltpu.VMEM((2, 4, 16, LANES), BF16),
            pltpu.VMEM((2, depth, 8, cols), F32),
            pltpu.VMEM((2, depth, 16, cols), BF16),
            pltpu.VMEM((2, depth, 8, LANES), F32),
            pltpu.VMEM((2, depth, 32, LANES), BF16),
            pltpu.VMEM((4, 8, LANES), F32),
            pltpu.VMEM((4, 16, LANES), BF16),
        ]
        + [pltpu.VMEM(w.shape, w.dtype) for w in wells]
        + [pltpu.VMEM((8, groups * LANES), F32)]
        + [pltpu.VMEM((n, groups + 8, LANES), F32) for n in (2, n_z, n_east, n_x)]
        + [pltpu.SemaphoreType.DMA((14,))]
        + [pltpu.SemaphoreType.DMA((copies,))] * 2
        + [pltpu.SemaphoreType.DMA((peers,))] * 2,
        compiler_params=pltpu.CompilerParams(
            collective_id=0, has_side_effects=True, vmem_limit_bytes=60 * 1024 * 1024
        ),
        name="whole_step",
    )(*operands)


def hand_over(new, adjoint, slope, sums, o_new, o_adjoint, o_slope, o_cost, o_misfit, cost, misfit, sem):
    cost[...] = sums[0:1, 0:1]
    misfit[...] = sums[1:2, 0:1]
    copies = [
        pltpu.make_async_copy(src_ref, dst_ref, sem.at[k])
        for k, (src_ref, dst_ref) in enumerate((
            (new, o_new), (adjoint, o_adjoint), (slope, o_slope), (cost, o_cost), (misfit, o_misfit),
        ))
    ]
    for copy in copies:
        copy.start()
    for copy in copies:
        copy.wait()


def run_hand_over(new, adjoint, slope, sums):
    block = jax.ShapeDtypeStruct(new.shape, F32)
    one = jax.ShapeDtypeStruct((1, 1), F32)
    return pl.pallas_call(
        hand_over,
        out_shape=[block, block, jax.ShapeDtypeStruct(slope.shape, F32), one, one],
        in_specs=[pl.BlockSpec(memory_space=pltpu.VMEM)] * 4,
        out_specs=[pl.BlockSpec(memory_space=pltpu.HBM)] * 5,
        scratch_shapes=[pltpu.VMEM((1, 1), F32)] * 2 + [pltpu.SemaphoreType.DMA((5,))],
        compiler_params=pltpu.CompilerParams(vmem_limit_bytes=8 * 1024 * 1024),
        name="hand_over",
    )(new, adjoint, slope, sums)


def in_order(value):
    return with_layout_constraint(value, Layout(major_to_minor=(0, 1, 2)))


def per_device(sizes, *arguments):
    fields = arguments[:6]
    e, n, top, bottom, tariff, rates, ground, prices = arguments[6:]
    wells = [w.reshape(1, -1) for w in (e, n, top, bottom, rates, tariff, ground, prices)]
    *results, crowded = run_kernel(sizes, fields, wells)
    found = tuple(run_hand_over(*results))

    def again(state):
        blocks = [in_order(x) for x in fields]
        first, second, *others = plain(*blocks, *arguments[6:])
        others = [x.reshape(1, -1) for x in others]
        return jnp.zeros((), F32), (in_order(first), in_order(second), *others)

    _, found = lax.while_loop(lambda state: state[0] > 0, again, (crowded.reshape(()), found))
    new, adjoint, slope, cost, misfit = found
    return new, adjoint, slope.reshape(-1), cost.reshape(()), misfit.reshape(())


def solution(mesh):
    field = P("layer", "north", "east")
    n_north = mesh.shape["north"]
    n_x = 4 if n_north % 4 == 0 else 1
    sizes = (mesh.shape["east"], n_x, n_north // n_x)
    return jax.shard_map(
        functools.partial(per_device, sizes),
        mesh=mesh,
        in_specs=(field,) * 6 + (P(),) * 8,
        out_specs=(field, field, P(), P(), P()),
        check_vma=False,
    )
```

```python
import functools

import jax
import jax.numpy as jnp
from jax import lax
from jax.experimental import pallas as pl
from jax.experimental.layout import Layout, with_layout_constraint
from jax.experimental.pallas import tpu as pltpu
from jax.sharding import PartitionSpec as P

MESH = pl.DeviceIdType.MESH
F32 = jnp.float32
BF16 = jnp.bfloat16

SWEEPS = 3
CENTRE = 1.0
HALF_WIDTH = 0.95

HALO = 8
REACH = 5
LANES = 128
SLOTS = 128
START_UNIT, START_LAYERS = 9, 1
SWEEP_LAYERS = 4


def steps_of():
    sigma = CENTRE / HALF_WIDTH
    factor = 1.0 / sigma
    found = []
    for _ in range(SWEEPS - 1):
        after = 1.0 / (2.0 * sigma - factor)
        found.append((after * factor, 2.0 * after / HALF_WIDTH))
        factor = after
    return found


def iota(shape, dim):
    return lax.broadcasted_iota(jnp.int32, shape, dim)


def roll(value, shift, dim):
    shift = shift % value.shape[dim]
    return pltpu.roll(value, shift, dim) if shift else value


def extended(value, sides, width):
    for axis, dim in sides:
        size, length = (lax.axis_size(axis), value.shape[dim])
        up = [(i, (i + 1) % size) for i in range(size - 1)]
        down = [(j, i) for i, j in up]
        last = lax.slice_in_dim(value, length - width, length, axis=dim)
        initial = lax.slice_in_dim(value, 0, width, axis=dim)
        before = lax.ppermute(last, axis, up)
        after = lax.ppermute(initial, axis, down)
        value = jnp.concatenate([before, value, after], axis=dim)
    return value


def harmonic(first, second):
    total = first + second
    return 2.0 * first * second / jnp.where(total > 0, total, 1.0)


def face_terms(east_pad, north_pad, up_pad, stored):
    face_east = harmonic(east_pad[:, :, :-1], east_pad[:, :, 1:])
    face_north = harmonic(north_pad[:, :-1], north_pad[:, 1:])
    face_up = harmonic(up_pad[:-1], up_pad[1:])
    diagonal = stored + face_east[:, :, :-1] + face_east[:, :, 1:]
    diagonal = diagonal + face_north[:, :-1] + face_north[:, 1:]
    diagonal = diagonal + face_up[:-1] + face_up[1:]
    positive = diagonal > 0
    inverse = jnp.where(positive, 1.0 / jnp.where(positive, diagonal, 1.0), 0.0)
    return (stored, face_east, face_north, face_up, inverse)


def coefficients(padded_coefs):
    stacked = padded_coefs.astype(jnp.float32)
    east_pad = stacked[0][1:-1, 1:-1, :]
    north_pad = stacked[1][1:-1, :, 1:-1]
    up_pad = stacked[2][:, 1:-1, 1:-1]
    stored = stacked[3][1:-1, 1:-1, 1:-1]
    return face_terms(east_pad, north_pad, up_pad, stored)


def apply_operator(padded, storage_part, face_east, face_north, face_up):
    center = padded[1:-1, 1:-1, 1:-1]
    step_east = padded[1:-1, 1:-1, 1:] - padded[1:-1, 1:-1, :-1]
    step_north = padded[1:-1, 1:, 1:-1] - padded[1:-1, :-1, 1:-1]
    step_up = padded[1:, 1:-1, 1:-1] - padded[:-1, 1:-1, 1:-1]
    flux_east = face_east * step_east
    flux_north = face_north * step_north
    flux_up = face_up * step_up
    total = storage_part * center + (flux_east[:, :, :-1] - flux_east[:, :, 1:])
    total = total + (flux_north[:, :-1] - flux_north[:, 1:])
    return total + (flux_up[:-1] - flux_up[1:])


def keep_whole(field):
    return field


def chebyshev(start, rhs, operate, trim, precondition):
    if start is None:
        residual = rhs
    else:
        residual = trim(rhs) - operate(start)
    direction = precondition(residual) / CENTRE
    if start is None:
        iterate = direction
    else:
        iterate = trim(start) + direction
    sigma = CENTRE / HALF_WIDTH
    factor = 1.0 / sigma
    for sweep_index in range(SWEEPS - 1):
        residual = trim(residual) - operate(direction)
        factor_next = 1.0 / (2.0 * sigma - factor)
        direction = factor_next * factor * trim(
            direction
        ) + 2.0 * factor_next / HALF_WIDTH * precondition(residual)
        iterate = trim(iterate) + direction
        factor = factor_next
    return iterate


def plain(
    head_old,
    head_target,
    conductivity_east,
    conductivity_north,
    conductivity_vertical,
    storage,
    well_east,
    well_north,
    screen_top,
    screen_bottom,
    tariff_band,
    pump_rates,
    ground_level,
    band_prices,
):
    depth_cells, north_cells, east_cells = head_old.shape
    stacked_coefs = jnp.stack(
        (conductivity_east, conductivity_north, conductivity_vertical, storage)
    )
    padded_coefs = extended(stacked_coefs, (("east", 3), ("north", 2), ("layer", 1)), 1)
    margin = 0
    top_level = coefficients(padded_coefs)
    levels = [None] * (margin + 1)
    levels[margin] = top_level

    def margin_of(field):
        return (field.shape[0] - depth_cells) // 2

    def precondition(residual):
        return levels[margin_of(residual)][4] * residual

    def operate(field):
        padded = extended(field, (("east", 2), ("north", 1), ("layer", 0)), 1)
        level = levels[0]
        return apply_operator(padded, level[0], level[1], level[2], level[3])

    east_start = lax.axis_index("east") * east_cells
    north_start = lax.axis_index("north") * north_cells
    layer_start = lax.axis_index("layer") * depth_cells
    local_east = well_east - east_start
    local_north = well_north - north_start
    owning = (
        (local_east >= 0)
        & (local_east < east_cells)
        & (local_north >= 0)
        & (local_north < north_cells)
    ).astype(jnp.float32)
    cells = jnp.clip(local_north, 0, north_cells - 1) * east_cells + jnp.clip(
        local_east, 0, east_cells - 1
    )
    depth = layer_start + jnp.arange(depth_cells, dtype=jnp.int32)[:, None]
    screened = ((depth >= screen_top[None, :]) & (depth <= screen_bottom[None, :])).astype(
        jnp.float32
    ) * owning[None, :]
    weights = (
        conductivity_east.reshape(depth_cells, north_cells * east_cells)[:, cells].astype(
            jnp.float32
        )
        * screened
    )
    totals = lax.psum(jnp.sum(weights, axis=0), "layer")
    shares = weights / (totals + (1.0 - owning))[None, :]
    flat_shape = (depth_cells, north_cells * east_cells)
    source = (
        jnp.zeros(flat_shape, jnp.float32)
        .at[:, cells]
        .add(pump_rates[None, :] * shares)
        .reshape(head_old.shape)
    )
    stored = storage.astype(jnp.float32)
    rhs = stored * head_old - source
    head_new = chebyshev(head_old, rhs, operate, keep_whole, precondition)
    departure = head_new - head_target
    misfit_part = jnp.sum(departure * departure)
    all_cells = float(
        depth_cells
        * north_cells
        * east_cells
        * lax.axis_size("east")
        * lax.axis_size("north")
        * lax.axis_size("layer")
    )
    head_part = jnp.sum(shares * head_new.reshape(flat_shape)[:, cells], axis=0)
    head_screen, misfit_total = lax.psum((head_part, misfit_part), ("east", "north", "layer"))
    band_ids = jnp.arange(band_prices.shape[0], dtype=jnp.int32)
    prices = jnp.sum(
        jnp.where(tariff_band[:, None] == band_ids[None, :], band_prices[None, :], 0.0), axis=1
    )
    load = (
        departure.reshape(flat_shape)
        .at[:, cells]
        .add(-(prices * pump_rates)[None, :] * shares)
        .reshape(head_old.shape)
    )
    adjoint_head = chebyshev(None, load, operate, keep_whole, precondition)
    adjoint_part = jnp.sum(shares * adjoint_head.reshape(flat_shape)[:, cells], axis=0)
    adjoint_screen = lax.psum(adjoint_part, ("east", "north", "layer"))
    misfit = misfit_total / all_cells
    lift = ground_level - head_screen
    rate_gradient = prices * lift - adjoint_screen
    pumping_cost = jnp.sum(prices * pump_rates * lift)
    return (head_new, adjoint_head, rate_gradient, pumping_cost, misfit)


def split(value, parts):
    found = []
    for _ in range(parts):
        top = value.astype(BF16)
        found.append(top)
        value = value - top.astype(F32)
    return found


def dot(a, b, dims):
    return lax.dot_general(a, b, (dims, ((), ())), preferred_element_type=F32)


NN = ((1,), (0,))
NT = ((1,), (1,))


def reciprocal(x):
    first = pl.reciprocal(x, approx=True)
    return first * (2.0 - x * first)


def kernel(sizes, *refs):
    n_east, n_x, n_z = sizes
    n_north = n_x * n_z
    fields, well_refs, refs = refs[:6], refs[6:14], refs[14:]
    head_new, adjoint, out_slope, out_sums, out_crowded = refs[:5]
    hx, tx, ke, kn, kv, st, fe, fn, fu, inv, src, lw, d0, d1, s1, pt = refs[5:21]
    parts, staged, (nbs, efs, ebs, cfs), refs = refs[21], refs[22:26], refs[26:30], refs[30:]
    (s_nf, s_nb, s_ef, s_eb, s_cf), refs = refs[:5], refs[5:]
    well_rows, wells, boxes, refs = refs[:8], refs[8], refs[9:13], refs[13:]
    load_sem, send_sem, recv_sem, sum_send, sum_recv = refs
    depth, rows, cols = head_new.shape
    layers, ext_rows, ext_cols = hx.shape
    chunks_of_rows = ext_rows // 8
    groups = wells.shape[1] // LANES
    me_e, me_n, me_l = lax.axis_index("east"), lax.axis_index("north"), lax.axis_index("layer")
    me_x, me_z = me_n // n_z, lax.rem(me_n, n_z)
    own, other = depth * me_l, depth * (1 - me_l)
    own_layers = pl.ds(own, depth)

    def east_of(side):
        return lax.rem(me_e + (n_east - 1 if side == 0 else 1), n_east)

    def north_of(side):
        return lax.rem(me_n + (n_north - 1 if side == 0 else 1), n_north)

    partner = (me_e, me_n, 1 - me_l)
    to_north = [(me_e, north_of(s), me_l) for s in (0, 1)]
    to_east = [(east_of(s), me_n, me_l) for s in (0, 1)]
    to_corner = [(east_of(c), north_of(r), me_l) for r in (0, 1) for c in (0, 1)]
    phases = []
    for box, size, mine, device in (
        (boxes[0], 2, me_l, lambda i: (me_e, me_n, i)),
        (boxes[1], n_z, me_z, lambda i: (me_e, me_x * n_z + i, me_l)),
        (boxes[2], n_east, me_e, lambda i: (i, me_n, me_l)),
        (boxes[3], n_x, me_x, lambda i: (me_e, i * n_z + me_z, me_l)),
    ):
        phases.append((box, mine, [device(lax.rem(mine + k, size)) for k in range(1, size)]))

    z_peers, east_peers, x_peers = (peers for _, _, peers in phases[1:])
    greeted = to_corner + to_north + x_peers + z_peers + east_peers[1:-1] + to_east + [partner]
    barrier = pltpu.get_barrier_semaphore()
    for device in greeted:
        pl.semaphore_signal(barrier, inc=1, device_id=device, device_id_type=MESH)

    loaded = [0]

    def load(src_ref, dst_ref):
        copy = pltpu.make_async_copy(src_ref, dst_ref, load_sem.at[loaded[0]])
        loaded[0] += 1
        copy.start()
        return copy

    lane = iota((8, LANES), 1)
    group = lane // HALO
    wide_sub = iota((8, cols), 0)
    last = cols - LANES
    low_half = lane < LANES // 2
    extra = pl.ds(cols, LANES)
    inside_cols = pl.ds(0, cols)
    inner = pl.ds(8, rows)
    edge_rows = (pl.ds(rows + 8, 8), pl.ds(0, 8))

    block_loads = [
        load(fields[0], hx.at[own_layers, inner, inside_cols]),
        load(fields[1], tx.at[own_layers, inner, inside_cols]),
    ] + [load(fields[2 + a], staged[a].at[own_layers]) for a in range(4)]
    well_loads = [load(a, b) for a, b in zip(well_refs, well_rows)]
    for copy in block_loads:
        copy.wait()

    def pack(z, carry):
        for side in (0, 1):
            c0 = last * side
            kept = jnp.zeros((8, LANES), F32)
            fields = [jnp.zeros((8, LANES), F32) for _ in staged]
            for pair in range(rows // 16):
                tiles = [
                    ref[own + z, pl.ds(16 * pair, 16), pl.ds(c0, LANES)].astype(F32) for ref in staged
                ]
                for half in (0, 1):
                    j = 2 * pair + half
                    shift = HALO * j - (LANES - HALO) * side
                    h = hx[own + z, pl.ds(8 + 8 * j, 8), pl.ds(c0, LANES)]
                    t = tx[own + z, pl.ds(8 + 8 * j, 8), pl.ds(c0, LANES)]
                    if side == 0:
                        both = jnp.where(lane >= HALO - 2, roll(t, HALO - 2, 1), h)
                    else:
                        both = jnp.where(lane < LANES - HALO + 2, roll(t, 2 - HALO, 1), h)
                    here = group == j
                    kept = jnp.where(here, roll(both, shift, 1), kept)
                    for a in range(4):
                        piece = tiles[a][8 * half:8 * half + 8]
                        fields[a] = jnp.where(here, roll(piece, shift, 1), fields[a])
            s_ef[side, z] = kept
            s_eb[side, z, pl.ds(0, 16)] = jnp.concatenate(fields[:2], axis=0).astype(BF16)
            s_eb[side, z, pl.ds(16, 16)] = jnp.concatenate(fields[2:], axis=0).astype(BF16)
            r0 = (rows - 8) * side
            h = hx[own + z, pl.ds(8 + r0, 8), inside_cols]
            t = tx[own + z, pl.ds(8 + r0, 8), inside_cols]
            edge = [
                ref[own + z, pl.ds((rows - 16) * side, 16), :].astype(F32)[8 * side:8 * side + 8]
                for ref in staged
            ]
            if side == 0:
                both = jnp.where(wide_sub == 5, roll(edge[1], 1, 0), h)
                both = jnp.where(wide_sub >= 6, roll(t, 6, 0), both)
                first = jnp.where(wide_sub < 4, edge[0], roll(edge[1], 4, 0))
                second = jnp.where(wide_sub < 4, edge[2], roll(edge[3], 4, 0))
            else:
                both = jnp.where(wide_sub == 2, roll(edge[1], 7, 0), h)
                both = jnp.where(wide_sub < 2, roll(t, 2, 0), both)
                first = jnp.where(wide_sub < 4, roll(edge[0], 4, 0), edge[1])
                second = jnp.where(wide_sub < 4, roll(edge[2], 4, 0), edge[3])
            s_nf[side, z] = both
            s_nb[side, z] = jnp.concatenate([first, second], axis=0).astype(BF16)
        return carry

    lax.fori_loop(0, depth, pack, 0)

    for r in (0, 1):
        for c in (0, 1):
            c0 = last * c
            kept = jnp.zeros((8, LANES), F32)
            mixed = jnp.zeros((8, LANES), F32)
            for z in range(depth):
                both = s_nf[r, z, :, pl.ds(c0, LANES)]
                kept = jnp.where(group == z, roll(both, HALO * z - (LANES - HALO) * c, 1), kept)
                pieces = s_nb[r, z, :, pl.ds(c0, LANES)].astype(F32)
                for half in (0, 1):
                    slot = half * depth + z
                    moved = roll(
                        pieces[8 * half:8 * half + 8], HALO * slot - (LANES - HALO) * c, 1
                    )
                    mixed = jnp.where(group == slot, moved, mixed)
            s_cf[2 * r + c] = jnp.concatenate([kept, mixed], axis=0)

    pl.semaphore_wait(barrier, len(greeted))

    sent = [0]

    def send(src_ref, dst_ref, device):
        copy = pltpu.make_async_remote_copy(
            src_ref=src_ref,
            dst_ref=dst_ref,
            send_sem=send_sem.at[sent[0]],
            recv_sem=recv_sem.at[sent[0]],
            device_id=device,
            device_id_type=MESH,
        )
        sent[0] += 1
        copy.start()
        return copy

    norths, easts, corners = [], [], []
    for side in (0, 1):
        norths.append(send(s_nb.at[side], nbs.at[0, side], to_north[side]))
        norths.append(
            send(s_nf.at[side], hx.at[own_layers, edge_rows[side], inside_cols], to_north[side])
        )
    for d in range(4):
        corners.append(send(s_cf.at[d], cfs.at[0, d], to_corner[d]))
    for side in (0, 1):
        easts.append(send(s_eb.at[side], ebs.at[0, side], to_east[side]))
        easts.append(send(s_ef.at[side], efs.at[0, side], to_east[side]))
    two = (depth - 2) * (1 - me_l)
    blocks = [send(fields[2 + a], staged[a].at[own_layers], partner) for a in range(4)]
    blocks.append(send(fields[0], hx.at[own_layers, inner, inside_cols], partner))
    blocks.append(
        send(
            fields[1].at[pl.ds(two, 2)], tx.at[pl.ds(own + two, 2), inner, inside_cols], partner
        )
    )

    for copy in well_loads:
        copy.wait()
    wells[...] = jnp.full(wells.shape, -1e6, F32)
    width = pl.ds(0, well_rows[0].shape[1])
    for row, ref in enumerate(well_rows[:5]):
        wells[pl.ds(row, 1), width] = ref[...].astype(F32)
    band = well_rows[5][...]
    bands = well_rows[7][...]
    price = jnp.zeros(band.shape, F32)
    for b in range(bands.shape[1]):
        price = jnp.where(band == b, bands[0:1, b:b + 1], price)
    wells[pl.ds(5, 1), width] = price
    wells[pl.ds(6, 1), width] = well_rows[6][...]

    at_east = wells[0:1, :] - (me_e * cols).astype(F32)
    at_north = wells[1:2, :] - (me_n * rows).astype(F32)
    near = (
        (at_east >= -REACH) & (at_east < cols + REACH)
        & (at_north >= -REACH) & (at_north < rows + REACH)
    )
    mine = (at_east >= 0) & (at_east < cols) & (at_north >= 0) & (at_north < rows)
    near_row = jnp.where(near, 1.0, 0.0)
    near_tile = jnp.concatenate(
        [near_row[:, LANES * k:LANES * (k + 1)] for k in range(groups)], axis=0
    )
    before = (iota((LANES, LANES), 0) < iota((LANES, LANES), 1)).astype(F32).astype(BF16)
    in_row = dot(near_tile.astype(BF16), before, NN)
    above = (iota((groups, groups), 1) < iota((groups, groups), 0)).astype(F32).astype(BF16)
    rows_above = jnp.sum(dot(above, near_tile.astype(BF16), NN), axis=1, keepdims=True)
    rank = jnp.where(near_tile > 0, in_row + rows_above, -1.0)
    found = jnp.sum(jnp.sum(near_tile, axis=1, keepdims=True), axis=0, keepdims=True)
    crowded = jnp.where(found > SLOTS, 1.0, 0.0)

    place = jnp.concatenate(
        [
            jnp.where(at_east < 0, at_east + ext_cols, at_east),
            at_north + 8.0,
            wells[2:7, :],
            jnp.where(mine, 1.0, 0.0),
        ],
        axis=0,
    )
    place_parts = jnp.concatenate([p.astype(F32) for p in split(place, 3)], axis=0).astype(BF16)
    slot_of = iota((SLOTS, LANES), 0).astype(F32)

    for k in range(groups):
        pt[:, pl.ds(LANES * k, LANES)] = jnp.where(slot_of == rank[k:k + 1, :], 1.0, 0.0).astype(BF16)
    three = dot(place_parts, pt[...], NT)
    comp = three[0:8] + three[8:16] + three[16:24]
    col_hot = jnp.where(iota((ext_cols, SLOTS), 0).astype(F32) == comp[0:1], 1.0, 0.0)
    row_hot = jnp.where(iota((ext_rows, SLOTS), 0).astype(F32) == comp[1:2], 1.0, 0.0)
    col_hot = col_hot.astype(BF16)


    def fill_inner(base):
        def fill(z, carry):
            for dst, ref in zip((ke, kn, kv, st), staged):
                dst[base + z, inner, inside_cols] = ref[base + z].astype(F32)
            return carry

        lax.fori_loop(0, depth, fill, 0)

    def fill_east(who, base):
        def fill(z, carry):
            zz = base + z
            right, left = efs[who, 0, z], efs[who, 1, z]
            for j in range(rows // 8):
                both = jnp.where(
                    low_half, roll(right, -HALO * j, 1), roll(left, LANES - HALO - HALO * j, 1)
                )
                hx[zz, pl.ds(8 + 8 * j, 8), extra] = both
                tx[zz, pl.ds(8 + 8 * j, 8), extra] = jnp.where(
                    low_half, roll(both, 2 - HALO, 1), roll(both, HALO - 2, 1)
                )
            for half, pair in ((0, (ke, kn)), (1, (kv, st))):
                rights = ebs[who, 0, z, pl.ds(16 * half, 16)].astype(F32)
                lefts = ebs[who, 1, z, pl.ds(16 * half, 16)].astype(F32)
                for k in (0, 1):
                    right, left = rights[8 * k:8 * k + 8], lefts[8 * k:8 * k + 8]
                    for j in range(rows // 8):
                        pair[k][zz, pl.ds(8 + 8 * j, 8), extra] = jnp.where(
                            low_half,
                            roll(right, -HALO * j, 1),
                            roll(left, LANES - HALO - HALO * j, 1),
                        )
            return carry

        lax.fori_loop(0, depth, fill, 0)

    def put_rows(side, zz, at_rows, at_cols, both, first, second):
        row = iota(both.shape, 0)
        if side == 0:
            tx[zz, at_rows, at_cols] = roll(both, 2, 0)
            ke[zz, at_rows, at_cols] = first
            kn[zz, at_rows, at_cols] = jnp.where(row == 4, roll(both, 7, 0), roll(first, 4, 0))
            kv[zz, at_rows, at_cols] = second
            st[zz, at_rows, at_cols] = roll(second, 4, 0)
        else:
            tx[zz, at_rows, at_cols] = roll(both, 6, 0)
            ke[zz, at_rows, at_cols] = roll(first, 4, 0)
            kn[zz, at_rows, at_cols] = jnp.where(row == 3, roll(both, 1, 0), first)
            kv[zz, at_rows, at_cols] = roll(second, 4, 0)
            st[zz, at_rows, at_cols] = second

    def fill_north(who, base):
        def fill(z, carry):
            for side, at_rows in enumerate(edge_rows):
                pieces = nbs[who, side, z].astype(F32)
                both = hx[base + z, at_rows, inside_cols]
                put_rows(side, base + z, at_rows, inside_cols, both, pieces[:8], pieces[8:])
            return carry

        lax.fori_loop(0, depth, fill, 0)

    def fill_corners(who, base):
        for side, at_rows in enumerate(edge_rows):
            right, rights = cfs[who, 2 * side, :8], cfs[who, 2 * side, 8:]
            left, lefts = cfs[who, 2 * side + 1, :8], cfs[who, 2 * side + 1, 8:]

            def taken(a, b, slot):
                return jnp.where(
                    low_half, roll(a, -HALO * slot, 1), roll(b, LANES - HALO - HALO * slot, 1)
                )

            for z in range(depth):
                both = taken(right, left, z)
                hx[base + z, at_rows, extra] = both
                put_rows(
                    side, base + z, at_rows, extra, both,
                    taken(rights, lefts, z), taken(rights, lefts, depth + z),
                )

    wide = (8, ext_cols)
    sub = iota(wide, 0)
    col = iota(wide, 1)
    closed_col = ((col == cols - 1) & (me_e == n_east - 1)) | ((col == ext_cols - 1) & (me_e == 0))
    open_east = jnp.where(closed_col, 0.0, 2.0)

    def east(v):
        return roll(v, ext_cols - 1, 1)

    def west(v):
        return roll(v, 1, 1)

    def north(now, after):
        return jnp.where(sub < 7, roll(now, 7, 0), roll(after, 7, 0))

    def south(now, prior):
        return jnp.where(sub > 0, roll(now, 1, 0), roll(prior, 1, 0))

    fu[0] = jnp.zeros((ext_rows, ext_cols), F32)
    fu[layers] = jnp.zeros((ext_rows, ext_cols), F32)

    def at(j):
        return pl.ds(8 * j if isinstance(j, int) else pl.multiple_of(8 * j, 8), 8)

    def next_of(j):
        return min(j + 1, chunks_of_rows - 1) if isinstance(j, int) else jnp.minimum(j + 1, chunks_of_rows - 1)

    def layer_of(k):
        return jnp.where(me_l == 0, k, layers - 1 - k)

    def start(first, count, with_wells):
        zs = [layer_of(first + i) for i in range(count)]
        above = layer_of(jnp.minimum(first + count, layers - 1))
        below = layer_of(jnp.maximum(first - 1, 0))
        opens = [jnp.where(first + i < layers - 1, 2.0, 0.0) for i in range(count)]

        def chunk(j, carry):
            f_priors, g_priors, k_now, h_now = carry
            k_ups = [kv[z, at(j)] for z in zs] + [kv[above, at(j)]]
            heads = h_now + [hx[above, at(j)]]
            edge = ((j == 0) & (me_n == 0)) | ((j == chunks_of_rows - 2) & (me_n == n_north - 1))
            opened = jnp.where((sub == 7) & edge, 0.0, 2.0)
            f_d = fu[zs[0] + me_l, at(j)]
            g_d = f_d * (h_now[0] - hx[below, at(j)])
            faces, flows, k_after, h_after = [], [], [], []
            for i, z in enumerate(zs):
                k_e, k_n, h = ke[z, at(j)], k_now[i], h_now[i]
                k_after.append(kn[z, at(next_of(j))])
                h_after.append(hx[z, at(next_of(j))])
                k_e2 = east(k_e)
                k_n2 = north(k_n, k_after[i])
                f_e = open_east * k_e * k_e2 * reciprocal(k_e + k_e2)
                f_n = opened * k_n * k_n2 * reciprocal(k_n + k_n2)
                f_u = opens[i] * k_ups[i] * k_ups[i + 1] * reciprocal(k_ups[i] + k_ups[i + 1])
                fe[z, at(j)] = f_e
                fn[z, at(j)] = f_n
                fu[z + 1 - me_l, at(j)] = f_u
                diagonal = st[z, at(j)] + f_e + west(f_e) + f_n + south(f_n, f_priors[i]) + f_u + f_d
                inverse = reciprocal(diagonal)
                inv[z, at(j)] = inverse
                g_e = f_e * (east(h) - h)
                g_n = f_n * (north(h, h_after[i]) - h)
                g_u = f_u * (heads[i + 1] - h)
                residual = (g_e - west(g_e)) + (g_n - south(g_n, g_priors[i])) + (g_u - g_d)
                if with_wells:
                    residual = residual - src[z, at(j)]
                d0[z, at(j)] = inverse * residual
                faces.append(f_n)
                flows.append(g_n)
                f_d, g_d = f_u, g_u
            return faces, flows, k_after, h_after

        def several(i, carry):
            for m in range(START_UNIT):
                carry = chunk(i * START_UNIT + m, carry)
            return carry

        none = [jnp.zeros(wide, F32)] * count
        carry = (none, none, [kn[z, at(0)] for z in zs], [hx[z, at(0)] for z in zs])
        lax.fori_loop(0, chunks_of_rows // START_UNIT, several, carry)

    def start_layers(begin, end, with_wells):
        def some(i, carry):
            start(begin + START_LAYERS * i, START_LAYERS, with_wells)
            return carry

        whole = (end - begin) // START_LAYERS
        lax.fori_loop(0, whole, some, 0)
        if begin + whole * START_LAYERS < end:
            start(begin + whole * START_LAYERS, end - begin - whole * START_LAYERS, with_wells)

    def pump(k, carry):
        z = layer_of(k)
        d0[z] = d0[z] - inv[z] * src[z]
        return carry

    fill_inner(own)
    for copy in easts:
        copy.wait_recv()
    forwards = [send(efs.at[0], efs.at[1], partner), send(ebs.at[0], ebs.at[1], partner)]
    fill_east(0, own)
    for copy in norths:
        copy.wait_recv()
    forwards.append(send(nbs.at[0], nbs.at[1], partner))
    for side in (0, 1):
        place_of = hx.at[own_layers, edge_rows[side], inside_cols]
        forwards.append(send(place_of, place_of, partner))
    for copy in corners:
        copy.wait_recv()
    forwards.append(send(cfs.at[0], cfs.at[1], partner))
    fill_north(0, own)
    fill_corners(0, own)
    start_layers(0, depth - 1, False)
    for copy in blocks:
        copy.wait_recv()
    fill_inner(other)
    for copy in forwards:
        copy.wait_recv()
    fill_east(1, other)
    fill_north(1, other)
    fill_corners(1, other)
    for copy in norths + easts + corners + blocks + forwards:
        copy.wait_send()

    weights = []
    for z in range(layers):
        found = dot(ke[z].astype(BF16), col_hot, NN)
        k_at = jnp.sum(found * row_hot, axis=0, keepdims=True)
        screened = (comp[2:3] <= z) & (comp[3:4] >= z)
        weights.append(jnp.where(screened, k_at, 0.0))
    weight = jnp.concatenate(weights, axis=0)
    total = jnp.sum(weight, axis=0, keepdims=True)
    share = weight / jnp.where(total > 0, total, 1.0)
    pumped = share * comp[4:5]
    priced = pumped * comp[5:6]
    col_two = jnp.concatenate([col_hot, col_hot], axis=1)
    for z in range(layers):
        left = []
        for value in (pumped, priced):
            top, rest = split(value[z:z + 1], 2)
            left.append(
                jnp.concatenate([row_hot * top.astype(F32), row_hot * rest.astype(F32)], axis=1)
            )
        left = jnp.concatenate(left, axis=0).astype(BF16)
        field = dot(left, col_two, NT)
        src[z] = field[:ext_rows]
        lw[z] = field[ext_rows:]

    lax.fori_loop(0, depth - 1, pump, 0)
    start_layers(depth - 1, layers, True)

    def sweep(field, margin, finish, chunk_from, chunk_to):
        first = (depth - margin) * me_l

        def together(i, count):
            zs = [first + i + k for k in range(count)]
            below = jnp.maximum(zs[0] - 1, 0)
            above = jnp.minimum(zs[-1] + 1, layers - 1)
            if chunk_from == 0:
                priors = [jnp.zeros(wide, F32)] * count
            else:
                before = at(chunk_from - 1)
                priors = [fn[z, before] * field[z, before] for z in zs]
            now = [field[z, at(chunk_from)] for z in zs]
            for j in range(chunk_from, chunk_to):
                after = [field[z, at(min(j + 1, chunks_of_rows - 1))] for z in zs]
                stack = [field[below, at(j)]] + now + [field[above, at(j)]]
                for k, z in enumerate(zs):
                    d = now[k]
                    f_e, f_n = fe[z, at(j)], fn[z, at(j)]
                    b = f_n * d
                    moved = f_e * east(d) + west(f_e * d)
                    moved = moved + f_n * north(d, after[k]) + south(b, priors[k])
                    moved = moved + fu[z + 1, at(j)] * stack[k + 2] + fu[z, at(j)] * stack[k]
                    finish(i + k, z, j, d, inv[z, at(j)] * moved)
                    priors[k] = b
                now = after

        def some(i, carry):
            together(SWEEP_LAYERS * i, SWEEP_LAYERS)
            return carry

        total = depth + margin
        lax.fori_loop(0, total // SWEEP_LAYERS, some, 0)
        if total % SWEEP_LAYERS:
            together(total - total % SWEEP_LAYERS, total % SWEEP_LAYERS)

    (a1, b1), (a2, b2) = steps_of()

    def first_sweep(i, z, j, d, pulled):
        s1[z, at(j)] = pulled
        d1[z, at(j)] = a1 * d + b1 * pulled

    def end_forward(i, z, j, d, pulled):
        s2 = s1[z, at(j)] - d + pulled
        d2 = a2 * d + b2 * s2
        new = hx[z, at(j)] + d0[z, at(j)] + d + d2
        hx[z, at(j)] = new
        load = new - tx[z, at(j)] - lw[z, at(j)]
        src[z, at(j)] = inv[z, at(j)] * load

    sweep(d0, 3, first_sweep, 0, chunks_of_rows)
    sweep(d1, 2, end_forward, 0, chunks_of_rows)
    sweep(src, 1, first_sweep, 0, chunks_of_rows)

    st[0, at(0)] = jnp.zeros(wide, F32)

    def end_adjoint(i, z, j, d, pulled):
        s2 = s1[z, at(j)] - d + pulled
        d2 = a2 * d + b2 * s2
        adj = src[z, at(j)] + d + d2
        adjoint[i, at(j - 1)] = adj[:, :cols]
        new = hx[z, at(j), inside_cols]
        head_new[i, at(j - 1)] = new
        departure = new - tx[z, at(j), inside_cols]
        st[0, at(0), inside_cols] = st[0, at(0), inside_cols] + departure * departure

    sweep(d1, 0, end_adjoint, 1, chunks_of_rows - 1)

    squared = st[0, at(0), inside_cols]
    squared = jnp.sum(squared, axis=0, keepdims=True)
    squared = sum(squared[:, LANES * k:LANES * (k + 1)] for k in range(cols // LANES))
    squared = squared * (1.0 / (float(layers * rows * cols) * n_east * n_north))
    base_layer = jnp.where(me_l == 0, 1.0, 0.0)

    col_hot, row_hot = col_hot[:cols], row_hot[8:8 + rows]
    head_at = jnp.zeros((1, SLOTS), F32)
    adj_at = jnp.zeros((1, SLOTS), F32)
    for i in range(depth):
        z_share = jnp.where(me_l == 0, share[i:i + 1], share[depth + i:depth + i + 1])
        stack = split(head_new[i], 2) + split(adjoint[i], 2)
        found = [dot(piece, col_hot, NN) for piece in stack]
        head_at += z_share * jnp.sum((found[0] + found[1]) * row_hot, axis=0, keepdims=True)
        adj_at += z_share * jnp.sum((found[2] + found[3]) * row_hot, axis=0, keepdims=True)
    lift = (comp[6:7] * base_layer - head_at) * comp[7:8]
    priced = comp[5:6] * lift
    slope = priced - adj_at * comp[7:8]
    three = jnp.concatenate(
        [p.astype(F32) for p in split(slope, 3)] + [jnp.zeros((5, SLOTS), F32)], axis=0
    ).astype(BF16)
    spread = dot(three, pt[...], NN)
    spread = spread[0:1] + spread[1:2] + spread[2:3]
    tile = jnp.concatenate(
        [spread[:, LANES * k:LANES * (k + 1)] for k in range(groups)], axis=0
    )
    parts[pl.ds(0, groups)] = tile
    parts[pl.ds(groups, 8)] = jnp.concatenate(
        [
            priced * comp[4:5],
            squared,
            jnp.broadcast_to(crowded, (1, LANES)),
            jnp.zeros((5, LANES), F32),
        ],
        axis=0,
    )

    total = parts[...]
    used = 0
    for box, mine, peers in phases:
        box[mine] = total
        copies = []
        for device in peers:
            copy = pltpu.make_async_remote_copy(
                src_ref=box.at[mine],
                dst_ref=box.at[mine],
                send_sem=sum_send.at[used],
                recv_sem=sum_recv.at[used],
                device_id=device,
                device_id_type=MESH,
            )
            copy.start()
            copies.append(copy)
            used += 1
        for copy in copies:
            copy.wait()
        total = box[0]
        for k in range(1, len(peers) + 1):
            total = total + box[k]
    n_wells = out_slope.shape[1]
    for k in range(groups):
        width = min(LANES, n_wells - LANES * k)
        out_slope[:, pl.ds(LANES * k, width)] = total[k:k + 1, :width]
    sums = jnp.sum(total[groups:], axis=1, keepdims=True)
    out_sums[...] = jnp.broadcast_to(sums, out_sums.shape)
    out_crowded[...] = sums[2:3]


def run_kernel(sizes, fields, wells):
    depth, rows, cols = fields[0].shape
    layers, ext_rows, ext_cols = 2 * depth, rows + 16, cols + LANES
    n_wells = wells[0].shape[1]
    groups = -(-n_wells // LANES)
    n_east, n_x, n_z = sizes
    block = pltpu.VMEM((depth, rows, cols), F32)
    ext = pltpu.VMEM((layers, ext_rows, ext_cols), F32)
    operands = (*fields, *wells)
    copies = 4 + 4 + 4 + 6 + 6
    peers = 1 + n_z + n_east + n_x - 3
    return pl.pallas_call(
        functools.partial(kernel, sizes),
        out_shape=[
            block, block, pltpu.VMEM((1, n_wells), F32), pltpu.VMEM((8, LANES), F32),
            jax.ShapeDtypeStruct((1, 1), F32),
        ],
        in_specs=[pl.BlockSpec(memory_space=pltpu.HBM)] * len(operands),
        out_specs=[pl.BlockSpec(memory_space=pltpu.VMEM)] * 5,
        scratch_shapes=[ext] * 8
        + [pltpu.VMEM((layers + 1, ext_rows, ext_cols), F32)]
        + [ext] * 6
        + [pltpu.VMEM((SLOTS, groups * LANES), BF16)]
        + [pltpu.VMEM((groups + 8, LANES), F32)]
        + [pltpu.VMEM((layers, rows, cols), BF16)] * 4
        + [
            pltpu.VMEM((2, 2, depth, 16, cols), BF16),
            pltpu.VMEM((2, 2, depth, 8, LANES), F32),
            pltpu.VMEM((2, 2, depth, 32, LANES), BF16),
            pltpu.VMEM((2, 4, 16, LANES), F32),
            pltpu.VMEM((2, depth, 8, cols), F32),
            pltpu.VMEM((2, depth, 16, cols), BF16),
            pltpu.VMEM((2, depth, 8, LANES), F32),
            pltpu.VMEM((2, depth, 32, LANES), BF16),
            pltpu.VMEM((4, 16, LANES), F32),
        ]
        + [pltpu.VMEM(w.shape, w.dtype) for w in wells]
        + [pltpu.VMEM((8, groups * LANES), F32)]
        + [pltpu.VMEM((n, groups + 8, LANES), F32) for n in (2, n_z, n_east, n_x)]
        + [pltpu.SemaphoreType.DMA((14,))]
        + [pltpu.SemaphoreType.DMA((copies,))] * 2
        + [pltpu.SemaphoreType.DMA((peers,))] * 2,
        compiler_params=pltpu.CompilerParams(
            collective_id=0, has_side_effects=True, vmem_limit_bytes=60 * 1024 * 1024
        ),
        name="whole_step",
    )(*operands)


def hand_over(new, adjoint, slope, sums, o_new, o_adjoint, o_slope, o_cost, o_misfit, cost, misfit, sem):
    cost[...] = sums[0:1, 0:1]
    misfit[...] = sums[1:2, 0:1]
    copies = [
        pltpu.make_async_copy(src_ref, dst_ref, sem.at[k])
        for k, (src_ref, dst_ref) in enumerate((
            (new, o_new), (adjoint, o_adjoint), (slope, o_slope), (cost, o_cost), (misfit, o_misfit),
        ))
    ]
    for copy in copies:
        copy.start()
    for copy in copies:
        copy.wait()


def run_hand_over(new, adjoint, slope, sums):
    block = jax.ShapeDtypeStruct(new.shape, F32)
    one = jax.ShapeDtypeStruct((1, 1), F32)
    return pl.pallas_call(
        hand_over,
        out_shape=[block, block, jax.ShapeDtypeStruct(slope.shape, F32), one, one],
        in_specs=[pl.BlockSpec(memory_space=pltpu.VMEM)] * 4,
        out_specs=[pl.BlockSpec(memory_space=pltpu.HBM)] * 5,
        scratch_shapes=[pltpu.VMEM((1, 1), F32)] * 2 + [pltpu.SemaphoreType.DMA((5,))],
        compiler_params=pltpu.CompilerParams(vmem_limit_bytes=8 * 1024 * 1024),
        name="hand_over",
    )(new, adjoint, slope, sums)


def in_order(value):
    return with_layout_constraint(value, Layout(major_to_minor=(0, 1, 2)))


def per_device(sizes, *arguments):
    fields = arguments[:6]
    e, n, top, bottom, tariff, rates, ground, prices = arguments[6:]
    wells = [w.reshape(1, -1) for w in (e, n, top, bottom, rates, tariff, ground, prices)]
    *results, crowded = run_kernel(sizes, fields, wells)
    found = tuple(run_hand_over(*results))

    def again(state):
        blocks = [in_order(x) for x in fields]
        first, second, *others = plain(*blocks, *arguments[6:])
        others = [x.reshape(1, -1) for x in others]
        return jnp.zeros((), F32), (in_order(first), in_order(second), *others)

    _, found = lax.while_loop(lambda state: state[0] > 0, again, (crowded.reshape(()), found))
    new, adjoint, slope, cost, misfit = found
    return new, adjoint, slope.reshape(-1), cost.reshape(()), misfit.reshape(())


def solution(mesh):
    field = P("layer", "north", "east")
    n_north = mesh.shape["north"]
    n_x = 4 if n_north % 4 == 0 else 1
    sizes = (mesh.shape["east"], n_x, n_north // n_x)
    return jax.shard_map(
        functools.partial(per_device, sizes),
        mesh=mesh,
        in_specs=(field,) * 6 + (P(),) * 8,
        out_specs=(field, field, P(), P(), P()),
        check_vma=False,
    )
```

```python
import functools

import jax
import jax.numpy as jnp
from jax import lax
from jax.experimental import pallas as pl
from jax.experimental.layout import Layout, with_layout_constraint
from jax.experimental.pallas import tpu as pltpu
from jax.sharding import PartitionSpec as P

MESH = pl.DeviceIdType.MESH
F32 = jnp.float32
BF16 = jnp.bfloat16

SWEEPS = 3
CENTRE = 1.0
HALF_WIDTH = 0.95

HALO = 8
REACH = 5
LANES = 128
SLOTS = 128
START_UNIT, START_LAYERS = 9, 1
SWEEP_LAYERS = 4


def steps_of():
    sigma = CENTRE / HALF_WIDTH
    factor = 1.0 / sigma
    found = []
    for _ in range(SWEEPS - 1):
        after = 1.0 / (2.0 * sigma - factor)
        found.append((after * factor, 2.0 * after / HALF_WIDTH))
        factor = after
    return found


def iota(shape, dim):
    return lax.broadcasted_iota(jnp.int32, shape, dim)


def roll(value, shift, dim):
    shift = shift % value.shape[dim]
    return pltpu.roll(value, shift, dim) if shift else value


def extended(value, sides, width):
    for axis, dim in sides:
        size, length = (lax.axis_size(axis), value.shape[dim])
        up = [(i, (i + 1) % size) for i in range(size - 1)]
        down = [(j, i) for i, j in up]
        last = lax.slice_in_dim(value, length - width, length, axis=dim)
        initial = lax.slice_in_dim(value, 0, width, axis=dim)
        before = lax.ppermute(last, axis, up)
        after = lax.ppermute(initial, axis, down)
        value = jnp.concatenate([before, value, after], axis=dim)
    return value


def harmonic(first, second):
    total = first + second
    return 2.0 * first * second / jnp.where(total > 0, total, 1.0)


def face_terms(east_pad, north_pad, up_pad, stored):
    face_east = harmonic(east_pad[:, :, :-1], east_pad[:, :, 1:])
    face_north = harmonic(north_pad[:, :-1], north_pad[:, 1:])
    face_up = harmonic(up_pad[:-1], up_pad[1:])
    diagonal = stored + face_east[:, :, :-1] + face_east[:, :, 1:]
    diagonal = diagonal + face_north[:, :-1] + face_north[:, 1:]
    diagonal = diagonal + face_up[:-1] + face_up[1:]
    positive = diagonal > 0
    inverse = jnp.where(positive, 1.0 / jnp.where(positive, diagonal, 1.0), 0.0)
    return (stored, face_east, face_north, face_up, inverse)


def coefficients(padded_coefs):
    stacked = padded_coefs.astype(jnp.float32)
    east_pad = stacked[0][1:-1, 1:-1, :]
    north_pad = stacked[1][1:-1, :, 1:-1]
    up_pad = stacked[2][:, 1:-1, 1:-1]
    stored = stacked[3][1:-1, 1:-1, 1:-1]
    return face_terms(east_pad, north_pad, up_pad, stored)


def apply_operator(padded, storage_part, face_east, face_north, face_up):
    center = padded[1:-1, 1:-1, 1:-1]
    step_east = padded[1:-1, 1:-1, 1:] - padded[1:-1, 1:-1, :-1]
    step_north = padded[1:-1, 1:, 1:-1] - padded[1:-1, :-1, 1:-1]
    step_up = padded[1:, 1:-1, 1:-1] - padded[:-1, 1:-1, 1:-1]
    flux_east = face_east * step_east
    flux_north = face_north * step_north
    flux_up = face_up * step_up
    total = storage_part * center + (flux_east[:, :, :-1] - flux_east[:, :, 1:])
    total = total + (flux_north[:, :-1] - flux_north[:, 1:])
    return total + (flux_up[:-1] - flux_up[1:])


def keep_whole(field):
    return field


def chebyshev(start, rhs, operate, trim, precondition):
    if start is None:
        residual = rhs
    else:
        residual = trim(rhs) - operate(start)
    direction = precondition(residual) / CENTRE
    if start is None:
        iterate = direction
    else:
        iterate = trim(start) + direction
    sigma = CENTRE / HALF_WIDTH
    factor = 1.0 / sigma
    for sweep_index in range(SWEEPS - 1):
        residual = trim(residual) - operate(direction)
        factor_next = 1.0 / (2.0 * sigma - factor)
        direction = factor_next * factor * trim(
            direction
        ) + 2.0 * factor_next / HALF_WIDTH * precondition(residual)
        iterate = trim(iterate) + direction
        factor = factor_next
    return iterate


def plain(
    head_old,
    head_target,
    conductivity_east,
    conductivity_north,
    conductivity_vertical,
    storage,
    well_east,
    well_north,
    screen_top,
    screen_bottom,
    tariff_band,
    pump_rates,
    ground_level,
    band_prices,
):
    depth_cells, north_cells, east_cells = head_old.shape
    stacked_coefs = jnp.stack(
        (conductivity_east, conductivity_north, conductivity_vertical, storage)
    )
    padded_coefs = extended(stacked_coefs, (("east", 3), ("north", 2), ("layer", 1)), 1)
    margin = 0
    top_level = coefficients(padded_coefs)
    levels = [None] * (margin + 1)
    levels[margin] = top_level

    def margin_of(field):
        return (field.shape[0] - depth_cells) // 2

    def precondition(residual):
        return levels[margin_of(residual)][4] * residual

    def operate(field):
        padded = extended(field, (("east", 2), ("north", 1), ("layer", 0)), 1)
        level = levels[0]
        return apply_operator(padded, level[0], level[1], level[2], level[3])

    east_start = lax.axis_index("east") * east_cells
    north_start = lax.axis_index("north") * north_cells
    layer_start = lax.axis_index("layer") * depth_cells
    local_east = well_east - east_start
    local_north = well_north - north_start
    owning = (
        (local_east >= 0)
        & (local_east < east_cells)
        & (local_north >= 0)
        & (local_north < north_cells)
    ).astype(jnp.float32)
    cells = jnp.clip(local_north, 0, north_cells - 1) * east_cells + jnp.clip(
        local_east, 0, east_cells - 1
    )
    depth = layer_start + jnp.arange(depth_cells, dtype=jnp.int32)[:, None]
    screened = ((depth >= screen_top[None, :]) & (depth <= screen_bottom[None, :])).astype(
        jnp.float32
    ) * owning[None, :]
    weights = (
        conductivity_east.reshape(depth_cells, north_cells * east_cells)[:, cells].astype(
            jnp.float32
        )
        * screened
    )
    totals = lax.psum(jnp.sum(weights, axis=0), "layer")
    shares = weights / (totals + (1.0 - owning))[None, :]
    flat_shape = (depth_cells, north_cells * east_cells)
    source = (
        jnp.zeros(flat_shape, jnp.float32)
        .at[:, cells]
        .add(pump_rates[None, :] * shares)
        .reshape(head_old.shape)
    )
    stored = storage.astype(jnp.float32)
    rhs = stored * head_old - source
    head_new = chebyshev(head_old, rhs, operate, keep_whole, precondition)
    departure = head_new - head_target
    misfit_part = jnp.sum(departure * departure)
    all_cells = float(
        depth_cells
        * north_cells
        * east_cells
        * lax.axis_size("east")
        * lax.axis_size("north")
        * lax.axis_size("layer")
    )
    head_part = jnp.sum(shares * head_new.reshape(flat_shape)[:, cells], axis=0)
    head_screen, misfit_total = lax.psum((head_part, misfit_part), ("east", "north", "layer"))
    band_ids = jnp.arange(band_prices.shape[0], dtype=jnp.int32)
    prices = jnp.sum(
        jnp.where(tariff_band[:, None] == band_ids[None, :], band_prices[None, :], 0.0), axis=1
    )
    load = (
        departure.reshape(flat_shape)
        .at[:, cells]
        .add(-(prices * pump_rates)[None, :] * shares)
        .reshape(head_old.shape)
    )
    adjoint_head = chebyshev(None, load, operate, keep_whole, precondition)
    adjoint_part = jnp.sum(shares * adjoint_head.reshape(flat_shape)[:, cells], axis=0)
    adjoint_screen = lax.psum(adjoint_part, ("east", "north", "layer"))
    misfit = misfit_total / all_cells
    lift = ground_level - head_screen
    rate_gradient = prices * lift - adjoint_screen
    pumping_cost = jnp.sum(prices * pump_rates * lift)
    return (head_new, adjoint_head, rate_gradient, pumping_cost, misfit)


def split(value, parts):
    found = []
    for _ in range(parts):
        top = value.astype(BF16)
        found.append(top)
        value = value - top.astype(F32)
    return found


def dot(a, b, dims):
    return lax.dot_general(a, b, (dims, ((), ())), preferred_element_type=F32)


NN = ((1,), (0,))
NT = ((1,), (1,))


def reciprocal(x):
    first = pl.reciprocal(x, approx=True)
    return first * (2.0 - x * first)


def kernel(sizes, *refs):
    n_east, n_x, n_z = sizes
    n_north = n_x * n_z
    fields, well_refs, refs = refs[:6], refs[6:14], refs[14:]
    head_new, adjoint, out_slope, out_sums, out_crowded = refs[:5]
    hx, tx, ke, kn, kv, st, fe, fn, fu, inv, src, lw, d0, d1, s1, pt = refs[5:21]
    parts, staged, (nbs, efs, ebs, cfs), refs = refs[21], refs[22:26], refs[26:30], refs[30:]
    (s_nf, s_nb, s_ef, s_eb, s_cf), refs = refs[:5], refs[5:]
    well_rows, wells, boxes, refs = refs[:8], refs[8], refs[9:13], refs[13:]
    load_sem, send_sem, recv_sem, sum_send, sum_recv = refs
    depth, rows, cols = head_new.shape
    layers, ext_rows, ext_cols = hx.shape
    chunks_of_rows = ext_rows // 8
    groups = wells.shape[1] // LANES
    me_e, me_n, me_l = lax.axis_index("east"), lax.axis_index("north"), lax.axis_index("layer")
    me_x, me_z = me_n // n_z, lax.rem(me_n, n_z)
    own, other = depth * me_l, depth * (1 - me_l)
    own_layers = pl.ds(own, depth)

    def east_of(side):
        return lax.rem(me_e + (n_east - 1 if side == 0 else 1), n_east)

    def north_of(side):
        return lax.rem(me_n + (n_north - 1 if side == 0 else 1), n_north)

    partner = (me_e, me_n, 1 - me_l)
    to_north = [(me_e, north_of(s), me_l) for s in (0, 1)]
    to_east = [(east_of(s), me_n, me_l) for s in (0, 1)]
    to_corner = [(east_of(c), north_of(r), me_l) for r in (0, 1) for c in (0, 1)]
    phases = []
    for box, size, mine, device in (
        (boxes[0], 2, me_l, lambda i: (me_e, me_n, i)),
        (boxes[1], n_z, me_z, lambda i: (me_e, me_x * n_z + i, me_l)),
        (boxes[2], n_east, me_e, lambda i: (i, me_n, me_l)),
        (boxes[3], n_x, me_x, lambda i: (me_e, i * n_z + me_z, me_l)),
    ):
        phases.append((box, mine, [device(lax.rem(mine + k, size)) for k in range(1, size)]))

    z_peers, east_peers, x_peers = (peers for _, _, peers in phases[1:])
    greeted = to_corner + to_north + x_peers + z_peers + east_peers[1:-1] + to_east + [partner]
    barrier = pltpu.get_barrier_semaphore()
    for device in greeted:
        pl.semaphore_signal(barrier, inc=1, device_id=device, device_id_type=MESH)

    loaded = [0]

    def load(src_ref, dst_ref):
        copy = pltpu.make_async_copy(src_ref, dst_ref, load_sem.at[loaded[0]])
        loaded[0] += 1
        copy.start()
        return copy

    lane = iota((8, LANES), 1)
    group = lane // HALO
    wide_sub = iota((8, cols), 0)
    last = cols - LANES
    low_half = lane < LANES // 2
    extra = pl.ds(cols, LANES)
    inside_cols = pl.ds(0, cols)
    inner = pl.ds(8, rows)
    edge_rows = (pl.ds(rows + 8, 8), pl.ds(0, 8))

    block_loads = [
        load(fields[0], hx.at[own_layers, inner, inside_cols]),
        load(fields[1], tx.at[own_layers, inner, inside_cols]),
    ] + [load(fields[2 + a], staged[a].at[own_layers]) for a in range(4)]
    well_loads = [load(a, b) for a, b in zip(well_refs, well_rows)]
    for copy in block_loads:
        copy.wait()

    def pack(z, carry):
        for side in (0, 1):
            c0 = last * side
            kept = jnp.zeros((8, LANES), F32)
            fields = [jnp.zeros((8, LANES), F32) for _ in staged]
            for pair in range(rows // 16):
                tiles = [
                    ref[own + z, pl.ds(16 * pair, 16), pl.ds(c0, LANES)].astype(F32) for ref in staged
                ]
                for half in (0, 1):
                    j = 2 * pair + half
                    shift = HALO * j - (LANES - HALO) * side
                    h = hx[own + z, pl.ds(8 + 8 * j, 8), pl.ds(c0, LANES)]
                    t = tx[own + z, pl.ds(8 + 8 * j, 8), pl.ds(c0, LANES)]
                    if side == 0:
                        both = jnp.where(lane >= HALO - 2, roll(t, HALO - 2, 1), h)
                    else:
                        both = jnp.where(lane < LANES - HALO + 2, roll(t, 2 - HALO, 1), h)
                    here = group == j
                    kept = jnp.where(here, roll(both, shift, 1), kept)
                    for a in range(4):
                        piece = tiles[a][8 * half:8 * half + 8]
                        fields[a] = jnp.where(here, roll(piece, shift, 1), fields[a])
            s_ef[side, z] = kept
            s_eb[side, z, pl.ds(0, 16)] = jnp.concatenate(fields[:2], axis=0).astype(BF16)
            s_eb[side, z, pl.ds(16, 16)] = jnp.concatenate(fields[2:], axis=0).astype(BF16)
            r0 = (rows - 8) * side
            h = hx[own + z, pl.ds(8 + r0, 8), inside_cols]
            t = tx[own + z, pl.ds(8 + r0, 8), inside_cols]
            edge = [
                ref[own + z, pl.ds((rows - 16) * side, 16), :].astype(F32)[8 * side:8 * side + 8]
                for ref in staged
            ]
            if side == 0:
                both = jnp.where(wide_sub == 5, roll(edge[1], 1, 0), h)
                both = jnp.where(wide_sub >= 6, roll(t, 6, 0), both)
                first = jnp.where(wide_sub < 4, edge[0], roll(edge[1], 4, 0))
                second = jnp.where(wide_sub < 4, edge[2], roll(edge[3], 4, 0))
            else:
                both = jnp.where(wide_sub == 2, roll(edge[1], 7, 0), h)
                both = jnp.where(wide_sub < 2, roll(t, 2, 0), both)
                first = jnp.where(wide_sub < 4, roll(edge[0], 4, 0), edge[1])
                second = jnp.where(wide_sub < 4, roll(edge[2], 4, 0), edge[3])
            s_nf[side, z] = both
            s_nb[side, z] = jnp.concatenate([first, second], axis=0).astype(BF16)
        return carry

    lax.fori_loop(0, depth, pack, 0)

    for r in (0, 1):
        for c in (0, 1):
            c0 = last * c
            kept = jnp.zeros((8, LANES), F32)
            mixed = jnp.zeros((8, LANES), F32)
            for z in range(depth):
                both = s_nf[r, z, :, pl.ds(c0, LANES)]
                kept = jnp.where(group == z, roll(both, HALO * z - (LANES - HALO) * c, 1), kept)
                pieces = s_nb[r, z, :, pl.ds(c0, LANES)].astype(F32)
                for half in (0, 1):
                    slot = half * depth + z
                    moved = roll(
                        pieces[8 * half:8 * half + 8], HALO * slot - (LANES - HALO) * c, 1
                    )
                    mixed = jnp.where(group == slot, moved, mixed)
            s_cf[2 * r + c] = jnp.concatenate([kept, mixed], axis=0)

    pl.semaphore_wait(barrier, len(greeted))

    sent = [0]

    def send(src_ref, dst_ref, device):
        copy = pltpu.make_async_remote_copy(
            src_ref=src_ref,
            dst_ref=dst_ref,
            send_sem=send_sem.at[sent[0]],
            recv_sem=recv_sem.at[sent[0]],
            device_id=device,
            device_id_type=MESH,
        )
        sent[0] += 1
        copy.start()
        return copy

    norths, easts, corners = [], [], []
    for side in (0, 1):
        norths.append(send(s_nb.at[side], nbs.at[0, side], to_north[side]))
        norths.append(
            send(s_nf.at[side], hx.at[own_layers, edge_rows[side], inside_cols], to_north[side])
        )
    for d in range(4):
        corners.append(send(s_cf.at[d], cfs.at[0, d], to_corner[d]))
    for side in (0, 1):
        easts.append(send(s_eb.at[side], ebs.at[0, side], to_east[side]))
        easts.append(send(s_ef.at[side], efs.at[0, side], to_east[side]))
    two = (depth - 2) * (1 - me_l)
    blocks = [send(fields[2 + a], staged[a].at[own_layers], partner) for a in range(4)]
    blocks.append(send(fields[0], hx.at[own_layers, inner, inside_cols], partner))
    blocks.append(
        send(
            fields[1].at[pl.ds(two, 2)], tx.at[pl.ds(own + two, 2), inner, inside_cols], partner
        )
    )

    for copy in well_loads:
        copy.wait()
    wells[...] = jnp.full(wells.shape, -1e6, F32)
    width = pl.ds(0, well_rows[0].shape[1])
    for row, ref in enumerate(well_rows[:5]):
        wells[pl.ds(row, 1), width] = ref[...].astype(F32)
    band = well_rows[5][...]
    bands = well_rows[7][...]
    price = jnp.zeros(band.shape, F32)
    for b in range(bands.shape[1]):
        price = jnp.where(band == b, bands[0:1, b:b + 1], price)
    wells[pl.ds(5, 1), width] = price
    wells[pl.ds(6, 1), width] = well_rows[6][...]

    at_east = wells[0:1, :] - (me_e * cols).astype(F32)
    at_north = wells[1:2, :] - (me_n * rows).astype(F32)
    near = (
        (at_east >= -REACH) & (at_east < cols + REACH)
        & (at_north >= -REACH) & (at_north < rows + REACH)
    )
    mine = (at_east >= 0) & (at_east < cols) & (at_north >= 0) & (at_north < rows)
    near_row = jnp.where(near, 1.0, 0.0)
    near_tile = jnp.concatenate(
        [near_row[:, LANES * k:LANES * (k + 1)] for k in range(groups)], axis=0
    )
    before = (iota((LANES, LANES), 0) < iota((LANES, LANES), 1)).astype(F32).astype(BF16)
    in_row = dot(near_tile.astype(BF16), before, NN)
    above = (iota((groups, groups), 1) < iota((groups, groups), 0)).astype(F32).astype(BF16)
    rows_above = jnp.sum(dot(above, near_tile.astype(BF16), NN), axis=1, keepdims=True)
    rank = jnp.where(near_tile > 0, in_row + rows_above, -1.0)
    found = jnp.sum(jnp.sum(near_tile, axis=1, keepdims=True), axis=0, keepdims=True)
    crowded = jnp.where(found > SLOTS, 1.0, 0.0)

    place = jnp.concatenate(
        [
            jnp.where(at_east < 0, at_east + ext_cols, at_east),
            at_north + 8.0,
            wells[2:7, :],
            jnp.where(mine, 1.0, 0.0),
        ],
        axis=0,
    )
    place_parts = jnp.concatenate([p.astype(F32) for p in split(place, 3)], axis=0).astype(BF16)
    slot_of = iota((SLOTS, LANES), 0).astype(F32)

    for k in range(groups):
        pt[:, pl.ds(LANES * k, LANES)] = jnp.where(slot_of == rank[k:k + 1, :], 1.0, 0.0).astype(BF16)
    three = dot(place_parts, pt[...], NT)
    comp = three[0:8] + three[8:16] + three[16:24]
    col_hot = jnp.where(iota((ext_cols, SLOTS), 0).astype(F32) == comp[0:1], 1.0, 0.0)
    row_hot = jnp.where(iota((ext_rows, SLOTS), 0).astype(F32) == comp[1:2], 1.0, 0.0)
    col_hot = col_hot.astype(BF16)


    def fill_inner(base):
        def fill(z, carry):
            for dst, ref in zip((ke, kn, kv, st), staged):
                dst[base + z, inner, inside_cols] = ref[base + z].astype(F32)
            return carry

        lax.fori_loop(0, depth, fill, 0)

    def fill_east(who, base):
        def fill(z, carry):
            zz = base + z
            right, left = efs[who, 0, z], efs[who, 1, z]
            for j in range(rows // 8):
                both = jnp.where(
                    low_half, roll(right, -HALO * j, 1), roll(left, LANES - HALO - HALO * j, 1)
                )
                hx[zz, pl.ds(8 + 8 * j, 8), extra] = both
                tx[zz, pl.ds(8 + 8 * j, 8), extra] = jnp.where(
                    low_half, roll(both, 2 - HALO, 1), roll(both, HALO - 2, 1)
                )
            for half, pair in ((0, (ke, kn)), (1, (kv, st))):
                rights = ebs[who, 0, z, pl.ds(16 * half, 16)].astype(F32)
                lefts = ebs[who, 1, z, pl.ds(16 * half, 16)].astype(F32)
                for k in (0, 1):
                    right, left = rights[8 * k:8 * k + 8], lefts[8 * k:8 * k + 8]
                    for j in range(rows // 8):
                        pair[k][zz, pl.ds(8 + 8 * j, 8), extra] = jnp.where(
                            low_half,
                            roll(right, -HALO * j, 1),
                            roll(left, LANES - HALO - HALO * j, 1),
                        )
            return carry

        lax.fori_loop(0, depth, fill, 0)

    def put_rows(side, zz, at_rows, at_cols, both, first, second):
        row = iota(both.shape, 0)
        if side == 0:
            tx[zz, at_rows, at_cols] = roll(both, 2, 0)
            ke[zz, at_rows, at_cols] = first
            kn[zz, at_rows, at_cols] = jnp.where(row == 4, roll(both, 7, 0), roll(first, 4, 0))
            kv[zz, at_rows, at_cols] = second
            st[zz, at_rows, at_cols] = roll(second, 4, 0)
        else:
            tx[zz, at_rows, at_cols] = roll(both, 6, 0)
            ke[zz, at_rows, at_cols] = roll(first, 4, 0)
            kn[zz, at_rows, at_cols] = jnp.where(row == 3, roll(both, 1, 0), first)
            kv[zz, at_rows, at_cols] = roll(second, 4, 0)
            st[zz, at_rows, at_cols] = second

    def fill_north(who, base):
        def fill(z, carry):
            for side, at_rows in enumerate(edge_rows):
                pieces = nbs[who, side, z].astype(F32)
                both = hx[base + z, at_rows, inside_cols]
                put_rows(side, base + z, at_rows, inside_cols, both, pieces[:8], pieces[8:])
            return carry

        lax.fori_loop(0, depth, fill, 0)

    def fill_corners(who, base):
        for side, at_rows in enumerate(edge_rows):
            right, rights = cfs[who, 2 * side, :8], cfs[who, 2 * side, 8:]
            left, lefts = cfs[who, 2 * side + 1, :8], cfs[who, 2 * side + 1, 8:]

            def taken(a, b, slot):
                return jnp.where(
                    low_half, roll(a, -HALO * slot, 1), roll(b, LANES - HALO - HALO * slot, 1)
                )

            for z in range(depth):
                both = taken(right, left, z)
                hx[base + z, at_rows, extra] = both
                put_rows(
                    side, base + z, at_rows, extra, both,
                    taken(rights, lefts, z), taken(rights, lefts, depth + z),
                )

    wide = (8, ext_cols)
    sub = iota(wide, 0)
    col = iota(wide, 1)
    closed_col = ((col == cols - 1) & (me_e == n_east - 1)) | ((col == ext_cols - 1) & (me_e == 0))
    open_east = jnp.where(closed_col, 0.0, 2.0)

    def east(v):
        return roll(v, ext_cols - 1, 1)

    def west(v):
        return roll(v, 1, 1)

    def north(now, after):
        return jnp.where(sub < 7, roll(now, 7, 0), roll(after, 7, 0))

    def south(now, prior):
        return jnp.where(sub > 0, roll(now, 1, 0), roll(prior, 1, 0))

    fu[0] = jnp.zeros((ext_rows, ext_cols), F32)
    fu[layers] = jnp.zeros((ext_rows, ext_cols), F32)

    def at(j):
        return pl.ds(8 * j if isinstance(j, int) else pl.multiple_of(8 * j, 8), 8)

    def next_of(j):
        return min(j + 1, chunks_of_rows - 1) if isinstance(j, int) else jnp.minimum(j + 1, chunks_of_rows - 1)

    def layer_of(k):
        return jnp.where(me_l == 0, k, layers - 1 - k)

    def start(first, count, with_wells):
        zs = [layer_of(first + i) for i in range(count)]
        above = layer_of(jnp.minimum(first + count, layers - 1))
        below = layer_of(jnp.maximum(first - 1, 0))
        opens = [jnp.where(first + i < layers - 1, 2.0, 0.0) for i in range(count)]

        def chunk(j, carry):
            f_priors, g_priors, k_now, h_now = carry
            k_ups = [kv[z, at(j)] for z in zs] + [kv[above, at(j)]]
            heads = h_now + [hx[above, at(j)]]
            edge = ((j == 0) & (me_n == 0)) | ((j == chunks_of_rows - 2) & (me_n == n_north - 1))
            opened = jnp.where((sub == 7) & edge, 0.0, 2.0)
            f_d = fu[zs[0] + me_l, at(j)]
            g_d = f_d * (h_now[0] - hx[below, at(j)])
            faces, flows, k_after, h_after = [], [], [], []
            for i, z in enumerate(zs):
                k_e, k_n, h = ke[z, at(j)], k_now[i], h_now[i]
                k_after.append(kn[z, at(next_of(j))])
                h_after.append(hx[z, at(next_of(j))])
                k_e2 = east(k_e)
                k_n2 = north(k_n, k_after[i])
                f_e = open_east * k_e * k_e2 * reciprocal(k_e + k_e2)
                f_n = opened * k_n * k_n2 * reciprocal(k_n + k_n2)
                f_u = opens[i] * k_ups[i] * k_ups[i + 1] * reciprocal(k_ups[i] + k_ups[i + 1])
                fe[z, at(j)] = f_e
                fn[z, at(j)] = f_n
                fu[z + 1 - me_l, at(j)] = f_u
                diagonal = st[z, at(j)] + f_e + west(f_e) + f_n + south(f_n, f_priors[i]) + f_u + f_d
                inverse = reciprocal(diagonal)
                inv[z, at(j)] = inverse
                g_e = f_e * (east(h) - h)
                g_n = f_n * (north(h, h_after[i]) - h)
                g_u = f_u * (heads[i + 1] - h)
                residual = (g_e - west(g_e)) + (g_n - south(g_n, g_priors[i])) + (g_u - g_d)
                if with_wells:
                    residual = residual - src[z, at(j)]
                d0[z, at(j)] = inverse * residual
                faces.append(f_n)
                flows.append(g_n)
                f_d, g_d = f_u, g_u
            return faces, flows, k_after, h_after

        def several(i, carry):
            for m in range(START_UNIT):
                carry = chunk(i * START_UNIT + m, carry)
            return carry

        none = [jnp.zeros(wide, F32)] * count
        carry = (none, none, [kn[z, at(0)] for z in zs], [hx[z, at(0)] for z in zs])
        lax.fori_loop(0, chunks_of_rows // START_UNIT, several, carry)

    def start_layers(begin, end, with_wells):
        def some(i, carry):
            start(begin + START_LAYERS * i, START_LAYERS, with_wells)
            return carry

        whole = (end - begin) // START_LAYERS
        lax.fori_loop(0, whole, some, 0)
        if begin + whole * START_LAYERS < end:
            start(begin + whole * START_LAYERS, end - begin - whole * START_LAYERS, with_wells)

    def pump(k, carry):
        z = layer_of(k)
        d0[z] = d0[z] - inv[z] * src[z]
        return carry

    fill_inner(own)
    for copy in easts:
        copy.wait_recv()
    forwards = [send(efs.at[0], efs.at[1], partner), send(ebs.at[0], ebs.at[1], partner)]
    fill_east(0, own)
    for copy in blocks:
        copy.wait_recv()
    fill_inner(other)
    for copy in norths:
        copy.wait_recv()
    forwards.append(send(nbs.at[0], nbs.at[1], partner))
    for side in (0, 1):
        place_of = hx.at[own_layers, edge_rows[side], inside_cols]
        forwards.append(send(place_of, place_of, partner))
    for copy in corners:
        copy.wait_recv()
    forwards.append(send(cfs.at[0], cfs.at[1], partner))
    fill_north(0, own)
    fill_corners(0, own)
    start_layers(0, depth - 1, False)
    for copy in forwards:
        copy.wait_recv()
    fill_east(1, other)
    fill_north(1, other)
    fill_corners(1, other)
    for copy in norths + easts + corners + blocks + forwards:
        copy.wait_send()

    weights = []
    for z in range(layers):
        found = dot(ke[z].astype(BF16), col_hot, NN)
        k_at = jnp.sum(found * row_hot, axis=0, keepdims=True)
        screened = (comp[2:3] <= z) & (comp[3:4] >= z)
        weights.append(jnp.where(screened, k_at, 0.0))
    weight = jnp.concatenate(weights, axis=0)
    total = jnp.sum(weight, axis=0, keepdims=True)
    share = weight / jnp.where(total > 0, total, 1.0)
    pumped = share * comp[4:5]
    priced = pumped * comp[5:6]
    col_two = jnp.concatenate([col_hot, col_hot], axis=1)
    for z in range(layers):
        left = []
        for value in (pumped, priced):
            top, rest = split(value[z:z + 1], 2)
            left.append(
                jnp.concatenate([row_hot * top.astype(F32), row_hot * rest.astype(F32)], axis=1)
            )
        left = jnp.concatenate(left, axis=0).astype(BF16)
        field = dot(left, col_two, NT)
        src[z] = field[:ext_rows]
        lw[z] = field[ext_rows:]

    lax.fori_loop(0, depth - 1, pump, 0)
    start_layers(depth - 1, layers, True)

    def sweep(field, margin, finish, chunk_from, chunk_to):
        first = (depth - margin) * me_l

        def together(i, count):
            zs = [first + i + k for k in range(count)]
            below = jnp.maximum(zs[0] - 1, 0)
            above = jnp.minimum(zs[-1] + 1, layers - 1)
            if chunk_from == 0:
                priors = [jnp.zeros(wide, F32)] * count
            else:
                before = at(chunk_from - 1)
                priors = [fn[z, before] * field[z, before] for z in zs]
            now = [field[z, at(chunk_from)] for z in zs]
            for j in range(chunk_from, chunk_to):
                after = [field[z, at(min(j + 1, chunks_of_rows - 1))] for z in zs]
                stack = [field[below, at(j)]] + now + [field[above, at(j)]]
                for k, z in enumerate(zs):
                    d = now[k]
                    f_e, f_n = fe[z, at(j)], fn[z, at(j)]
                    b = f_n * d
                    moved = f_e * east(d) + west(f_e * d)
                    moved = moved + f_n * north(d, after[k]) + south(b, priors[k])
                    moved = moved + fu[z + 1, at(j)] * stack[k + 2] + fu[z, at(j)] * stack[k]
                    finish(i + k, z, j, d, inv[z, at(j)] * moved)
                    priors[k] = b
                now = after

        def some(i, carry):
            together(SWEEP_LAYERS * i, SWEEP_LAYERS)
            return carry

        total = depth + margin
        lax.fori_loop(0, total // SWEEP_LAYERS, some, 0)
        if total % SWEEP_LAYERS:
            together(total - total % SWEEP_LAYERS, total % SWEEP_LAYERS)

    (a1, b1), (a2, b2) = steps_of()

    def first_sweep(i, z, j, d, pulled):
        s1[z, at(j)] = pulled
        d1[z, at(j)] = a1 * d + b1 * pulled

    def end_forward(i, z, j, d, pulled):
        s2 = s1[z, at(j)] - d + pulled
        d2 = a2 * d + b2 * s2
        new = hx[z, at(j)] + d0[z, at(j)] + d + d2
        hx[z, at(j)] = new
        load = new - tx[z, at(j)] - lw[z, at(j)]
        src[z, at(j)] = inv[z, at(j)] * load

    sweep(d0, 3, first_sweep, 0, chunks_of_rows)
    sweep(d1, 2, end_forward, 0, chunks_of_rows)
    sweep(src, 1, first_sweep, 0, chunks_of_rows)

    st[0, at(0)] = jnp.zeros(wide, F32)

    def end_adjoint(i, z, j, d, pulled):
        s2 = s1[z, at(j)] - d + pulled
        d2 = a2 * d + b2 * s2
        adj = src[z, at(j)] + d + d2
        adjoint[i, at(j - 1)] = adj[:, :cols]
        new = hx[z, at(j), inside_cols]
        head_new[i, at(j - 1)] = new
        departure = new - tx[z, at(j), inside_cols]
        st[0, at(0), inside_cols] = st[0, at(0), inside_cols] + departure * departure

    sweep(d1, 0, end_adjoint, 1, chunks_of_rows - 1)

    squared = st[0, at(0), inside_cols]
    squared = jnp.sum(squared, axis=0, keepdims=True)
    squared = sum(squared[:, LANES * k:LANES * (k + 1)] for k in range(cols // LANES))
    squared = squared * (1.0 / (float(layers * rows * cols) * n_east * n_north))
    base_layer = jnp.where(me_l == 0, 1.0, 0.0)

    col_hot, row_hot = col_hot[:cols], row_hot[8:8 + rows]
    head_at = jnp.zeros((1, SLOTS), F32)
    adj_at = jnp.zeros((1, SLOTS), F32)
    for i in range(depth):
        z_share = jnp.where(me_l == 0, share[i:i + 1], share[depth + i:depth + i + 1])
        stack = split(head_new[i], 2) + split(adjoint[i], 2)
        found = [dot(piece, col_hot, NN) for piece in stack]
        head_at += z_share * jnp.sum((found[0] + found[1]) * row_hot, axis=0, keepdims=True)
        adj_at += z_share * jnp.sum((found[2] + found[3]) * row_hot, axis=0, keepdims=True)
    lift = (comp[6:7] * base_layer - head_at) * comp[7:8]
    priced = comp[5:6] * lift
    slope = priced - adj_at * comp[7:8]
    three = jnp.concatenate(
        [p.astype(F32) for p in split(slope, 3)] + [jnp.zeros((5, SLOTS), F32)], axis=0
    ).astype(BF16)
    spread = dot(three, pt[...], NN)
    spread = spread[0:1] + spread[1:2] + spread[2:3]
    tile = jnp.concatenate(
        [spread[:, LANES * k:LANES * (k + 1)] for k in range(groups)], axis=0
    )
    parts[pl.ds(0, groups)] = tile
    parts[pl.ds(groups, 8)] = jnp.concatenate(
        [
            priced * comp[4:5],
            squared,
            jnp.broadcast_to(crowded, (1, LANES)),
            jnp.zeros((5, LANES), F32),
        ],
        axis=0,
    )

    total = parts[...]
    used = 0
    for box, mine, peers in phases:
        box[mine] = total
        copies = []
        for device in peers:
            copy = pltpu.make_async_remote_copy(
                src_ref=box.at[mine],
                dst_ref=box.at[mine],
                send_sem=sum_send.at[used],
                recv_sem=sum_recv.at[used],
                device_id=device,
                device_id_type=MESH,
            )
            copy.start()
            copies.append(copy)
            used += 1
        for copy in copies:
            copy.wait()
        total = box[0]
        for k in range(1, len(peers) + 1):
            total = total + box[k]
    n_wells = out_slope.shape[1]
    for k in range(groups):
        width = min(LANES, n_wells - LANES * k)
        out_slope[:, pl.ds(LANES * k, width)] = total[k:k + 1, :width]
    sums = jnp.sum(total[groups:], axis=1, keepdims=True)
    out_sums[...] = jnp.broadcast_to(sums, out_sums.shape)
    out_crowded[...] = sums[2:3]


def run_kernel(sizes, fields, wells):
    depth, rows, cols = fields[0].shape
    layers, ext_rows, ext_cols = 2 * depth, rows + 16, cols + LANES
    n_wells = wells[0].shape[1]
    groups = -(-n_wells // LANES)
    n_east, n_x, n_z = sizes
    block = pltpu.VMEM((depth, rows, cols), F32)
    ext = pltpu.VMEM((layers, ext_rows, ext_cols), F32)
    operands = (*fields, *wells)
    copies = 4 + 4 + 4 + 6 + 6
    peers = 1 + n_z + n_east + n_x - 3
    return pl.pallas_call(
        functools.partial(kernel, sizes),
        out_shape=[
            block, block, pltpu.VMEM((1, n_wells), F32), pltpu.VMEM((8, LANES), F32),
            jax.ShapeDtypeStruct((1, 1), F32),
        ],
        in_specs=[pl.BlockSpec(memory_space=pltpu.HBM)] * len(operands),
        out_specs=[pl.BlockSpec(memory_space=pltpu.VMEM)] * 5,
        scratch_shapes=[ext] * 8
        + [pltpu.VMEM((layers + 1, ext_rows, ext_cols), F32)]
        + [ext] * 6
        + [pltpu.VMEM((SLOTS, groups * LANES), BF16)]
        + [pltpu.VMEM((groups + 8, LANES), F32)]
        + [pltpu.VMEM((layers, rows, cols), BF16)] * 4
        + [
            pltpu.VMEM((2, 2, depth, 16, cols), BF16),
            pltpu.VMEM((2, 2, depth, 8, LANES), F32),
            pltpu.VMEM((2, 2, depth, 32, LANES), BF16),
            pltpu.VMEM((2, 4, 16, LANES), F32),
            pltpu.VMEM((2, depth, 8, cols), F32),
            pltpu.VMEM((2, depth, 16, cols), BF16),
            pltpu.VMEM((2, depth, 8, LANES), F32),
            pltpu.VMEM((2, depth, 32, LANES), BF16),
            pltpu.VMEM((4, 16, LANES), F32),
        ]
        + [pltpu.VMEM(w.shape, w.dtype) for w in wells]
        + [pltpu.VMEM((8, groups * LANES), F32)]
        + [pltpu.VMEM((n, groups + 8, LANES), F32) for n in (2, n_z, n_east, n_x)]
        + [pltpu.SemaphoreType.DMA((14,))]
        + [pltpu.SemaphoreType.DMA((copies,))] * 2
        + [pltpu.SemaphoreType.DMA((peers,))] * 2,
        compiler_params=pltpu.CompilerParams(
            collective_id=0, has_side_effects=True, vmem_limit_bytes=60 * 1024 * 1024
        ),
        name="whole_step",
    )(*operands)


def hand_over(new, adjoint, slope, sums, o_new, o_adjoint, o_slope, o_cost, o_misfit, cost, misfit, sem):
    cost[...] = sums[0:1, 0:1]
    misfit[...] = sums[1:2, 0:1]
    copies = [
        pltpu.make_async_copy(src_ref, dst_ref, sem.at[k])
        for k, (src_ref, dst_ref) in enumerate((
            (new, o_new), (adjoint, o_adjoint), (slope, o_slope), (cost, o_cost), (misfit, o_misfit),
        ))
    ]
    for copy in copies:
        copy.start()
    for copy in copies:
        copy.wait()


def run_hand_over(new, adjoint, slope, sums):
    block = jax.ShapeDtypeStruct(new.shape, F32)
    one = jax.ShapeDtypeStruct((1, 1), F32)
    return pl.pallas_call(
        hand_over,
        out_shape=[block, block, jax.ShapeDtypeStruct(slope.shape, F32), one, one],
        in_specs=[pl.BlockSpec(memory_space=pltpu.VMEM)] * 4,
        out_specs=[pl.BlockSpec(memory_space=pltpu.HBM)] * 5,
        scratch_shapes=[pltpu.VMEM((1, 1), F32)] * 2 + [pltpu.SemaphoreType.DMA((5,))],
        compiler_params=pltpu.CompilerParams(vmem_limit_bytes=8 * 1024 * 1024),
        name="hand_over",
    )(new, adjoint, slope, sums)


def in_order(value):
    return with_layout_constraint(value, Layout(major_to_minor=(0, 1, 2)))


def per_device(sizes, *arguments):
    fields = arguments[:6]
    e, n, top, bottom, tariff, rates, ground, prices = arguments[6:]
    wells = [w.reshape(1, -1) for w in (e, n, top, bottom, rates, tariff, ground, prices)]
    *results, crowded = run_kernel(sizes, fields, wells)
    found = tuple(run_hand_over(*results))

    def again(state):
        blocks = [in_order(x) for x in fields]
        first, second, *others = plain(*blocks, *arguments[6:])
        others = [x.reshape(1, -1) for x in others]
        return jnp.zeros((), F32), (in_order(first), in_order(second), *others)

    _, found = lax.while_loop(lambda state: state[0] > 0, again, (crowded.reshape(()), found))
    new, adjoint, slope, cost, misfit = found
    return new, adjoint, slope.reshape(-1), cost.reshape(()), misfit.reshape(())


def solution(mesh):
    field = P("layer", "north", "east")
    n_north = mesh.shape["north"]
    n_x = 4 if n_north % 4 == 0 else 1
    sizes = (mesh.shape["east"], n_x, n_north // n_x)
    return jax.shard_map(
        functools.partial(per_device, sizes),
        mesh=mesh,
        in_specs=(field,) * 6 + (P(),) * 8,
        out_specs=(field, field, P(), P(), P()),
        check_vma=False,
    )
```
